32 devices in a mesh: dp: 16 (over z, y, core), tensor: 2 (over x).
Axes of the slice: x: 2, y: 2, z: 4, core: 2. Of those that a mesh axis runs over, the one named last changes fastest.
Arguments:
- tokens: bfloat16 [1, 16384, 1024], P(None, 'dp', 'tensor'), may hold values from -6 to 6
- cotangent: bfloat16 [1, 16384, 1024], P(None, 'dp', 'tensor'), may hold values from -6 to 6
- segments: int32 [1, 16384], P(None, 'dp'), may hold values from 0 to 7, as said below
- owners: int32 [6], replicated, may hold values from 0 to 3, as said below
- attn_master: float32 [2, 4096, 1024], P(None, 'dp', 'tensor')
- attn_first: float32 [2, 4096, 1024], P(None, 'dp', 'tensor')
- attn_second: float32 [2, 4096, 1024], P(None, 'dp', 'tensor'), as said below
- mlp_master: float32 [1, 4096, 4096], P(None, 'dp', 'tensor')
- mlp_first: float32 [1, 4096, 4096], P(None, 'dp', 'tensor')
- mlp_second: float32 [1, 4096, 4096], P(None, 'dp', 'tensor'), as said below
- ssm_params: float32 [3, 1024, 16], P(None, 'tensor'), as said below
- ssm_first: float32 [3, 1024, 16], P(None, 'tensor')
- ssm_second: float32 [3, 1024, 16], P(None, 'tensor'), as said below
- norm_gains: float32 [2, 1024], P(None, 'tensor'), may hold values from 0.5 to 1.5
- gains_first: float32 [2, 1024], P(None, 'tensor')
- gains_second: float32 [2, 1024], P(None, 'tensor'), as said below
Outputs:
- block_out: bfloat16 [1, 16384, 1024], P(None, 'dp', 'tensor')
- grad_tokens: float32 [1, 16384, 1024], P(None, 'dp', 'tensor')
- attn_grad: float32 [2, 4096, 1024], P(None, 'dp', 'tensor')
- attn_first_new: float32 [2, 4096, 1024], P(None, 'dp', 'tensor')
- attn_second_new: float32 [2, 4096, 1024], P(None, 'dp', 'tensor')
- attn_new: float32 [2, 4096, 1024], P(None, 'dp', 'tensor')
- attn_new_low: bfloat16 [2, 4096, 1024], P(None, 'dp', 'tensor')
- mlp_grad: float32 [1, 4096, 4096], P(None, 'dp', 'tensor')
- mlp_first_new: float32 [1, 4096, 4096], P(None, 'dp', 'tensor')
- mlp_second_new: float32 [1, 4096, 4096], P(None, 'dp', 'tensor')
- mlp_new: float32 [1, 4096, 4096], P(None, 'dp', 'tensor')
- mlp_new_low: bfloat16 [1, 4096, 4096], P(None, 'dp', 'tensor')
- ssm_grad: float32 [3, 1024, 16], P(None, 'tensor')
- ssm_first_new: float32 [3, 1024, 16], P(None, 'tensor')
- ssm_second_new: float32 [3, 1024, 16], P(None, 'tensor')
- ssm_new: float32 [3, 1024, 16], P(None, 'tensor')
- gains_grad: float32 [2, 1024], P(None, 'tensor')
- gains_first_new: float32 [2, 1024], P(None, 'tensor')
- gains_second_new: float32 [2, 1024], P(None, 'tensor')
- gains_new: float32 [2, 1024], P(None, 'tensor')
The draws below stay inside these ranges and needn't reach their ends.
Inputs may be any that keep to these rules, and one draw needn't show every extreme that they name: `segments`: in each row ids start at 0, never fall, and each row holds exactly 8 documents. No group owns more than 2 of the first four matrices, and one group owns exactly that many; no group owns more than 1 of the last two, so these two have different owners. `attn_second`: positive. `mlp_second`: positive. `ssm_params`: the first row lies between -log(512) / 2 and log(512) / 2. `ssm_second`: positive. `gains_second`: positive.
All inputs are finite; a program needn't handle non-finite values.
Results may differ from the reference program's by a relative error of at most 0.012.
Values may be sent and summed in bfloat16 or wider, within the bound.
No kernel may reach another device: no remote copies, remote signals or barrier semaphores. Data moves between devices by JAX's collectives and lax.ppermute only.
A program may use at most 448 MiB of HBM per device.

```python
import math
import jax
import jax.numpy as jnp
from jax import lax

D = 1024
HEADS = 8
HEAD_DIM = 128
FF = 4096
STATE = 16
CTX = 128
BL = 512
OWNER_GROUPS = 4
ATTN_SLOTS = 2
MLP_SLOTS = 1
STEP = 5
ROWS = 1
ROW_LEN = 16384
TOKENS = 16384
DOCS = 8


attn_grad_scales = [0.5, 0.5, 1.0, 0.1]


mlp_grad_scales = [0.3, 0.6]


ssm_grad_scales = [0.05, 0.3, 0.3]


gain_grad_scales = [0.5, 0.5]


def bounded_normal(key, shape):
    return jax.random.truncated_normal(key, -4.0, 4.0, shape, jnp.float32)


def scale_column(scale_list, rank):
    return jnp.asarray(scale_list, jnp.float32).reshape((-1,) + (1,) * (rank - 1))


def owner_list(key):
    key_groups, key_order, key_mlp = jax.random.split(jax.random.fold_in(key, 7), 3)
    groups = jax.random.permutation(key_groups, OWNER_GROUPS).astype(jnp.int32)
    attn_part = jnp.stack([groups[0], groups[0], groups[1], groups[2]])
    attn_part = attn_part[jax.random.permutation(key_order, 4)]
    mlp_part = jax.random.permutation(key_mlp, OWNER_GROUPS).astype(jnp.int32)[:2]
    return jnp.concatenate([attn_part, mlp_part]).astype(jnp.int32)


def slot_numbers_drawn(owner_part):
    count = owner_part.shape[0]
    order = jnp.arange(count, dtype=jnp.int32)
    earlier = (order[None, :] < order[:, None]).astype(jnp.int32)
    same = (owner_part[:, None] == owner_part[None, :]).astype(jnp.int32)
    return jnp.sum(same * earlier, axis=1).astype(jnp.int32)


def slot_values_drawn(owner_part, value_list, slot_count, fallback):
    slots = slot_numbers_drawn(owner_part)
    slot_hit = slots[:, None, None] == jnp.arange(slot_count, dtype=jnp.int32)[None, :, None]
    group_hit = owner_part[:, None, None] == jnp.arange(OWNER_GROUPS, dtype=jnp.int32)[None, None, :]
    hits = jnp.logical_and(slot_hit, group_hit).astype(jnp.float32)
    values = jnp.asarray(value_list, jnp.float32)[:, None, None]
    table = jnp.sum(hits * values, axis=0) + (1.0 - jnp.sum(hits, axis=0)) * fallback
    return jnp.repeat(table, D, axis=1)[:, :, None]


def attn_scales(key, value_list, fallback):
    return slot_values_drawn(owner_list(key)[:4], value_list, ATTN_SLOTS, fallback)


def mlp_scales(key, value_list, fallback):
    return slot_values_drawn(owner_list(key)[4:], value_list, MLP_SLOTS, fallback)


def first_bank(key, shape, scales):
    return bounded_normal(key, shape) * scales * (math.sqrt(TOKENS) * 0.1 / 0.9)


def second_bank(key, shape, scales):
    factor = jnp.exp(jax.random.uniform(key, shape, jnp.float32, 0.0, math.log(4.0)))
    return factor * scales * scales * (TOKENS * 0.05 / 0.95)


def first_moment(key, shape, grad_scales):
    return bounded_normal(key, shape) * scale_column(grad_scales, len(shape)) * (math.sqrt(TOKENS) * 0.1 / 0.9)


def second_moment(key, shape, grad_scales):
    factor = jnp.exp(jax.random.uniform(key, shape, jnp.float32, 0.0, math.log(4.0)))
    squares = scale_column(grad_scales, len(shape)) * scale_column(grad_scales, len(shape))
    return factor * squares * (TOKENS * 0.05 / 0.95)


def draw_segments(key, part):
    packed_rows = []
    for row_number in range(ROWS):
        order = jax.random.permutation(jax.random.fold_in(key, 60 + row_number), ROW_LEN - 1).astype(jnp.int32) + 1
        marks = jnp.zeros((ROW_LEN,), jnp.int32).at[order[:DOCS - 1]].set(1)
        packed_rows.append(jnp.cumsum(marks).astype(jnp.int32))
    return jnp.stack(packed_rows).astype(jnp.int32)


def draw_owners(key, part):
    return owner_list(key)


def draw_attn_master(key, part):
    scales = attn_scales(key, [D ** (-0.5)] * 3 + [(D // 16) ** (-0.5)], D ** (-0.5))
    return bounded_normal(jax.random.fold_in(key, 11), (ATTN_SLOTS, OWNER_GROUPS * D, D)) * scales


def draw_attn_first(key, part):
    scales = attn_scales(key, attn_grad_scales, 0.5)
    return first_bank(jax.random.fold_in(key, 12), (ATTN_SLOTS, OWNER_GROUPS * D, D), scales)


def draw_attn_second(key, part):
    scales = attn_scales(key, attn_grad_scales, 0.5)
    return second_bank(jax.random.fold_in(key, 13), (ATTN_SLOTS, OWNER_GROUPS * D, D), scales)


def draw_mlp_master(key, part):
    scales = mlp_scales(key, [D ** (-0.5), FF ** (-0.5)], D ** (-0.5))
    return bounded_normal(jax.random.fold_in(key, 21), (MLP_SLOTS, OWNER_GROUPS * D, FF)) * scales


def draw_mlp_first(key, part):
    scales = mlp_scales(key, mlp_grad_scales, 0.3)
    return first_bank(jax.random.fold_in(key, 22), (MLP_SLOTS, OWNER_GROUPS * D, FF), scales)


def draw_mlp_second(key, part):
    scales = mlp_scales(key, mlp_grad_scales, 0.3)
    return second_bank(jax.random.fold_in(key, 23), (MLP_SLOTS, OWNER_GROUPS * D, FF), scales)


def draw_ssm_params(key, part):
    key_rate, key_drive, key_read = jax.random.split(jax.random.fold_in(key, 31), 3)
    half_range = 0.5 * math.log(BL)
    log_rates = jax.random.uniform(key_rate, (1, D, STATE), jnp.float32, -half_range, half_range)
    drive_part = bounded_normal(key_drive, (1, D, STATE))
    readout = bounded_normal(key_read, (1, D, STATE)) * 0.25
    return jnp.concatenate([log_rates, drive_part, readout], axis=0)


def draw_ssm_first(key, part):
    return first_moment(jax.random.fold_in(key, 32), (3, D, STATE), ssm_grad_scales)


def draw_ssm_second(key, part):
    return second_moment(jax.random.fold_in(key, 33), (3, D, STATE), ssm_grad_scales)


def draw_gains_first(key, part):
    return first_moment(jax.random.fold_in(key, 42), (2, D), gain_grad_scales)


def draw_gains_second(key, part):
    return second_moment(jax.random.fold_in(key, 43), (2, D), gain_grad_scales)


def levels(stream_key, extent, cuts, low, top_value):
    loudness = 1.0
    for axis_at, shards_of in cuts:
        heights = jax.random.uniform(jax.random.fold_in(jax.random.fold_in(stream_key, 6), axis_at), (shards_of,), jnp.float32, low / len(cuts), top_value / len(cuts))
        loudness = loudness * jnp.repeat(jnp.exp(heights), extent[axis_at] // shards_of).reshape((-1,) + (1,) * (len(extent) - 1 - axis_at))
    return loudness


def noise(key, shape, spread, limit, shards=(), kind=jnp.bfloat16):
    loudness = levels(key, shape, shards, -0.22, 0.18) if shards else 1.0
    entries = jax.random.normal(key, shape, jnp.float32) * spread * loudness
    return jnp.minimum(jnp.maximum(entries, -limit), limit).astype(kind)


def setup_inputs(seed: int = 0) -> dict:
    key_of = jax.random.split(jax.random.key(seed), 17)
    tokens = noise(key_of[0], (ROWS, ROW_LEN, D), 1.0, 6.0, ((1, 16), (2, 2)))
    cotangent = noise(key_of[1], (ROWS, ROW_LEN, D), 1.0, 6.0, ((1, 16), (2, 2)))
    segments = draw_segments(jax.random.fold_in(key_of[16], 71), 0)
    owners = draw_owners(jax.random.fold_in(key_of[16], 71), 0)
    attn_master = draw_attn_master(jax.random.fold_in(key_of[16], 71), 0)
    attn_first = draw_attn_first(jax.random.fold_in(key_of[16], 71), 0)
    attn_second = draw_attn_second(jax.random.fold_in(key_of[16], 71), 0)
    mlp_master = draw_mlp_master(jax.random.fold_in(key_of[16], 71), 0)
    mlp_first = draw_mlp_first(jax.random.fold_in(key_of[16], 71), 0)
    mlp_second = draw_mlp_second(jax.random.fold_in(key_of[16], 71), 0)
    ssm_params = draw_ssm_params(jax.random.fold_in(key_of[16], 71), 0)
    ssm_first = draw_ssm_first(jax.random.fold_in(key_of[16], 71), 0)
    ssm_second = draw_ssm_second(jax.random.fold_in(key_of[16], 71), 0)
    norm_gains = jnp.clip(1.0 + 0.1 * jax.random.normal(key_of[13], (2, D), jnp.float32), 0.5, 1.5)
    gains_first = draw_gains_first(jax.random.fold_in(key_of[16], 71), 0)
    gains_second = draw_gains_second(jax.random.fold_in(key_of[16], 71), 0)
    return {"tokens": tokens, "cotangent": cotangent, "segments": segments, "owners": owners, "attn_master": attn_master, "attn_first": attn_first, "attn_second": attn_second, "mlp_master": mlp_master, "mlp_first": mlp_first, "mlp_second": mlp_second, "ssm_params": ssm_params, "ssm_first": ssm_first, "ssm_second": ssm_second, "norm_gains": norm_gains, "gains_first": gains_first, "gains_second": gains_second}


@jax.custom_vjp
def low(v):
    return lax.optimization_barrier(v.astype(jnp.bfloat16)).astype(jnp.float32)

@jax.custom_vjp
def low_back(v):
    return v

def low_keep(v):
    return (low(v), None)

def low_pass(kept, grad):
    return (grad,)

def back_keep(v):
    return (v, None)

def back_low(kept, grad):
    return (low(grad),)
low.defvjp(low_keep, low_pass)
low_back.defvjp(back_keep, back_low)
epsilon_norm = 1e-05
beta_first = 0.9
beta_second = 0.95
epsilon_adam = 1e-08
matrix_decay = 0.1
masked_score = -1e+30
highest = lax.Precision.HIGHEST

def rounded_both(values):
    return low_back(low(values))

def matmul_high(left, right):
    return jnp.dot(left, right, precision=highest)

def rms_norm(values, gain_row):
    return values * lax.rsqrt(lax.optimization_barrier(jnp.mean(values * values, axis=-1, keepdims=True)) + epsilon_norm) * gain_row

def activation(values):
    return jax.nn.gelu(values, approximate=True)

def decay_rates(log_rates):
    return jnp.exp(log_rates) * (BL ** (-0.5) / 32.0)

def rate_column(rate_list, rank):
    return jnp.asarray(rate_list, jnp.float32).reshape((-1,) + (1,) * (rank - 1))

def slot_numbers(owner_part):
    count = owner_part.shape[0]
    order = jnp.arange(count, dtype=jnp.int32)
    earlier = (order[None, :] < order[:, None]).astype(jnp.int32)
    same = (owner_part[:, None] == owner_part[None, :]).astype(jnp.int32)
    return lax.optimization_barrier(jnp.sum(same * earlier, axis=1)).astype(jnp.int32)

def slot_values(owner_part, value_list, slot_count, fallback):
    slots = slot_numbers(owner_part)
    slot_hit = slots[:, None, None] == jnp.arange(slot_count, dtype=jnp.int32)[None, :, None]
    group_hit = owner_part[:, None, None] == jnp.arange(OWNER_GROUPS, dtype=jnp.int32)[None, None, :]
    hits = jnp.logical_and(slot_hit, group_hit).astype(jnp.float32)
    values = jnp.asarray(value_list, jnp.float32)[:, None, None]
    return lax.optimization_barrier(jnp.sum(hits * values, axis=0)) + (1.0 - lax.optimization_barrier(jnp.sum(hits, axis=0))) * fallback

def pick_matrix(bank, slot, owner):
    return lax.dynamic_slice(bank, (slot.astype(jnp.int32), (owner * D).astype(jnp.int32), jnp.int32(0)), (1, D, bank.shape[2]))[0]

def adam_step(gradient, moment_one, moment_two, weight, step_count, rate_table, decay_weight):
    first_new = beta_first * moment_one + (1.0 - beta_first) * gradient
    second_new = beta_second * moment_two + (1.0 - beta_second) * gradient * gradient
    fixed_one = 1.0 - jnp.power(beta_first, step_count)
    fixed_two = 1.0 - jnp.power(beta_second, step_count)
    update = first_new / fixed_one / (jnp.sqrt(second_new / fixed_two) + epsilon_adam)
    return (first_new, second_new, weight - rate_table * (update + decay_weight * weight))

def ssm_outputs(hidden, keep_flags, params):
    decay_step = jnp.exp(-decay_rates(params[0]))
    drive_gain = jnp.sqrt(1.0 - decay_step * decay_step) * params[1]
    readout = params[2]

    def run_block(carried, block_item):
        block_rows, block_keep = block_item

        def advance(state_now, token_item):
            row_now, keep_now = token_item
            state_next = decay_step * keep_now * state_now + drive_gain * row_now[:, None]
            return (state_next, lax.optimization_barrier(jnp.sum(readout * state_next, axis=1)))
        return lax.scan(advance, carried, (block_rows, block_keep))
    initial = jnp.zeros(params.shape[1:], jnp.float32)
    _, outputs = lax.scan(jax.checkpoint(run_block), initial, (hidden.reshape(-1, BL, D), keep_flags.reshape(-1, BL)))
    return outputs.reshape(-1, D)

def attend_block(block_item):
    query_block, key_block, value_block, context_key, context_value, seg_block, ids_block = block_item
    query_heads = query_block.reshape(BL, HEADS, HEAD_DIM)
    key_heads = jnp.concatenate([context_key, key_block], axis=0).reshape(CTX + BL, HEADS, HEAD_DIM)
    value_heads = jnp.concatenate([context_value, value_block], axis=0).reshape(CTX + BL, HEADS, HEAD_DIM)
    raw = jnp.einsum('ihd,jhd->hij', query_heads, key_heads, precision=highest) * HEAD_DIM ** (-0.5)
    scores = low_back(raw)
    positions = jnp.arange(BL)
    local_ok = jnp.logical_and(positions[None, :] <= positions[:, None], seg_block[None, :] == seg_block[:, None])
    context_ok = ids_block[None, :] == seg_block[:, None] + 1
    allowed = jnp.concatenate([context_ok, local_ok], axis=1)
    scores = jnp.where(allowed[None], scores, masked_score)
    row_top = lax.optimization_barrier(jnp.max(scores, axis=2, keepdims=True))
    raised = jnp.exp(scores - row_top)
    probs = low(raised / lax.optimization_barrier(jnp.sum(raised, axis=2, keepdims=True)))
    mixed_rows = jnp.einsum('hij,jhd->ihd', probs, value_heads, precision=highest).reshape(BL, D)
    return rounded_both(mixed_rows)

def reference(tokens, cotangent, segments, owners, attn_master, attn_first, attn_second, mlp_master, mlp_first, mlp_second, ssm_params, ssm_first, ssm_second, norm_gains, gains_first, gains_second):
    block_row = ROW_LEN // BL
    block_total = ROWS * block_row
    seg_blocks = segments.reshape(ROWS, block_row, BL)
    context_ids = jnp.concatenate([jnp.zeros((ROWS, 1, CTX), jnp.int32), seg_blocks[:, :-1, BL - CTX:] + 1], axis=1).reshape(block_total, CTX)
    flat_blocks = seg_blocks.reshape(block_total, BL)
    previous = jnp.concatenate([segments[:, :1], segments[:, :-1]], axis=1)
    keep_flags = (segments == previous).astype(jnp.float32)
    attn_owner = owners[:4]
    mlp_owner = owners[4:]
    attn_slots = slot_numbers(attn_owner)
    mlp_slots = slot_numbers(mlp_owner)

    def forward(inputs, attn_bank, mlp_bank, ssm_values, gain_values):
        flat = inputs.reshape(TOKENS, D)
        hidden_one = low(rms_norm(flat, gain_values[0]))
        attn_low = low(attn_bank)
        mlp_low = low(mlp_bank)
        weight_query = pick_matrix(attn_low, attn_slots[0], attn_owner[0])
        weight_key = pick_matrix(attn_low, attn_slots[1], attn_owner[1])
        weight_value = pick_matrix(attn_low, attn_slots[2], attn_owner[2])
        weight_out = pick_matrix(attn_low, attn_slots[3], attn_owner[3])
        weight_in = pick_matrix(mlp_low, mlp_slots[0], mlp_owner[0])
        weight_down = pick_matrix(mlp_low, mlp_slots[1], mlp_owner[1])
        queries = rounded_both(matmul_high(hidden_one, weight_query))
        keys_tok = rounded_both(matmul_high(hidden_one, weight_key))
        values_tok = rounded_both(matmul_high(hidden_one, weight_value))
        states = jax.vmap(ssm_outputs, in_axes=(0, 0, None))(hidden_one.reshape(ROWS, ROW_LEN, D), keep_flags, ssm_values)
        tails = low(states.reshape(ROWS, block_row, BL, D)[:, :, BL - CTX:])
        context = jnp.concatenate([jnp.zeros((ROWS, 1, CTX, D), jnp.float32), tails[:, :-1]], axis=1).reshape(-1, D)
        context_keys = rounded_both(matmul_high(context, weight_key)).reshape(block_total, CTX, D)
        context_values = rounded_both(matmul_high(context, weight_value)).reshape(block_total, CTX, D)
        mixed = lax.map(jax.checkpoint(attend_block), (queries.reshape(block_total, BL, D), keys_tok.reshape(block_total, BL, D), values_tok.reshape(block_total, BL, D), context_keys, context_values, flat_blocks, context_ids)).reshape(TOKENS, D)
        middle = flat + low_back(matmul_high(mixed, weight_out.T))
        hidden_two = low(rms_norm(middle, gain_values[1]))
        pre_act = low_back(matmul_high(hidden_two, weight_in))
        act_low = low(activation(pre_act))
        return (middle + low_back(matmul_high(act_low, weight_down.T))).reshape(ROWS, ROW_LEN, D)
    block_value, pullback = jax.vjp(forward, tokens.astype(jnp.float32), attn_master, mlp_master, ssm_params, norm_gains)
    grad_tokens, attn_grad, mlp_grad, ssm_grad, gains_grad = pullback(cotangent.astype(jnp.float32))
    step_count = jnp.float32(STEP)
    attn_table = slot_values(attn_owner, [0.5 * D ** (-0.5)] * 3 + [0.5 * (D // 16) ** (-0.5)], ATTN_SLOTS, 0.5 * D ** (-0.5))
    mlp_table = slot_values(mlp_owner, [0.5 * D ** (-0.5), 0.5 * FF ** (-0.5)], MLP_SLOTS, 0.5 * D ** (-0.5))
    attn_rates = jnp.repeat(attn_table, D, axis=1)[:, :, None]
    mlp_rates = jnp.repeat(mlp_table, D, axis=1)[:, :, None]
    ssm_rates = rate_column([1.0, 0.8, 0.25], 3)
    gain_rates = rate_column([0.6, 0.6], 2)
    attn_one, attn_two, attn_new = adam_step(attn_grad, attn_first, attn_second, attn_master, step_count, attn_rates, matrix_decay)
    mlp_one, mlp_two, mlp_new = adam_step(mlp_grad, mlp_first, mlp_second, mlp_master, step_count, mlp_rates, matrix_decay)
    ssm_one, ssm_two, ssm_new = adam_step(ssm_grad, ssm_first, ssm_second, ssm_params, step_count, ssm_rates, 0.0)
    gain_one, gain_two, gains_new = adam_step(gains_grad, gains_first, gains_second, norm_gains, step_count, gain_rates, 0.0)
    return (block_value.astype(jnp.bfloat16), grad_tokens, attn_grad, attn_one, attn_two, attn_new, attn_new.astype(jnp.bfloat16), mlp_grad, mlp_one, mlp_two, mlp_new, mlp_new.astype(jnp.bfloat16), ssm_grad, ssm_one, ssm_two, ssm_new, gains_grad, gain_one, gain_two, gains_new)
```

```python
import functools
import itertools

import jax
import jax.numpy as jnp
from jax import lax
from jax.experimental import pallas as pl
from jax.experimental.pallas import tpu as pltpu
from jax.sharding import PartitionSpec as P

D = 1024
HEAD_DIM = 128
FF = 4096
STATE = 16
CTX = 128
BL = 512
OWNER_GROUPS = 4
STEP = 5

epsilon_norm = 1e-05
beta_first = 0.9
beta_second = 0.95
epsilon_adam = 1e-08
matrix_decay = 0.1
masked_score = -1e30
score_scale = HEAD_DIM ** (-0.5)
f32 = jnp.float32
bf16 = jnp.bfloat16
i32 = jnp.int32
VMEM_BYTES = 56 * 1024 * 1024
SWAP = [(0, 1), (1, 0)]
TILE = 256
QT = 128


def dot_nn(left, right):
    return lax.dot_general(left, right, (((1,), (0,)), ((), ())), preferred_element_type=f32)


def dot_nt(left, right):
    return lax.dot_general(left, right, (((1,), (1,)), ((), ())), preferred_element_type=f32)


def dot_tn(left, right):
    return lax.dot_general(left, right, (((0,), (0,)), ((), ())), preferred_element_type=f32)


def call(kernel, grid, in_specs, out_specs, out_shape, scratch=(), prefetch=0, flops=0, nbytes=0):
    return pl.pallas_call(
        kernel,
        grid_spec=pltpu.PrefetchScalarGridSpec(
            num_scalar_prefetch=prefetch,
            grid=grid,
            in_specs=in_specs,
            out_specs=out_specs,
            scratch_shapes=scratch,
        ),
        out_shape=out_shape,
        compiler_params=pltpu.CompilerParams(vmem_limit_bytes=VMEM_BYTES),
        cost_estimate=pl.CostEstimate(flops=flops, bytes_accessed=nbytes, transcendentals=0),
    )


def whole(shape):
    return pl.BlockSpec(shape, lambda *_: (0,) * len(shape))


def sds(shape, dtype):
    return jax.ShapeDtypeStruct(shape, dtype)


def swap_x(values):
    return lax.ppermute(values, "tensor", SWAP)


def gather_dp(values):
    count = lax.axis_size("dp")
    here = lax.axis_index("dp")
    held = values[None]
    step = 1
    while step < count:
        other = lax.ppermute(held, "dp", [(i, i ^ step) for i in range(count)])
        later = (here // step) % 2 == 1
        held = jnp.where(
            later,
            jnp.concatenate([other, held], axis=0),
            jnp.concatenate([held, other], axis=0),
        )
        step *= 2
    return held


def total_dp(values):
    count = lax.axis_size("dp")
    step = 1
    while step < count:
        values = values + lax.ppermute(values, "dp", [(i, i ^ step) for i in range(count)])
        step *= 2
    return values


def slot_numbers(owner_part):
    count = owner_part.shape[0]
    order = jnp.arange(count, dtype=i32)
    earlier = (order[None, :] < order[:, None]).astype(i32)
    same = (owner_part[:, None] == owner_part[None, :]).astype(i32)
    return jnp.sum(same * earlier, axis=1)


def slot_rates(owner_part, rate_list, slot_count, fallback):
    slots = slot_numbers(owner_part)
    slot_hit = slots[:, None, None] == jnp.arange(slot_count, dtype=i32)[None, :, None]
    group_hit = owner_part[:, None, None] == jnp.arange(OWNER_GROUPS, dtype=i32)[None, None, :]
    hits = jnp.logical_and(slot_hit, group_hit).astype(f32)
    rates = jnp.asarray(rate_list, f32)[:, None, None]
    return jnp.sum(hits * rates, axis=0) + (1.0 - jnp.sum(hits, axis=0)) * fallback


def routes(full_count, empty_count):
    groups = range(OWNER_GROUPS)
    ways = []
    for full in itertools.combinations(groups, full_count):
        rest = [g for g in groups if g not in full]
        for empty in itertools.combinations(rest, empty_count):
            ways.append((full, empty))
    return ways


ATTN_WAYS = routes(1, 1) + routes(2, 2)
MLP_WAYS = routes(2, 2)


def way_code(full, empty):
    code = 0
    for g in range(OWNER_GROUPS):
        digit = 2 if g in full else (0 if g in empty else 1)
        code += digit * 3**g
    return code


def plan(surplus, ways):
    weights = jnp.asarray([3**g for g in range(OWNER_GROUPS)], i32)
    code = jnp.sum(surplus * weights)
    hit = (code == jnp.asarray([way_code(*way) for way in ways], i32)).astype(i32)
    index = jnp.sum(hit * jnp.arange(len(ways), dtype=i32))
    taker = [[0] * OWNER_GROUPS for _ in ways]
    for w, (full, empty) in enumerate(ways):
        for a, b in zip(full, empty):
            taker[w][a] = b
    return index, jnp.sum(hit[:, None] * jnp.asarray(taker, i32), axis=0)


def move(values, index, ways, back):
    size = lax.axis_size("dp") // OWNER_GROUPS

    def branch(way):
        pairs = []
        for a, b in zip(*way):
            if back:
                a, b = b, a
            pairs += [(a * size + j, b * size + j) for j in range(size)]
        return lambda v: lax.ppermute(v, "dp", pairs)

    return lax.switch(index, [branch(way) for way in ways], values)


def first_half():
    return lax.broadcasted_iota(i32, (8, 128), 0) < 4


def flag(condition):
    return jnp.where(condition, f32(1.0), f32(0.0))


def keep_at(seg_ref, t, half):
    return jnp.where(
        half, flag(seg_ref[t + 1] == seg_ref[t]), flag(seg_ref[BL + t + 1] == seg_ref[BL + t])
    )


def scan_kernel(seg_ref, h_ref, rate_ref, c_ref, y_ref, s_ref, e_ref):
    half = first_half()
    decay = [jnp.exp(-rate_ref[n]) for n in range(STATE)]

    def step(t, states):
        keep = keep_at(seg_ref, t, half)
        row = h_ref[t]
        return [(states[n] * keep) * decay[n] + row for n in range(STATE)]

    def step_out(t, states):
        states = step(t, states)
        total = c_ref[0] * states[0]
        for n in range(1, STATE):
            total = total + c_ref[n] * states[n]
        y_ref[t - (BL - CTX)] = total
        return states

    states = [jnp.zeros((8, 128), f32)] * STATE
    states = lax.fori_loop(0, BL - CTX, step, states, unroll=4)
    states = lax.fori_loop(BL - CTX, BL, step_out, states, unroll=2)
    joined = flag(seg_ref[2 * BL] == seg_ref[BL])
    for n in range(STATE):
        s_ref[n] = states[n]
        e_ref[n] = states[n] + (joined * jnp.exp(-rate_ref[n] * BL)) * pltpu.roll(states[n], 4, 0)


def tail_kernel(seg_ref, carry_ref, s_ref, rate_ref, c_ref, y_ref, out_ref, start_ref):
    half = first_half()
    before = seg_ref[0]
    joined = flag(seg_ref[BL] == before)
    decay = [jnp.exp(-rate_ref[n]) for n in range(STATE)]
    weighted = []
    for n in range(STATE):
        carried = carry_ref[n]
        mid = pltpu.roll(s_ref[n], 4, 0) + (joined * jnp.exp(-rate_ref[n] * BL)) * carried
        start = jnp.where(half, carried, mid)
        start_ref[n] = start
        weighted.append(c_ref[n] * start * jnp.exp(-rate_ref[n] * (BL - CTX + 1)))

    def step(t, parts):
        mask = jnp.where(
            half,
            flag(seg_ref[t + 1 + BL - CTX] == before),
            flag(seg_ref[BL + t + 1 + BL - CTX] == seg_ref[BL]),
        )
        total = parts[0]
        for n in range(1, STATE):
            total = total + parts[n]
        out_ref[t] = y_ref[t] + mask * total
        return [parts[n] * decay[n] for n in range(STATE)]

    lax.fori_loop(0, CTX, step, weighted, unroll=4)


def back_total_kernel(seg_ref, g_ref, rate_ref, c_ref, own_ref, out_ref):
    half = first_half()
    decay = [jnp.exp(-rate_ref[n]) for n in range(STATE)]

    def step(k, sums):
        t = CTX - 1 - k
        mask = jnp.where(
            half,
            flag(seg_ref[t + 1 + BL - CTX] == seg_ref[1]),
            flag(seg_ref[BL + t + 1 + BL - CTX] == seg_ref[BL]),
        )
        grad = mask * g_ref[t]
        return [decay[n] * (sums[n] + grad) for n in range(STATE)]

    sums = lax.fori_loop(0, CTX, step, [jnp.zeros((8, 128), f32)] * STATE, unroll=4)
    joined = flag(seg_ref[1] == seg_ref[BL])
    for n in range(STATE):
        total = sums[n] * c_ref[n] * jnp.exp(-rate_ref[n] * (BL - CTX))
        own_ref[n] = total
        out_ref[n] = total + (joined * jnp.exp(-rate_ref[n] * BL)) * pltpu.roll(total, 4, 0)


def sens_kernel(seg_ref, h_ref, g_ref, start_ref, rate_ref, gc_ref, ga_ref, z_ref):
    half = first_half()
    group = 8
    for first in range(0, STATE, group):
        ids = range(first, first + group)
        decay = [jnp.exp(-rate_ref[n]) for n in ids]

        def step(t, both, decay=decay):
            keep = keep_at(seg_ref, t, half)
            row = h_ref[t]
            kept = [v * keep for v in both[0]]
            sens = [(both[1][n] * keep) * decay[n] + kept[n] for n in range(group)]
            states = [kept[n] * decay[n] + row for n in range(group)]
            return states, sens

        def step_sum(t, carried, step=step):
            states, sens = step(t, carried[:2])
            grad = g_ref[t - (BL - CTX)]
            by_c = [carried[2][n] + grad * states[n] for n in range(group)]
            by_a = [carried[3][n] + grad * sens[n] for n in range(group)]
            return states, sens, by_c, by_a

        zeros = [jnp.zeros((8, 128), f32)] * group
        both = ([start_ref[n] for n in ids], zeros)
        both = lax.fori_loop(0, BL - CTX, step, both, unroll=4)
        carried = lax.fori_loop(BL - CTX, BL, step_sum, (both[0], both[1], zeros, zeros), unroll=2)
        for k, n in enumerate(ids):
            z_ref[n] = carried[1][k]
            gc_ref[n] = carried[2][k]
            ga_ref[n] = carried[3][k]


def back_scan_kernel(
    seg_ref, g_ref, own_ref, later_ref, z_ref, ga_ref, rate_ref, c_ref, gh_ref, out_ref
):
    half = first_half()
    decay = [jnp.exp(-rate_ref[n]) for n in range(STATE)]
    joined = flag(seg_ref[2 * BL] == seg_ref[BL])
    sums = []
    for n in range(STATE):
        later = later_ref[n]
        first = pltpu.roll(own_ref[n], 4, 0) + (joined * jnp.exp(-rate_ref[n] * BL)) * later
        entering = jnp.where(half, first, later)
        sums.append(entering)
        out_ref[n] = ga_ref[n] * c_ref[n] + entering * z_ref[n]

    def finish(t, sums):
        total = sums[0]
        for n in range(1, STATE):
            total = total + sums[n]
        gh_ref[t] = total
        keep = keep_at(seg_ref, t, half)
        return [(v * keep) * decay[n] for n, v in enumerate(sums)]

    def step_tail(k, sums):
        t = BL - 1 - k
        grad = g_ref[t - (BL - CTX)]
        return finish(t, [sums[n] + c_ref[n] * grad for n in range(STATE)])

    def step(k, sums):
        return finish(BL - 1 - k, sums)

    sums = lax.fori_loop(0, CTX, step_tail, sums, unroll=2)
    lax.fori_loop(CTX, BL, step, sums, unroll=4)


def to_lanes(values, blocks, steps):
    return (
        values.reshape(blocks, steps, 4, 128).transpose(1, 0, 2, 3).reshape(steps, blocks * 4, 128)
    )


def from_lanes(values, blocks, steps):
    return values.reshape(steps, blocks, 4, 128).transpose(1, 0, 2, 3).reshape(blocks, steps, 512)


def attend_kernel(
    host_ref,
    hid_ref,
    ctx_ref,
    wq_ref,
    wk_ref,
    wv_ref,
    segq_ref,
    segk_ref,
    q_ref,
    k_ref,
    v_ref,
    ck_ref,
    cv_ref,
    pc_ref,
    pb_ref,
    mix_ref,
):
    hid = hid_ref[...]
    ctx = ctx_ref[...]
    q_ref[...] = dot_nn(hid, wq_ref[0]).astype(bf16)
    k_ref[...] = dot_nn(hid, wk_ref[0]).astype(bf16)
    v_ref[...] = dot_nn(hid, wv_ref[0]).astype(bf16)
    ck_ref[...] = dot_nn(ctx, wk_ref[0]).astype(bf16)
    cv_ref[...] = dot_nn(ctx, wv_ref[0]).astype(bf16)
    ctx_ids = segk_ref[:, :CTX]
    for i in range(BL // QT):
        rows = slice(i * QT, (i + 1) * QT)
        reach = (i + 1) * QT
        ids = segq_ref[rows]
        ctx_ok = ctx_ids == ids
        place_q = lax.broadcasted_iota(i32, (QT, reach), 0) + i * QT
        place_k = lax.broadcasted_iota(i32, (QT, reach), 1)
        block_ok = jnp.logical_and(place_k <= place_q, segk_ref[:, CTX : CTX + reach] == ids)
        for head in range(TILE // HEAD_DIM):
            cols = slice(head * HEAD_DIM, (head + 1) * HEAD_DIM)
            query = q_ref[rows, cols]
            sc = dot_nt(query, ck_ref[:, cols]) * score_scale
            sb = dot_nt(query, k_ref[:reach, cols]) * score_scale
            sc = jnp.where(ctx_ok, sc, masked_score)
            sb = jnp.where(block_ok, sb, masked_score)
            top = jnp.maximum(
                jnp.max(sc, axis=1, keepdims=True), jnp.max(sb, axis=1, keepdims=True)
            )
            ec = jnp.exp(sc - top)
            eb = jnp.exp(sb - top)
            total = jnp.sum(ec, axis=1, keepdims=True) + jnp.sum(eb, axis=1, keepdims=True)
            inverse = 1.0 / total
            pc = (ec * inverse).astype(bf16)
            pb = (eb * inverse).astype(bf16)
            pc_ref[head, rows, :] = pc
            pb_ref[head, rows, :reach] = pb
            if reach < BL:
                pb_ref[head, rows, reach:] = jnp.zeros((QT, BL - reach), bf16)
            mixed = dot_nn(pc, cv_ref[:, cols]) + dot_nn(pb, v_ref[:reach, cols])
            mix_ref[rows, cols] = mixed.astype(bf16)


def attend_forward(hosts, block, hidden, context, attn_full, seg_col, seg_row, half_width):
    pairs = half_width // TILE

    def weight(position):
        return pl.BlockSpec((1, D, TILE), lambda p, s: (s[position], 0, p))

    def tile(rows):
        return pl.BlockSpec((rows, TILE), lambda p, s: (0, p))

    heads = half_width // HEAD_DIM
    per = TILE // HEAD_DIM
    return call(
        attend_kernel,
        (pairs,),
        [
            pl.BlockSpec((BL, D), lambda p, s: (block, 0)),
            pl.BlockSpec((CTX, D), lambda p, s: (block, 0)),
            weight(0),
            weight(1),
            weight(2),
            pl.BlockSpec((BL, 1), lambda p, s: (block, 0)),
            whole((1, CTX + BL)),
        ],
        [
            tile(BL),
            tile(BL),
            tile(BL),
            tile(CTX),
            tile(CTX),
            pl.BlockSpec((per, BL, CTX), lambda p, s: (p, 0, 0)),
            pl.BlockSpec((per, BL, BL), lambda p, s: (p, 0, 0)),
            tile(BL),
        ],
        [
            sds((BL, half_width), bf16),
            sds((BL, half_width), bf16),
            sds((BL, half_width), bf16),
            sds((CTX, half_width), bf16),
            sds((CTX, half_width), bf16),
            sds((heads, BL, CTX), bf16),
            sds((heads, BL, BL), bf16),
            sds((BL, half_width), bf16),
        ],
        prefetch=1,
        flops=8 * 10**9,
        nbytes=12 * 10**6,
    )(hosts, hidden, context, attn_full, attn_full, attn_full, seg_col, seg_row)


def attend_back_kernel(
    host_ref,
    own_ref,
    other_ref,
    cot_ref,
    mid_ref,
    gain_ref,
    wo_ref,
    wq_ref,
    wk_ref,
    wv_ref,
    q_ref,
    k_ref,
    v_ref,
    ck_ref,
    cv_ref,
    pc_ref,
    pb_ref,
    low_ref,
    gmid_ref,
    ggain_ref,
    dq_ref,
    dk_ref,
    dv_ref,
    dck_ref,
    dcv_ref,
    hid_ref,
    ctx_ref,
    dsc_ref,
    dsb_ref,
):
    pair = pl.program_id(0)

    @pl.when(pair == 0)
    def _():
        grad = own_ref[...] + other_ref[...].astype(f32)
        middle = mid_ref[...]
        inverse = lax.rsqrt(jnp.mean(middle * middle, axis=1, keepdims=True) + epsilon_norm)
        scaled = middle * inverse
        ggain_ref[...] = jnp.sum(grad * scaled, axis=0, keepdims=True)
        weighted = grad * gain_ref[...]
        centre = jnp.mean(weighted * scaled, axis=1, keepdims=True)
        result = cot_ref[...].astype(f32) + inverse * (weighted - scaled * centre)
        gmid_ref[...] = result
        low_ref[...] = result.astype(bf16)
        hid_ref[...] = jnp.zeros_like(hid_ref)
        ctx_ref[...] = jnp.zeros_like(ctx_ref)

    grad_mixed = dot_nn(low_ref[...], wo_ref[0]).astype(bf16)
    for head in range(TILE // HEAD_DIM):
        cols = slice(head * HEAD_DIM, (head + 1) * HEAD_DIM)
        grad_head = grad_mixed[:, cols]
        for i in range(BL // QT):
            rows = slice(i * QT, (i + 1) * QT)
            reach = (i + 1) * QT
            grad_rows = grad_head[rows]
            gpc = dot_nt(grad_rows, cv_ref[:, cols])
            gpb = dot_nt(grad_rows, v_ref[:reach, cols])
            pc = pc_ref[head, rows, :].astype(f32)
            pb = pb_ref[head, rows, :reach].astype(f32)
            tc = pc * gpc
            tb = pb * gpb
            centre = jnp.sum(tc, axis=1, keepdims=True) + jnp.sum(tb, axis=1, keepdims=True)
            dsc_ref[rows, :] = (tc - pc * centre).astype(bf16)
            dsb_ref[rows, :reach] = (tb - pb * centre).astype(bf16)
            if reach < BL:
                dsb_ref[rows, reach:] = jnp.zeros((QT, BL - reach), bf16)
        dsc = dsc_ref[...]
        dsb = dsb_ref[...]
        dq = (dot_nn(dsc, ck_ref[:, cols]) + dot_nn(dsb, k_ref[:, cols])) * score_scale
        dq_ref[:, cols] = dq.astype(bf16)
        query = q_ref[:, cols]
        dk_ref[:, cols] = (dot_tn(dsb, query) * score_scale).astype(bf16)
        dck_ref[:, cols] = (dot_tn(dsc, query) * score_scale).astype(bf16)
        dv_ref[:, cols] = dot_tn(pb_ref[head], grad_head).astype(bf16)
        dcv_ref[:, cols] = dot_tn(pc_ref[head], grad_head).astype(bf16)
    hid_ref[...] += (
        dot_nt(dq_ref[...], wq_ref[0])
        + dot_nt(dk_ref[...], wk_ref[0])
        + dot_nt(dv_ref[...], wv_ref[0])
    )
    ctx_ref[...] += dot_nt(dck_ref[...], wk_ref[0]) + dot_nt(dcv_ref[...], wv_ref[0])


def attend_backward(hosts, block, own, other, cot_full, middle, gain, attn_full, kept, half_width):
    pairs = half_width // TILE
    per = TILE // HEAD_DIM

    def weight(position):
        return pl.BlockSpec((1, D, TILE), lambda p, s: (s[position], 0, p))

    def tile(rows):
        return pl.BlockSpec((rows, TILE), lambda p, s: (0, p))

    return call(
        attend_back_kernel,
        (pairs,),
        [
            whole((BL, D)),
            whole((BL, D)),
            pl.BlockSpec((BL, D), lambda p, s: (block, 0)),
            whole((BL, D)),
            whole((1, D)),
            weight(3),
            weight(0),
            weight(1),
            weight(2),
            tile(BL),
            tile(BL),
            tile(BL),
            tile(CTX),
            tile(CTX),
            pl.BlockSpec((per, BL, CTX), lambda p, s: (p, 0, 0)),
            pl.BlockSpec((per, BL, BL), lambda p, s: (p, 0, 0)),
        ],
        [
            whole((BL, D)),
            whole((BL, D)),
            whole((1, D)),
            tile(BL),
            tile(BL),
            tile(BL),
            tile(CTX),
            tile(CTX),
            whole((BL, D)),
            whole((CTX, D)),
        ],
        [
            sds((BL, D), bf16),
            sds((BL, D), f32),
            sds((1, D), f32),
            sds((BL, half_width), bf16),
            sds((BL, half_width), bf16),
            sds((BL, half_width), bf16),
            sds((CTX, half_width), bf16),
            sds((CTX, half_width), bf16),
            sds((BL, D), f32),
            sds((CTX, D), f32),
        ],
        scratch=[pltpu.VMEM((BL, CTX), bf16), pltpu.VMEM((BL, BL), bf16)],
        prefetch=1,
        flops=12 * 10**9,
        nbytes=20 * 10**6,
    )(
        hosts,
        own,
        other,
        cot_full,
        middle,
        gain,
        attn_full,
        attn_full,
        attn_full,
        attn_full,
        *kept,
    )


def attn_grad_kernel(host_ref, *refs):
    (hid0, hid1, ctx0, ctx1, low0, low1), rest = refs[:6], refs[6:]
    (dq0, dk0, dv0, dck0, dcv0, mix0), rest = rest[:6], rest[6:]
    (dq1, dk1, dv1, dck1, dcv1, mix1), (out_ref,) = rest[:6], rest[6:]
    matrix = pl.program_id(0)

    @pl.when(matrix == 0)
    def _():
        out_ref[0] = (dot_tn(hid0[...], dq0[...]) + dot_tn(hid1[...], dq1[...])).astype(bf16)

    @pl.when(matrix == 1)
    def _():
        out_ref[0] = (
            dot_tn(hid0[...], dk0[...])
            + dot_tn(hid1[...], dk1[...])
            + dot_tn(ctx0[...], dck0[...])
            + dot_tn(ctx1[...], dck1[...])
        ).astype(bf16)

    @pl.when(matrix == 2)
    def _():
        out_ref[0] = (
            dot_tn(hid0[...], dv0[...])
            + dot_tn(hid1[...], dv1[...])
            + dot_tn(ctx0[...], dcv0[...])
            + dot_tn(ctx1[...], dcv1[...])
        ).astype(bf16)

    @pl.when(matrix == 3)
    def _():
        out_ref[0] = (dot_tn(low0[...], mix0[...]) + dot_tn(low1[...], mix1[...])).astype(bf16)


def attn_grads(hosts, hidden, context, lows, blocks, half_width):
    hid_specs = [
        pl.BlockSpec((BL, D), lambda m, s: (0, 0)),
        pl.BlockSpec((BL, D), lambda m, s: (1, 0)),
        pl.BlockSpec((CTX, D), lambda m, s: (0, 0)),
        pl.BlockSpec((CTX, D), lambda m, s: (1, 0)),
    ]
    block_specs = [
        whole((BL, half_width)),
        whole((BL, half_width)),
        whole((BL, half_width)),
        whole((CTX, half_width)),
        whole((CTX, half_width)),
        whole((BL, half_width)),
    ]
    return call(
        attn_grad_kernel,
        (4,),
        hid_specs + [whole((BL, D))] * 2 + block_specs * 2,
        [pl.BlockSpec((1, D, half_width), lambda m, s: (s[m], 0, 0))],
        [sds((OWNER_GROUPS, D, half_width), bf16)],
        prefetch=1,
        flops=46 * 10**8,
        nbytes=14 * 10**6,
    )(hosts, hidden, hidden, context, context, *lows, *blocks[0], *blocks[1])[0]


def mlp_kernel(
    host_ref,
    own_ref,
    other_ref,
    wo_ref,
    woo_ref,
    tok_ref,
    gain_ref,
    cot_ref,
    w1_ref,
    w2_ref,
    mid_ref,
    hid_ref,
    act_ref,
    pre_ref,
    grad_ref,
    low_ref,
):
    step = pl.program_id(0)

    @pl.when(step == 0)
    def _():
        middle = (
            tok_ref[...].astype(f32)
            + dot_nt(own_ref[...], wo_ref[0])
            + dot_nt(other_ref[...], woo_ref[...])
        )
        inverse = lax.rsqrt(jnp.mean(middle * middle, axis=1, keepdims=True) + epsilon_norm)
        mid_ref[...] = middle
        hid_ref[...] = (middle * inverse * gain_ref[...]).astype(bf16)
        grad_ref[...] = jnp.zeros_like(grad_ref)

    w1 = w1_ref[0]
    w2 = w2_ref[0]
    pre = dot_nn(hid_ref[...], w1)
    grad_act = dot_nn(cot_ref[...], w2)
    inner = 0.7978845608028654 * (pre + 0.044715 * (pre * pre * pre))
    bent = jnp.tanh(inner)
    gate = 0.5 * (1.0 + bent)
    act_ref[...] = (pre * gate).astype(bf16)
    slope = gate + 0.5 * pre * (1.0 - bent * bent) * (
        0.7978845608028654 * (1.0 + 0.134145 * (pre * pre))
    )
    grad_pre = (slope * grad_act).astype(bf16)
    pre_ref[...] = grad_pre
    grad_ref[...] += dot_nt(grad_pre, w1)

    @pl.when(step == pl.num_programs(0) - 1)
    def _():
        low_ref[...] = grad_ref[...].astype(bf16)


def mlp_block(hosts, block, own, other, attn_full, wo_other, tok_full, gain, cot_full, mlp_full):
    half_width = own.shape[1]
    quarter = mlp_full.shape[2]
    hidden = 2 * quarter
    per = quarter // TILE

    def weight(position):
        return pl.BlockSpec(
            (1, D, TILE), lambda f, s: (s[4 + 2 * position + f // per], 0, lax.rem(f, per))
        )

    return call(
        mlp_kernel,
        (2 * per,),
        [
            whole((BL, half_width)),
            whole((BL, half_width)),
            pl.BlockSpec((1, D, half_width), lambda f, s: (s[3], 0, 0)),
            whole((D, half_width)),
            pl.BlockSpec((BL, D), lambda f, s: (block, 0)),
            whole((1, D)),
            pl.BlockSpec((BL, D), lambda f, s: (block, 0)),
            weight(0),
            weight(1),
        ],
        [
            whole((BL, D)),
            whole((BL, D)),
            pl.BlockSpec((BL, TILE), lambda f, s: (0, f)),
            pl.BlockSpec((BL, TILE), lambda f, s: (0, f)),
            whole((BL, D)),
            whole((BL, D)),
        ],
        [
            sds((BL, D), f32),
            sds((BL, D), bf16),
            sds((BL, hidden), bf16),
            sds((BL, hidden), bf16),
            sds((BL, D), f32),
            sds((BL, D), bf16),
        ],
        prefetch=1,
        flops=8 * 10**9,
        nbytes=24 * 10**6,
    )(hosts, own, other, attn_full, wo_other, tok_full, gain, cot_full, mlp_full, mlp_full)


def mlp_grad_kernel(host_ref, h0, h1, g0, g1, p0, p1, a0, a1, out_ref):
    matrix = pl.program_id(0)

    @pl.when(matrix == 0)
    def _():
        out_ref[0] = (dot_tn(h0[...], p0[...]) + dot_tn(h1[...], p1[...])).astype(bf16)

    @pl.when(matrix == 1)
    def _():
        out_ref[0] = (dot_tn(g0[...], a0[...]) + dot_tn(g1[...], a1[...])).astype(bf16)


def mlp_grads(hosts, hiddens, cot_full, pres, acts):
    hidden = acts[0].shape[1]
    quarter = hidden // 2
    per = quarter // TILE
    last = 2 * per - 1
    used_first = pl.BlockSpec((BL, TILE), lambda m, f, s: (0, jnp.where(m == 0, f, last)))
    used_second = pl.BlockSpec((BL, TILE), lambda m, f, s: (0, jnp.where(m == 1, f, 0)))
    return call(
        mlp_grad_kernel,
        (2, 2 * per),
        [
            whole((BL, D)),
            whole((BL, D)),
            pl.BlockSpec((BL, D), lambda m, f, s: (0, 0)),
            pl.BlockSpec((BL, D), lambda m, f, s: (1, 0)),
            used_first,
            used_first,
            used_second,
            used_second,
        ],
        [
            pl.BlockSpec(
                (1, D, TILE), lambda m, f, s: (s[4 + 2 * m + f // per], 0, lax.rem(f, per))
            )
        ],
        [sds((OWNER_GROUPS, D, quarter), bf16)],
        prefetch=1,
        flops=86 * 10**8,
        nbytes=20 * 10**6,
    )(hosts, hiddens[0], hiddens[1], cot_full, cot_full, pres[0], pres[1], acts[0], acts[1])[0]


def mlp_out_kernel(host_ref, a_ref, w2_ref, out_ref):
    step = pl.program_id(0)

    @pl.when(step == 0)
    def _():
        out_ref[...] = jnp.zeros_like(out_ref)

    out_ref[...] += dot_nt(a_ref[...], w2_ref[0])


def mlp_out(hosts, act, mlp_full):
    quarter = mlp_full.shape[2]
    per = quarter // TILE
    return call(
        mlp_out_kernel,
        (2 * per,),
        [
            pl.BlockSpec((BL, TILE), lambda f, s: (0, f)),
            pl.BlockSpec((1, D, TILE), lambda f, s: (s[6 + f // per], 0, lax.rem(f, per))),
        ],
        [whole((BL, D))],
        [sds((BL, D), f32)],
        prefetch=1,
        flops=22 * 10**8,
        nbytes=8 * 10**6,
    )(hosts, act, mlp_full)[0]


def adam_step(gradient, moment_one, moment_two, weight, rate_table, decay_weight):
    step_count = f32(STEP)
    first_new = beta_first * moment_one + (1.0 - beta_first) * gradient
    second_new = beta_second * moment_two + (1.0 - beta_second) * gradient * gradient
    fixed_one = 1.0 - jnp.power(beta_first, step_count)
    fixed_two = 1.0 - jnp.power(beta_second, step_count)
    update = first_new / fixed_one / (jnp.sqrt(second_new / fixed_two) + epsilon_adam)
    return (first_new, second_new, weight - rate_table * (update + decay_weight * weight))


def body(
    tokens,
    cotangent,
    segments,
    owners,
    attn_master,
    attn_first,
    attn_second,
    mlp_master,
    mlp_first,
    mlp_second,
    ssm_params,
    ssm_first,
    ssm_second,
    norm_gains,
    gains_first,
    gains_second,
):
    rows = tokens.shape[1]
    width = tokens.shape[2]
    blocks = rows // BL
    dp_count = lax.axis_size("dp")
    dp_here = lax.axis_index("dp")
    side = lax.axis_index("tensor")
    group = dp_here // (dp_count // OWNER_GROUPS)
    bank_rows = attn_master.shape[1]
    quarter = mlp_master.shape[2] // 2

    def both_sides(own, other):
        return jnp.where(
            side == 0,
            jnp.concatenate([own, other], axis=-1),
            jnp.concatenate([other, own], axis=-1),
        )

    def side_of(values, which):
        return lax.dynamic_slice_in_dim(values, which * width, width, values.ndim - 1)

    attn_owner = owners[:4]
    mlp_owner = owners[4:]
    groups = jnp.arange(OWNER_GROUPS, dtype=i32)
    attn_count = jnp.sum((attn_owner[:, None] == groups[None, :]).astype(i32), axis=0)
    mlp_count = jnp.sum((mlp_owner[:, None] == groups[None, :]).astype(i32), axis=0)
    attn_way, attn_taker = plan(attn_count, ATTN_WAYS)
    mlp_way, mlp_taker = plan(2 * mlp_count, MLP_WAYS)
    attn_slot = slot_numbers(attn_owner)
    attn_host = jnp.where(attn_slot == 0, attn_owner, attn_taker[attn_owner])
    mlp_host = jnp.stack([mlp_owner, mlp_taker[mlp_owner]], axis=1).reshape(-1)
    hosts = jnp.concatenate([attn_host, mlp_host]).astype(i32)
    attn_here = attn_count[group]
    mlp_here = mlp_count[group]

    attn_low = attn_master.astype(bf16)
    mlp_low = mlp_master[0].astype(bf16)
    attn_moved = move(attn_low[1], attn_way, ATTN_WAYS, False)
    mlp_moved = move(mlp_low[:, quarter:], mlp_way, MLP_WAYS, False)
    attn_block = jnp.where(attn_here == 0, attn_moved, attn_low[0])
    mlp_block_low = jnp.where(mlp_here == 0, mlp_moved, mlp_low[:, :quarter])
    attn_full = lax.all_gather(attn_block, "dp", axis=0, tiled=True)
    mlp_full = lax.all_gather(mlp_block_low, "dp", axis=0, tiled=True)
    attn_full = attn_full.reshape(OWNER_GROUPS, D, width)
    mlp_full = mlp_full.reshape(OWNER_GROUPS, D, quarter)

    tok = tokens.reshape(rows, width)
    cot = cotangent.reshape(rows, width)
    tok_f = tok.astype(f32)
    square_here = jnp.sum(tok_f * tok_f, axis=1)
    square_other = swap_x(square_here)
    tok_other = swap_x(tok)
    cot_other = swap_x(cot)
    gains_other = swap_x(norm_gains)
    inverse_one = lax.rsqrt((square_here + square_other) / D + epsilon_norm)
    scaled_own = tok_f * inverse_one[:, None]
    hidden_own = (scaled_own * norm_gains[0]).astype(bf16)
    hidden_other = (tok_other.astype(f32) * inverse_one[:, None] * gains_other[0]).astype(bf16)
    hidden_full = both_sides(hidden_own, hidden_other)
    tok_full = both_sides(tok, tok_other)
    cot_full = both_sides(cot, cot_other)
    gains_full = both_sides(norm_gains, gains_other)

    seg = segments.reshape(rows)
    prior = lax.ppermute(seg[rows - CTX :] + 1, "dp", [(i, i + 1) for i in range(dp_count - 1)]) - 1
    seg_ext = jnp.concatenate([prior[CTX - 1 :], seg])
    seg_col = seg[:, None]

    param_lanes = ssm_params.transpose(0, 2, 1)
    decay_rate = jnp.exp(param_lanes[0]) * (BL ** (-0.5) / 32.0)
    drive_root = jnp.sqrt(-jnp.expm1(-2.0 * decay_rate))
    reading = param_lanes[2] * drive_root * param_lanes[1]

    def doubled(values):
        lanes = values.reshape(STATE, 4, 128)
        return jnp.concatenate([lanes] * blocks, axis=1)

    rate_lanes = doubled(decay_rate)
    reading_lanes = doubled(reading)
    smem = pl.BlockSpec(memory_space=pltpu.SMEM)
    vmem = pl.BlockSpec(memory_space=pltpu.VMEM)
    state_shape = sds((STATE, 8, 128), f32)

    def plain(kernel, count, outs, cost):
        return pl.pallas_call(
            kernel,
            in_specs=[smem] + [vmem] * count,
            out_specs=[vmem] * len(outs),
            out_shape=outs,
            compiler_params=pltpu.CompilerParams(vmem_limit_bytes=VMEM_BYTES),
            cost_estimate=pl.CostEstimate(flops=cost, bytes_accessed=4 * 10**6, transcendentals=0),
        )

    hidden_lanes = to_lanes(hidden_own.astype(f32), blocks, BL)
    tail_lanes = sds((CTX, 8, 128), f32)
    tail_part, state_ends, device_end = plain(
        scan_kernel, 3, [tail_lanes, state_shape, state_shape], 4 * 10**9
    )(seg_ext, hidden_lanes, rate_lanes, reading_lanes)
    end_rows = device_end[:, 4:].reshape(STATE, width).astype(bf16)
    id_rows = jnp.where(
        (jnp.arange(STATE) == 0)[:, None], seg[rows - 1].astype(f32), seg[0].astype(f32)
    )
    id_rows = jnp.broadcast_to(id_rows, (STATE, 128)).astype(bf16)
    states_all = gather_dp(jnp.concatenate([end_rows, id_rows], axis=1))
    ids_all = states_all[:, :2, width].astype(f32)
    places = jnp.arange(dp_count, dtype=i32)
    gap_before = dp_here - 1 - places
    use_before = jnp.logical_and(gap_before >= 0, ids_all[:, 0] == seg_ext[0].astype(f32))
    power_before = jnp.exp(
        -decay_rate[None] * (rows * jnp.maximum(gap_before, 0)).astype(f32)[:, None, None]
    )
    carry_in = jnp.sum(
        jnp.where(
            use_before[:, None, None], power_before * states_all[:, :, :width].astype(f32), 0.0
        ),
        axis=0,
    )
    tails, state_starts = plain(tail_kernel, 5, [tail_lanes, state_shape], 10**9)(
        seg_ext, doubled(carry_in), state_ends, rate_lanes, reading_lanes, tail_part
    )
    tails = from_lanes(tails, blocks, CTX).astype(bf16)
    handed = lax.ppermute(tails[blocks - 1], "dp", [(i, i + 1) for i in range(dp_count - 1)])
    context_own = jnp.concatenate([handed[None], tails[: blocks - 1]], axis=0).reshape(-1, width)
    context_full = both_sides(context_own, swap_x(context_own))

    seg_rows = []
    for b in range(blocks):
        before = prior if b == 0 else seg[b * BL - CTX : b * BL]
        seg_rows.append(jnp.concatenate([before, seg[b * BL : (b + 1) * BL]])[None])
    kept = []
    mixed = []
    mixed_other = []
    for b in range(blocks):
        outs = attend_forward(
            hosts, b, hidden_full, context_full, attn_full, seg_col, seg_rows[b], width
        )
        kept.append(outs[:7])
        mixed.append(outs[7])
        mixed_other.append(swap_x(outs[7]))
    wo_other = swap_x(lax.dynamic_index_in_dim(attn_full, attn_host[3], 0, keepdims=False))

    gain_two = gains_full[1:2]
    middles, hiddens, acts, pres, grads, grads_other = [], [], [], [], [], []
    for b in range(blocks):
        middle, hidden_two, act, grad_pre, grad_two, grad_low = mlp_block(
            hosts,
            b,
            mixed[b],
            mixed_other[b],
            attn_full,
            wo_other,
            tok_full,
            gain_two,
            cot_full,
            mlp_full,
        )
        middles.append(middle)
        hiddens.append(hidden_two)
        acts.append(act)
        pres.append(grad_pre)
        grads.append(grad_two)
        grads_other.append(swap_x(grad_low))
    mlp_sum_in = mlp_grads(hosts, hiddens, cot_full, pres, acts)
    mlp_sum = lax.psum_scatter(
        mlp_sum_in.reshape(OWNER_GROUPS * D, quarter), "dp", scatter_dimension=0, tiled=True
    )
    out_rows = []
    for b in range(blocks):
        partial = mlp_out(hosts, acts[b], mlp_full)
        received = swap_x(side_of(partial, 1 - side).astype(bf16))
        out_rows.append(
            (side_of(middles[b], side) + side_of(partial, side) + received.astype(f32)).astype(bf16)
        )
    block_out = jnp.concatenate(out_rows, axis=0)

    lows, grad_mids, gain_twos, grad_blocks, parts, ctx_parts = [], [], [], [], [], []
    for b in range(blocks):
        outs = attend_backward(
            hosts,
            b,
            grads[b],
            grads_other[b],
            cot_full,
            middles[b],
            gain_two,
            attn_full,
            kept[b],
            width,
        )
        lows.append(outs[0])
        grad_mids.append(side_of(outs[1], side))
        gain_twos.append(side_of(outs[2], side))
        grad_blocks.append(list(outs[3:8]) + [mixed[b]])
        parts.append(outs[8])
        ctx_parts.append(outs[9])
    ctx_part = jnp.stack(ctx_parts)
    ctx_received = swap_x(side_of(ctx_part, 1 - side).astype(bf16))
    grad_context = side_of(ctx_part, side) + ctx_received.astype(f32)
    handed_back = lax.ppermute(
        grad_context[0].astype(bf16), "dp", [(i + 1, i) for i in range(dp_count - 1)]
    ).astype(f32)
    grad_tails = jnp.concatenate([grad_context[1:], handed_back[None]], axis=0)
    tail_grad_lanes = to_lanes(grad_tails.reshape(blocks * CTX, width), blocks, CTX)
    attn_sum_in = attn_grads(hosts, hidden_full, context_full, lows, grad_blocks, width)
    attn_sum = lax.psum_scatter(
        attn_sum_in.reshape(OWNER_GROUPS * D, width), "dp", scatter_dimension=0, tiled=True
    )

    own_back, device_back = plain(back_total_kernel, 3, [state_shape, state_shape], 10**9)(
        seg_ext, tail_grad_lanes, rate_lanes, reading_lanes
    )
    back_all = gather_dp(device_back[:, :4].reshape(STATE, width).astype(bf16))
    grad_c_lanes, grad_a_lanes, sens_end = plain(sens_kernel, 4, [state_shape] * 3, 8 * 10**9)(
        seg_ext, hidden_lanes, tail_grad_lanes, state_starts, rate_lanes
    )
    gap_after = places - dp_here - 1
    use_after = jnp.logical_and(gap_after >= 0, ids_all[:, 1] == seg[rows - 1].astype(f32))
    power_after = jnp.exp(
        -decay_rate[None] * (rows * jnp.maximum(gap_after, 0)).astype(f32)[:, None, None]
    )
    later = jnp.sum(
        jnp.where(use_after[:, None, None], power_after * back_all.astype(f32), 0.0), axis=0
    )
    grad_lanes, grad_a_lanes = plain(
        back_scan_kernel, 7, [sds((BL, 8, 128), f32), state_shape], 4 * 10**9
    )(
        seg_ext,
        tail_grad_lanes,
        own_back,
        doubled(later),
        sens_end,
        grad_a_lanes,
        rate_lanes,
        reading_lanes,
    )
    grad_channels = from_lanes(grad_lanes, blocks, BL).reshape(rows, width)

    part = jnp.concatenate(parts, axis=0)
    received = swap_x(side_of(part, 1 - side).astype(bf16))
    scaled_full_weight = hidden_scaled(tok_full, inverse_one, gains_full[0])
    row_here = jnp.sum(part * scaled_full_weight, axis=1) + jnp.sum(
        grad_channels * (scaled_own * norm_gains[0]), axis=1
    )
    row_total = row_here + swap_x(row_here)
    grad_hidden = side_of(part, side) + received.astype(f32) + grad_channels
    grad_tokens = jnp.concatenate(grad_mids, axis=0) + inverse_one[:, None] * (
        grad_hidden * norm_gains[0] - scaled_own * (row_total / D)[:, None]
    )
    gain_one = jnp.sum(grad_hidden * scaled_own, axis=0)
    gain_two_sum = sum(gain_twos)[0]

    def merged(values):
        return sum(values[:, 4 * b : 4 * b + 4] for b in range(blocks)).reshape(STATE, width)

    small = total_dp(
        jnp.concatenate(
            [merged(grad_c_lanes), merged(grad_a_lanes), gain_one[None], gain_two_sum[None]], axis=0
        )
    )
    grad_c, grad_a = small[:STATE], small[STATE : 2 * STATE]
    gains_grad = small[2 * STATE :]
    decay_step = jnp.exp(-decay_rate)
    grad_read = grad_c * drive_root * param_lanes[1]
    grad_drive = grad_c * drive_root * param_lanes[2]
    grad_a = grad_a - grad_c * param_lanes[1] * param_lanes[2] * decay_step / drive_root
    grad_log = -decay_rate * decay_step * grad_a
    ssm_grad = jnp.stack([grad_log, grad_drive, grad_read]).transpose(0, 2, 1)

    attn_back = move(attn_sum, attn_way, ATTN_WAYS, True)
    mlp_back = move(mlp_sum, mlp_way, MLP_WAYS, True)
    attn_grad = jnp.stack(
        [
            jnp.where(attn_here >= 1, attn_sum.astype(f32), 0.0),
            jnp.where(attn_here == 2, attn_back.astype(f32), 0.0),
        ]
    )
    mlp_grad = jnp.where(
        mlp_here == 1, jnp.concatenate([mlp_sum, mlp_back], axis=1).astype(f32), 0.0
    )[None]

    attn_table = slot_rates(
        attn_owner,
        [0.5 * D ** (-0.5)] * 3 + [0.5 * (D // 16) ** (-0.5)],
        attn_master.shape[0],
        0.5 * D ** (-0.5),
    )
    mlp_table = slot_rates(
        mlp_owner, [0.5 * D ** (-0.5), 0.5 * FF ** (-0.5)], mlp_master.shape[0], 0.5 * D ** (-0.5)
    )
    attn_rates = lax.dynamic_index_in_dim(attn_table, group, 1, keepdims=False)[:, None, None]
    mlp_rates = lax.dynamic_index_in_dim(mlp_table, group, 1, keepdims=False)[:, None, None]
    ssm_rates = jnp.asarray([1.0, 0.8, 0.25], f32)[:, None, None]
    gain_rates = jnp.asarray([0.6, 0.6], f32)[:, None]
    attn_one, attn_two, attn_new = adam_step(
        attn_grad, attn_first, attn_second, attn_master, attn_rates, matrix_decay
    )
    mlp_one, mlp_two, mlp_new = adam_step(
        mlp_grad, mlp_first, mlp_second, mlp_master, mlp_rates, matrix_decay
    )
    ssm_one, ssm_two, ssm_new = adam_step(
        ssm_grad, ssm_first, ssm_second, ssm_params, ssm_rates, 0.0
    )
    gain_first_new, gain_second_new, gains_new = adam_step(
        gains_grad, gains_first, gains_second, norm_gains, gain_rates, 0.0
    )
    return (
        block_out.reshape(tokens.shape),
        grad_tokens.reshape(tokens.shape),
        attn_grad,
        attn_one,
        attn_two,
        attn_new,
        attn_new.astype(bf16),
        mlp_grad,
        mlp_one,
        mlp_two,
        mlp_new,
        mlp_new.astype(bf16),
        ssm_grad,
        ssm_one,
        ssm_two,
        ssm_new,
        gains_grad,
        gain_first_new,
        gain_second_new,
        gains_new,
    )


def hidden_scaled(tok_full, inverse_one, gain):
    return tok_full.astype(f32) * inverse_one[:, None] * gain[None]


def solution(mesh):
    in_specs = (
        P(None, "dp", "tensor"),
        P(None, "dp", "tensor"),
        P(None, "dp"),
        P(),
        P(None, "dp", "tensor"),
        P(None, "dp", "tensor"),
        P(None, "dp", "tensor"),
        P(None, "dp", "tensor"),
        P(None, "dp", "tensor"),
        P(None, "dp", "tensor"),
        P(None, "tensor", None),
        P(None, "tensor", None),
        P(None, "tensor", None),
        P(None, "tensor"),
        P(None, "tensor"),
        P(None, "tensor"),
    )
    out_specs = (
        P(None, "dp", "tensor"),
        P(None, "dp", "tensor"),
        P(None, "dp", "tensor"),
        P(None, "dp", "tensor"),
        P(None, "dp", "tensor"),
        P(None, "dp", "tensor"),
        P(None, "dp", "tensor"),
        P(None, "dp", "tensor"),
        P(None, "dp", "tensor"),
        P(None, "dp", "tensor"),
        P(None, "dp", "tensor"),
        P(None, "dp", "tensor"),
        P(None, "tensor", None),
        P(None, "tensor", None),
        P(None, "tensor", None),
        P(None, "tensor", None),
        P(None, "tensor"),
        P(None, "tensor"),
        P(None, "tensor"),
        P(None, "tensor"),
    )
    return jax.shard_map(body, mesh=mesh, in_specs=in_specs, out_specs=out_specs, check_vma=False)
```

```python
import functools
import itertools

import jax
import jax.numpy as jnp
from jax import lax
from jax.experimental import pallas as pl
from jax.experimental.pallas import tpu as pltpu
from jax.sharding import PartitionSpec as P

D = 1024
HEAD_DIM = 128
FF = 4096
STATE = 16
CTX = 128
BL = 512
OWNER_GROUPS = 4
STEP = 5

epsilon_norm = 1e-05
beta_first = 0.9
beta_second = 0.95
epsilon_adam = 1e-08
matrix_decay = 0.1
masked_score = -1e30
score_scale = HEAD_DIM ** (-0.5)
f32 = jnp.float32
bf16 = jnp.bfloat16
i32 = jnp.int32
SWAP = [(0, 1), (1, 0)]
COST = 1000
TILE = 256
QT = 256
FT = 512
LOG2E = 1.4426950408889634


def dot_nn(left, right):
    return lax.dot_general(left, right, (((1,), (0,)), ((), ())), preferred_element_type=f32)


def dot_nt(left, right):
    return lax.dot_general(left, right, (((1,), (1,)), ((), ())), preferred_element_type=f32)


def dot_tn(left, right):
    return lax.dot_general(left, right, (((0,), (0,)), ((), ())), preferred_element_type=f32)


def call(
    kernel, grid, in_specs, out_specs, out_shape, scratch=(), prefetch=0, flops=0, nbytes=0, room=36
):
    return pl.pallas_call(
        kernel,
        grid_spec=pltpu.PrefetchScalarGridSpec(
            num_scalar_prefetch=prefetch,
            grid=grid,
            in_specs=in_specs,
            out_specs=out_specs,
            scratch_shapes=scratch,
        ),
        out_shape=out_shape,
        name=kernel.__name__,
        compiler_params=pltpu.CompilerParams(vmem_limit_bytes=room * 1024 * 1024),
        cost_estimate=pl.CostEstimate(flops=flops // COST, bytes_accessed=nbytes // COST, transcendentals=0),
    )


def whole(shape):
    return pl.BlockSpec(shape, lambda *_: (0,) * len(shape), pipeline_mode=pl.Buffered(1))


def sds(shape, dtype):
    return jax.ShapeDtypeStruct(shape, dtype)


def swap_x(values):
    return lax.ppermute(values, "tensor", SWAP)


def gate(value, *others):
    if not others:
        return value
    return lax.optimization_barrier((value,) + others)[0]


def together(*values):
    return lax.optimization_barrier(values)


def gather_rounds():
    return max(lax.axis_size("dp") - 1, 0).bit_length()


def gather_round(held, k):
    step = 1 << k
    count = lax.axis_size("dp")
    other = lax.ppermute(held, "dp", [(i, i ^ step) for i in range(count)])
    later = (lax.axis_index("dp") // step) % 2 == 1
    return jnp.where(
        later,
        jnp.concatenate([other, held], axis=0),
        jnp.concatenate([held, other], axis=0),
    )


def total_dp(values, beside):
    count = lax.axis_size("dp")
    for k in range(gather_rounds()):
        if k == 2:
            values, beside = together(values, beside)
        values = values + lax.ppermute(values, "dp", [(i, i ^ (1 << k)) for i in range(count)])
    return values, beside


def routes(full_count, empty_count):
    groups = range(OWNER_GROUPS)
    ways = []
    for full in itertools.combinations(groups, full_count):
        rest = [g for g in groups if g not in full]
        for empty in itertools.combinations(rest, empty_count):
            ways.append((full, empty))
    return ways


ATTN_WAYS = routes(1, 1) + routes(2, 2)


def way_code(full, empty):
    code = 0
    for g in range(OWNER_GROUPS):
        digit = 2 if g in full else (0 if g in empty else 1)
        code += digit * 3**g
    return code


def one_if(condition):
    return jnp.where(condition, jnp.int32(1), jnp.int32(0))


HOST_MLP, SIDE, WAY, NEAR, ATTN_HERE, MLP_HERE, PLAN_SIZE = 4, 8, 9, 10, 11, 12, 16
ATTN_RATES = [0.5 * D ** (-0.5)] * 3 + [0.5 * (D // 16) ** (-0.5)]
MLP_RATES = [0.5 * D ** (-0.5), 0.5 * FF ** (-0.5)]
IDLE_RATE = 0.5 * D ** (-0.5)


def plan_kernel(owner_ref, here_ref, out_ref, rate_ref):
    groups = range(OWNER_GROUPS)
    side, group = here_ref[0], here_ref[1]
    owner = [owner_ref[m] for m in range(6)]
    slot = [
        sum([one_if(owner[k] == owner[m]) for k in range(m)], jnp.int32(0)) for m in range(4)
    ]
    count = [sum([one_if(owner[m] == g) for m in range(4)], jnp.int32(0)) for g in groups]
    full_rank = [sum([one_if(count[h] == 2) for h in range(g)], jnp.int32(0)) for g in groups]
    empty_rank = [sum([one_if(count[h] == 0) for h in range(g)], jnp.int32(0)) for g in groups]
    taker = [
        sum(
            [
                jnp.where(
                    jnp.logical_and(count[h] == 0, empty_rank[h] == full_rank[g]), jnp.int32(h), 0
                )
                for h in groups
            ],
            jnp.int32(0),
        )
        for g in groups
    ]
    for m in range(4):
        second = sum([jnp.where(owner[m] == g, taker[g], 0) for g in groups], jnp.int32(0))
        out_ref[m] = jnp.where(slot[m] == 0, owner[m], second)
    code = sum([count[g] * 3**g for g in groups], jnp.int32(0))
    out_ref[WAY] = sum(
        [
            jnp.where(code == way_code(*way), jnp.int32(k), 0)
            for k, way in enumerate(ATTN_WAYS)
        ],
        jnp.int32(0),
    )
    low = sum([one_if(owner[m] < 2) for m in (4, 5)], jnp.int32(0))
    near = low == 1
    for k, m in enumerate((4, 5)):
        out_ref[HOST_MLP + 2 * k] = owner[m]
        bit = jnp.where(near, jnp.int32(1), jnp.int32(2))
        out_ref[HOST_MLP + 2 * k + 1] = jnp.bitwise_xor(owner[m], bit)
    out_ref[SIDE] = side
    out_ref[NEAR] = one_if(near)
    out_ref[ATTN_HERE] = sum([one_if(owner[m] == group) for m in range(4)], jnp.int32(0))
    out_ref[MLP_HERE] = sum([one_if(owner[m] == group) for m in (4, 5)], jnp.int32(0))
    for k in range(MLP_HERE + 1, PLAN_SIZE):
        out_ref[k] = jnp.int32(0)
    for place in range(2):
        rate = f32(IDLE_RATE)
        for m in range(4):
            hit = jnp.logical_and(owner[m] == group, slot[m] == place)
            rate = jnp.where(hit, f32(ATTN_RATES[m]), rate)
        rate_ref[place] = rate
    rate = f32(IDLE_RATE)
    for k, m in enumerate((4, 5)):
        rate = jnp.where(owner[m] == group, f32(MLP_RATES[k]), rate)
    rate_ref[2] = rate
    rate_ref[3] = f32(0.0)


def move(values, index, ways, back):
    size = lax.axis_size("dp") // OWNER_GROUPS

    def branch(way):
        pairs = []
        for a, b in zip(*way):
            if back:
                a, b = b, a
            pairs += [(a * size + j, b * size + j) for j in range(size)]
        return lambda v: lax.ppermute(v, "dp", pairs)

    return lax.switch(index, [branch(way) for way in ways], values)


def exchange_groups(values, near):
    size = lax.axis_size("dp") // OWNER_GROUPS

    def across(bit):
        return lax.ppermute(
            values,
            "dp",
            [(g * size + j, (g ^ bit) * size + j) for g in range(OWNER_GROUPS) for j in range(size)],
        )

    return jnp.where(near, across(1), across(2))


def ring_order(count):
    chips = count // 2
    if chips == 8:
        return [0, 2, 4, 6, 7, 5, 3, 1]
    return list(range(chips))


def join_kernel(host_ref, own_ref, other_ref, out_ref):
    @pl.when(pl.program_id(0) == 0)
    def _():
        out_ref[...] = own_ref[...]

    @pl.when(pl.program_id(0) == 1)
    def _():
        out_ref[...] = other_ref[...]


def join_scaled_kernel(
    host_ref, own_ref, other_ref, inverse_ref, gain_ref, gain_other_ref, out_ref
):
    @pl.when(pl.program_id(0) == 0)
    def _():
        out_ref[...] = (own_ref[...].astype(f32) * inverse_ref[...] * gain_ref[...]).astype(bf16)

    @pl.when(pl.program_id(0) == 1)
    def _():
        out_ref[...] = (
            other_ref[...].astype(f32) * inverse_ref[...] * gain_other_ref[...]
        ).astype(bf16)


def join_sides(hosts, own, other, scales=()):
    rows, width = own.shape
    return call(
        join_scaled_kernel if scales else join_kernel,
        (2,),
        [whole(v.shape) for v in (own, other) + tuple(scales)],
        [
            pl.BlockSpec(
                (rows, width), lambda d, s: (0, jnp.where(d == 0, s[SIDE], 1 - s[SIDE]))
            )
        ],
        [sds((rows, 2 * width), bf16)],
        prefetch=1,
        nbytes=8 * rows * width,
        room=12,
    )(hosts, own, other, *scales)[0]


class Ring:
    def __init__(self):
        self.count = lax.axis_size("dp")
        self.chips = self.count // 2
        order = ring_order(self.count)
        here = lax.axis_index("dp")
        self.core = here % 2
        chip = here // 2
        self.place = jnp.where(chip % 2 == 0, chip // 2, 7 - chip // 2) if self.chips == 8 else chip
        self.up = [
            (2 * order[p] + c, 2 * order[(p + 1) % self.chips] + c)
            for p in range(self.chips)
            for c in range(2)
        ]
        self.down = [(b, a) for a, b in self.up]
        self.cores = [(i, i ^ 1) for i in range(self.count)]
        self.far_up = self.chips // 2
        self.far_down = self.chips - 1 - self.far_up

    def chip(self, offset):
        place = (self.place + self.chips + offset) % self.chips
        if self.chips != 8:
            return place
        return jnp.where(place < 4, 2 * place, 15 - 2 * place)

    def reduce_scatter(self, blocks, values, last):
        pairs = blocks.reshape((self.chips, 2) + blocks.shape[1:])
        mine = lax.dynamic_index_in_dim(pairs, self.core, 1, keepdims=False)
        theirs = lax.dynamic_index_in_dim(pairs, 1 - self.core, 1, keepdims=False)
        received = lax.ppermute(theirs, "dp", self.cores)

        def block(offset):
            chip = self.chip(offset)
            return lax.dynamic_index_in_dim(mine, chip, 0, keepdims=False).astype(
                f32
            ) + lax.dynamic_index_in_dim(received, chip, 0, keepdims=False).astype(f32)

        held = gather_round(values[None], 0)
        up = block(self.far_up).astype(bf16)
        down = block(-self.far_down).astype(bf16)
        for step in range(max(self.far_up, gather_rounds() - 1)):
            if step == gather_rounds() - 2:
                up, down, held, last = together(up, down, held, last)
            else:
                up, down, held = together(up, down, held)
            if step + 1 < gather_rounds():
                held = gather_round(held, step + 1)
            if step < self.far_up:
                up = lax.ppermute(up, "dp", self.up)
                if step < self.far_up - 1:
                    up = (up.astype(f32) + block(self.far_up - 1 - step)).astype(bf16)
            if step < self.far_down:
                down = lax.ppermute(down, "dp", self.down)
                if step < self.far_down - 1:
                    down = (down.astype(f32) + block(step + 1 - self.far_down)).astype(bf16)
        return block(0) + up.astype(f32) + down.astype(f32), held, last

    def all_gather(self, block, values, gates):
        ups, downs, held = [block], [block], values[None]
        for step in range(max(self.far_up, gather_rounds())):
            joined = together(ups[-1], downs[-1], held, *gates.get(step, ()))
            ups[-1], downs[-1], held = joined[:3]
            if step < gather_rounds():
                held = gather_round(held, step)
            if step < self.far_up:
                ups.append(lax.ppermute(ups[-1], "dp", self.up))
            if step < self.far_down:
                downs.append(lax.ppermute(downs[-1], "dp", self.down))
        mine = jnp.stack(ups + downs[1:])
        theirs = lax.ppermute(mine, "dp", self.cores)
        offsets = [-k for k in range(self.far_up + 1)] + [k + 1 for k in range(self.far_down)]
        table = jnp.stack([self.chip(k) for k in offsets] + [self.core]).astype(i32)
        rows, columns = block.shape

        def place_kernel(table_ref, mine_ref, theirs_ref, out_ref):
            core = table_ref[self.chips]
            out_ref[0, core] = mine_ref[0]
            out_ref[0, 1 - core] = theirs_ref[0]

        spec = pl.BlockSpec((1, rows, columns), lambda k, s: (k, 0, 0))
        out = call(
            place_kernel,
            (self.chips,),
            [spec, spec],
            [pl.BlockSpec((1, 2, rows, columns), lambda k, s: (s[k], 0, 0, 0))],
            [sds((self.chips, 2, rows, columns), block.dtype)],
            prefetch=1,
            nbytes=4 * self.count * rows * columns,
        )(table, mine, theirs)[0]
        return out.reshape(self.count * rows, columns), held, mine


def shift_tails(values, by, cross):
    count = lax.axis_size("dp")
    pairs = [
        (2 * i + s, 2 * (i + by) + (1 - s if cross else s))
        for i in range(count)
        for s in range(2)
        if 0 <= i + by < count
    ]
    return lax.ppermute(values, ("dp", "tensor"), pairs)


def first_half():
    return lax.broadcasted_iota(i32, (8, 128), 0) < 4


def flag(condition):
    return jnp.where(condition, f32(1.0), f32(0.0))


def keep_at(seg_ref, t, half):
    return jnp.where(
        half, flag(seg_ref[t + 1] == seg_ref[t]), flag(seg_ref[BL + t + 1] == seg_ref[BL + t])
    )


def chunked(seg_ref, begin, end, plain, kept, carried, back=False):
    size = 8
    count = (end - begin) // size

    def chunk(c, carried):
        first = begin + (count - 1 - c if back else c) * size
        same = jnp.logical_and(
            seg_ref[first] == seg_ref[first + size],
            seg_ref[BL + first] == seg_ref[BL + first + size],
        )

        def run(step):
            def go(carried):
                for k in range(size):
                    carried = step(first + (size - 1 - k if back else k), carried)
                return carried

            return go

        return lax.cond(same, run(plain), run(kept), carried)

    return lax.fori_loop(0, count, chunk, carried)


def scan_kernel(seg_ref, h_ref, rate_ref, c_ref, y_ref, s_ref, e_ref):
    half = first_half()
    decay = [jnp.exp(-rate_ref[n]) for n in range(STATE)]

    def plain(t, states):
        row = h_ref[t]
        return [states[n] * decay[n] + row for n in range(STATE)]

    def kept(t, states):
        keep = keep_at(seg_ref, t, half)
        row = h_ref[t]
        return [(states[n] * keep) * decay[n] + row for n in range(STATE)]

    def reading(step):
        def go(t, states):
            states = step(t, states)
            total = c_ref[0] * states[0]
            for n in range(1, STATE):
                total = total + c_ref[n] * states[n]
            y_ref[t - (BL - CTX)] = total
            return states

        return go

    states = [jnp.zeros((8, 128), f32)] * STATE
    states = chunked(seg_ref, 0, BL - CTX, plain, kept, states)
    states = chunked(seg_ref, BL - CTX, BL, reading(plain), reading(kept), states)
    joined = flag(seg_ref[2 * BL] == seg_ref[BL])
    for n in range(STATE):
        s_ref[n] = states[n]
        ends = states[n] + (joined * jnp.exp(-rate_ref[n] * BL)) * pltpu.roll(states[n], 4, 0)
        e_ref[n] = ends


def tail_kernel(
    seg_ref, use_ref, all_ref, s_ref, rate_ref, c_ref, y_ref, out_ref, start_ref, carry_ref
):
    half = first_half()
    before = seg_ref[0]
    joined = flag(seg_ref[BL] == before)
    decay = [jnp.exp(-rate_ref[n]) for n in range(STATE)]
    carry_ref[...] = jnp.zeros_like(carry_ref)

    def gather(j, _):
        @pl.when(use_ref[j] > 0)
        def _():
            for m in range(STATE // 2):
                pair = all_ref[j, 16 * m : 16 * m + 16, :].astype(f32)
                for k in range(2):
                    n = 2 * m + k
                    power = jnp.exp(-rate_ref[n] * (2 * BL))
                    carry_ref[n] = carry_ref[n] * power + pair[8 * k : 8 * k + 8]

        return 0

    lax.fori_loop(0, all_ref.shape[0], gather, 0)
    weighted = []
    for n in range(STATE):
        carried = pltpu.roll(carry_ref[n], 4, 0)
        mid = pltpu.roll(s_ref[n], 4, 0) + (joined * jnp.exp(-rate_ref[n] * BL)) * carry_ref[n]
        start = jnp.where(half, carried, mid)
        start_ref[n] = start
        weighted.append(c_ref[n] * start * jnp.exp(-rate_ref[n] * (BL - CTX + 1)))

    def step(t, parts):
        mask = jnp.where(
            half,
            flag(seg_ref[t + 1 + BL - CTX] == before),
            flag(seg_ref[BL + t + 1 + BL - CTX] == seg_ref[BL]),
        )
        total = parts[0]
        for n in range(1, STATE):
            total = total + parts[n]
        out_ref[t] = y_ref[t] + mask * total
        return [parts[n] * decay[n] for n in range(STATE)]

    lax.fori_loop(0, CTX, step, weighted, unroll=4)


def back_total_kernel(seg_ref, g_ref, rate_ref, c_ref, own_ref, out_ref):
    half = first_half()
    decay = [jnp.exp(-rate_ref[n]) for n in range(STATE)]

    def step(k, sums):
        t = CTX - 1 - k
        mask = jnp.where(
            half,
            flag(seg_ref[t + 1 + BL - CTX] == seg_ref[1]),
            flag(seg_ref[BL + t + 1 + BL - CTX] == seg_ref[BL]),
        )
        grad = mask * g_ref[t]
        return [decay[n] * (sums[n] + grad) for n in range(STATE)]

    sums = lax.fori_loop(0, CTX, step, [jnp.zeros((8, 128), f32)] * STATE, unroll=4)
    joined = flag(seg_ref[1] == seg_ref[BL])
    for n in range(STATE):
        total = sums[n] * c_ref[n] * jnp.exp(-rate_ref[n] * (BL - CTX))
        own_ref[n] = total
        out_ref[n] = total + (joined * jnp.exp(-rate_ref[n] * BL)) * pltpu.roll(total, 4, 0)


def sens_steps(seg_ref, h_ref, half, decay, count):
    def plain(t, both):
        row = h_ref[t]
        sens = [both[1][n] * decay[n] + both[0][n] for n in range(count)]
        states = [both[0][n] * decay[n] + row for n in range(count)]
        return [states, sens] + list(both[2:])

    def kept(t, both):
        keep = keep_at(seg_ref, t, half)
        row = h_ref[t]
        held = [v * keep for v in both[0]]
        sens = [(both[1][n] * keep) * decay[n] + held[n] for n in range(count)]
        states = [held[n] * decay[n] + row for n in range(count)]
        return [states, sens] + list(both[2:])

    return plain, kept


SENS_GROUP = 8


def sens_kernel(seg_ref, h_ref, start_ref, rate_ref, s_ref, z_ref):
    half = first_half()
    for first in range(0, STATE, SENS_GROUP):
        ids = range(first, first + SENS_GROUP)
        decay = [jnp.exp(-rate_ref[n]) for n in ids]
        plain, kept = sens_steps(seg_ref, h_ref, half, decay, SENS_GROUP)
        both = [[start_ref[n] for n in ids], [jnp.zeros((8, 128), f32)] * SENS_GROUP]
        both = chunked(seg_ref, 0, BL - CTX, plain, kept, both)
        for k, n in enumerate(ids):
            s_ref[n] = both[0][k]
            z_ref[n] = both[1][k]


def sens_tail_kernel(seg_ref, h_ref, g_ref, s_ref, z_ref, rate_ref, gc_ref, ga_ref, zend_ref):
    half = first_half()
    for first in range(0, STATE, SENS_GROUP):
        ids = range(first, first + SENS_GROUP)
        decay = [jnp.exp(-rate_ref[n]) for n in ids]

        def summing(step):
            def go(t, carried):
                states, sens, by_c, by_a = step(t, carried)
                grad = g_ref[t - (BL - CTX)]
                by_c = [by_c[n] + grad * states[n] for n in range(SENS_GROUP)]
                by_a = [by_a[n] + grad * sens[n] for n in range(SENS_GROUP)]
                return [states, sens, by_c, by_a]

            return go

        plain, kept = sens_steps(seg_ref, h_ref, half, decay, SENS_GROUP)
        zeros = [jnp.zeros((8, 128), f32)] * SENS_GROUP
        carried = [[s_ref[n] for n in ids], [z_ref[n] for n in ids], zeros, zeros]
        carried = chunked(seg_ref, BL - CTX, BL, summing(plain), summing(kept), carried)
        for k, n in enumerate(ids):
            zend_ref[n] = carried[1][k]
            gc_ref[n] = carried[2][k]
            ga_ref[n] = carried[3][k]


def back_scan_kernel(
    seg_ref,
    use_ref,
    all_ref,
    g_ref,
    own_ref,
    z_ref,
    ga_ref,
    rate_ref,
    c_ref,
    gh_ref,
    out_ref,
    later_ref,
):
    half = first_half()
    decay = [jnp.exp(-rate_ref[n]) for n in range(STATE)]
    joined = flag(seg_ref[2 * BL] == seg_ref[BL])
    later_ref[...] = jnp.zeros_like(later_ref)
    count = all_ref.shape[0]

    def gather(k, _):
        j = count - 1 - k

        @pl.when(use_ref[j] > 0)
        def _():
            for m in range(STATE // 2):
                pair = all_ref[j, 16 * m : 16 * m + 16, :].astype(f32)
                for k in range(2):
                    n = 2 * m + k
                    power = jnp.exp(-rate_ref[n] * (2 * BL))
                    later_ref[n] = later_ref[n] * power + pair[8 * k : 8 * k + 8]

        return 0

    lax.fori_loop(0, count, gather, 0)
    sums = []
    for n in range(STATE):
        first = (
            pltpu.roll(own_ref[n], 4, 0) + (joined * jnp.exp(-rate_ref[n] * BL)) * later_ref[n]
        )
        entering = jnp.where(half, first, pltpu.roll(later_ref[n], 4, 0))
        sums.append(entering)
        out_ref[n] = ga_ref[n] * c_ref[n] + entering * z_ref[n]

    def total_of(t, sums):
        total = sums[0]
        for n in range(1, STATE):
            total = total + sums[n]
        gh_ref[t] = total

    def plain(t, sums):
        total_of(t, sums)
        return [v * decay[n] for n, v in enumerate(sums)]

    def kept(t, sums):
        total_of(t, sums)
        keep = keep_at(seg_ref, t, half)
        return [(v * keep) * decay[n] for n, v in enumerate(sums)]

    def entered(step):
        def go(t, sums):
            grad = g_ref[t - (BL - CTX)]
            return step(t, [sums[n] + c_ref[n] * grad for n in range(STATE)])

        return go

    sums = chunked(seg_ref, BL - CTX, BL, entered(plain), entered(kept), sums, back=True)
    chunked(seg_ref, 0, BL - CTX, plain, kept, sums, back=True)


def to_lanes(values, blocks, steps):
    return (
        values.reshape(blocks, steps, 4, 128).transpose(1, 0, 2, 3).reshape(steps, blocks * 4, 128)
    )


def from_lanes(values, blocks, steps):
    return values.reshape(steps, blocks, 4, 128).transpose(1, 0, 2, 3).reshape(blocks, steps, 512)


def attend_kernel(
    host_ref,
    hid_ref,
    ctx_ref,
    wq_ref,
    wk_ref,
    wv_ref,
    segq_ref,
    segk_ref,
    q_ref,
    k_ref,
    v_ref,
    ck_ref,
    cv_ref,
    pc_ref,
    pb_ref,
    mix_ref,
):
    hid = hid_ref[...]
    ctx = ctx_ref[...]
    q_ref[...] = dot_nn(hid, wq_ref[0]).astype(bf16)
    k_ref[...] = dot_nn(hid, wk_ref[0]).astype(bf16)
    v_ref[...] = dot_nn(hid, wv_ref[0]).astype(bf16)
    ck_ref[...] = dot_nn(ctx, wk_ref[0]).astype(bf16)
    cv_ref[...] = dot_nn(ctx, wv_ref[0]).astype(bf16)
    ctx_ids = segk_ref[:, :CTX]
    for i in range(BL // QT):
        rows = slice(i * QT, (i + 1) * QT)
        reach = (i + 1) * QT
        ids = segq_ref[rows]
        ctx_ok = ctx_ids == ids
        place_q = lax.broadcasted_iota(i32, (QT, reach), 0) + i * QT
        place_k = lax.broadcasted_iota(i32, (QT, reach), 1)
        block_ok = jnp.logical_and(place_k <= place_q, segk_ref[:, CTX : CTX + reach] == ids)
        for head in range(TILE // HEAD_DIM):
            cols = slice(head * HEAD_DIM, (head + 1) * HEAD_DIM)
            query = q_ref[rows, cols]
            sc = dot_nt(query, ck_ref[:, cols]) * (score_scale * LOG2E)
            sb = dot_nt(query, k_ref[:reach, cols]) * (score_scale * LOG2E)
            sc = jnp.where(ctx_ok, sc, masked_score)
            sb = jnp.where(block_ok, sb, masked_score)
            top = jnp.maximum(
                jnp.max(sc, axis=1, keepdims=True), jnp.max(sb, axis=1, keepdims=True)
            )
            ec = jnp.exp2(sc - top)
            eb = jnp.exp2(sb - top)
            total = jnp.sum(ec, axis=1, keepdims=True) + jnp.sum(eb, axis=1, keepdims=True)
            inverse = 1.0 / total
            pc = (ec * inverse).astype(bf16)
            pb = (eb * inverse).astype(bf16)
            pc_ref[head, rows, :] = pc
            pb_ref[head, rows, :reach] = pb
            if reach < BL:
                pb_ref[head, rows, reach:] = jnp.zeros((QT, BL - reach), bf16)
            mixed = dot_nn(pc, cv_ref[:, cols]) + dot_nn(pb, v_ref[:reach, cols])
            mix_ref[rows, cols] = mixed.astype(bf16)


def attend_forward(hosts, block, hidden, context, attn_full, seg_col, seg_row, half_width):
    pairs = half_width // TILE

    def weight(position):
        return pl.BlockSpec((1, D, TILE), lambda p, s: (s[position], 0, p))

    def tile(rows):
        return pl.BlockSpec((rows, TILE), lambda p, s: (0, p))

    heads = half_width // HEAD_DIM
    per = TILE // HEAD_DIM
    return call(
        attend_kernel,
        (pairs,),
        [
            pl.BlockSpec((BL, D), lambda p, s: (block, 0)),
            pl.BlockSpec((CTX, D), lambda p, s: (block, 0)),
            weight(0),
            weight(1),
            weight(2),
            pl.BlockSpec((BL, 1), lambda p, s: (block, 0)),
            whole((1, CTX + BL)),
        ],
        [
            tile(BL),
            tile(BL),
            tile(BL),
            tile(CTX),
            tile(CTX),
            pl.BlockSpec((per, BL, CTX), lambda p, s: (p, 0, 0)),
            pl.BlockSpec((per, BL, BL), lambda p, s: (p, 0, 0)),
            tile(BL),
        ],
        [
            sds((BL, half_width), bf16),
            sds((BL, half_width), bf16),
            sds((BL, half_width), bf16),
            sds((CTX, half_width), bf16),
            sds((CTX, half_width), bf16),
            sds((heads, BL, CTX), bf16),
            sds((heads, BL, BL), bf16),
            sds((BL, half_width), bf16),
        ],
        prefetch=1,
        flops=8 * 10**9,
        nbytes=12 * 10**6,
    )(hosts, hidden, context, attn_full, attn_full, attn_full, seg_col, seg_row)


def attend_back_kernel(
    host_ref,
    own_ref,
    other_ref,
    cot_ref,
    mid_ref,
    gain_ref,
    tok_ref,
    first_gain_ref,
    wo_ref,
    wq_ref,
    wk_ref,
    wv_ref,
    q_ref,
    k_ref,
    v_ref,
    ck_ref,
    cv_ref,
    pc_ref,
    pb_ref,
    low_ref,
    gmid_ref,
    ggain_ref,
    dq_ref,
    dk_ref,
    dv_ref,
    dck_ref,
    dcv_ref,
    hown_ref,
    hsend_ref,
    cown_ref,
    csend_ref,
    sum_ref,
    dsc_ref,
    dsb_ref,
):
    step = pl.program_id(0)
    pairs = pl.num_programs(0) - 2

    @pl.when(step == 0)
    def _():
        grad = own_ref[...].astype(f32) + other_ref[...].astype(f32)
        middle = mid_ref[...]
        inverse = lax.rsqrt(jnp.mean(middle * middle, axis=1, keepdims=True) + epsilon_norm)
        scaled = middle * inverse
        ggain_ref[...] = jnp.sum(grad * scaled, axis=0, keepdims=True)
        weighted = grad * gain_ref[...]
        centre = jnp.mean(weighted * scaled, axis=1, keepdims=True)
        result = cot_ref[...].astype(f32) + inverse * (weighted - scaled * centre)
        gmid_ref[...] = result
        low_ref[...] = result.astype(bf16)

    @pl.when(step < pairs)
    def _():
        grad_mixed = dot_nn(low_ref[...], wo_ref[0]).astype(bf16)
        base = step * TILE
        for head in range(TILE // HEAD_DIM):
            cols = slice(head * HEAD_DIM, (head + 1) * HEAD_DIM)
            to = pl.ds(pl.multiple_of(base + head * HEAD_DIM, HEAD_DIM), HEAD_DIM)
            grad_head = grad_mixed[:, cols]
            for i in range(BL // QT):
                rows = slice(i * QT, (i + 1) * QT)
                reach = (i + 1) * QT
                grad_rows = grad_head[rows]
                gpc = dot_nt(grad_rows, cv_ref[:, cols])
                gpb = dot_nt(grad_rows, v_ref[:reach, cols])
                pc = pc_ref[head, rows, :].astype(f32)
                pb = pb_ref[head, rows, :reach].astype(f32)
                tc = pc * gpc
                tb = pb * gpb
                centre = jnp.sum(tc, axis=1, keepdims=True) + jnp.sum(tb, axis=1, keepdims=True)
                dsc_ref[head, rows, :] = (tc - pc * centre).astype(bf16)
                dsb_ref[head, rows, :reach] = (tb - pb * centre).astype(bf16)
                if reach < BL:
                    dsb_ref[head, rows, reach:] = jnp.zeros((QT, BL - reach), bf16)
            dsc = dsc_ref[head]
            dsb = dsb_ref[head]
            dq = (dot_nn(dsc, ck_ref[:, cols]) + dot_nn(dsb, k_ref[:, cols])) * score_scale
            dq_ref[:, to] = dq.astype(bf16)
            query = q_ref[:, cols]
            dk_ref[:, to] = (dot_tn(dsb, query) * score_scale).astype(bf16)
            dck_ref[:, to] = (dot_tn(dsc, query) * score_scale).astype(bf16)
            dv_ref[:, to] = dot_tn(pb_ref[head], grad_head).astype(bf16)
            dcv_ref[:, to] = dot_tn(pc_ref[head], grad_head).astype(bf16)

    def half():
        part = (
            dot_nt(dq_ref[...], wq_ref[0])
            + dot_nt(dk_ref[...], wk_ref[0])
            + dot_nt(dv_ref[...], wv_ref[0])
        )
        ctx_part = dot_nt(dck_ref[...], wk_ref[0]) + dot_nt(dcv_ref[...], wv_ref[0])
        row_sum = jnp.sum(
            part * (tok_ref[...].astype(f32) * first_gain_ref[...]), axis=1, keepdims=True
        )
        return part, ctx_part, row_sum

    @pl.when(step == pairs)
    def _():
        part, ctx_part, row_sum = half()
        hsend_ref[...] = part.astype(bf16)
        csend_ref[...] = ctx_part.astype(bf16)
        sum_ref[...] = row_sum

    @pl.when(step == pairs + 1)
    def _():
        part, ctx_part, row_sum = half()
        hown_ref[...] = part
        cown_ref[...] = ctx_part
        sum_ref[...] += row_sum


def attend_backward(
    hosts, block, own, other, cot_full, middle, gain, tok_full, first_gain, attn_full, kept, width
):
    pairs = width // TILE
    per = TILE // HEAD_DIM

    def pair(p):
        return jnp.minimum(p, pairs - 1)

    def side(p, s):
        return jnp.where(p <= pairs, 1 - s[8], s[8])

    def weight(position):
        return pl.BlockSpec((1, width, width), lambda p, s: (s[position], side(p, s), 0))

    def tile(rows):
        return pl.BlockSpec((rows, TILE), lambda p, s: (0, pair(p)))

    return call(
        attend_back_kernel,
        (pairs + 2,),
        [
            whole((BL, D)),
            whole((BL, D)),
            pl.BlockSpec((BL, D), lambda p, s: (block, 0)),
            whole((BL, D)),
            whole((1, D)),
            pl.BlockSpec((BL, width), lambda p, s: (block, side(p, s))),
            pl.BlockSpec((1, width), lambda p, s: (0, side(p, s))),
            pl.BlockSpec((1, D, TILE), lambda p, s: (s[3], 0, pair(p))),
            weight(0),
            weight(1),
            weight(2),
            tile(BL),
            tile(BL),
            tile(BL),
            tile(CTX),
            tile(CTX),
            pl.BlockSpec((per, BL, CTX), lambda p, s: (pair(p), 0, 0)),
            pl.BlockSpec((per, BL, BL), lambda p, s: (pair(p), 0, 0)),
        ],
        [
            whole((BL, D)),
            whole((BL, D)),
            whole((1, D)),
            whole((BL, width)),
            whole((BL, width)),
            whole((BL, width)),
            whole((CTX, width)),
            whole((CTX, width)),
            whole((BL, width)),
            whole((BL, width)),
            whole((CTX, width)),
            whole((CTX, width)),
            whole((BL, 1)),
        ],
        [
            sds((BL, D), bf16),
            sds((BL, D), f32),
            sds((1, D), f32),
            sds((BL, width), bf16),
            sds((BL, width), bf16),
            sds((BL, width), bf16),
            sds((CTX, width), bf16),
            sds((CTX, width), bf16),
            sds((BL, width), f32),
            sds((BL, width), bf16),
            sds((CTX, width), f32),
            sds((CTX, width), bf16),
            sds((BL, 1), f32),
        ],
        scratch=[pltpu.VMEM((per, BL, CTX), bf16), pltpu.VMEM((per, BL, BL), bf16)],
        prefetch=1,
        flops=12 * 10**9,
        nbytes=20 * 10**6,
    )(
        hosts,
        own,
        other,
        cot_full,
        middle,
        gain,
        tok_full,
        first_gain,
        attn_full,
        attn_full,
        attn_full,
        attn_full,
        *kept,
    )


def attn_grad_kernel(host_ref, *refs):
    (hid0, hid1, ctx0, ctx1, low0, low1), rest = refs[:6], refs[6:]
    (dq0, dk0, dv0, dck0, dcv0, mix0), rest = rest[:6], rest[6:]
    (dq1, dk1, dv1, dck1, dcv1, mix1), (out_ref,) = rest[:6], rest[6:]
    matrix = pl.program_id(0)

    @pl.when(matrix == 0)
    def _():
        out_ref[0] = (dot_tn(hid0[...], dq0[...]) + dot_tn(hid1[...], dq1[...])).astype(bf16)

    @pl.when(matrix == 1)
    def _():
        out_ref[0] = (
            dot_tn(hid0[...], dk0[...])
            + dot_tn(hid1[...], dk1[...])
            + dot_tn(ctx0[...], dck0[...])
            + dot_tn(ctx1[...], dck1[...])
        ).astype(bf16)

    @pl.when(matrix == 2)
    def _():
        out_ref[0] = (
            dot_tn(hid0[...], dv0[...])
            + dot_tn(hid1[...], dv1[...])
            + dot_tn(ctx0[...], dcv0[...])
            + dot_tn(ctx1[...], dcv1[...])
        ).astype(bf16)

    @pl.when(matrix == 3)
    def _():
        out_ref[0] = (dot_tn(low0[...], mix0[...]) + dot_tn(low1[...], mix1[...])).astype(bf16)


def attn_grads(hosts, hidden, context, lows, blocks, half_width):
    hid_specs = [
        pl.BlockSpec((BL, D), lambda m, s: (0, 0)),
        pl.BlockSpec((BL, D), lambda m, s: (1, 0)),
        pl.BlockSpec((CTX, D), lambda m, s: (0, 0)),
        pl.BlockSpec((CTX, D), lambda m, s: (1, 0)),
    ]
    block_specs = [
        whole((BL, half_width)),
        whole((BL, half_width)),
        whole((BL, half_width)),
        whole((CTX, half_width)),
        whole((CTX, half_width)),
        whole((BL, half_width)),
    ]
    return call(
        attn_grad_kernel,
        (4,),
        hid_specs + [whole((BL, D))] * 2 + block_specs * 2,
        [pl.BlockSpec((1, D, half_width), lambda m, s: (s[m], 0, 0))],
        [sds((OWNER_GROUPS, D, half_width), bf16)],
        prefetch=1,
        flops=46 * 10**8,
        nbytes=14 * 10**6,
    )(hosts, hidden, hidden, context, context, *lows, *blocks[0], *blocks[1])[0]


def mlp_kernel(
    host_ref,
    own_ref,
    other_ref,
    wo_ref,
    woo_ref,
    tok_ref,
    gain_ref,
    cot_ref,
    w1_ref,
    w2_ref,
    mid_ref,
    hid_ref,
    act_ref,
    pre_ref,
    low_ref,
    grad_ref,
):
    step = pl.program_id(0)

    @pl.when(step == 0)
    def _():
        middle = (
            tok_ref[...].astype(f32)
            + dot_nt(own_ref[...], wo_ref[0])
            + dot_nt(other_ref[...], woo_ref[...])
        )
        inverse = lax.rsqrt(jnp.mean(middle * middle, axis=1, keepdims=True) + epsilon_norm)
        mid_ref[...] = middle
        hid_ref[...] = (middle * inverse * gain_ref[...]).astype(bf16)
        grad_ref[...] = jnp.zeros_like(grad_ref)

    w1 = w1_ref[0]
    w2 = w2_ref[0]
    pre = dot_nn(hid_ref[...], w1)
    grad_act = dot_nn(cot_ref[...], w2)
    root = 0.7978845608028654
    square = pre * pre
    gate = 0.5 + 0.5 * jnp.tanh(pre * (root + (root * 0.044715) * square))
    act = pre * gate
    act_ref[...] = act.astype(bf16)
    slope = gate + act * (1.0 - gate) * (2.0 * root + (6.0 * root * 0.044715) * square)
    grad_pre = (slope * grad_act).astype(bf16)
    pre_ref[...] = grad_pre
    grad_ref[...] += dot_nt(grad_pre, w1)

    @pl.when(step == pl.num_programs(0) - 1)
    def _():
        low_ref[...] = grad_ref[...].astype(bf16)


def mlp_block(hosts, block, own, other, attn_full, wo_other, tok_full, gain, cot_full, mlp_full):
    half_width = own.shape[1]
    quarter = mlp_full.shape[2]
    hidden = 2 * quarter
    per = quarter // FT

    def weight(position):
        return pl.BlockSpec(
            (1, D, FT), lambda f, s: (s[4 + 2 * position + f // per], 0, lax.rem(f, per))
        )

    return call(
        mlp_kernel,
        (2 * per,),
        [
            whole((BL, half_width)),
            whole((BL, half_width)),
            pl.BlockSpec((1, D, half_width), lambda f, s: (s[3], 0, 0)),
            whole((D, half_width)),
            pl.BlockSpec((BL, D), lambda f, s: (block, 0)),
            whole((1, D)),
            pl.BlockSpec((BL, D), lambda f, s: (block, 0)),
            weight(0),
            weight(1),
        ],
        [
            whole((BL, D)),
            whole((BL, D)),
            pl.BlockSpec((BL, FT), lambda f, s: (0, f)),
            pl.BlockSpec((BL, FT), lambda f, s: (0, f)),
            whole((BL, D)),
        ],
        [
            sds((BL, D), f32),
            sds((BL, D), bf16),
            sds((BL, hidden), bf16),
            sds((BL, hidden), bf16),
            sds((BL, D), bf16),
        ],
        scratch=[pltpu.VMEM((BL, D), f32)],
        prefetch=1,
        flops=8 * 10**9,
        nbytes=24 * 10**6,
    )(hosts, own, other, attn_full, wo_other, tok_full, gain, cot_full, mlp_full, mlp_full)


def mlp_grad_kernel(host_ref, h0, h1, g0, g1, p0, p1, a0, a1, out_ref):
    matrix = pl.program_id(0)

    @pl.when(matrix == 0)
    def _():
        out_ref[0] = (dot_tn(h0[...], p0[...]) + dot_tn(h1[...], p1[...])).astype(bf16)

    @pl.when(matrix == 1)
    def _():
        out_ref[0] = (dot_tn(g0[...], a0[...]) + dot_tn(g1[...], a1[...])).astype(bf16)


def mlp_grads(hosts, hiddens, cot_full, pres, acts):
    hidden = acts[0].shape[1]
    quarter = hidden // 2
    per = quarter // FT
    last = 2 * per - 1
    used_first = pl.BlockSpec((BL, FT), lambda m, f, s: (0, jnp.where(m == 0, f, last)))
    used_second = pl.BlockSpec((BL, FT), lambda m, f, s: (0, jnp.where(m == 1, f, 0)))
    return call(
        mlp_grad_kernel,
        (2, 2 * per),
        [
            whole((BL, D)),
            whole((BL, D)),
            pl.BlockSpec((BL, D), lambda m, f, s: (0, 0)),
            pl.BlockSpec((BL, D), lambda m, f, s: (1, 0)),
            used_first,
            used_first,
            used_second,
            used_second,
        ],
        [
            pl.BlockSpec(
                (1, D, FT), lambda m, f, s: (s[4 + 2 * m + f // per], 0, lax.rem(f, per))
            )
        ],
        [sds((OWNER_GROUPS, D, quarter), bf16)],
        prefetch=1,
        flops=86 * 10**8,
        nbytes=20 * 10**6,
    )(hosts, hiddens[0], hiddens[1], cot_full, cot_full, pres[0], pres[1], acts[0], acts[1])[0]


def mlp_out_kernel(host_ref, a0, a1, wa_ref, wb_ref, mid0, mid1, send_ref, own_ref):
    step = pl.program_id(0)
    quarter = wa_ref.shape[2]

    def rows(a_ref):
        return dot_nt(a_ref[:, :quarter], wa_ref[0]) + dot_nt(a_ref[:, quarter:], wb_ref[0])

    @pl.when(step == 0)
    def _():
        send_ref[:BL, :] = rows(a0).astype(bf16)
        send_ref[BL:, :] = rows(a1).astype(bf16)

    @pl.when(step == 1)
    def _():
        own_ref[:BL, :] = rows(a0) + mid0[...]
        own_ref[BL:, :] = rows(a1) + mid1[...]


def mlp_out(hosts, acts, mlp_full, middles, width):
    quarter = mlp_full.shape[2]

    def side(d, s):
        return jnp.where(d == 0, 1 - s[8], s[8])

    def weight(position):
        return pl.BlockSpec((1, width, quarter), lambda d, s: (s[position], side(d, s), 0))

    middle = pl.BlockSpec((BL, width), lambda d, s: (0, s[8]))
    return call(
        mlp_out_kernel,
        (2,),
        [whole((BL, 2 * quarter))] * 2 + [weight(6), weight(7), middle, middle],
        [whole((2 * BL, width))] * 2,
        [sds((2 * BL, width), bf16), sds((2 * BL, width), f32)],
        prefetch=1,
        flops=44 * 10**8,
        nbytes=12 * 10**6,
    )(hosts, *acts, mlp_full, mlp_full, *middles)


def adam_step(gradient, moment_one, moment_two, weight, rate_table, decay_weight):
    step_count = f32(STEP)
    first_new = beta_first * moment_one + (1.0 - beta_first) * gradient
    second_new = beta_second * moment_two + (1.0 - beta_second) * gradient * gradient
    fixed_one = 1.0 - jnp.power(beta_first, step_count)
    fixed_two = 1.0 - jnp.power(beta_second, step_count)
    update = first_new / fixed_one / (jnp.sqrt(second_new / fixed_two) + epsilon_adam)
    return (first_new, second_new, weight - rate_table * (update + decay_weight * weight))


def body(
    tokens,
    cotangent,
    segments,
    owners,
    attn_master,
    attn_first,
    attn_second,
    mlp_master,
    mlp_first,
    mlp_second,
    ssm_params,
    ssm_first,
    ssm_second,
    norm_gains,
    gains_first,
    gains_second,
):
    rows = tokens.shape[1]
    width = tokens.shape[2]
    blocks = rows // BL
    dp_count = lax.axis_size("dp")
    dp_here = lax.axis_index("dp")
    side = lax.axis_index("tensor")
    group = dp_here // (dp_count // OWNER_GROUPS)
    quarter = mlp_master.shape[2] // 2

    def both_sides(own, other):
        return jnp.where(
            side == 0,
            jnp.concatenate([own, other], axis=-1),
            jnp.concatenate([other, own], axis=-1),
        )

    def side_of(values, which):
        return lax.dynamic_slice_in_dim(values, which * width, width, values.ndim - 1)

    smem = pl.BlockSpec(memory_space=pltpu.SMEM)
    vmem = pl.BlockSpec(memory_space=pltpu.VMEM)
    hosts, rates = pl.pallas_call(
        plan_kernel,
        in_specs=[smem, smem],
        out_specs=[smem, smem],
        out_shape=[sds((PLAN_SIZE,), i32), sds((4,), f32)],
    )(owners, jnp.stack([side, group]).astype(i32))
    attn_here = hosts[ATTN_HERE]
    mlp_here = hosts[MLP_HERE]
    near = hosts[NEAR] == 1
    ring = Ring()

    attn_low = attn_master.astype(bf16)
    mlp_low = mlp_master[0].astype(bf16)
    attn_moved = move(attn_low[1], hosts[WAY], ATTN_WAYS, False)
    attn_block = jnp.where(attn_here == 0, attn_moved, attn_low[0])
    mlp_moved = exchange_groups(mlp_low[:, quarter:], near)

    tok = tokens.reshape(rows, width)
    cot = cotangent.reshape(rows, width)
    tok_f = tok.astype(f32)
    square_here = jnp.sum(tok_f * tok_f, axis=1)
    square_other = swap_x(square_here)
    tok_other = swap_x(tok)
    gains_other = swap_x(norm_gains)
    inverse_one = lax.rsqrt((square_here + square_other) / D + epsilon_norm)
    scaled_own = tok_f * inverse_one[:, None]
    hidden_own = (scaled_own * norm_gains[0]).astype(bf16)
    gains_full = both_sides(norm_gains, gains_other)

    seg = segments.reshape(rows)
    prior = lax.ppermute(seg[rows - CTX :] + 1, "dp", [(i, i + 1) for i in range(dp_count - 1)]) - 1
    seg_ext = jnp.concatenate([prior[CTX - 1 :], seg])
    seg_col = seg[:, None]

    param_lanes = ssm_params.transpose(0, 2, 1)
    decay_rate = jnp.exp(param_lanes[0]) * (BL ** (-0.5) / 32.0)
    drive_root = jnp.sqrt(-jnp.expm1(-2.0 * decay_rate))
    reading = param_lanes[2] * drive_root * param_lanes[1]

    def doubled(values):
        lanes = values.reshape(STATE, 4, 128)
        return jnp.concatenate([lanes] * blocks, axis=1)

    rate_lanes = doubled(decay_rate)
    reading_lanes = doubled(reading)
    state_shape = sds((STATE, 8, 128), f32)

    def plain(kernel, scalars, count, outs, cost, scratch=()):
        return pl.pallas_call(
            kernel,
            in_specs=[smem] * scalars + [vmem] * count,
            out_specs=[vmem] * len(outs),
            out_shape=outs,
            scratch_shapes=scratch,
            name=kernel.__name__,
            compiler_params=pltpu.CompilerParams(vmem_limit_bytes=16 * 1024 * 1024),
            cost_estimate=pl.CostEstimate(flops=cost // COST, bytes_accessed=10**6 // COST, transcendentals=0),
        )

    hidden_lanes = to_lanes(hidden_own.astype(f32), blocks, BL)
    tail_lanes = sds((CTX, 8, 128), f32)
    tail_part, state_ends, device_end = plain(
        scan_kernel, 1, 3, [tail_lanes, state_shape, state_shape], 4 * 10**9
    )(gate(seg_ext, attn_moved), hidden_lanes, rate_lanes, reading_lanes)
    id_rows = jnp.where(
        (jnp.arange(16) == 0)[:, None], seg[rows - 1].astype(f32), seg[0].astype(f32)
    )
    message = jnp.concatenate(
        [device_end.reshape(STATE * 8, 128), jnp.broadcast_to(id_rows, (16, 128))], axis=0
    ).astype(bf16)
    attn_full, states_all, gathered = ring.all_gather(attn_block, message, {0: (mlp_moved,), 2: (tok_other,)})
    mlp_block_low = jnp.where(
        mlp_here == 0, gate(mlp_moved, gathered, states_all), mlp_low[:, :quarter]
    )
    mlp_full = lax.all_gather(mlp_block_low, "dp", axis=0, tiled=True)
    mlp_full = mlp_full.reshape(OWNER_GROUPS, D, quarter)
    attn_full = attn_full.reshape(OWNER_GROUPS, D, width)
    hidden_full = join_sides(
        hosts,
        tok,
        tok_other,
        (inverse_one[:, None], norm_gains[0:1], gains_other[0:1]),
    )
    tok_full = join_sides(hosts, tok, tok_other)
    ids_all = states_all[:, STATE * 8 : STATE * 8 + 2, 0].astype(i32)
    places = jnp.arange(dp_count, dtype=i32)
    use_before = jnp.logical_and(places < dp_here, ids_all[:, 0] == seg_ext[0]).astype(i32)
    use_after = jnp.logical_and(places > dp_here, ids_all[:, 1] == seg[rows - 1]).astype(i32)
    tails, state_starts = plain(
        tail_kernel, 2, 5, [tail_lanes, state_shape], 10**9, [pltpu.VMEM((STATE, 8, 128), f32)]
    )(seg_ext, use_before, states_all, state_ends, rate_lanes, reading_lanes, tail_part)
    sens_states, sens_starts = plain(sens_kernel, 1, 3, [state_shape] * 2, 6 * 10**9)(
        seg_ext, hidden_lanes, state_starts, rate_lanes
    )
    tails = from_lanes(tails, blocks, CTX).astype(bf16)
    context_own = shift_tails(tails[blocks - 1], 1, False)
    context_other = shift_tails(tails[blocks - 1], 1, True)
    inner_own = tails[: blocks - 1]
    inner_other = swap_x(inner_own)
    context_full = jnp.concatenate(
        [
            both_sides(context_own, context_other)[None],
            both_sides(inner_own, inner_other),
        ],
        axis=0,
    ).reshape(-1, D)

    cot_other = swap_x(gate(cot, inner_other))

    seg_rows = []
    for b in range(blocks):
        before = prior if b == 0 else seg[b * BL - CTX : b * BL]
        seg_rows.append(jnp.concatenate([before, seg[b * BL : (b + 1) * BL]])[None])
    kept = []
    mixed = []
    mixed_other = []
    for b in range(blocks):
        outs = attend_forward(
            hosts, b, hidden_full, context_full, attn_full, seg_col, seg_rows[b], width
        )
        kept.append(outs[:7])
        mixed.append(outs[7])
        mixed_other.append(swap_x(outs[7]))
    wo_own = lax.dynamic_index_in_dim(attn_full, hosts[3], 0, keepdims=False)
    wo_half = lax.dynamic_slice_in_dim(wo_own, ring.core * (D // 2), D // 2, 0)
    wo_first = swap_x(wo_half)
    wo_second = lax.ppermute(gate(wo_first, mixed[0]), "dp", ring.cores)
    joined = together(*mixed_other, sens_states, sens_starts)
    mixed_other, (sens_states, sens_starts) = list(joined[:blocks]), joined[blocks:]
    wo_other = jnp.where(
        ring.core == 0,
        jnp.concatenate([wo_first, wo_second], axis=0),
        jnp.concatenate([wo_second, wo_first], axis=0),
    )

    cot_full = join_sides(hosts, gate(cot, mixed[0]), cot_other)

    gain_two = gains_full[1:2]
    middles, hiddens, acts, pres, grads, grads_other = [], [], [], [], [], []
    for b in range(blocks):
        middle, hidden_two, act, grad_pre, grad_low = mlp_block(
            hosts,
            b,
            mixed[b],
            mixed_other[b],
            attn_full,
            wo_other,
            tok_full,
            gain_two,
            cot_full,
            mlp_full,
        )
        middles.append(middle)
        hiddens.append(hidden_two)
        acts.append(act)
        pres.append(grad_pre)
        grads.append(grad_low)
        grads_other.append(swap_x(grad_low))
    mlp_sum_in = mlp_grads(hosts, hiddens, cot_full, pres, acts)
    grads_other[0], mlp_sum_in = lax.optimization_barrier((grads_other[0], mlp_sum_in))
    mlp_sum = lax.psum_scatter(
        mlp_sum_in.reshape(OWNER_GROUPS * D, quarter), "dp", scatter_dimension=0, tiled=True
    )

    lows, grad_mids, gain_twos, grad_blocks = [], [], [], []
    parts, parts_sent, ctx_parts, ctx_sent, row_sums = [], [], [], [], []
    for b in range(blocks):
        outs = attend_backward(
            hosts,
            b,
            gate(grads[b], *lows),
            grads_other[b],
            cot_full,
            middles[b],
            gain_two,
            tok_full,
            gains_full[0:1],
            attn_full,
            kept[b],
            width,
        )
        lows.append(outs[0])
        grad_mids.append(side_of(outs[1], side))
        gain_twos.append(side_of(outs[2], side))
        grad_blocks.append(list(outs[3:8]) + [mixed[b]])
        parts.append(outs[8])
        parts_sent.append(outs[9])
        ctx_parts.append(outs[10])
        ctx_sent.append(outs[11])
        row_sums.append(outs[12][:, 0])
    grad_tails = jnp.stack(
        [ctx_parts[b] + swap_x(ctx_sent[b]).astype(f32) for b in range(1, blocks)]
        + [
            shift_tails(ctx_parts[0].astype(bf16), -1, False).astype(f32)
            + shift_tails(ctx_sent[0], -1, True).astype(f32)
        ]
    )
    tail_grad_lanes = to_lanes(grad_tails.reshape(blocks * CTX, width), blocks, CTX)
    own_back, device_back = plain(back_total_kernel, 1, 3, [state_shape, state_shape], 10**9)(
        seg_ext, tail_grad_lanes, rate_lanes, reading_lanes
    )
    attn_sum_in = attn_grads(hosts, hidden_full, context_full, lows, grad_blocks, width)
    acts[0] = gate(acts[0], device_back)
    out_send, out_own = mlp_out(hosts, acts, mlp_full, middles, width)
    received = [swap_x(v) for v in parts_sent]
    block_out = (out_own + swap_x(gate(out_send, *received)).astype(f32)).astype(bf16)

    attn_sum, back_all, mlp_sum = ring.reduce_scatter(
        attn_sum_in.reshape(dp_count, -1, width),
        device_back.reshape(STATE * 8, 128).astype(bf16),
        mlp_sum,
    )
    mlp_back = exchange_groups(mlp_sum, near)
    attn_sum = attn_sum.astype(bf16)
    grad_c_lanes, grad_a_lanes, sens_end = plain(
        sens_tail_kernel, 1, 5, [state_shape] * 3, 2 * 10**9
    )(seg_ext, hidden_lanes, tail_grad_lanes, sens_states, sens_starts, rate_lanes)
    grad_lanes, grad_a_lanes = plain(
        back_scan_kernel,
        2,
        7,
        [sds((BL, 8, 128), f32), state_shape],
        4 * 10**9,
        [pltpu.VMEM((STATE, 8, 128), f32)],
    )(
        seg_ext,
        use_after,
        back_all,
        tail_grad_lanes,
        own_back,
        sens_end,
        grad_a_lanes,
        rate_lanes,
        reading_lanes,
    )
    grad_channels = lax.optimization_barrier(
        from_lanes(grad_lanes, blocks, BL).reshape(rows, width)
    )

    part = jnp.concatenate(parts, axis=0)
    received = jnp.concatenate(received, axis=0)
    row_here = inverse_one * jnp.concatenate(row_sums) + jnp.sum(
        grad_channels * (scaled_own * norm_gains[0]), axis=1
    )
    row_total = row_here + swap_x(row_here)
    grad_hidden = part + received.astype(f32) + grad_channels
    grad_tokens = jnp.concatenate(grad_mids, axis=0) + inverse_one[:, None] * (
        grad_hidden * norm_gains[0] - scaled_own * (row_total / D)[:, None]
    )
    gain_one = jnp.sum(grad_hidden * scaled_own, axis=0)
    gain_two_sum = sum(gain_twos)[0]

    def merged(values):
        return sum(values[:, 4 * b : 4 * b + 4] for b in range(blocks)).reshape(STATE, width)

    small, mlp_back = total_dp(
        jnp.concatenate(
            [merged(grad_c_lanes), merged(grad_a_lanes), gain_one[None], gain_two_sum[None]], axis=0
        ),
        mlp_back,
    )
    grad_c, grad_a = small[:STATE], small[STATE : 2 * STATE]
    gains_grad = small[2 * STATE :]
    decay_step = jnp.exp(-decay_rate)
    grad_read = grad_c * drive_root * param_lanes[1]
    grad_drive = grad_c * drive_root * param_lanes[2]
    grad_a = grad_a - grad_c * param_lanes[1] * param_lanes[2] * decay_step / drive_root
    grad_log = -decay_rate * decay_step * grad_a
    ssm_grad = jnp.stack([grad_log, grad_drive, grad_read]).transpose(0, 2, 1)

    attn_back = move(attn_sum, hosts[WAY], ATTN_WAYS, True)
    attn_grad = jnp.stack(
        [
            jnp.where(attn_here >= 1, attn_sum.astype(f32), 0.0),
            jnp.where(attn_here == 2, attn_back.astype(f32), 0.0),
        ]
    )
    mlp_grad = jnp.where(
        mlp_here == 1, jnp.concatenate([mlp_sum, mlp_back], axis=1).astype(f32), 0.0
    )[None]

    attn_rates = rates[:2, None, None]
    mlp_rates = rates[2]
    ssm_rates = jnp.asarray([1.0, 0.8, 0.25], f32)[:, None, None]
    gain_rates = jnp.asarray([0.6, 0.6], f32)[:, None]
    attn_one, attn_two, attn_new = adam_step(
        attn_grad, attn_first, attn_second, attn_master, attn_rates, matrix_decay
    )
    mlp_one, mlp_two, mlp_new = adam_step(
        mlp_grad, mlp_first, mlp_second, mlp_master, mlp_rates, matrix_decay
    )
    ssm_one, ssm_two, ssm_new = adam_step(
        ssm_grad, ssm_first, ssm_second, ssm_params, ssm_rates, 0.0
    )
    gain_first_new, gain_second_new, gains_new = adam_step(
        gains_grad, gains_first, gains_second, norm_gains, gain_rates, 0.0
    )
    return (
        block_out.reshape(tokens.shape),
        grad_tokens.reshape(tokens.shape),
        attn_grad,
        attn_one,
        attn_two,
        attn_new,
        attn_new.astype(bf16),
        mlp_grad,
        mlp_one,
        mlp_two,
        mlp_new,
        mlp_new.astype(bf16),
        ssm_grad,
        ssm_one,
        ssm_two,
        ssm_new,
        gains_grad,
        gain_first_new,
        gain_second_new,
        gains_new,
    )


def solution(mesh):
    in_specs = (
        P(None, "dp", "tensor"),
        P(None, "dp", "tensor"),
        P(None, "dp"),
        P(),
        P(None, "dp", "tensor"),
        P(None, "dp", "tensor"),
        P(None, "dp", "tensor"),
        P(None, "dp", "tensor"),
        P(None, "dp", "tensor"),
        P(None, "dp", "tensor"),
        P(None, "tensor", None),
        P(None, "tensor", None),
        P(None, "tensor", None),
        P(None, "tensor"),
        P(None, "tensor"),
        P(None, "tensor"),
    )
    out_specs = (
        P(None, "dp", "tensor"),
        P(None, "dp", "tensor"),
        P(None, "dp", "tensor"),
        P(None, "dp", "tensor"),
        P(None, "dp", "tensor"),
        P(None, "dp", "tensor"),
        P(None, "dp", "tensor"),
        P(None, "dp", "tensor"),
        P(None, "dp", "tensor"),
        P(None, "dp", "tensor"),
        P(None, "dp", "tensor"),
        P(None, "dp", "tensor"),
        P(None, "tensor", None),
        P(None, "tensor", None),
        P(None, "tensor", None),
        P(None, "tensor", None),
        P(None, "tensor"),
        P(None, "tensor"),
        P(None, "tensor"),
        P(None, "tensor"),
    )
    return jax.shard_map(body, mesh=mesh, in_specs=in_specs, out_specs=out_specs, check_vma=False)
```

```python
import functools
import itertools

import jax
import jax.numpy as jnp
from jax import lax
from jax.experimental import pallas as pl
from jax.experimental.pallas import tpu as pltpu
from jax.sharding import PartitionSpec as P

D = 1024
HEAD_DIM = 128
FF = 4096
STATE = 16
CTX = 128
BL = 512
OWNER_GROUPS = 4
STEP = 5

epsilon_norm = 1e-05
beta_first = 0.9
beta_second = 0.95
epsilon_adam = 1e-08
matrix_decay = 0.1
masked_score = -1e30
score_scale = HEAD_DIM ** (-0.5)
f32 = jnp.float32
bf16 = jnp.bfloat16
i32 = jnp.int32
SWAP = [(0, 1), (1, 0)]
COST = 1000
TILE = 256
QT = 256
FT = 512
LOG2E = 1.4426950408889634


def dot_nn(left, right):
    return lax.dot_general(left, right, (((1,), (0,)), ((), ())), preferred_element_type=f32)


def dot_nt(left, right):
    return lax.dot_general(left, right, (((1,), (1,)), ((), ())), preferred_element_type=f32)


def dot_tn(left, right):
    return lax.dot_general(left, right, (((0,), (0,)), ((), ())), preferred_element_type=f32)


def call(
    kernel, grid, in_specs, out_specs, out_shape, scratch=(), prefetch=0, flops=0, nbytes=0, room=36
):
    return pl.pallas_call(
        kernel,
        grid_spec=pltpu.PrefetchScalarGridSpec(
            num_scalar_prefetch=prefetch,
            grid=grid,
            in_specs=in_specs,
            out_specs=out_specs,
            scratch_shapes=scratch,
        ),
        out_shape=out_shape,
        name=kernel.__name__,
        compiler_params=pltpu.CompilerParams(vmem_limit_bytes=room * 1024 * 1024),
        cost_estimate=pl.CostEstimate(flops=flops // COST, bytes_accessed=nbytes // COST, transcendentals=0),
    )


def whole(shape):
    return pl.BlockSpec(shape, lambda *_: (0,) * len(shape), pipeline_mode=pl.Buffered(1))


def sds(shape, dtype):
    return jax.ShapeDtypeStruct(shape, dtype)


def hbm(*values):
    held = tuple(pltpu.with_memory_space_constraint(v, pltpu.HBM) for v in values)
    return held[0] if len(held) == 1 else held


def swap_x(values):
    return lax.ppermute(values, "tensor", SWAP)


def gate(value, *others):
    if not others:
        return value
    return lax.optimization_barrier((value,) + others)[0]


def together(*values):
    return lax.optimization_barrier(values)


def gather_rounds():
    return max(lax.axis_size("dp") - 1, 0).bit_length()


def gather_round(held, k):
    step = 1 << k
    count = lax.axis_size("dp")
    other = lax.ppermute(held, "dp", [(i, i ^ step) for i in range(count)])
    later = (lax.axis_index("dp") // step) % 2 == 1
    return jnp.where(
        later,
        jnp.concatenate([other, held], axis=0),
        jnp.concatenate([held, other], axis=0),
    )


def total_dp(values, beside):
    count = lax.axis_size("dp")
    for k in range(gather_rounds()):
        if k == 1:
            values, beside = together(values, beside)
        values = values + lax.ppermute(values, "dp", [(i, i ^ (1 << k)) for i in range(count)])
    return values, beside


def routes(full_count, empty_count):
    groups = range(OWNER_GROUPS)
    ways = []
    for full in itertools.combinations(groups, full_count):
        rest = [g for g in groups if g not in full]
        for empty in itertools.combinations(rest, empty_count):
            ways.append((full, empty))
    return ways


ATTN_WAYS = routes(1, 1) + routes(2, 2)


def way_code(full, empty):
    code = 0
    for g in range(OWNER_GROUPS):
        digit = 2 if g in full else (0 if g in empty else 1)
        code += digit * 3**g
    return code


def one_if(condition):
    return jnp.where(condition, jnp.int32(1), jnp.int32(0))


HOST_MLP, SIDE, WAY, NEAR, ATTN_HERE, MLP_HERE, PLAN_SIZE = 4, 8, 9, 10, 11, 12, 16
ATTN_RATES = [0.5 * D ** (-0.5)] * 3 + [0.5 * (D // 16) ** (-0.5)]
MLP_RATES = [0.5 * D ** (-0.5), 0.5 * FF ** (-0.5)]
IDLE_RATE = 0.5 * D ** (-0.5)


def plan_kernel(owner_ref, here_ref, out_ref, rate_ref):
    groups = range(OWNER_GROUPS)
    side, group = here_ref[0], here_ref[1]
    owner = [owner_ref[m] for m in range(6)]
    slot = [
        sum([one_if(owner[k] == owner[m]) for k in range(m)], jnp.int32(0)) for m in range(4)
    ]
    count = [sum([one_if(owner[m] == g) for m in range(4)], jnp.int32(0)) for g in groups]
    full_rank = [sum([one_if(count[h] == 2) for h in range(g)], jnp.int32(0)) for g in groups]
    empty_rank = [sum([one_if(count[h] == 0) for h in range(g)], jnp.int32(0)) for g in groups]
    taker = [
        sum(
            [
                jnp.where(
                    jnp.logical_and(count[h] == 0, empty_rank[h] == full_rank[g]), jnp.int32(h), 0
                )
                for h in groups
            ],
            jnp.int32(0),
        )
        for g in groups
    ]
    for m in range(4):
        second = sum([jnp.where(owner[m] == g, taker[g], 0) for g in groups], jnp.int32(0))
        out_ref[m] = jnp.where(slot[m] == 0, owner[m], second)
    code = sum([count[g] * 3**g for g in groups], jnp.int32(0))
    out_ref[WAY] = sum(
        [
            jnp.where(code == way_code(*way), jnp.int32(k), 0)
            for k, way in enumerate(ATTN_WAYS)
        ],
        jnp.int32(0),
    )
    low = sum([one_if(owner[m] < 2) for m in (4, 5)], jnp.int32(0))
    near = low == 1
    for k, m in enumerate((4, 5)):
        out_ref[HOST_MLP + 2 * k] = owner[m]
        bit = jnp.where(near, jnp.int32(1), jnp.int32(2))
        out_ref[HOST_MLP + 2 * k + 1] = jnp.bitwise_xor(owner[m], bit)
    out_ref[SIDE] = side
    out_ref[NEAR] = one_if(near)
    out_ref[ATTN_HERE] = sum([one_if(owner[m] == group) for m in range(4)], jnp.int32(0))
    out_ref[MLP_HERE] = sum([one_if(owner[m] == group) for m in (4, 5)], jnp.int32(0))
    for k in range(MLP_HERE + 1, PLAN_SIZE):
        out_ref[k] = jnp.int32(0)
    for place in range(2):
        rate = f32(IDLE_RATE)
        for m in range(4):
            hit = jnp.logical_and(owner[m] == group, slot[m] == place)
            rate = jnp.where(hit, f32(ATTN_RATES[m]), rate)
        rate_ref[place] = rate
    rate = f32(IDLE_RATE)
    for k, m in enumerate((4, 5)):
        rate = jnp.where(owner[m] == group, f32(MLP_RATES[k]), rate)
    rate_ref[2] = rate
    rate_ref[3] = f32(0.0)


def move(values, index, ways, back):
    size = lax.axis_size("dp") // OWNER_GROUPS

    def branch(way):
        pairs = []
        for a, b in zip(*way):
            if back:
                a, b = b, a
            pairs += [(a * size + j, b * size + j) for j in range(size)]
        return lambda v: lax.ppermute(v, "dp", pairs)

    return lax.switch(index, [branch(way) for way in ways], values)


def exchange_groups(values, near):
    size = lax.axis_size("dp") // OWNER_GROUPS

    def across(bit):
        return lax.ppermute(
            values,
            "dp",
            [(g * size + j, (g ^ bit) * size + j) for g in range(OWNER_GROUPS) for j in range(size)],
        )

    return jnp.where(near, across(1), across(2))


def ring_order(count):
    chips = count // 2
    if chips == 8:
        return [0, 2, 4, 6, 7, 5, 3, 1]
    return list(range(chips))


def join_kernel(host_ref, own_ref, other_ref, out_ref):
    @pl.when(pl.program_id(0) == 0)
    def _():
        out_ref[...] = own_ref[...]

    @pl.when(pl.program_id(0) == 1)
    def _():
        out_ref[...] = other_ref[...]


def join_scaled_kernel(
    host_ref, own_ref, other_ref, inverse_ref, gain_ref, gain_other_ref, out_ref
):
    @pl.when(pl.program_id(0) == 0)
    def _():
        out_ref[...] = (own_ref[...].astype(f32) * inverse_ref[...] * gain_ref[...]).astype(bf16)

    @pl.when(pl.program_id(0) == 1)
    def _():
        out_ref[...] = (
            other_ref[...].astype(f32) * inverse_ref[...] * gain_other_ref[...]
        ).astype(bf16)


def join_sides(hosts, own, other, scales=()):
    rows, width = own.shape
    return call(
        join_scaled_kernel if scales else join_kernel,
        (2,),
        [whole(v.shape) for v in (own, other) + tuple(scales)],
        [
            pl.BlockSpec(
                (rows, width), lambda d, s: (0, jnp.where(d == 0, s[SIDE], 1 - s[SIDE]))
            )
        ],
        [pltpu.HBM((rows, 2 * width), bf16)],
        prefetch=1,
        nbytes=8 * rows * width,
        room=12,
    )(hosts, own, other, *scales)[0]


class Ring:
    def __init__(self):
        self.count = lax.axis_size("dp")
        self.chips = self.count // 2
        order = ring_order(self.count)
        here = lax.axis_index("dp")
        self.core = here % 2
        chip = here // 2
        self.place = jnp.where(chip % 2 == 0, chip // 2, 7 - chip // 2) if self.chips == 8 else chip
        self.up = [
            (2 * order[p] + c, 2 * order[(p + 1) % self.chips] + c)
            for p in range(self.chips)
            for c in range(2)
        ]
        self.down = [(b, a) for a, b in self.up]
        self.cores = [(i, i ^ 1) for i in range(self.count)]
        self.far_up = self.chips // 2
        self.far_down = self.chips - 1 - self.far_up

    def chip(self, offset):
        place = (self.place + self.chips + offset) % self.chips
        if self.chips != 8:
            return place
        return jnp.where(place < 4, 2 * place, 15 - 2 * place)

    def start(self, blocks):
        pairs = blocks.reshape((self.chips, 2) + blocks.shape[1:])
        mine = lax.dynamic_index_in_dim(pairs, self.core, 1, keepdims=False)
        theirs = lax.dynamic_index_in_dim(pairs, 1 - self.core, 1, keepdims=False)
        received = lax.ppermute(theirs, "dp", self.cores)

        def part(offset):
            chip = self.chip(offset)
            return lax.dynamic_index_in_dim(mine, chip, 0, keepdims=False).astype(
                f32
            ) + lax.dynamic_index_in_dim(received, chip, 0, keepdims=False).astype(f32)

        return part, part(self.far_up).astype(bf16), part(-self.far_down).astype(bf16)

    def step(self, k, part, up, down):
        if k < self.far_up:
            up = lax.ppermute(up, "dp", self.up)
            if k < self.far_up - 1:
                up = (up.astype(f32) + part(self.far_up - 1 - k)).astype(bf16)
        if k < self.far_down:
            down = lax.ppermute(down, "dp", self.down)
            if k < self.far_down - 1:
                down = (down.astype(f32) + part(k + 1 - self.far_down)).astype(bf16)
        return up, down


def shift_tails(values, by, cross):
    count = lax.axis_size("dp")
    pairs = [
        (2 * i + s, 2 * (i + by) + (1 - s if cross else s))
        for i in range(count)
        for s in range(2)
        if 0 <= i + by < count
    ]
    return lax.ppermute(values, ("dp", "tensor"), pairs)


def first_half():
    return lax.broadcasted_iota(i32, (8, 128), 0) < 4


def flag(condition):
    return jnp.where(condition, f32(1.0), f32(0.0))


def keep_at(seg_ref, t, half):
    return jnp.where(
        half, flag(seg_ref[t + 1] == seg_ref[t]), flag(seg_ref[BL + t + 1] == seg_ref[BL + t])
    )


def chunked(seg_ref, begin, end, plain, kept, carried, back=False):
    size = 8
    count = (end - begin) // size

    def chunk(c, carried):
        first = begin + (count - 1 - c if back else c) * size
        same = jnp.logical_and(
            seg_ref[first] == seg_ref[first + size],
            seg_ref[BL + first] == seg_ref[BL + first + size],
        )

        def run(step):
            def go(carried):
                for k in range(size):
                    carried = step(first + (size - 1 - k if back else k), carried)
                return carried

            return go

        return lax.cond(same, run(plain), run(kept), carried)

    return lax.fori_loop(0, count, chunk, carried)


def scan_kernel(seg_ref, h_ref, rate_ref, c_ref, y_ref, s_ref, e_ref):
    half = first_half()
    decay = [jnp.exp(-rate_ref[n]) for n in range(STATE)]

    def plain(t, states):
        row = h_ref[t]
        return [states[n] * decay[n] + row for n in range(STATE)]

    def kept(t, states):
        keep = keep_at(seg_ref, t, half)
        row = h_ref[t]
        return [(states[n] * keep) * decay[n] + row for n in range(STATE)]

    def reading(step):
        def go(t, states):
            states = step(t, states)
            total = c_ref[0] * states[0]
            for n in range(1, STATE):
                total = total + c_ref[n] * states[n]
            y_ref[t - (BL - CTX)] = total
            return states

        return go

    states = [jnp.zeros((8, 128), f32)] * STATE
    states = chunked(seg_ref, 0, BL - CTX, plain, kept, states)
    states = chunked(seg_ref, BL - CTX, BL, reading(plain), reading(kept), states)
    joined = flag(seg_ref[2 * BL] == seg_ref[BL])
    for n in range(STATE):
        s_ref[n] = states[n]
        ends = states[n] + (joined * jnp.exp(-rate_ref[n] * BL)) * pltpu.roll(states[n], 4, 0)
        e_ref[n] = ends


def tail_kernel(
    seg_ref, use_ref, all_ref, s_ref, rate_ref, c_ref, y_ref, out_ref, start_ref, carry_ref
):
    half = first_half()
    before = seg_ref[0]
    joined = flag(seg_ref[BL] == before)
    decay = [jnp.exp(-rate_ref[n]) for n in range(STATE)]
    carry_ref[...] = jnp.zeros_like(carry_ref)

    def gather(j, _):
        @pl.when(use_ref[j] > 0)
        def _():
            for m in range(STATE // 2):
                pair = all_ref[j, 16 * m : 16 * m + 16, :].astype(f32)
                for k in range(2):
                    n = 2 * m + k
                    power = jnp.exp(-rate_ref[n] * (2 * BL))
                    carry_ref[n] = carry_ref[n] * power + pair[8 * k : 8 * k + 8]

        return 0

    lax.fori_loop(0, all_ref.shape[0], gather, 0)
    weighted = []
    for n in range(STATE):
        carried = pltpu.roll(carry_ref[n], 4, 0)
        mid = pltpu.roll(s_ref[n], 4, 0) + (joined * jnp.exp(-rate_ref[n] * BL)) * carry_ref[n]
        start = jnp.where(half, carried, mid)
        start_ref[n] = start
        weighted.append(c_ref[n] * start * jnp.exp(-rate_ref[n] * (BL - CTX + 1)))

    def step(t, parts):
        mask = jnp.where(
            half,
            flag(seg_ref[t + 1 + BL - CTX] == before),
            flag(seg_ref[BL + t + 1 + BL - CTX] == seg_ref[BL]),
        )
        total = parts[0]
        for n in range(1, STATE):
            total = total + parts[n]
        out_ref[t] = y_ref[t] + mask * total
        return [parts[n] * decay[n] for n in range(STATE)]

    lax.fori_loop(0, CTX, step, weighted, unroll=4)


def back_total_kernel(seg_ref, g_ref, rate_ref, c_ref, own_ref, out_ref):
    half = first_half()
    decay = [jnp.exp(-rate_ref[n]) for n in range(STATE)]

    def step(k, sums):
        t = CTX - 1 - k
        mask = jnp.where(
            half,
            flag(seg_ref[t + 1 + BL - CTX] == seg_ref[1]),
            flag(seg_ref[BL + t + 1 + BL - CTX] == seg_ref[BL]),
        )
        grad = mask * g_ref[t]
        return [decay[n] * (sums[n] + grad) for n in range(STATE)]

    sums = lax.fori_loop(0, CTX, step, [jnp.zeros((8, 128), f32)] * STATE, unroll=4)
    joined = flag(seg_ref[1] == seg_ref[BL])
    for n in range(STATE):
        total = sums[n] * c_ref[n] * jnp.exp(-rate_ref[n] * (BL - CTX))
        own_ref[n] = total
        out_ref[n] = total + (joined * jnp.exp(-rate_ref[n] * BL)) * pltpu.roll(total, 4, 0)


def sens_steps(seg_ref, h_ref, half, decay, count):
    def plain(t, both):
        row = h_ref[t]
        sens = [both[1][n] * decay[n] + both[0][n] for n in range(count)]
        states = [both[0][n] * decay[n] + row for n in range(count)]
        return [states, sens] + list(both[2:])

    def kept(t, both):
        keep = keep_at(seg_ref, t, half)
        row = h_ref[t]
        held = [v * keep for v in both[0]]
        sens = [(both[1][n] * keep) * decay[n] + held[n] for n in range(count)]
        states = [held[n] * decay[n] + row for n in range(count)]
        return [states, sens] + list(both[2:])

    return plain, kept


SENS_GROUP = 8


def sens_kernel(seg_ref, h_ref, start_ref, rate_ref, s_ref, z_ref):
    half = first_half()
    for first in range(0, STATE, SENS_GROUP):
        ids = range(first, first + SENS_GROUP)
        decay = [jnp.exp(-rate_ref[n]) for n in ids]
        plain, kept = sens_steps(seg_ref, h_ref, half, decay, SENS_GROUP)
        both = [[start_ref[n] for n in ids], [jnp.zeros((8, 128), f32)] * SENS_GROUP]
        both = chunked(seg_ref, 0, BL - CTX, plain, kept, both)
        for k, n in enumerate(ids):
            s_ref[n] = both[0][k]
            z_ref[n] = both[1][k]


def sens_tail_kernel(seg_ref, h_ref, g_ref, s_ref, z_ref, rate_ref, gc_ref, ga_ref, zend_ref):
    half = first_half()
    for first in range(0, STATE, SENS_GROUP):
        ids = range(first, first + SENS_GROUP)
        decay = [jnp.exp(-rate_ref[n]) for n in ids]

        def summing(step):
            def go(t, carried):
                states, sens, by_c, by_a = step(t, carried)
                grad = g_ref[t - (BL - CTX)]
                by_c = [by_c[n] + grad * states[n] for n in range(SENS_GROUP)]
                by_a = [by_a[n] + grad * sens[n] for n in range(SENS_GROUP)]
                return [states, sens, by_c, by_a]

            return go

        plain, kept = sens_steps(seg_ref, h_ref, half, decay, SENS_GROUP)
        zeros = [jnp.zeros((8, 128), f32)] * SENS_GROUP
        carried = [[s_ref[n] for n in ids], [z_ref[n] for n in ids], zeros, zeros]
        carried = chunked(seg_ref, BL - CTX, BL, summing(plain), summing(kept), carried)
        for k, n in enumerate(ids):
            zend_ref[n] = carried[1][k]
            gc_ref[n] = carried[2][k]
            ga_ref[n] = carried[3][k]


def back_scan_kernel(
    seg_ref,
    use_ref,
    all_ref,
    g_ref,
    own_ref,
    z_ref,
    ga_ref,
    rate_ref,
    c_ref,
    gh_ref,
    out_ref,
    later_ref,
):
    half = first_half()
    decay = [jnp.exp(-rate_ref[n]) for n in range(STATE)]
    joined = flag(seg_ref[2 * BL] == seg_ref[BL])
    later_ref[...] = jnp.zeros_like(later_ref)
    count = all_ref.shape[0]

    def gather(k, _):
        j = count - 1 - k

        @pl.when(use_ref[j] > 0)
        def _():
            for m in range(STATE // 2):
                pair = all_ref[j, 16 * m : 16 * m + 16, :].astype(f32)
                for k in range(2):
                    n = 2 * m + k
                    power = jnp.exp(-rate_ref[n] * (2 * BL))
                    later_ref[n] = later_ref[n] * power + pair[8 * k : 8 * k + 8]

        return 0

    lax.fori_loop(0, count, gather, 0)
    sums = []
    for n in range(STATE):
        first = (
            pltpu.roll(own_ref[n], 4, 0) + (joined * jnp.exp(-rate_ref[n] * BL)) * later_ref[n]
        )
        entering = jnp.where(half, first, pltpu.roll(later_ref[n], 4, 0))
        sums.append(entering)
        out_ref[n] = ga_ref[n] * c_ref[n] + entering * z_ref[n]

    def total_of(t, sums):
        total = sums[0]
        for n in range(1, STATE):
            total = total + sums[n]
        gh_ref[t] = total

    def plain(t, sums):
        total_of(t, sums)
        return [v * decay[n] for n, v in enumerate(sums)]

    def kept(t, sums):
        total_of(t, sums)
        keep = keep_at(seg_ref, t, half)
        return [(v * keep) * decay[n] for n, v in enumerate(sums)]

    def entered(step):
        def go(t, sums):
            grad = g_ref[t - (BL - CTX)]
            return step(t, [sums[n] + c_ref[n] * grad for n in range(STATE)])

        return go

    sums = chunked(seg_ref, BL - CTX, BL, entered(plain), entered(kept), sums, back=True)
    chunked(seg_ref, 0, BL - CTX, plain, kept, sums, back=True)


def to_lanes(values, blocks, steps):
    return (
        values.reshape(blocks, steps, 4, 128).transpose(1, 0, 2, 3).reshape(steps, blocks * 4, 128)
    )


def from_lanes(values, blocks, steps):
    return values.reshape(steps, blocks, 4, 128).transpose(1, 0, 2, 3).reshape(blocks, steps, 512)


def attend_kernel(
    host_ref,
    hid_ref,
    ctx_ref,
    wq_ref,
    wk_ref,
    wv_ref,
    segq_ref,
    segk_ref,
    q_ref,
    k_ref,
    v_ref,
    ck_ref,
    cv_ref,
    pc_ref,
    pb_ref,
    mix_ref,
):
    hid = hid_ref[...]
    ctx = ctx_ref[...]
    q_ref[...] = dot_nn(hid, wq_ref[0]).astype(bf16)
    k_ref[...] = dot_nn(hid, wk_ref[0]).astype(bf16)
    v_ref[...] = dot_nn(hid, wv_ref[0]).astype(bf16)
    ck_ref[...] = dot_nn(ctx, wk_ref[0]).astype(bf16)
    cv_ref[...] = dot_nn(ctx, wv_ref[0]).astype(bf16)
    ctx_ids = segk_ref[:, :CTX]
    for i in range(BL // QT):
        rows = slice(i * QT, (i + 1) * QT)
        reach = (i + 1) * QT
        ids = segq_ref[rows]
        ctx_ok = ctx_ids == ids
        place_q = lax.broadcasted_iota(i32, (QT, reach), 0) + i * QT
        place_k = lax.broadcasted_iota(i32, (QT, reach), 1)
        block_ok = jnp.logical_and(place_k <= place_q, segk_ref[:, CTX : CTX + reach] == ids)
        for head in range(TILE // HEAD_DIM):
            cols = slice(head * HEAD_DIM, (head + 1) * HEAD_DIM)
            query = q_ref[rows, cols]
            sc = dot_nt(query, ck_ref[:, cols]) * (score_scale * LOG2E)
            sb = dot_nt(query, k_ref[:reach, cols]) * (score_scale * LOG2E)
            sc = jnp.where(ctx_ok, sc, masked_score)
            sb = jnp.where(block_ok, sb, masked_score)
            top = jnp.maximum(
                jnp.max(sc, axis=1, keepdims=True), jnp.max(sb, axis=1, keepdims=True)
            )
            ec = jnp.exp2(sc - top)
            eb = jnp.exp2(sb - top)
            total = jnp.sum(ec, axis=1, keepdims=True) + jnp.sum(eb, axis=1, keepdims=True)
            inverse = 1.0 / total
            pc = (ec * inverse).astype(bf16)
            pb = (eb * inverse).astype(bf16)
            pc_ref[head, rows, :] = pc
            pb_ref[head, rows, :reach] = pb
            if reach < BL:
                pb_ref[head, rows, reach:] = jnp.zeros((QT, BL - reach), bf16)
            mixed = dot_nn(pc, cv_ref[:, cols]) + dot_nn(pb, v_ref[:reach, cols])
            mix_ref[rows, cols] = mixed.astype(bf16)


def attend_forward(hosts, block, hidden, context, attn_full, seg_col, seg_row, half_width):
    pairs = half_width // TILE

    def weight(position):
        return pl.BlockSpec((1, D, TILE), lambda p, s: (s[position], 0, p))

    def tile(rows):
        return pl.BlockSpec((rows, TILE), lambda p, s: (0, p))

    heads = half_width // HEAD_DIM
    per = TILE // HEAD_DIM
    return call(
        attend_kernel,
        (pairs,),
        [
            pl.BlockSpec((BL, D), lambda p, s: (block, 0)),
            pl.BlockSpec((CTX, D), lambda p, s: (block, 0)),
            weight(0),
            weight(1),
            weight(2),
            pl.BlockSpec((BL, 1), lambda p, s: (block, 0)),
            whole((1, CTX + BL)),
        ],
        [
            tile(BL),
            tile(BL),
            tile(BL),
            tile(CTX),
            tile(CTX),
            pl.BlockSpec((per, BL, CTX), lambda p, s: (p, 0, 0)),
            pl.BlockSpec((per, BL, BL), lambda p, s: (p, 0, 0)),
            tile(BL),
        ],
        [
            pltpu.HBM((BL, half_width), bf16),
            pltpu.HBM((BL, half_width), bf16),
            pltpu.HBM((BL, half_width), bf16),
            pltpu.HBM((CTX, half_width), bf16),
            pltpu.HBM((CTX, half_width), bf16),
            pltpu.HBM((heads, BL, CTX), bf16),
            pltpu.HBM((heads, BL, BL), bf16),
            sds((BL, half_width), bf16),
        ],
        prefetch=1,
        flops=8 * 10**9,
        nbytes=12 * 10**6,
    )(
        hosts,
        hbm(hidden),
        context,
        *hbm(attn_full, attn_full, attn_full),
        seg_col,
        seg_row,
    )


def attend_back_kernel(
    host_ref,
    own_ref,
    other_ref,
    cot_ref,
    mid_ref,
    gain_ref,
    tok_ref,
    first_gain_ref,
    wo_ref,
    wq_ref,
    wk_ref,
    wv_ref,
    q_ref,
    k_ref,
    v_ref,
    ck_ref,
    cv_ref,
    pc_ref,
    pb_ref,
    low_ref,
    gmid_ref,
    ggain_ref,
    dq_ref,
    dk_ref,
    dv_ref,
    dck_ref,
    dcv_ref,
    hown_ref,
    hsend_ref,
    cown_ref,
    csend_ref,
    sum_ref,
    dsc_ref,
    dsb_ref,
):
    step = pl.program_id(0)
    pairs = pl.num_programs(0) - 2

    @pl.when(step == 0)
    def _():
        grad = own_ref[...].astype(f32) + other_ref[...].astype(f32)
        middle = mid_ref[...]
        inverse = lax.rsqrt(jnp.mean(middle * middle, axis=1, keepdims=True) + epsilon_norm)
        scaled = middle * inverse
        ggain_ref[...] = jnp.sum(grad * scaled, axis=0, keepdims=True)
        weighted = grad * gain_ref[...]
        centre = jnp.mean(weighted * scaled, axis=1, keepdims=True)
        result = cot_ref[...].astype(f32) + inverse * (weighted - scaled * centre)
        gmid_ref[...] = result
        low_ref[...] = result.astype(bf16)

    @pl.when(step < pairs)
    def _():
        grad_mixed = dot_nn(low_ref[...], wo_ref[0]).astype(bf16)
        base = step * TILE
        for head in range(TILE // HEAD_DIM):
            cols = slice(head * HEAD_DIM, (head + 1) * HEAD_DIM)
            to = pl.ds(pl.multiple_of(base + head * HEAD_DIM, HEAD_DIM), HEAD_DIM)
            grad_head = grad_mixed[:, cols]
            for i in range(BL // QT):
                rows = slice(i * QT, (i + 1) * QT)
                reach = (i + 1) * QT
                grad_rows = grad_head[rows]
                gpc = dot_nt(grad_rows, cv_ref[:, cols])
                gpb = dot_nt(grad_rows, v_ref[:reach, cols])
                pc = pc_ref[head, rows, :].astype(f32)
                pb = pb_ref[head, rows, :reach].astype(f32)
                tc = pc * gpc
                tb = pb * gpb
                centre = jnp.sum(tc, axis=1, keepdims=True) + jnp.sum(tb, axis=1, keepdims=True)
                dsc_ref[head, rows, :] = (tc - pc * centre).astype(bf16)
                dsb_ref[head, rows, :reach] = (tb - pb * centre).astype(bf16)
                if reach < BL:
                    dsb_ref[head, rows, reach:] = jnp.zeros((QT, BL - reach), bf16)
            dsc = dsc_ref[head]
            dsb = dsb_ref[head]
            dq = (dot_nn(dsc, ck_ref[:, cols]) + dot_nn(dsb, k_ref[:, cols])) * score_scale
            dq_ref[:, to] = dq.astype(bf16)
            query = q_ref[:, cols]
            dk_ref[:, to] = (dot_tn(dsb, query) * score_scale).astype(bf16)
            dck_ref[:, to] = (dot_tn(dsc, query) * score_scale).astype(bf16)
            dv_ref[:, to] = dot_tn(pb_ref[head], grad_head).astype(bf16)
            dcv_ref[:, to] = dot_tn(pc_ref[head], grad_head).astype(bf16)

    def half():
        part = (
            dot_nt(dq_ref[...], wq_ref[0])
            + dot_nt(dk_ref[...], wk_ref[0])
            + dot_nt(dv_ref[...], wv_ref[0])
        )
        ctx_part = dot_nt(dck_ref[...], wk_ref[0]) + dot_nt(dcv_ref[...], wv_ref[0])
        row_sum = jnp.sum(
            part * (tok_ref[...].astype(f32) * first_gain_ref[...]), axis=1, keepdims=True
        )
        return part, ctx_part, row_sum

    @pl.when(step == pairs)
    def _():
        part, ctx_part, row_sum = half()
        hsend_ref[...] = part.astype(bf16)
        csend_ref[...] = ctx_part.astype(bf16)
        sum_ref[...] = row_sum

    @pl.when(step == pairs + 1)
    def _():
        part, ctx_part, row_sum = half()
        hown_ref[...] = part
        cown_ref[...] = ctx_part
        sum_ref[...] += row_sum


def attend_backward(
    hosts, block, own, other, cot_full, middle, gain, tok_full, first_gain, attn_full, kept, width
):
    pairs = width // TILE
    per = TILE // HEAD_DIM

    def pair(p):
        return jnp.minimum(p, pairs - 1)

    def side(p, s):
        return jnp.where(p <= pairs, 1 - s[8], s[8])

    def weight(position):
        return pl.BlockSpec((1, width, width), lambda p, s: (s[position], side(p, s), 0))

    def tile(rows):
        return pl.BlockSpec((rows, TILE), lambda p, s: (0, pair(p)))

    return call(
        attend_back_kernel,
        (pairs + 2,),
        [
            whole((BL, D)),
            whole((BL, D)),
            pl.BlockSpec((BL, D), lambda p, s: (block, 0)),
            whole((BL, D)),
            whole((1, D)),
            pl.BlockSpec((BL, width), lambda p, s: (block, side(p, s))),
            pl.BlockSpec((1, width), lambda p, s: (0, side(p, s))),
            pl.BlockSpec((1, D, TILE), lambda p, s: (s[3], 0, pair(p))),
            weight(0),
            weight(1),
            weight(2),
            tile(BL),
            tile(BL),
            tile(BL),
            tile(CTX),
            tile(CTX),
            pl.BlockSpec((per, BL, CTX), lambda p, s: (pair(p), 0, 0)),
            pl.BlockSpec((per, BL, BL), lambda p, s: (pair(p), 0, 0)),
        ],
        [
            whole((BL, D)),
            whole((BL, D)),
            whole((1, D)),
            whole((BL, width)),
            whole((BL, width)),
            whole((BL, width)),
            whole((CTX, width)),
            whole((CTX, width)),
            whole((BL, width)),
            whole((BL, width)),
            whole((CTX, width)),
            whole((CTX, width)),
            whole((BL, 1)),
        ],
        [
            pltpu.HBM((BL, D), bf16),
            pltpu.HBM((BL, D), f32),
            sds((1, D), f32),
            pltpu.HBM((BL, width), bf16),
            pltpu.HBM((BL, width), bf16),
            pltpu.HBM((BL, width), bf16),
            pltpu.HBM((CTX, width), bf16),
            pltpu.HBM((CTX, width), bf16),
            pltpu.HBM((BL, width), f32),
            sds((BL, width), bf16),
            sds((CTX, width), f32),
            sds((CTX, width), bf16),
            sds((BL, 1), f32),
        ],
        scratch=[pltpu.VMEM((per, BL, CTX), bf16), pltpu.VMEM((per, BL, BL), bf16)],
        prefetch=1,
        flops=12 * 10**9,
        nbytes=20 * 10**6,
    )(
        hosts,
        *hbm(own, other, cot_full, middle),
        gain,
        hbm(tok_full),
        first_gain,
        *hbm(attn_full, attn_full, attn_full, attn_full, *kept),
    )


def attn_grad_kernel(host_ref, *refs):
    (hid0, hid1, ctx0, ctx1, low0, low1), rest = refs[:6], refs[6:]
    (dq0, dk0, dv0, dck0, dcv0, mix0), rest = rest[:6], rest[6:]
    (dq1, dk1, dv1, dck1, dcv1, mix1), (out_ref,) = rest[:6], rest[6:]
    matrix = pl.program_id(0)

    @pl.when(matrix == 0)
    def _():
        out_ref[0] = (dot_tn(hid0[...], dq0[...]) + dot_tn(hid1[...], dq1[...])).astype(bf16)

    @pl.when(matrix == 1)
    def _():
        out_ref[0] = (
            dot_tn(hid0[...], dk0[...])
            + dot_tn(hid1[...], dk1[...])
            + dot_tn(ctx0[...], dck0[...])
            + dot_tn(ctx1[...], dck1[...])
        ).astype(bf16)

    @pl.when(matrix == 2)
    def _():
        out_ref[0] = (
            dot_tn(hid0[...], dv0[...])
            + dot_tn(hid1[...], dv1[...])
            + dot_tn(ctx0[...], dcv0[...])
            + dot_tn(ctx1[...], dcv1[...])
        ).astype(bf16)

    @pl.when(matrix == 3)
    def _():
        out_ref[0] = (dot_tn(low0[...], mix0[...]) + dot_tn(low1[...], mix1[...])).astype(bf16)


def attn_grads(hosts, hidden, context, lows, blocks, half_width):
    hid_specs = [
        pl.BlockSpec((BL, D), lambda m, s: (0, 0)),
        pl.BlockSpec((BL, D), lambda m, s: (1, 0)),
        pl.BlockSpec((CTX, D), lambda m, s: (0, 0)),
        pl.BlockSpec((CTX, D), lambda m, s: (1, 0)),
    ]
    block_specs = [
        whole((BL, half_width)),
        whole((BL, half_width)),
        whole((BL, half_width)),
        whole((CTX, half_width)),
        whole((CTX, half_width)),
        whole((BL, half_width)),
    ]
    return call(
        attn_grad_kernel,
        (4,),
        hid_specs + [whole((BL, D))] * 2 + block_specs * 2,
        [pl.BlockSpec((1, D, half_width), lambda m, s: (s[m], 0, 0))],
        [pltpu.HBM((OWNER_GROUPS, D, half_width), bf16)],
        prefetch=1,
        flops=46 * 10**8,
        nbytes=14 * 10**6,
    )(hosts, *hbm(hidden, hidden, context, context, *lows, *blocks[0], *blocks[1]))[0]


def mlp_kernel(
    host_ref,
    own_ref,
    other_ref,
    wo_ref,
    woo_ref,
    tok_ref,
    gain_ref,
    cot_ref,
    w1_ref,
    w2_ref,
    mid_ref,
    hid_ref,
    act_ref,
    pre_ref,
    low_ref,
    grad_ref,
):
    step = pl.program_id(0)

    @pl.when(step == 0)
    def _():
        middle = (
            tok_ref[...].astype(f32)
            + dot_nt(own_ref[...], wo_ref[0])
            + dot_nt(other_ref[...], woo_ref[...])
        )
        inverse = lax.rsqrt(jnp.mean(middle * middle, axis=1, keepdims=True) + epsilon_norm)
        mid_ref[...] = middle
        hid_ref[...] = (middle * inverse * gain_ref[...]).astype(bf16)
        grad_ref[...] = jnp.zeros_like(grad_ref)

    w1 = w1_ref[0]
    w2 = w2_ref[0]
    pre = dot_nn(hid_ref[...], w1)
    grad_act = dot_nn(cot_ref[...], w2)
    root = 0.7978845608028654
    square = pre * pre
    gate = 0.5 + 0.5 * jnp.tanh(pre * (root + (root * 0.044715) * square))
    act = pre * gate
    act_ref[...] = act.astype(bf16)
    slope = gate + act * (1.0 - gate) * (2.0 * root + (6.0 * root * 0.044715) * square)
    grad_pre = (slope * grad_act).astype(bf16)
    pre_ref[...] = grad_pre
    grad_ref[...] += dot_nt(grad_pre, w1)

    @pl.when(step == pl.num_programs(0) - 1)
    def _():
        low_ref[...] = grad_ref[...].astype(bf16)


def mlp_block(hosts, block, own, other, attn_full, wo_other, tok_full, gain, cot_full, mlp_full):
    half_width = own.shape[1]
    quarter = mlp_full.shape[2]
    hidden = 2 * quarter
    per = quarter // FT

    def weight(position):
        return pl.BlockSpec(
            (1, D, FT), lambda f, s: (s[4 + 2 * position + f // per], 0, lax.rem(f, per))
        )

    return call(
        mlp_kernel,
        (2 * per,),
        [
            whole((BL, half_width)),
            whole((BL, half_width)),
            pl.BlockSpec((1, D, half_width), lambda f, s: (s[3], 0, 0)),
            whole((D, half_width)),
            pl.BlockSpec((BL, D), lambda f, s: (block, 0)),
            whole((1, D)),
            pl.BlockSpec((BL, D), lambda f, s: (block, 0)),
            weight(0),
            weight(1),
        ],
        [
            whole((BL, D)),
            whole((BL, D)),
            pl.BlockSpec((BL, FT), lambda f, s: (0, f)),
            pl.BlockSpec((BL, FT), lambda f, s: (0, f)),
            whole((BL, D)),
        ],
        [
            pltpu.HBM((BL, D), f32),
            sds((BL, D), bf16),
            pltpu.HBM((BL, hidden), bf16),
            sds((BL, hidden), bf16),
            pltpu.HBM((BL, D), bf16),
        ],
        scratch=[pltpu.VMEM((BL, D), f32)],
        prefetch=1,
        flops=8 * 10**9,
        nbytes=24 * 10**6,
    )(
        hosts,
        own,
        other,
        hbm(attn_full),
        wo_other,
        tok_full,
        gain,
        cot_full,
        *hbm(mlp_full, mlp_full),
    )


def mlp_grad_kernel(host_ref, h0, h1, g0, g1, p0, p1, a0, a1, out_ref):
    matrix = pl.program_id(0)

    @pl.when(matrix == 0)
    def _():
        out_ref[0] = (dot_tn(h0[...], p0[...]) + dot_tn(h1[...], p1[...])).astype(bf16)

    @pl.when(matrix == 1)
    def _():
        out_ref[0] = (dot_tn(g0[...], a0[...]) + dot_tn(g1[...], a1[...])).astype(bf16)


def mlp_grads(hosts, hiddens, cot_full, pres, acts):
    hidden = acts[0].shape[1]
    quarter = hidden // 2
    per = quarter // FT
    last = 2 * per - 1
    used_first = pl.BlockSpec((BL, FT), lambda m, f, s: (0, jnp.where(m == 0, f, last)))
    used_second = pl.BlockSpec((BL, FT), lambda m, f, s: (0, jnp.where(m == 1, f, 0)))
    return call(
        mlp_grad_kernel,
        (2, 2 * per),
        [
            whole((BL, D)),
            whole((BL, D)),
            pl.BlockSpec((BL, D), lambda m, f, s: (0, 0)),
            pl.BlockSpec((BL, D), lambda m, f, s: (1, 0)),
            used_first,
            used_first,
            used_second,
            used_second,
        ],
        [
            pl.BlockSpec(
                (1, D, FT), lambda m, f, s: (s[4 + 2 * m + f // per], 0, lax.rem(f, per))
            )
        ],
        [pltpu.HBM((OWNER_GROUPS, D, quarter), bf16)],
        prefetch=1,
        flops=86 * 10**8,
        nbytes=20 * 10**6,
    )(
        hosts,
        hiddens[0],
        hiddens[1],
        cot_full,
        cot_full,
        *pres,
        *acts,
    )[0]


def mlp_out_kernel(host_ref, a0, a1, wa_ref, wb_ref, mid0, mid1, send_ref, own_ref):
    step = pl.program_id(0)
    quarter = wa_ref.shape[2]

    def rows(a_ref):
        return dot_nt(a_ref[:, :quarter], wa_ref[0]) + dot_nt(a_ref[:, quarter:], wb_ref[0])

    @pl.when(step == 0)
    def _():
        send_ref[:BL, :] = rows(a0).astype(bf16)
        send_ref[BL:, :] = rows(a1).astype(bf16)

    @pl.when(step == 1)
    def _():
        own_ref[:BL, :] = rows(a0) + mid0[...]
        own_ref[BL:, :] = rows(a1) + mid1[...]


def mlp_out(hosts, acts, mlp_full, middles, width):
    quarter = mlp_full.shape[2]

    def side(d, s):
        return jnp.where(d == 0, 1 - s[8], s[8])

    def weight(position):
        return pl.BlockSpec((1, width, quarter), lambda d, s: (s[position], side(d, s), 0))

    middle = pl.BlockSpec((BL, width), lambda d, s: (0, s[8]))
    return call(
        mlp_out_kernel,
        (2,),
        [whole((BL, 2 * quarter))] * 2 + [weight(6), weight(7), middle, middle],
        [whole((2 * BL, width))] * 2,
        [sds((2 * BL, width), bf16), pltpu.HBM((2 * BL, width), f32)],
        prefetch=1,
        flops=44 * 10**8,
        nbytes=12 * 10**6,
    )(hosts, *hbm(*acts, mlp_full, mlp_full, *middles))


def adam_step(gradient, moment_one, moment_two, weight, rate_table, decay_weight):
    step_count = f32(STEP)
    first_new = beta_first * moment_one + (1.0 - beta_first) * gradient
    second_new = beta_second * moment_two + (1.0 - beta_second) * gradient * gradient
    fixed_one = 1.0 - jnp.power(beta_first, step_count)
    fixed_two = 1.0 - jnp.power(beta_second, step_count)
    update = first_new / fixed_one / (jnp.sqrt(second_new / fixed_two) + epsilon_adam)
    return (first_new, second_new, weight - rate_table * (update + decay_weight * weight))


def body(
    tokens,
    cotangent,
    segments,
    owners,
    attn_master,
    attn_first,
    attn_second,
    mlp_master,
    mlp_first,
    mlp_second,
    ssm_params,
    ssm_first,
    ssm_second,
    norm_gains,
    gains_first,
    gains_second,
):
    rows = tokens.shape[1]
    width = tokens.shape[2]
    blocks = rows // BL
    dp_count = lax.axis_size("dp")
    dp_here = lax.axis_index("dp")
    side = lax.axis_index("tensor")
    group = dp_here // (dp_count // OWNER_GROUPS)
    quarter = mlp_master.shape[2] // 2

    def both_sides(own, other):
        return jnp.where(
            side == 0,
            jnp.concatenate([own, other], axis=-1),
            jnp.concatenate([other, own], axis=-1),
        )

    def side_of(values, which):
        return lax.dynamic_slice_in_dim(values, which * width, width, values.ndim - 1)

    smem = pl.BlockSpec(memory_space=pltpu.SMEM)
    vmem = pl.BlockSpec(memory_space=pltpu.VMEM)
    hosts, rates = pl.pallas_call(
        plan_kernel,
        in_specs=[smem, smem],
        out_specs=[smem, smem],
        out_shape=[sds((PLAN_SIZE,), i32), sds((4,), f32)],
    )(owners, jnp.stack([side, group]).astype(i32))
    attn_here = hosts[ATTN_HERE]
    mlp_here = hosts[MLP_HERE]
    near = hosts[NEAR] == 1
    ring = Ring()

    tok = tokens.reshape(rows, width)
    cot = cotangent.reshape(rows, width)
    tok_f = tok.astype(f32)
    square_here = jnp.sum(tok_f * tok_f, axis=1)
    square_other = swap_x(square_here)
    tok_other = swap_x(tok)
    gains_other = swap_x(norm_gains)
    inverse_one = lax.rsqrt((square_here + square_other) / D + epsilon_norm)
    scaled_own = tok_f * inverse_one[:, None]
    hidden_own = (scaled_own * norm_gains[0]).astype(bf16)
    gains_full = both_sides(norm_gains, gains_other)

    attn_low = attn_master.astype(bf16)
    mlp_low = mlp_master[0].astype(bf16)
    attn_moved = move(attn_low[1], hosts[WAY], ATTN_WAYS, False)
    attn_block = jnp.where(attn_here == 0, attn_moved, attn_low[0])
    attn_full = lax.all_gather(attn_block, "dp", axis=0, tiled=True)
    attn_full = attn_full.reshape(OWNER_GROUPS, D, width)
    mlp_moved = exchange_groups(gate(mlp_low[:, quarter:], square_other), near)

    seg = segments.reshape(rows)
    prior = lax.ppermute(seg[rows - CTX :] + 1, "dp", [(i, i + 1) for i in range(dp_count - 1)]) - 1
    seg_ext = jnp.concatenate([prior[CTX - 1 :], seg])
    seg_col = seg[:, None]

    param_lanes = ssm_params.transpose(0, 2, 1)
    decay_rate = jnp.exp(param_lanes[0]) * (BL ** (-0.5) / 32.0)
    drive_root = jnp.sqrt(-jnp.expm1(-2.0 * decay_rate))
    reading = param_lanes[2] * drive_root * param_lanes[1]

    def doubled(values):
        lanes = values.reshape(STATE, 4, 128)
        return jnp.concatenate([lanes] * blocks, axis=1)

    rate_lanes = doubled(decay_rate)
    reading_lanes = doubled(reading)
    state_shape = sds((STATE, 8, 128), f32)

    def plain(kernel, scalars, count, outs, cost, scratch=()):
        return pl.pallas_call(
            kernel,
            in_specs=[smem] * scalars + [vmem] * count,
            out_specs=[vmem] * len(outs),
            out_shape=outs,
            scratch_shapes=scratch,
            name=kernel.__name__,
            compiler_params=pltpu.CompilerParams(vmem_limit_bytes=16 * 1024 * 1024),
            cost_estimate=pl.CostEstimate(flops=cost // COST, bytes_accessed=10**6 // COST, transcendentals=0),
        )

    hidden_lanes = to_lanes(hidden_own.astype(f32), blocks, BL)
    tail_lanes = sds((CTX, 8, 128), f32)
    tail_part, state_ends, device_end = plain(
        scan_kernel, 1, 3, [tail_lanes, state_shape, state_shape], 4 * 10**9
    )(seg_ext, hidden_lanes, rate_lanes, reading_lanes)
    id_rows = jnp.where(
        (jnp.arange(16) == 0)[:, None], seg[rows - 1].astype(f32), seg[0].astype(f32)
    )
    message = jnp.concatenate(
        [device_end.reshape(STATE * 8, 128), jnp.broadcast_to(id_rows, (16, 128))], axis=0
    ).astype(bf16)
    hidden_full = join_sides(
        hosts,
        tok,
        tok_other,
        (inverse_one[:, None], norm_gains[0:1], gains_other[0:1]),
    )
    states_all = gather_round(message[None], 0)
    cot_other = swap_x(gate(cot, tok_other))
    for k in range(1, gather_rounds()):
        if k == gather_rounds() - 2:
            tok_other, states_all = together(tok_other, states_all)
        if k == gather_rounds() - 1:
            mlp_moved, states_all = together(mlp_moved, states_all)
        states_all = gather_round(states_all, k)
    states_all = gate(states_all, cot_other, hidden_full)
    mlp_block_low = jnp.where(mlp_here == 0, mlp_moved, mlp_low[:, :quarter])
    mlp_full = lax.all_gather(mlp_block_low, "dp", axis=0, tiled=True)
    mlp_full = mlp_full.reshape(OWNER_GROUPS, D, quarter)
    tok_full = join_sides(hosts, tok, tok_other)
    ids_all = states_all[:, STATE * 8 : STATE * 8 + 2, 0].astype(i32)
    places = jnp.arange(dp_count, dtype=i32)
    use_before = jnp.logical_and(places < dp_here, ids_all[:, 0] == seg_ext[0]).astype(i32)
    use_after = jnp.logical_and(places > dp_here, ids_all[:, 1] == seg[rows - 1]).astype(i32)
    tails, state_starts = plain(
        tail_kernel, 2, 5, [tail_lanes, state_shape], 10**9, [pltpu.VMEM((STATE, 8, 128), f32)]
    )(seg_ext, use_before, states_all, state_ends, rate_lanes, reading_lanes, tail_part)
    sens_states, sens_starts = plain(sens_kernel, 1, 3, [state_shape] * 2, 6 * 10**9)(
        seg_ext, hidden_lanes, state_starts, rate_lanes
    )
    tails = from_lanes(tails, blocks, CTX).astype(bf16)
    context_own = shift_tails(tails[blocks - 1], 1, False)
    context_other = shift_tails(tails[blocks - 1], 1, True)
    inner_own = tails[: blocks - 1]
    inner_other = swap_x(inner_own)
    context_full = jnp.concatenate(
        [
            both_sides(context_own, context_other)[None],
            both_sides(inner_own, inner_other),
        ],
        axis=0,
    ).reshape(-1, D)

    seg_rows = []
    for b in range(blocks):
        before = prior if b == 0 else seg[b * BL - CTX : b * BL]
        seg_rows.append(jnp.concatenate([before, seg[b * BL : (b + 1) * BL]])[None])
    kept = []
    mixed = []
    mixed_other = []
    for b in range(blocks):
        outs = attend_forward(
            hosts, b, hidden_full, context_full, attn_full, seg_col, seg_rows[b], width
        )
        kept.append(outs[:7])
        mixed.append(outs[7])
        mixed_other.append(swap_x(outs[7]))
    wo_own = lax.dynamic_index_in_dim(attn_full, hosts[3], 0, keepdims=False)
    wo_half = lax.dynamic_slice_in_dim(wo_own, ring.core * (D // 2), D // 2, 0)
    wo_half = gate(wo_half, inner_other)
    wo_first = swap_x(wo_half)
    wo_second = lax.ppermute(gate(wo_first, mixed[0]), "dp", ring.cores)
    joined = together(*mixed_other, sens_states, sens_starts)
    mixed_other, (sens_states, sens_starts) = list(joined[:blocks]), joined[blocks:]
    wo_other = jnp.where(
        ring.core == 0,
        jnp.concatenate([wo_first, wo_second], axis=0),
        jnp.concatenate([wo_second, wo_first], axis=0),
    )

    cot_full = join_sides(hosts, gate(cot, mixed[0]), cot_other)

    gain_two = gains_full[1:2]
    middles, hiddens, acts, pres, grads, grads_other = [], [], [], [], [], []
    for b in range(blocks):
        middle, hidden_two, act, grad_pre, grad_low = mlp_block(
            hosts,
            b,
            mixed[b],
            mixed_other[b],
            attn_full,
            wo_other,
            tok_full,
            gain_two,
            cot_full,
            mlp_full,
        )
        middles.append(middle)
        hiddens.append(hidden_two)
        acts.append(act)
        pres.append(grad_pre)
        grads.append(grad_low)
        grads_other.append(swap_x(grad_low))
    mlp_sum_in = mlp_grads(hosts, hiddens, cot_full, pres, acts)
    grads_other[0], mlp_sum_in = lax.optimization_barrier((grads_other[0], mlp_sum_in))
    mlp_sum = lax.psum_scatter(
        mlp_sum_in.reshape(OWNER_GROUPS * D, quarter), "dp", scatter_dimension=0, tiled=True
    )

    lows, grad_mids, gain_twos, grad_blocks = [], [], [], []
    parts, parts_sent, ctx_parts, ctx_sent, row_sums = [], [], [], [], []
    for b in range(blocks):
        if b == blocks - 1:
            acts[0] = gate(acts[0], *lows)
            out_send, out_own = mlp_out(hosts, acts, mlp_full, middles, width)
            out_received = swap_x(out_send)
            grads[b] = gate(grads[b], out_own)
        outs = attend_backward(
            hosts,
            b,
            gate(grads[b], *lows),
            grads_other[b],
            cot_full,
            middles[b],
            gain_two,
            tok_full,
            gains_full[0:1],
            attn_full,
            kept[b],
            width,
        )
        lows.append(outs[0])
        grad_mids.append(side_of(outs[1], side))
        gain_twos.append(side_of(outs[2], side))
        grad_blocks.append(list(outs[3:8]) + [mixed[b]])
        parts.append(outs[8])
        parts_sent.append(outs[9])
        ctx_parts.append(outs[10])
        ctx_sent.append(outs[11])
        row_sums.append(outs[12][:, 0])
    grad_tails = jnp.stack(
        [ctx_parts[b] + swap_x(ctx_sent[b]).astype(f32) for b in range(1, blocks)]
        + [
            shift_tails(ctx_parts[0].astype(bf16), -1, False).astype(f32)
            + shift_tails(ctx_sent[0], -1, True).astype(f32)
        ]
    )
    tail_grad_lanes = to_lanes(grad_tails.reshape(blocks * CTX, width), blocks, CTX)
    own_back, device_back = plain(back_total_kernel, 1, 3, [state_shape, state_shape], 10**9)(
        seg_ext, tail_grad_lanes, rate_lanes, reading_lanes
    )
    attn_sum_in = attn_grads(hosts, hidden_full, context_full, lows, grad_blocks, width)
    received = [swap_x(v) for v in parts_sent]

    back_all = gather_round(device_back.reshape(STATE * 8, 128).astype(bf16)[None], 0)
    part, up, down = ring.start(attn_sum_in.reshape(dp_count, -1, width))
    steps = 0
    for k in range(1, gather_rounds()):
        up, down, back_all = together(up, down, back_all)
        back_all = gather_round(back_all, k)
        if steps < ring.far_up - 2:
            up, down = ring.step(steps, part, up, down)
            steps += 1
    mlp_sum, back_all, up, down = together(mlp_sum, back_all, up, down)
    mlp_back = exchange_groups(mlp_sum, near)
    grad_c_lanes, grad_a_lanes, sens_end = plain(
        sens_tail_kernel, 1, 5, [state_shape] * 3, 2 * 10**9
    )(seg_ext, hidden_lanes, tail_grad_lanes, sens_states, sens_starts, rate_lanes)
    grad_lanes, grad_a_lanes = plain(
        back_scan_kernel,
        2,
        7,
        [sds((BL, 8, 128), f32), state_shape],
        4 * 10**9,
        [pltpu.VMEM((STATE, 8, 128), f32)],
    )(
        seg_ext,
        use_after,
        back_all,
        tail_grad_lanes,
        own_back,
        sens_end,
        grad_a_lanes,
        rate_lanes,
        reading_lanes,
    )
    for k in range(steps, ring.far_up):
        up, down = ring.step(k, part, up, down)
    attn_sum = (part(0) + up.astype(f32) + down.astype(f32)).astype(bf16)
    grad_channels = lax.optimization_barrier(
        from_lanes(grad_lanes, blocks, BL).reshape(rows, width)
    )

    part_own = jnp.concatenate(parts, axis=0)
    received = jnp.concatenate(received, axis=0)
    row_here = inverse_one * jnp.concatenate(row_sums) + jnp.sum(
        grad_channels * (scaled_own * norm_gains[0]), axis=1
    )
    row_other = swap_x(row_here)
    row_total = row_here + row_other
    block_out = (out_own + out_received.astype(f32)).astype(bf16)
    grad_hidden = part_own + received.astype(f32) + grad_channels
    grad_tokens = jnp.concatenate(grad_mids, axis=0) + inverse_one[:, None] * (
        grad_hidden * norm_gains[0] - scaled_own * (row_total / D)[:, None]
    )
    gain_one = jnp.sum(grad_hidden * scaled_own, axis=0)
    gain_two_sum = sum(gain_twos)[0]

    def merged(values):
        return sum(values[:, 4 * b : 4 * b + 4] for b in range(blocks)).reshape(STATE, width)

    small = jnp.concatenate(
        [merged(grad_c_lanes), merged(grad_a_lanes), gain_one[None], gain_two_sum[None]], axis=0
    )
    small, mlp_back = total_dp(small, mlp_back)
    grad_c, grad_a = small[:STATE], small[STATE : 2 * STATE]
    gains_grad = small[2 * STATE :]
    decay_step = jnp.exp(-decay_rate)
    grad_read = grad_c * drive_root * param_lanes[1]
    grad_drive = grad_c * drive_root * param_lanes[2]
    grad_a = grad_a - grad_c * param_lanes[1] * param_lanes[2] * decay_step / drive_root
    grad_log = -decay_rate * decay_step * grad_a
    ssm_grad = jnp.stack([grad_log, grad_drive, grad_read]).transpose(0, 2, 1)

    attn_back = move(gate(attn_sum, small), hosts[WAY], ATTN_WAYS, True)
    attn_grad = jnp.stack(
        [
            jnp.where(attn_here >= 1, attn_sum.astype(f32), 0.0),
            jnp.where(attn_here == 2, attn_back.astype(f32), 0.0),
        ]
    )
    mlp_grad = jnp.where(
        mlp_here == 1, jnp.concatenate([mlp_sum, mlp_back], axis=1).astype(f32), 0.0
    )[None]

    attn_rates = rates[:2, None, None]
    mlp_rates = rates[2]
    ssm_rates = jnp.asarray([1.0, 0.8, 0.25], f32)[:, None, None]
    gain_rates = jnp.asarray([0.6, 0.6], f32)[:, None]
    attn_one, attn_two, attn_new = adam_step(
        attn_grad, attn_first, attn_second, attn_master, attn_rates, matrix_decay
    )
    mlp_one, mlp_two, mlp_new = adam_step(
        mlp_grad, mlp_first, mlp_second, mlp_master, mlp_rates, matrix_decay
    )
    ssm_one, ssm_two, ssm_new = adam_step(
        ssm_grad, ssm_first, ssm_second, ssm_params, ssm_rates, 0.0
    )
    gain_first_new, gain_second_new, gains_new = adam_step(
        gains_grad, gains_first, gains_second, norm_gains, gain_rates, 0.0
    )
    return (
        block_out.reshape(tokens.shape),
        grad_tokens.reshape(tokens.shape),
        attn_grad,
        attn_one,
        attn_two,
        attn_new,
        attn_new.astype(bf16),
        mlp_grad,
        mlp_one,
        mlp_two,
        mlp_new,
        mlp_new.astype(bf16),
        ssm_grad,
        ssm_one,
        ssm_two,
        ssm_new,
        gains_grad,
        gain_first_new,
        gain_second_new,
        gains_new,
    )


def solution(mesh):
    in_specs = (
        P(None, "dp", "tensor"),
        P(None, "dp", "tensor"),
        P(None, "dp"),
        P(),
        P(None, "dp", "tensor"),
        P(None, "dp", "tensor"),
        P(None, "dp", "tensor"),
        P(None, "dp", "tensor"),
        P(None, "dp", "tensor"),
        P(None, "dp", "tensor"),
        P(None, "tensor", None),
        P(None, "tensor", None),
        P(None, "tensor", None),
        P(None, "tensor"),
        P(None, "tensor"),
        P(None, "tensor"),
    )
    out_specs = (
        P(None, "dp", "tensor"),
        P(None, "dp", "tensor"),
        P(None, "dp", "tensor"),
        P(None, "dp", "tensor"),
        P(None, "dp", "tensor"),
        P(None, "dp", "tensor"),
        P(None, "dp", "tensor"),
        P(None, "dp", "tensor"),
        P(None, "dp", "tensor"),
        P(None, "dp", "tensor"),
        P(None, "dp", "tensor"),
        P(None, "dp", "tensor"),
        P(None, "tensor", None),
        P(None, "tensor", None),
        P(None, "tensor", None),
        P(None, "tensor", None),
        P(None, "tensor"),
        P(None, "tensor"),
        P(None, "tensor"),
        P(None, "tensor"),
    )
    return jax.shard_map(body, mesh=mesh, in_specs=in_specs, out_specs=out_specs, check_vma=False)
```

```python
import functools
import itertools

import jax
import jax.numpy as jnp
from jax import lax
from jax.experimental import pallas as pl
from jax.experimental.pallas import tpu as pltpu
from jax.sharding import PartitionSpec as P

D = 1024
HEAD_DIM = 128
FF = 4096
STATE = 16
CTX = 128
BL = 512
OWNER_GROUPS = 4
STEP = 5

epsilon_norm = 1e-05
beta_first = 0.9
beta_second = 0.95
epsilon_adam = 1e-08
matrix_decay = 0.1
masked_score = -1e30
score_scale = HEAD_DIM ** (-0.5)
f32 = jnp.float32
bf16 = jnp.bfloat16
i32 = jnp.int32
SWAP = [(0, 1), (1, 0)]
COST = 1000
TILE = 256
QT = 256
FT = 512
LOG2E = 1.4426950408889634


def dot_nn(left, right):
    return lax.dot_general(left, right, (((1,), (0,)), ((), ())), preferred_element_type=f32)


def dot_nt(left, right):
    return lax.dot_general(left, right, (((1,), (1,)), ((), ())), preferred_element_type=f32)


def dot_tn(left, right):
    return lax.dot_general(left, right, (((0,), (0,)), ((), ())), preferred_element_type=f32)


def call(
    kernel, grid, in_specs, out_specs, out_shape, scratch=(), prefetch=0, flops=0, nbytes=0, room=36
):
    return pl.pallas_call(
        kernel,
        grid_spec=pltpu.PrefetchScalarGridSpec(
            num_scalar_prefetch=prefetch,
            grid=grid,
            in_specs=in_specs,
            out_specs=out_specs,
            scratch_shapes=scratch,
        ),
        out_shape=out_shape,
        name=kernel.__name__,
        compiler_params=pltpu.CompilerParams(vmem_limit_bytes=room * 1024 * 1024),
        cost_estimate=pl.CostEstimate(flops=flops // COST, bytes_accessed=nbytes // COST, transcendentals=0),
    )


def whole(shape):
    return pl.BlockSpec(shape, lambda *_: (0,) * len(shape), pipeline_mode=pl.Buffered(1))


def sds(shape, dtype):
    return jax.ShapeDtypeStruct(shape, dtype)


def hbm(*values):
    held = tuple(pltpu.with_memory_space_constraint(v, pltpu.HBM) for v in values)
    return held[0] if len(held) == 1 else held


def swap_x(values):
    return lax.ppermute(values, "tensor", SWAP)


def gate(value, *others):
    if not others:
        return value
    return lax.optimization_barrier((value,) + others)[0]


def together(*values):
    return lax.optimization_barrier(values)


def gather_rounds():
    return max(lax.axis_size("dp") - 1, 0).bit_length()


def gather_round(held, k):
    step = 1 << k
    count = lax.axis_size("dp")
    other = lax.ppermute(held, "dp", [(i, i ^ step) for i in range(count)])
    later = (lax.axis_index("dp") // step) % 2 == 1
    return jnp.where(
        later,
        jnp.concatenate([other, held], axis=0),
        jnp.concatenate([held, other], axis=0),
    )


def total_dp(values, beside):
    count = lax.axis_size("dp")
    for k in range(gather_rounds()):
        if k == 1:
            values, *beside = together(values, *beside)
        values = values + lax.ppermute(values, "dp", [(i, i ^ (1 << k)) for i in range(count)])
    return values, beside


def routes(full_count, empty_count):
    groups = range(OWNER_GROUPS)
    ways = []
    for full in itertools.combinations(groups, full_count):
        rest = [g for g in groups if g not in full]
        for empty in itertools.combinations(rest, empty_count):
            ways.append((full, empty))
    return ways


ATTN_WAYS = routes(1, 1) + routes(2, 2)


def way_code(full, empty):
    code = 0
    for g in range(OWNER_GROUPS):
        digit = 2 if g in full else (0 if g in empty else 1)
        code += digit * 3**g
    return code


def one_if(condition):
    return jnp.where(condition, jnp.int32(1), jnp.int32(0))


HOST_MLP, SIDE, WAY, NEAR, ATTN_HERE, MLP_HERE, PLAN_SIZE = 4, 8, 9, 10, 11, 12, 16
ATTN_RATES = [0.5 * D ** (-0.5)] * 3 + [0.5 * (D // 16) ** (-0.5)]
MLP_RATES = [0.5 * D ** (-0.5), 0.5 * FF ** (-0.5)]
IDLE_RATE = 0.5 * D ** (-0.5)


def plan_kernel(owner_ref, here_ref, out_ref, rate_ref):
    groups = range(OWNER_GROUPS)
    side, group = here_ref[0], here_ref[1]
    owner = [owner_ref[m] for m in range(6)]
    slot = [
        sum([one_if(owner[k] == owner[m]) for k in range(m)], jnp.int32(0)) for m in range(4)
    ]
    count = [sum([one_if(owner[m] == g) for m in range(4)], jnp.int32(0)) for g in groups]
    full_rank = [sum([one_if(count[h] == 2) for h in range(g)], jnp.int32(0)) for g in groups]
    empty_rank = [sum([one_if(count[h] == 0) for h in range(g)], jnp.int32(0)) for g in groups]
    taker = [
        sum(
            [
                jnp.where(
                    jnp.logical_and(count[h] == 0, empty_rank[h] == full_rank[g]), jnp.int32(h), 0
                )
                for h in groups
            ],
            jnp.int32(0),
        )
        for g in groups
    ]
    for m in range(4):
        second = sum([jnp.where(owner[m] == g, taker[g], 0) for g in groups], jnp.int32(0))
        out_ref[m] = jnp.where(slot[m] == 0, owner[m], second)
    code = sum([count[g] * 3**g for g in groups], jnp.int32(0))
    out_ref[WAY] = sum(
        [
            jnp.where(code == way_code(*way), jnp.int32(k), 0)
            for k, way in enumerate(ATTN_WAYS)
        ],
        jnp.int32(0),
    )
    low = sum([one_if(owner[m] < 2) for m in (4, 5)], jnp.int32(0))
    near = low == 1
    for k, m in enumerate((4, 5)):
        out_ref[HOST_MLP + 2 * k] = owner[m]
        bit = jnp.where(near, jnp.int32(1), jnp.int32(2))
        out_ref[HOST_MLP + 2 * k + 1] = jnp.bitwise_xor(owner[m], bit)
    out_ref[SIDE] = side
    out_ref[NEAR] = one_if(near)
    out_ref[ATTN_HERE] = sum([one_if(owner[m] == group) for m in range(4)], jnp.int32(0))
    out_ref[MLP_HERE] = sum([one_if(owner[m] == group) for m in (4, 5)], jnp.int32(0))
    for k in range(MLP_HERE + 1, PLAN_SIZE):
        out_ref[k] = jnp.int32(0)
    for place in range(2):
        rate = f32(IDLE_RATE)
        for m in range(4):
            hit = jnp.logical_and(owner[m] == group, slot[m] == place)
            rate = jnp.where(hit, f32(ATTN_RATES[m]), rate)
        rate_ref[place] = rate
    rate = f32(IDLE_RATE)
    for k, m in enumerate((4, 5)):
        rate = jnp.where(owner[m] == group, f32(MLP_RATES[k]), rate)
    rate_ref[2] = rate
    rate_ref[3] = f32(0.0)


def move(values, index, ways, back):
    size = lax.axis_size("dp") // OWNER_GROUPS

    def branch(way):
        pairs = []
        for a, b in zip(*way):
            if back:
                a, b = b, a
            pairs += [(a * size + j, b * size + j) for j in range(size)]
        return lambda v: lax.ppermute(v, "dp", pairs)

    return lax.switch(index, [branch(way) for way in ways], values)


def exchange_groups(values, near):
    size = lax.axis_size("dp") // OWNER_GROUPS

    def across(bit):
        return lax.ppermute(
            values,
            "dp",
            [(g * size + j, (g ^ bit) * size + j) for g in range(OWNER_GROUPS) for j in range(size)],
        )

    return jnp.where(near, across(1), across(2))


def ring_order(count):
    chips = count // 2
    if chips == 8:
        return [0, 2, 4, 6, 7, 5, 3, 1]
    return list(range(chips))


def join_kernel(host_ref, own_ref, other_ref, out_ref):
    @pl.when(pl.program_id(0) == 0)
    def _():
        out_ref[...] = own_ref[...]

    @pl.when(pl.program_id(0) == 1)
    def _():
        out_ref[...] = other_ref[...]


def join_scaled_kernel(
    host_ref, own_ref, other_ref, inverse_ref, gain_ref, gain_other_ref, out_ref
):
    @pl.when(pl.program_id(0) == 0)
    def _():
        out_ref[...] = (own_ref[...].astype(f32) * inverse_ref[...] * gain_ref[...]).astype(bf16)

    @pl.when(pl.program_id(0) == 1)
    def _():
        out_ref[...] = (
            other_ref[...].astype(f32) * inverse_ref[...] * gain_other_ref[...]
        ).astype(bf16)


def join_sides(hosts, own, other, scales=()):
    rows, width = own.shape
    return call(
        join_scaled_kernel if scales else join_kernel,
        (2,),
        [whole(v.shape) for v in (own, other) + tuple(scales)],
        [
            pl.BlockSpec(
                (rows, width), lambda d, s: (0, jnp.where(d == 0, s[SIDE], 1 - s[SIDE]))
            )
        ],
        [pltpu.HBM((rows, 2 * width), bf16)],
        prefetch=1,
        nbytes=8 * rows * width,
        room=12,
    )(hosts, own, other, *scales)[0]


class Ring:
    def __init__(self):
        self.count = lax.axis_size("dp")
        self.chips = self.count // 2
        order = ring_order(self.count)
        here = lax.axis_index("dp")
        self.core = here % 2
        chip = here // 2
        self.place = jnp.where(chip % 2 == 0, chip // 2, 7 - chip // 2) if self.chips == 8 else chip
        self.up = [
            (2 * order[p] + c, 2 * order[(p + 1) % self.chips] + c)
            for p in range(self.chips)
            for c in range(2)
        ]
        self.down = [(b, a) for a, b in self.up]
        self.cores = [(i, i ^ 1) for i in range(self.count)]
        self.far_up = self.chips // 2
        self.far_down = self.chips - 1 - self.far_up

    def chip(self, offset):
        place = (self.place + self.chips + offset) % self.chips
        if self.chips != 8:
            return place
        return jnp.where(place < 4, 2 * place, 15 - 2 * place)

    def start(self, blocks):
        pairs = blocks.reshape((self.chips, 2) + blocks.shape[1:])
        mine = lax.dynamic_index_in_dim(pairs, self.core, 1, keepdims=False)
        theirs = lax.dynamic_index_in_dim(pairs, 1 - self.core, 1, keepdims=False)
        received = lax.ppermute(theirs, "dp", self.cores)

        def part(offset):
            chip = self.chip(offset)
            return lax.dynamic_index_in_dim(mine, chip, 0, keepdims=False).astype(
                f32
            ) + lax.dynamic_index_in_dim(received, chip, 0, keepdims=False).astype(f32)

        return part, part(self.far_up).astype(bf16), part(-self.far_down).astype(bf16)

    def step(self, k, part, up, down):
        if k < self.far_up:
            up = lax.ppermute(up, "dp", self.up)
            if k < self.far_up - 1:
                up = (up.astype(f32) + part(self.far_up - 1 - k)).astype(bf16)
        if k < self.far_down:
            down = lax.ppermute(down, "dp", self.down)
            if k < self.far_down - 1:
                down = (down.astype(f32) + part(k + 1 - self.far_down)).astype(bf16)
        return up, down


def shift_tails(values, by, cross):
    count = lax.axis_size("dp")
    pairs = [
        (2 * i + s, 2 * (i + by) + (1 - s if cross else s))
        for i in range(count)
        for s in range(2)
        if 0 <= i + by < count
    ]
    return lax.ppermute(values, ("dp", "tensor"), pairs)


def first_half():
    return lax.broadcasted_iota(i32, (8, 128), 0) < 4


def flag(condition):
    return jnp.where(condition, f32(1.0), f32(0.0))


def keep_at(seg_ref, t, half):
    return jnp.where(
        half, flag(seg_ref[t + 1] == seg_ref[t]), flag(seg_ref[BL + t + 1] == seg_ref[BL + t])
    )


def chunked(seg_ref, begin, end, plain, kept, carried, back=False):
    size = 8
    count = (end - begin) // size

    def chunk(c, carried):
        first = begin + (count - 1 - c if back else c) * size
        same = jnp.logical_and(
            seg_ref[first] == seg_ref[first + size],
            seg_ref[BL + first] == seg_ref[BL + first + size],
        )

        def run(step):
            def go(carried):
                for k in range(size):
                    carried = step(first + (size - 1 - k if back else k), carried)
                return carried

            return go

        return lax.cond(same, run(plain), run(kept), carried)

    return lax.fori_loop(0, count, chunk, carried)


def scan_kernel(seg_ref, h_ref, rate_ref, c_ref, y_ref, s_ref, e_ref):
    half = first_half()
    decay = [jnp.exp(-rate_ref[n]) for n in range(STATE)]

    def plain(t, states):
        row = h_ref[t]
        return [states[n] * decay[n] + row for n in range(STATE)]

    def kept(t, states):
        keep = keep_at(seg_ref, t, half)
        row = h_ref[t]
        return [(states[n] * keep) * decay[n] + row for n in range(STATE)]

    def reading(step):
        def go(t, states):
            states = step(t, states)
            total = c_ref[0] * states[0]
            for n in range(1, STATE):
                total = total + c_ref[n] * states[n]
            y_ref[t - (BL - CTX)] = total
            return states

        return go

    states = [jnp.zeros((8, 128), f32)] * STATE
    states = chunked(seg_ref, 0, BL - CTX, plain, kept, states)
    states = chunked(seg_ref, BL - CTX, BL, reading(plain), reading(kept), states)
    joined = flag(seg_ref[2 * BL] == seg_ref[BL])
    for n in range(STATE):
        s_ref[n] = states[n]
        ends = states[n] + (joined * jnp.exp(-rate_ref[n] * BL)) * pltpu.roll(states[n], 4, 0)
        e_ref[n] = ends


def tail_kernel(
    seg_ref, use_ref, all_ref, s_ref, rate_ref, c_ref, y_ref, out_ref, start_ref, carry_ref
):
    half = first_half()
    before = seg_ref[0]
    joined = flag(seg_ref[BL] == before)
    decay = [jnp.exp(-rate_ref[n]) for n in range(STATE)]
    carry_ref[...] = jnp.zeros_like(carry_ref)

    def gather(j, _):
        @pl.when(use_ref[j] > 0)
        def _():
            for m in range(STATE // 2):
                pair = all_ref[j, 16 * m : 16 * m + 16, :].astype(f32)
                for k in range(2):
                    n = 2 * m + k
                    power = jnp.exp(-rate_ref[n] * (2 * BL))
                    carry_ref[n] = carry_ref[n] * power + pair[8 * k : 8 * k + 8]

        return 0

    lax.fori_loop(0, all_ref.shape[0], gather, 0)
    weighted = []
    for n in range(STATE):
        carried = pltpu.roll(carry_ref[n], 4, 0)
        mid = pltpu.roll(s_ref[n], 4, 0) + (joined * jnp.exp(-rate_ref[n] * BL)) * carry_ref[n]
        start = jnp.where(half, carried, mid)
        start_ref[n] = start
        weighted.append(c_ref[n] * start * jnp.exp(-rate_ref[n] * (BL - CTX + 1)))

    def step(t, parts):
        mask = jnp.where(
            half,
            flag(seg_ref[t + 1 + BL - CTX] == before),
            flag(seg_ref[BL + t + 1 + BL - CTX] == seg_ref[BL]),
        )
        total = parts[0]
        for n in range(1, STATE):
            total = total + parts[n]
        out_ref[t] = y_ref[t] + mask * total
        return [parts[n] * decay[n] for n in range(STATE)]

    lax.fori_loop(0, CTX, step, weighted, unroll=4)


def back_total_kernel(seg_ref, g_ref, rate_ref, c_ref, own_ref, out_ref):
    half = first_half()
    decay = [jnp.exp(-rate_ref[n]) for n in range(STATE)]

    def step(k, sums):
        t = CTX - 1 - k
        mask = jnp.where(
            half,
            flag(seg_ref[t + 1 + BL - CTX] == seg_ref[1]),
            flag(seg_ref[BL + t + 1 + BL - CTX] == seg_ref[BL]),
        )
        grad = mask * g_ref[t]
        return [decay[n] * (sums[n] + grad) for n in range(STATE)]

    sums = lax.fori_loop(0, CTX, step, [jnp.zeros((8, 128), f32)] * STATE, unroll=4)
    joined = flag(seg_ref[1] == seg_ref[BL])
    for n in range(STATE):
        total = sums[n] * c_ref[n] * jnp.exp(-rate_ref[n] * (BL - CTX))
        own_ref[n] = total
        out_ref[n] = total + (joined * jnp.exp(-rate_ref[n] * BL)) * pltpu.roll(total, 4, 0)


def sens_steps(seg_ref, h_ref, half, decay, count):
    def plain(t, both):
        row = h_ref[t]
        sens = [both[1][n] * decay[n] + both[0][n] for n in range(count)]
        states = [both[0][n] * decay[n] + row for n in range(count)]
        return [states, sens] + list(both[2:])

    def kept(t, both):
        keep = keep_at(seg_ref, t, half)
        row = h_ref[t]
        held = [v * keep for v in both[0]]
        sens = [(both[1][n] * keep) * decay[n] + held[n] for n in range(count)]
        states = [held[n] * decay[n] + row for n in range(count)]
        return [states, sens] + list(both[2:])

    return plain, kept


SENS_GROUP = 8


def sens_kernel(seg_ref, h_ref, start_ref, rate_ref, s_ref, z_ref):
    half = first_half()
    for first in range(0, STATE, SENS_GROUP):
        ids = range(first, first + SENS_GROUP)
        decay = [jnp.exp(-rate_ref[n]) for n in ids]
        plain, kept = sens_steps(seg_ref, h_ref, half, decay, SENS_GROUP)
        both = [[start_ref[n] for n in ids], [jnp.zeros((8, 128), f32)] * SENS_GROUP]
        both = chunked(seg_ref, 0, BL - CTX, plain, kept, both)
        for k, n in enumerate(ids):
            s_ref[n] = both[0][k]
            z_ref[n] = both[1][k]


def sens_tail_kernel(seg_ref, h_ref, g_ref, s_ref, z_ref, rate_ref, gc_ref, ga_ref, zend_ref):
    half = first_half()
    for first in range(0, STATE, SENS_GROUP):
        ids = range(first, first + SENS_GROUP)
        decay = [jnp.exp(-rate_ref[n]) for n in ids]

        def summing(step):
            def go(t, carried):
                states, sens, by_c, by_a = step(t, carried)
                grad = g_ref[t - (BL - CTX)]
                by_c = [by_c[n] + grad * states[n] for n in range(SENS_GROUP)]
                by_a = [by_a[n] + grad * sens[n] for n in range(SENS_GROUP)]
                return [states, sens, by_c, by_a]

            return go

        plain, kept = sens_steps(seg_ref, h_ref, half, decay, SENS_GROUP)
        zeros = [jnp.zeros((8, 128), f32)] * SENS_GROUP
        carried = [[s_ref[n] for n in ids], [z_ref[n] for n in ids], zeros, zeros]
        carried = chunked(seg_ref, BL - CTX, BL, summing(plain), summing(kept), carried)
        for k, n in enumerate(ids):
            zend_ref[n] = carried[1][k]
            gc_ref[n] = carried[2][k]
            ga_ref[n] = carried[3][k]


def back_scan_kernel(
    seg_ref,
    use_ref,
    all_ref,
    g_ref,
    own_ref,
    z_ref,
    ga_ref,
    rate_ref,
    c_ref,
    gh_ref,
    out_ref,
    later_ref,
):
    half = first_half()
    decay = [jnp.exp(-rate_ref[n]) for n in range(STATE)]
    joined = flag(seg_ref[2 * BL] == seg_ref[BL])
    later_ref[...] = jnp.zeros_like(later_ref)
    count = all_ref.shape[0]

    def gather(k, _):
        j = count - 1 - k

        @pl.when(use_ref[j] > 0)
        def _():
            for m in range(STATE // 2):
                pair = all_ref[j, 16 * m : 16 * m + 16, :].astype(f32)
                for k in range(2):
                    n = 2 * m + k
                    power = jnp.exp(-rate_ref[n] * (2 * BL))
                    later_ref[n] = later_ref[n] * power + pair[8 * k : 8 * k + 8]

        return 0

    lax.fori_loop(0, count, gather, 0)
    sums = []
    for n in range(STATE):
        first = (
            pltpu.roll(own_ref[n], 4, 0) + (joined * jnp.exp(-rate_ref[n] * BL)) * later_ref[n]
        )
        entering = jnp.where(half, first, pltpu.roll(later_ref[n], 4, 0))
        sums.append(entering)
        out_ref[n] = ga_ref[n] * c_ref[n] + entering * z_ref[n]

    def total_of(t, sums):
        total = sums[0]
        for n in range(1, STATE):
            total = total + sums[n]
        gh_ref[t] = total

    def plain(t, sums):
        total_of(t, sums)
        return [v * decay[n] for n, v in enumerate(sums)]

    def kept(t, sums):
        total_of(t, sums)
        keep = keep_at(seg_ref, t, half)
        return [(v * keep) * decay[n] for n, v in enumerate(sums)]

    def entered(step):
        def go(t, sums):
            grad = g_ref[t - (BL - CTX)]
            return step(t, [sums[n] + c_ref[n] * grad for n in range(STATE)])

        return go

    sums = chunked(seg_ref, BL - CTX, BL, entered(plain), entered(kept), sums, back=True)
    chunked(seg_ref, 0, BL - CTX, plain, kept, sums, back=True)


def to_lanes(values, blocks, steps):
    return (
        values.reshape(blocks, steps, 4, 128).transpose(1, 0, 2, 3).reshape(steps, blocks * 4, 128)
    )


def from_lanes(values, blocks, steps):
    return values.reshape(steps, blocks, 4, 128).transpose(1, 0, 2, 3).reshape(blocks, steps, 512)


def attend_kernel(
    host_ref,
    hid_ref,
    ctx_ref,
    wq_ref,
    wk_ref,
    wv_ref,
    segq_ref,
    segk_ref,
    q_ref,
    k_ref,
    v_ref,
    ck_ref,
    cv_ref,
    pc_ref,
    pb_ref,
    mix_ref,
):
    hid = hid_ref[...]
    ctx = ctx_ref[...]
    q_ref[...] = dot_nn(hid, wq_ref[0]).astype(bf16)
    k_ref[...] = dot_nn(hid, wk_ref[0]).astype(bf16)
    v_ref[...] = dot_nn(hid, wv_ref[0]).astype(bf16)
    ck_ref[...] = dot_nn(ctx, wk_ref[0]).astype(bf16)
    cv_ref[...] = dot_nn(ctx, wv_ref[0]).astype(bf16)
    ctx_ids = segk_ref[:, :CTX]
    for i in range(BL // QT):
        rows = slice(i * QT, (i + 1) * QT)
        reach = (i + 1) * QT
        ids = segq_ref[rows]
        ctx_ok = ctx_ids == ids
        place_q = lax.broadcasted_iota(i32, (QT, reach), 0) + i * QT
        place_k = lax.broadcasted_iota(i32, (QT, reach), 1)
        block_ok = jnp.logical_and(place_k <= place_q, segk_ref[:, CTX : CTX + reach] == ids)
        for head in range(TILE // HEAD_DIM):
            cols = slice(head * HEAD_DIM, (head + 1) * HEAD_DIM)
            query = q_ref[rows, cols]
            sc = dot_nt(query, ck_ref[:, cols]) * (score_scale * LOG2E)
            sb = dot_nt(query, k_ref[:reach, cols]) * (score_scale * LOG2E)
            sc = jnp.where(ctx_ok, sc, masked_score)
            sb = jnp.where(block_ok, sb, masked_score)
            top = jnp.maximum(
                jnp.max(sc, axis=1, keepdims=True), jnp.max(sb, axis=1, keepdims=True)
            )
            ec = jnp.exp2(sc - top)
            eb = jnp.exp2(sb - top)
            total = jnp.sum(ec, axis=1, keepdims=True) + jnp.sum(eb, axis=1, keepdims=True)
            inverse = 1.0 / total
            pc = (ec * inverse).astype(bf16)
            pb = (eb * inverse).astype(bf16)
            pc_ref[head, rows, :] = pc
            pb_ref[head, rows, :reach] = pb
            if reach < BL:
                pb_ref[head, rows, reach:] = jnp.zeros((QT, BL - reach), bf16)
            mixed = dot_nn(pc, cv_ref[:, cols]) + dot_nn(pb, v_ref[:reach, cols])
            mix_ref[rows, cols] = mixed.astype(bf16)


def attend_forward(hosts, block, hidden, context, attn_full, seg_col, seg_row, half_width):
    pairs = half_width // TILE

    def weight(position):
        return pl.BlockSpec((1, D, TILE), lambda p, s: (s[position], 0, p))

    def tile(rows):
        return pl.BlockSpec((rows, TILE), lambda p, s: (0, p))

    heads = half_width // HEAD_DIM
    per = TILE // HEAD_DIM
    return call(
        attend_kernel,
        (pairs,),
        [
            pl.BlockSpec((BL, D), lambda p, s: (block, 0)),
            pl.BlockSpec((CTX, D), lambda p, s: (block, 0)),
            weight(0),
            weight(1),
            weight(2),
            pl.BlockSpec((BL, 1), lambda p, s: (block, 0)),
            whole((1, CTX + BL)),
        ],
        [
            tile(BL),
            tile(BL),
            tile(BL),
            tile(CTX),
            tile(CTX),
            pl.BlockSpec((per, BL, CTX), lambda p, s: (p, 0, 0)),
            pl.BlockSpec((per, BL, BL), lambda p, s: (p, 0, 0)),
            tile(BL),
        ],
        [
            pltpu.HBM((BL, half_width), bf16),
            pltpu.HBM((BL, half_width), bf16),
            pltpu.HBM((BL, half_width), bf16),
            pltpu.HBM((CTX, half_width), bf16),
            pltpu.HBM((CTX, half_width), bf16),
            pltpu.HBM((heads, BL, CTX), bf16),
            pltpu.HBM((heads, BL, BL), bf16),
            sds((BL, half_width), bf16),
        ],
        prefetch=1,
        flops=8 * 10**9,
        nbytes=12 * 10**6,
    )(
        hosts,
        hbm(hidden),
        context,
        *hbm(attn_full, attn_full, attn_full),
        seg_col,
        seg_row,
    )


def attend_back_kernel(
    host_ref,
    own_ref,
    other_ref,
    cot_ref,
    mid_ref,
    gain_ref,
    tok_ref,
    first_gain_ref,
    wo_ref,
    wq_ref,
    wk_ref,
    wv_ref,
    q_ref,
    k_ref,
    v_ref,
    ck_ref,
    cv_ref,
    pc_ref,
    pb_ref,
    low_ref,
    gmid_ref,
    ggain_ref,
    dq_ref,
    dk_ref,
    dv_ref,
    dck_ref,
    dcv_ref,
    hown_ref,
    hsend_ref,
    cown_ref,
    csend_ref,
    sum_ref,
    dsc_ref,
    dsb_ref,
):
    step = pl.program_id(0)
    pairs = pl.num_programs(0) - 2

    @pl.when(step == 0)
    def _():
        grad = own_ref[...].astype(f32) + other_ref[...].astype(f32)
        middle = mid_ref[...]
        inverse = lax.rsqrt(jnp.mean(middle * middle, axis=1, keepdims=True) + epsilon_norm)
        scaled = middle * inverse
        ggain_ref[...] = jnp.sum(grad * scaled, axis=0, keepdims=True)
        weighted = grad * gain_ref[...]
        centre = jnp.mean(weighted * scaled, axis=1, keepdims=True)
        result = cot_ref[...].astype(f32) + inverse * (weighted - scaled * centre)
        gmid_ref[...] = result
        low_ref[...] = result.astype(bf16)

    @pl.when(step < pairs)
    def _():
        grad_mixed = dot_nn(low_ref[...], wo_ref[0]).astype(bf16)
        base = step * TILE
        for head in range(TILE // HEAD_DIM):
            cols = slice(head * HEAD_DIM, (head + 1) * HEAD_DIM)
            to = pl.ds(pl.multiple_of(base + head * HEAD_DIM, HEAD_DIM), HEAD_DIM)
            grad_head = grad_mixed[:, cols]
            for i in range(BL // QT):
                rows = slice(i * QT, (i + 1) * QT)
                reach = (i + 1) * QT
                grad_rows = grad_head[rows]
                gpc = dot_nt(grad_rows, cv_ref[:, cols])
                gpb = dot_nt(grad_rows, v_ref[:reach, cols])
                pc = pc_ref[head, rows, :].astype(f32)
                pb = pb_ref[head, rows, :reach].astype(f32)
                tc = pc * gpc
                tb = pb * gpb
                centre = jnp.sum(tc, axis=1, keepdims=True) + jnp.sum(tb, axis=1, keepdims=True)
                dsc_ref[head, rows, :] = (tc - pc * centre).astype(bf16)
                dsb_ref[head, rows, :reach] = (tb - pb * centre).astype(bf16)
                if reach < BL:
                    dsb_ref[head, rows, reach:] = jnp.zeros((QT, BL - reach), bf16)
            dsc = dsc_ref[head]
            dsb = dsb_ref[head]
            dq = (dot_nn(dsc, ck_ref[:, cols]) + dot_nn(dsb, k_ref[:, cols])) * score_scale
            dq_ref[:, to] = dq.astype(bf16)
            query = q_ref[:, cols]
            dk_ref[:, to] = (dot_tn(dsb, query) * score_scale).astype(bf16)
            dck_ref[:, to] = (dot_tn(dsc, query) * score_scale).astype(bf16)
            dv_ref[:, to] = dot_tn(pb_ref[head], grad_head).astype(bf16)
            dcv_ref[:, to] = dot_tn(pc_ref[head], grad_head).astype(bf16)

    def half():
        part = (
            dot_nt(dq_ref[...], wq_ref[0])
            + dot_nt(dk_ref[...], wk_ref[0])
            + dot_nt(dv_ref[...], wv_ref[0])
        )
        ctx_part = dot_nt(dck_ref[...], wk_ref[0]) + dot_nt(dcv_ref[...], wv_ref[0])
        row_sum = jnp.sum(
            part * (tok_ref[...].astype(f32) * first_gain_ref[...]), axis=1, keepdims=True
        )
        return part, ctx_part, row_sum

    @pl.when(step == pairs)
    def _():
        part, ctx_part, row_sum = half()
        hsend_ref[...] = part.astype(bf16)
        csend_ref[...] = ctx_part.astype(bf16)
        sum_ref[...] = row_sum

    @pl.when(step == pairs + 1)
    def _():
        part, ctx_part, row_sum = half()
        hown_ref[...] = part
        cown_ref[...] = ctx_part
        sum_ref[...] += row_sum


def attend_backward(
    hosts, block, own, other, cot_full, middle, gain, tok_full, first_gain, attn_full, kept, width
):
    pairs = width // TILE
    per = TILE // HEAD_DIM

    def pair(p):
        return jnp.minimum(p, pairs - 1)

    def side(p, s):
        return jnp.where(p <= pairs, 1 - s[8], s[8])

    def weight(position):
        return pl.BlockSpec((1, width, width), lambda p, s: (s[position], side(p, s), 0))

    def tile(rows):
        return pl.BlockSpec((rows, TILE), lambda p, s: (0, pair(p)))

    return call(
        attend_back_kernel,
        (pairs + 2,),
        [
            whole((BL, D)),
            whole((BL, D)),
            pl.BlockSpec((BL, D), lambda p, s: (block, 0)),
            whole((BL, D)),
            whole((1, D)),
            pl.BlockSpec((BL, width), lambda p, s: (block, side(p, s))),
            pl.BlockSpec((1, width), lambda p, s: (0, side(p, s))),
            pl.BlockSpec((1, D, TILE), lambda p, s: (s[3], 0, pair(p))),
            weight(0),
            weight(1),
            weight(2),
            tile(BL),
            tile(BL),
            tile(BL),
            tile(CTX),
            tile(CTX),
            pl.BlockSpec((per, BL, CTX), lambda p, s: (pair(p), 0, 0)),
            pl.BlockSpec((per, BL, BL), lambda p, s: (pair(p), 0, 0)),
        ],
        [
            whole((BL, D)),
            whole((BL, D)),
            whole((1, D)),
            whole((BL, width)),
            whole((BL, width)),
            whole((BL, width)),
            whole((CTX, width)),
            whole((CTX, width)),
            whole((BL, width)),
            whole((BL, width)),
            whole((CTX, width)),
            whole((CTX, width)),
            whole((BL, 1)),
        ],
        [
            pltpu.HBM((BL, D), bf16),
            pltpu.HBM((BL, D), f32),
            sds((1, D), f32),
            pltpu.HBM((BL, width), bf16),
            pltpu.HBM((BL, width), bf16),
            pltpu.HBM((BL, width), bf16),
            pltpu.HBM((CTX, width), bf16),
            pltpu.HBM((CTX, width), bf16),
            pltpu.HBM((BL, width), f32),
            sds((BL, width), bf16),
            sds((CTX, width), f32),
            sds((CTX, width), bf16),
            sds((BL, 1), f32),
        ],
        scratch=[pltpu.VMEM((per, BL, CTX), bf16), pltpu.VMEM((per, BL, BL), bf16)],
        prefetch=1,
        flops=12 * 10**9,
        nbytes=20 * 10**6,
    )(
        hosts,
        *hbm(own, other, cot_full, middle),
        gain,
        hbm(tok_full),
        first_gain,
        *hbm(attn_full, attn_full, attn_full, attn_full, *kept),
    )


def attn_grad_kernel(host_ref, *refs):
    (hid0, hid1, ctx0, ctx1, low0, low1), rest = refs[:6], refs[6:]
    (dq0, dk0, dv0, dck0, dcv0, mix0), rest = rest[:6], rest[6:]
    (dq1, dk1, dv1, dck1, dcv1, mix1), (out_ref,) = rest[:6], rest[6:]
    matrix = pl.program_id(0)

    @pl.when(matrix == 0)
    def _():
        out_ref[0] = (dot_tn(hid0[...], dq0[...]) + dot_tn(hid1[...], dq1[...])).astype(bf16)

    @pl.when(matrix == 1)
    def _():
        out_ref[0] = (
            dot_tn(hid0[...], dk0[...])
            + dot_tn(hid1[...], dk1[...])
            + dot_tn(ctx0[...], dck0[...])
            + dot_tn(ctx1[...], dck1[...])
        ).astype(bf16)

    @pl.when(matrix == 2)
    def _():
        out_ref[0] = (
            dot_tn(hid0[...], dv0[...])
            + dot_tn(hid1[...], dv1[...])
            + dot_tn(ctx0[...], dcv0[...])
            + dot_tn(ctx1[...], dcv1[...])
        ).astype(bf16)

    @pl.when(matrix == 3)
    def _():
        out_ref[0] = (dot_tn(low0[...], mix0[...]) + dot_tn(low1[...], mix1[...])).astype(bf16)


def attn_grads(hosts, hidden, context, lows, blocks, half_width):
    hid_specs = [
        pl.BlockSpec((BL, D), lambda m, s: (0, 0)),
        pl.BlockSpec((BL, D), lambda m, s: (1, 0)),
        pl.BlockSpec((CTX, D), lambda m, s: (0, 0)),
        pl.BlockSpec((CTX, D), lambda m, s: (1, 0)),
    ]
    block_specs = [
        whole((BL, half_width)),
        whole((BL, half_width)),
        whole((BL, half_width)),
        whole((CTX, half_width)),
        whole((CTX, half_width)),
        whole((BL, half_width)),
    ]
    return call(
        attn_grad_kernel,
        (4,),
        hid_specs + [whole((BL, D))] * 2 + block_specs * 2,
        [pl.BlockSpec((1, D, half_width), lambda m, s: (s[m], 0, 0))],
        [pltpu.HBM((OWNER_GROUPS, D, half_width), bf16)],
        prefetch=1,
        flops=46 * 10**8,
        nbytes=14 * 10**6,
    )(hosts, *hbm(hidden, hidden, context, context, *lows, *blocks[0], *blocks[1]))[0]


def mlp_kernel(
    host_ref,
    own_ref,
    other_ref,
    wo_ref,
    woo_ref,
    tok_ref,
    gain_ref,
    cot_ref,
    w1_ref,
    w2_ref,
    mid_ref,
    hid_ref,
    act_ref,
    pre_ref,
    low_ref,
    grad_ref,
):
    step = pl.program_id(0)

    @pl.when(step == 0)
    def _():
        middle = (
            tok_ref[...].astype(f32)
            + dot_nt(own_ref[...], wo_ref[0])
            + dot_nt(other_ref[...], woo_ref[...])
        )
        inverse = lax.rsqrt(jnp.mean(middle * middle, axis=1, keepdims=True) + epsilon_norm)
        mid_ref[...] = middle
        hid_ref[...] = (middle * inverse * gain_ref[...]).astype(bf16)
        grad_ref[...] = jnp.zeros_like(grad_ref)

    w1 = w1_ref[0]
    w2 = w2_ref[0]
    pre = dot_nn(hid_ref[...], w1)
    grad_act = dot_nn(cot_ref[...], w2)
    root = 0.7978845608028654
    square = pre * pre
    gate = 0.5 + 0.5 * jnp.tanh(pre * (root + (root * 0.044715) * square))
    act = pre * gate
    act_ref[...] = act.astype(bf16)
    slope = gate + act * (1.0 - gate) * (2.0 * root + (6.0 * root * 0.044715) * square)
    grad_pre = (slope * grad_act).astype(bf16)
    pre_ref[...] = grad_pre
    grad_ref[...] += dot_nt(grad_pre, w1)

    @pl.when(step == pl.num_programs(0) - 1)
    def _():
        low_ref[...] = grad_ref[...].astype(bf16)


def mlp_block(hosts, block, own, other, attn_full, wo_other, tok_full, gain, cot_full, mlp_full):
    half_width = own.shape[1]
    quarter = mlp_full.shape[2]
    hidden = 2 * quarter
    per = quarter // FT

    def weight(position):
        return pl.BlockSpec(
            (1, D, FT), lambda f, s: (s[4 + 2 * position + f // per], 0, lax.rem(f, per))
        )

    return call(
        mlp_kernel,
        (2 * per,),
        [
            whole((BL, half_width)),
            whole((BL, half_width)),
            pl.BlockSpec((1, D, half_width), lambda f, s: (s[3], 0, 0)),
            whole((D, half_width)),
            pl.BlockSpec((BL, D), lambda f, s: (block, 0)),
            whole((1, D)),
            pl.BlockSpec((BL, D), lambda f, s: (block, 0)),
            weight(0),
            weight(1),
        ],
        [
            whole((BL, D)),
            whole((BL, D)),
            pl.BlockSpec((BL, FT), lambda f, s: (0, f)),
            pl.BlockSpec((BL, FT), lambda f, s: (0, f)),
            whole((BL, D)),
        ],
        [
            pltpu.HBM((BL, D), f32),
            sds((BL, D), bf16),
            pltpu.HBM((BL, hidden), bf16),
            sds((BL, hidden), bf16),
            pltpu.HBM((BL, D), bf16),
        ],
        scratch=[pltpu.VMEM((BL, D), f32)],
        prefetch=1,
        flops=8 * 10**9,
        nbytes=24 * 10**6,
    )(
        hosts,
        own,
        other,
        hbm(attn_full),
        wo_other,
        tok_full,
        gain,
        cot_full,
        *hbm(mlp_full, mlp_full),
    )


def mlp_grad_kernel(host_ref, h0, h1, g0, g1, p0, p1, a0, a1, out_ref):
    matrix = pl.program_id(0)

    @pl.when(matrix == 0)
    def _():
        out_ref[0] = (dot_tn(h0[...], p0[...]) + dot_tn(h1[...], p1[...])).astype(bf16)

    @pl.when(matrix == 1)
    def _():
        out_ref[0] = (dot_tn(g0[...], a0[...]) + dot_tn(g1[...], a1[...])).astype(bf16)


def mlp_grads(hosts, hiddens, cot_full, pres, acts):
    hidden = acts[0].shape[1]
    quarter = hidden // 2
    per = quarter // FT
    last = 2 * per - 1
    used_first = pl.BlockSpec((BL, FT), lambda m, f, s: (0, jnp.where(m == 0, f, last)))
    used_second = pl.BlockSpec((BL, FT), lambda m, f, s: (0, jnp.where(m == 1, f, 0)))
    return call(
        mlp_grad_kernel,
        (2, 2 * per),
        [
            whole((BL, D)),
            whole((BL, D)),
            pl.BlockSpec((BL, D), lambda m, f, s: (0, 0)),
            pl.BlockSpec((BL, D), lambda m, f, s: (1, 0)),
            used_first,
            used_first,
            used_second,
            used_second,
        ],
        [
            pl.BlockSpec(
                (1, D, FT), lambda m, f, s: (s[4 + 2 * m + f // per], 0, lax.rem(f, per))
            )
        ],
        [pltpu.HBM((OWNER_GROUPS, D, quarter), bf16)],
        prefetch=1,
        flops=86 * 10**8,
        nbytes=20 * 10**6,
    )(
        hosts,
        hiddens[0],
        hiddens[1],
        cot_full,
        cot_full,
        *pres,
        *acts,
    )[0]


def mlp_out_kernel(host_ref, a0, a1, wa_ref, wb_ref, mid0, mid1, send_ref, own_ref):
    step = pl.program_id(0)
    quarter = wa_ref.shape[2]

    def rows(a_ref):
        return dot_nt(a_ref[:, :quarter], wa_ref[0]) + dot_nt(a_ref[:, quarter:], wb_ref[0])

    @pl.when(step == 0)
    def _():
        send_ref[:BL, :] = rows(a0).astype(bf16)
        send_ref[BL:, :] = rows(a1).astype(bf16)

    @pl.when(step == 1)
    def _():
        own_ref[:BL, :] = rows(a0) + mid0[...]
        own_ref[BL:, :] = rows(a1) + mid1[...]


def mlp_out(hosts, acts, mlp_full, middles, width):
    quarter = mlp_full.shape[2]

    def side(d, s):
        return jnp.where(d == 0, 1 - s[8], s[8])

    def weight(position):
        return pl.BlockSpec((1, width, quarter), lambda d, s: (s[position], side(d, s), 0))

    middle = pl.BlockSpec((BL, width), lambda d, s: (0, s[8]))
    return call(
        mlp_out_kernel,
        (2,),
        [whole((BL, 2 * quarter))] * 2 + [weight(6), weight(7), middle, middle],
        [whole((2 * BL, width))] * 2,
        [sds((2 * BL, width), bf16), pltpu.HBM((2 * BL, width), f32)],
        prefetch=1,
        flops=44 * 10**8,
        nbytes=12 * 10**6,
    )(hosts, *hbm(*acts, mlp_full, mlp_full, *middles))


def adam_step(gradient, moment_one, moment_two, weight, rate_table, decay_weight):
    step_count = f32(STEP)
    first_new = beta_first * moment_one + (1.0 - beta_first) * gradient
    second_new = beta_second * moment_two + (1.0 - beta_second) * gradient * gradient
    fixed_one = 1.0 - jnp.power(beta_first, step_count)
    fixed_two = 1.0 - jnp.power(beta_second, step_count)
    update = first_new / fixed_one / (jnp.sqrt(second_new / fixed_two) + epsilon_adam)
    return (first_new, second_new, weight - rate_table * (update + decay_weight * weight))


def body(
    tokens,
    cotangent,
    segments,
    owners,
    attn_master,
    attn_first,
    attn_second,
    mlp_master,
    mlp_first,
    mlp_second,
    ssm_params,
    ssm_first,
    ssm_second,
    norm_gains,
    gains_first,
    gains_second,
):
    rows = tokens.shape[1]
    width = tokens.shape[2]
    blocks = rows // BL
    dp_count = lax.axis_size("dp")
    dp_here = lax.axis_index("dp")
    side = lax.axis_index("tensor")
    group = dp_here // (dp_count // OWNER_GROUPS)
    quarter = mlp_master.shape[2] // 2

    def both_sides(own, other):
        return jnp.where(
            side == 0,
            jnp.concatenate([own, other], axis=-1),
            jnp.concatenate([other, own], axis=-1),
        )

    def side_of(values, which):
        return lax.dynamic_slice_in_dim(values, which * width, width, values.ndim - 1)

    smem = pl.BlockSpec(memory_space=pltpu.SMEM)
    vmem = pl.BlockSpec(memory_space=pltpu.VMEM)
    hosts, rates = pl.pallas_call(
        plan_kernel,
        in_specs=[smem, smem],
        out_specs=[smem, smem],
        out_shape=[sds((PLAN_SIZE,), i32), sds((4,), f32)],
    )(owners, jnp.stack([side, group]).astype(i32))
    attn_here = hosts[ATTN_HERE]
    mlp_here = hosts[MLP_HERE]
    near = hosts[NEAR] == 1
    ring = Ring()

    tok = tokens.reshape(rows, width)
    cot = cotangent.reshape(rows, width)
    tok_f = tok.astype(f32)
    square_here = jnp.sum(tok_f * tok_f, axis=1)
    square_other = swap_x(square_here)
    tok_other = swap_x(gate(tok, square_other))
    gains_other = swap_x(norm_gains)
    inverse_one = lax.rsqrt((square_here + square_other) / D + epsilon_norm)
    scaled_own = tok_f * inverse_one[:, None]
    hidden_own = (scaled_own * norm_gains[0]).astype(bf16)
    gains_full = both_sides(norm_gains, gains_other)

    attn_low = attn_master.astype(bf16)
    mlp_low = mlp_master[0].astype(bf16)
    attn_moved = move(attn_low[1], hosts[WAY], ATTN_WAYS, False)
    attn_block = jnp.where(attn_here == 0, attn_moved, attn_low[0])
    attn_full = lax.all_gather(attn_block, "dp", axis=0, tiled=True)
    attn_full = attn_full.reshape(OWNER_GROUPS, D, width)

    seg = segments.reshape(rows)
    prior = lax.ppermute(seg[rows - CTX :] + 1, "dp", [(i, i + 1) for i in range(dp_count - 1)]) - 1
    seg_ext = jnp.concatenate([prior[CTX - 1 :], seg])
    seg_col = seg[:, None]

    param_lanes = ssm_params.transpose(0, 2, 1)
    decay_rate = jnp.exp(param_lanes[0]) * (BL ** (-0.5) / 32.0)
    drive_root = jnp.sqrt(-jnp.expm1(-2.0 * decay_rate))
    reading = param_lanes[2] * drive_root * param_lanes[1]

    def doubled(values):
        lanes = values.reshape(STATE, 4, 128)
        return jnp.concatenate([lanes] * blocks, axis=1)

    rate_lanes = doubled(decay_rate)
    reading_lanes = doubled(reading)
    state_shape = sds((STATE, 8, 128), f32)

    def plain(kernel, scalars, count, outs, cost, scratch=()):
        return pl.pallas_call(
            kernel,
            in_specs=[smem] * scalars + [vmem] * count,
            out_specs=[vmem] * len(outs),
            out_shape=outs,
            scratch_shapes=scratch,
            name=kernel.__name__,
            compiler_params=pltpu.CompilerParams(vmem_limit_bytes=16 * 1024 * 1024),
            cost_estimate=pl.CostEstimate(flops=cost // COST, bytes_accessed=10**6 // COST, transcendentals=0),
        )

    hidden_lanes = to_lanes(hidden_own.astype(f32), blocks, BL)
    tail_lanes = sds((CTX, 8, 128), f32)
    tail_part, state_ends, device_end = plain(
        scan_kernel, 1, 3, [tail_lanes, state_shape, state_shape], 4 * 10**9
    )(seg_ext, hidden_lanes, rate_lanes, reading_lanes)
    id_rows = jnp.where(
        (jnp.arange(16) == 0)[:, None], seg[rows - 1].astype(f32), seg[0].astype(f32)
    )
    message = jnp.concatenate(
        [device_end.reshape(STATE * 8, 128), jnp.broadcast_to(id_rows, (16, 128))], axis=0
    ).astype(bf16)
    hidden_full = join_sides(
        hosts,
        tok,
        tok_other,
        (inverse_one[:, None], norm_gains[0:1], gains_other[0:1]),
    )
    mlp_moved = exchange_groups(gate(mlp_low[:, quarter:], tail_part), near)
    states_all = gather_round(message[None], 0)
    cot_other = swap_x(gate(cot, tok_other))
    for k in range(1, gather_rounds()):
        if k == gather_rounds() - 2:
            tok_other, states_all = together(tok_other, states_all)
        if k == gather_rounds() - 1:
            mlp_moved, states_all = together(mlp_moved, states_all)
        states_all = gather_round(states_all, k)
    states_all = gate(states_all, cot_other, hidden_full)
    mlp_block_low = jnp.where(mlp_here == 0, mlp_moved, mlp_low[:, :quarter])
    mlp_full = lax.all_gather(mlp_block_low, "dp", axis=0, tiled=True)
    mlp_full = mlp_full.reshape(OWNER_GROUPS, D, quarter)
    tok_full = join_sides(hosts, tok, tok_other)
    ids_all = states_all[:, STATE * 8 : STATE * 8 + 2, 0].astype(i32)
    places = jnp.arange(dp_count, dtype=i32)
    use_before = jnp.logical_and(places < dp_here, ids_all[:, 0] == seg_ext[0]).astype(i32)
    use_after = jnp.logical_and(places > dp_here, ids_all[:, 1] == seg[rows - 1]).astype(i32)
    tails, state_starts = plain(
        tail_kernel, 2, 5, [tail_lanes, state_shape], 10**9, [pltpu.VMEM((STATE, 8, 128), f32)]
    )(seg_ext, use_before, states_all, state_ends, rate_lanes, reading_lanes, tail_part)
    sens_states, sens_starts = plain(sens_kernel, 1, 3, [state_shape] * 2, 6 * 10**9)(
        seg_ext, hidden_lanes, state_starts, rate_lanes
    )
    tails = from_lanes(tails, blocks, CTX).astype(bf16)
    context_own = shift_tails(tails[blocks - 1], 1, False)
    context_other = shift_tails(tails[blocks - 1], 1, True)
    inner_own = tails[: blocks - 1]
    inner_other = swap_x(inner_own)
    context_full = jnp.concatenate(
        [
            both_sides(context_own, context_other)[None],
            both_sides(inner_own, inner_other),
        ],
        axis=0,
    ).reshape(-1, D)

    seg_rows = []
    for b in range(blocks):
        before = prior if b == 0 else seg[b * BL - CTX : b * BL]
        seg_rows.append(jnp.concatenate([before, seg[b * BL : (b + 1) * BL]])[None])
    kept = []
    mixed = []
    mixed_other = []
    for b in range(blocks):
        outs = attend_forward(
            hosts, b, hidden_full, context_full, attn_full, seg_col, seg_rows[b], width
        )
        kept.append(outs[:7])
        mixed.append(outs[7])
        mixed_other.append(swap_x(outs[7]))
    wo_own = lax.dynamic_index_in_dim(attn_full, hosts[3], 0, keepdims=False)
    wo_half = lax.dynamic_slice_in_dim(wo_own, ring.core * (D // 2), D // 2, 0)
    wo_half = gate(wo_half, inner_other)
    wo_first = swap_x(wo_half)
    wo_second = lax.ppermute(gate(wo_first, mixed[0]), "dp", ring.cores)
    joined = together(*mixed_other, sens_states, sens_starts)
    mixed_other, (sens_states, sens_starts) = list(joined[:blocks]), joined[blocks:]
    wo_other = jnp.where(
        ring.core == 0,
        jnp.concatenate([wo_first, wo_second], axis=0),
        jnp.concatenate([wo_second, wo_first], axis=0),
    )

    cot_full = join_sides(hosts, gate(cot, mixed[0]), cot_other)

    gain_two = gains_full[1:2]
    middles, hiddens, acts, pres, grads, grads_other = [], [], [], [], [], []
    for b in range(blocks):
        middle, hidden_two, act, grad_pre, grad_low = mlp_block(
            hosts,
            b,
            mixed[b],
            mixed_other[b],
            attn_full,
            wo_other,
            tok_full,
            gain_two,
            cot_full,
            mlp_full,
        )
        middles.append(middle)
        hiddens.append(hidden_two)
        acts.append(act)
        pres.append(grad_pre)
        grads.append(grad_low)
        grads_other.append(swap_x(grad_low))
    mlp_sum_in = mlp_grads(hosts, hiddens, cot_full, pres, acts)
    grads_other[0], mlp_sum_in = lax.optimization_barrier((grads_other[0], mlp_sum_in))
    mlp_sum = lax.psum_scatter(
        mlp_sum_in.reshape(OWNER_GROUPS * D, quarter), "dp", scatter_dimension=0, tiled=True
    )

    lows, grad_mids, gain_twos, grad_blocks = [], [], [], []
    parts, parts_sent, ctx_parts, ctx_sent, row_sums = [], [], [], [], []
    for b in range(blocks):
        if b == blocks - 1:
            acts[0] = gate(acts[0], *lows)
            out_send, out_own = mlp_out(hosts, acts, mlp_full, middles, width)
            out_received = swap_x(out_send)
            grads[b] = gate(grads[b], out_own)
        outs = attend_backward(
            hosts,
            b,
            gate(grads[b], *lows),
            grads_other[b],
            cot_full,
            middles[b],
            gain_two,
            tok_full,
            gains_full[0:1],
            attn_full,
            kept[b],
            width,
        )
        lows.append(outs[0])
        grad_mids.append(side_of(outs[1], side))
        gain_twos.append(side_of(outs[2], side))
        grad_blocks.append(list(outs[3:8]) + [mixed[b]])
        parts.append(outs[8])
        parts_sent.append(outs[9])
        ctx_parts.append(outs[10])
        ctx_sent.append(outs[11])
        row_sums.append(outs[12][:, 0])
    grad_tails = jnp.stack(
        [ctx_parts[b] + swap_x(ctx_sent[b]).astype(f32) for b in range(1, blocks)]
        + [
            shift_tails(ctx_parts[0].astype(bf16), -1, False).astype(f32)
            + shift_tails(ctx_sent[0], -1, True).astype(f32)
        ]
    )
    tail_grad_lanes = to_lanes(grad_tails.reshape(blocks * CTX, width), blocks, CTX)
    own_back, device_back = plain(back_total_kernel, 1, 3, [state_shape, state_shape], 10**9)(
        seg_ext, tail_grad_lanes, rate_lanes, reading_lanes
    )
    back_all = gather_round(device_back.reshape(STATE * 8, 128).astype(bf16)[None], 0)
    lows[0] = gate(lows[0], back_all)
    attn_sum_in = attn_grads(hosts, hidden_full, context_full, lows, grad_blocks, width)
    received = [swap_x(v) for v in parts_sent]
    part, up, down = ring.start(attn_sum_in.reshape(dp_count, -1, width))
    back_all = gather_round(back_all, 1)
    steps = 0
    for k in range(2, gather_rounds()):
        up, down, back_all = together(up, down, back_all)
        back_all = gather_round(back_all, k)
        up, down = ring.step(steps, part, up, down)
        steps += 1
    mlp_sum = gate(mlp_sum, back_all)
    mlp_back = exchange_groups(mlp_sum, near)
    grad_c_lanes, grad_a_lanes, sens_end = plain(
        sens_tail_kernel, 1, 5, [state_shape] * 3, 2 * 10**9
    )(seg_ext, hidden_lanes, tail_grad_lanes, sens_states, sens_starts, rate_lanes)
    grad_lanes, grad_a_lanes = plain(
        back_scan_kernel,
        2,
        7,
        [sds((BL, 8, 128), f32), state_shape],
        4 * 10**9,
        [pltpu.VMEM((STATE, 8, 128), f32)],
    )(
        seg_ext,
        use_after,
        back_all,
        tail_grad_lanes,
        own_back,
        sens_end,
        grad_a_lanes,
        rate_lanes,
        reading_lanes,
    )
    for k in range(steps, ring.far_up):
        up, down = ring.step(k, part, up, down)
    attn_sum = (part(0) + up.astype(f32) + down.astype(f32)).astype(bf16)
    grad_channels = lax.optimization_barrier(
        from_lanes(grad_lanes, blocks, BL).reshape(rows, width)
    )

    part_own = jnp.concatenate(parts, axis=0)
    received = jnp.concatenate(received, axis=0)
    row_here = inverse_one * jnp.concatenate(row_sums) + jnp.sum(
        grad_channels * (scaled_own * norm_gains[0]), axis=1
    )
    row_other = swap_x(row_here)
    row_total = row_here + row_other
    block_out = (out_own + out_received.astype(f32)).astype(bf16)
    grad_hidden = part_own + received.astype(f32) + grad_channels
    grad_tokens = jnp.concatenate(grad_mids, axis=0) + inverse_one[:, None] * (
        grad_hidden * norm_gains[0] - scaled_own * (row_total / D)[:, None]
    )
    gain_one = jnp.sum(grad_hidden * scaled_own, axis=0)
    gain_two_sum = sum(gain_twos)[0]

    def merged(values):
        return sum(values[:, 4 * b : 4 * b + 4] for b in range(blocks)).reshape(STATE, width)

    small = jnp.concatenate(
        [merged(grad_c_lanes), merged(grad_a_lanes), gain_one[None], gain_two_sum[None]], axis=0
    )
    attn_back = move(attn_sum, hosts[WAY], ATTN_WAYS, True)
    small, (mlp_back, attn_back) = total_dp(small, (mlp_back, attn_back))
    grad_c, grad_a = small[:STATE], small[STATE : 2 * STATE]
    gains_grad = small[2 * STATE :]
    decay_step = jnp.exp(-decay_rate)
    grad_read = grad_c * drive_root * param_lanes[1]
    grad_drive = grad_c * drive_root * param_lanes[2]
    grad_a = grad_a - grad_c * param_lanes[1] * param_lanes[2] * decay_step / drive_root
    grad_log = -decay_rate * decay_step * grad_a
    ssm_grad = jnp.stack([grad_log, grad_drive, grad_read]).transpose(0, 2, 1)

    attn_grad = jnp.stack(
        [
            jnp.where(attn_here >= 1, attn_sum.astype(f32), 0.0),
            jnp.where(attn_here == 2, attn_back.astype(f32), 0.0),
        ]
    )
    mlp_grad = jnp.where(
        mlp_here == 1, jnp.concatenate([mlp_sum, mlp_back], axis=1).astype(f32), 0.0
    )[None]

    attn_rates = rates[:2, None, None]
    mlp_rates = rates[2]
    ssm_rates = jnp.asarray([1.0, 0.8, 0.25], f32)[:, None, None]
    gain_rates = jnp.asarray([0.6, 0.6], f32)[:, None]
    attn_one, attn_two, attn_new = adam_step(
        attn_grad, attn_first, attn_second, attn_master, attn_rates, matrix_decay
    )
    mlp_one, mlp_two, mlp_new = adam_step(
        mlp_grad, mlp_first, mlp_second, mlp_master, mlp_rates, matrix_decay
    )
    ssm_one, ssm_two, ssm_new = adam_step(
        ssm_grad, ssm_first, ssm_second, ssm_params, ssm_rates, 0.0
    )
    gain_first_new, gain_second_new, gains_new = adam_step(
        gains_grad, gains_first, gains_second, norm_gains, gain_rates, 0.0
    )
    return (
        block_out.reshape(tokens.shape),
        grad_tokens.reshape(tokens.shape),
        attn_grad,
        attn_one,
        attn_two,
        attn_new,
        attn_new.astype(bf16),
        mlp_grad,
        mlp_one,
        mlp_two,
        mlp_new,
        mlp_new.astype(bf16),
        ssm_grad,
        ssm_one,
        ssm_two,
        ssm_new,
        gains_grad,
        gain_first_new,
        gain_second_new,
        gains_new,
    )


def solution(mesh):
    in_specs = (
        P(None, "dp", "tensor"),
        P(None, "dp", "tensor"),
        P(None, "dp"),
        P(),
        P(None, "dp", "tensor"),
        P(None, "dp", "tensor"),
        P(None, "dp", "tensor"),
        P(None, "dp", "tensor"),
        P(None, "dp", "tensor"),
        P(None, "dp", "tensor"),
        P(None, "tensor", None),
        P(None, "tensor", None),
        P(None, "tensor", None),
        P(None, "tensor"),
        P(None, "tensor"),
        P(None, "tensor"),
    )
    out_specs = (
        P(None, "dp", "tensor"),
        P(None, "dp", "tensor"),
        P(None, "dp", "tensor"),
        P(None, "dp", "tensor"),
        P(None, "dp", "tensor"),
        P(None, "dp", "tensor"),
        P(None, "dp", "tensor"),
        P(None, "dp", "tensor"),
        P(None, "dp", "tensor"),
        P(None, "dp", "tensor"),
        P(None, "dp", "tensor"),
        P(None, "dp", "tensor"),
        P(None, "tensor", None),
        P(None, "tensor", None),
        P(None, "tensor", None),
        P(None, "tensor", None),
        P(None, "tensor"),
        P(None, "tensor"),
        P(None, "tensor"),
        P(None, "tensor"),
    )
    return jax.shard_map(body, mesh=mesh, in_specs=in_specs, out_specs=out_specs, check_vma=False)
```

```python
import functools
import itertools

import jax
import jax.numpy as jnp
from jax import lax
from jax.experimental import pallas as pl
from jax.experimental.pallas import tpu as pltpu
from jax.sharding import PartitionSpec as P

D = 1024
HEAD_DIM = 128
FF = 4096
STATE = 16
CTX = 128
BL = 512
OWNER_GROUPS = 4
STEP = 5

epsilon_norm = 1e-05
beta_first = 0.9
beta_second = 0.95
epsilon_adam = 1e-08
matrix_decay = 0.1
masked_score = -1e30
score_scale = HEAD_DIM ** (-0.5)
f32 = jnp.float32
bf16 = jnp.bfloat16
i32 = jnp.int32
SWAP = [(0, 1), (1, 0)]
COST = 1000
TILE = 256
QT = 256
FT = 512
LOG2E = 1.4426950408889634


def dot_nn(left, right):
    return lax.dot_general(left, right, (((1,), (0,)), ((), ())), preferred_element_type=f32)


def dot_nt(left, right):
    return lax.dot_general(left, right, (((1,), (1,)), ((), ())), preferred_element_type=f32)


def dot_tn(left, right):
    return lax.dot_general(left, right, (((0,), (0,)), ((), ())), preferred_element_type=f32)


def call(
    kernel, grid, in_specs, out_specs, out_shape, scratch=(), prefetch=0, flops=0, nbytes=0, room=36
):
    return pl.pallas_call(
        kernel,
        grid_spec=pltpu.PrefetchScalarGridSpec(
            num_scalar_prefetch=prefetch,
            grid=grid,
            in_specs=in_specs,
            out_specs=out_specs,
            scratch_shapes=scratch,
        ),
        out_shape=out_shape,
        name=kernel.__name__,
        compiler_params=pltpu.CompilerParams(vmem_limit_bytes=room * 1024 * 1024),
        cost_estimate=pl.CostEstimate(flops=flops // COST, bytes_accessed=nbytes // COST, transcendentals=0),
    )


def whole(shape):
    return pl.BlockSpec(shape, lambda *_: (0,) * len(shape), pipeline_mode=pl.Buffered(1))


def sds(shape, dtype):
    return jax.ShapeDtypeStruct(shape, dtype)


def hbm(*values):
    held = tuple(pltpu.with_memory_space_constraint(v, pltpu.HBM) for v in values)
    return held[0] if len(held) == 1 else held


def swap_x(values):
    return lax.ppermute(values, "tensor", SWAP)


def gate(value, *others):
    if not others:
        return value
    return lax.optimization_barrier((value,) + others)[0]


def together(*values):
    return lax.optimization_barrier(values)


def gather_rounds():
    return max(lax.axis_size("dp") - 1, 0).bit_length()


def gather_round(held, k):
    step = 1 << k
    count = lax.axis_size("dp")
    other = lax.ppermute(held, "dp", [(i, i ^ step) for i in range(count)])
    later = (lax.axis_index("dp") // step) % 2 == 1
    return jnp.where(
        later,
        jnp.concatenate([other, held], axis=0),
        jnp.concatenate([held, other], axis=0),
    )


def total_dp(values, beside):
    count = lax.axis_size("dp")
    for k in range(gather_rounds()):
        if k == 1:
            values, beside = together(values, beside)
        values = values + lax.ppermute(values, "dp", [(i, i ^ (1 << k)) for i in range(count)])
    return values, beside


def routes(full_count, empty_count):
    groups = range(OWNER_GROUPS)
    ways = []
    for full in itertools.combinations(groups, full_count):
        rest = [g for g in groups if g not in full]
        for empty in itertools.combinations(rest, empty_count):
            ways.append((full, empty))
    return ways


ATTN_WAYS = routes(1, 1) + routes(2, 2)


def way_code(full, empty):
    code = 0
    for g in range(OWNER_GROUPS):
        digit = 2 if g in full else (0 if g in empty else 1)
        code += digit * 3**g
    return code


def one_if(condition):
    return jnp.where(condition, jnp.int32(1), jnp.int32(0))


HOST_MLP, SIDE, WAY, NEAR, ATTN_HERE, MLP_HERE, PLAN_SIZE = 4, 8, 9, 10, 11, 12, 16
ATTN_RATES = [0.5 * D ** (-0.5)] * 3 + [0.5 * (D // 16) ** (-0.5)]
MLP_RATES = [0.5 * D ** (-0.5), 0.5 * FF ** (-0.5)]
IDLE_RATE = 0.5 * D ** (-0.5)


def plan_kernel(owner_ref, here_ref, out_ref, rate_ref):
    groups = range(OWNER_GROUPS)
    side, group = here_ref[0], here_ref[1]
    owner = [owner_ref[m] for m in range(6)]
    slot = [
        sum([one_if(owner[k] == owner[m]) for k in range(m)], jnp.int32(0)) for m in range(4)
    ]
    count = [sum([one_if(owner[m] == g) for m in range(4)], jnp.int32(0)) for g in groups]
    full_rank = [sum([one_if(count[h] == 2) for h in range(g)], jnp.int32(0)) for g in groups]
    empty_rank = [sum([one_if(count[h] == 0) for h in range(g)], jnp.int32(0)) for g in groups]
    taker = [
        sum(
            [
                jnp.where(
                    jnp.logical_and(count[h] == 0, empty_rank[h] == full_rank[g]), jnp.int32(h), 0
                )
                for h in groups
            ],
            jnp.int32(0),
        )
        for g in groups
    ]
    for m in range(4):
        second = sum([jnp.where(owner[m] == g, taker[g], 0) for g in groups], jnp.int32(0))
        out_ref[m] = jnp.where(slot[m] == 0, owner[m], second)
    code = sum([count[g] * 3**g for g in groups], jnp.int32(0))
    out_ref[WAY] = sum(
        [
            jnp.where(code == way_code(*way), jnp.int32(k), 0)
            for k, way in enumerate(ATTN_WAYS)
        ],
        jnp.int32(0),
    )
    low = sum([one_if(owner[m] < 2) for m in (4, 5)], jnp.int32(0))
    near = low == 1
    for k, m in enumerate((4, 5)):
        out_ref[HOST_MLP + 2 * k] = owner[m]
        bit = jnp.where(near, jnp.int32(1), jnp.int32(2))
        out_ref[HOST_MLP + 2 * k + 1] = jnp.bitwise_xor(owner[m], bit)
    out_ref[SIDE] = side
    out_ref[NEAR] = one_if(near)
    out_ref[ATTN_HERE] = sum([one_if(owner[m] == group) for m in range(4)], jnp.int32(0))
    out_ref[MLP_HERE] = sum([one_if(owner[m] == group) for m in (4, 5)], jnp.int32(0))
    for k in range(MLP_HERE + 1, PLAN_SIZE):
        out_ref[k] = jnp.int32(0)
    for place in range(2):
        rate = f32(IDLE_RATE)
        for m in range(4):
            hit = jnp.logical_and(owner[m] == group, slot[m] == place)
            rate = jnp.where(hit, f32(ATTN_RATES[m]), rate)
        rate_ref[place] = rate
    rate = f32(IDLE_RATE)
    for k, m in enumerate((4, 5)):
        rate = jnp.where(owner[m] == group, f32(MLP_RATES[k]), rate)
    rate_ref[2] = rate
    rate_ref[3] = f32(0.0)


def move(values, index, ways, back):
    size = lax.axis_size("dp") // OWNER_GROUPS

    def branch(way):
        pairs = []
        for a, b in zip(*way):
            if back:
                a, b = b, a
            pairs += [(a * size + j, b * size + j) for j in range(size)]
        return lambda v: lax.ppermute(v, "dp", pairs)

    return lax.switch(index, [branch(way) for way in ways], values)


def exchange_groups(values, near):
    size = lax.axis_size("dp") // OWNER_GROUPS

    def across(bit):
        return lax.ppermute(
            values,
            "dp",
            [(g * size + j, (g ^ bit) * size + j) for g in range(OWNER_GROUPS) for j in range(size)],
        )

    return jnp.where(near, across(1), across(2))


def ring_order(count):
    chips = count // 2
    if chips == 8:
        return [0, 2, 4, 6, 7, 5, 3, 1]
    return list(range(chips))


def join_kernel(host_ref, own_ref, other_ref, out_ref):
    @pl.when(pl.program_id(0) == 0)
    def _():
        out_ref[...] = own_ref[...]

    @pl.when(pl.program_id(0) == 1)
    def _():
        out_ref[...] = other_ref[...]


def join_scaled_kernel(
    host_ref, own_ref, other_ref, inverse_ref, gain_ref, gain_other_ref, out_ref
):
    @pl.when(pl.program_id(0) == 0)
    def _():
        out_ref[...] = (own_ref[...].astype(f32) * inverse_ref[...] * gain_ref[...]).astype(bf16)

    @pl.when(pl.program_id(0) == 1)
    def _():
        out_ref[...] = (
            other_ref[...].astype(f32) * inverse_ref[...] * gain_other_ref[...]
        ).astype(bf16)


def join_sides(hosts, own, other, scales=()):
    rows, width = own.shape
    return call(
        join_scaled_kernel if scales else join_kernel,
        (2,),
        [whole(v.shape) for v in (own, other) + tuple(scales)],
        [
            pl.BlockSpec(
                (rows, width), lambda d, s: (0, jnp.where(d == 0, s[SIDE], 1 - s[SIDE]))
            )
        ],
        [pltpu.HBM((rows, 2 * width), bf16)],
        prefetch=1,
        nbytes=8 * rows * width,
        room=12,
    )(hosts, own, other, *scales)[0]


class Ring:
    def __init__(self):
        self.count = lax.axis_size("dp")
        self.chips = self.count // 2
        order = ring_order(self.count)
        here = lax.axis_index("dp")
        self.core = here % 2
        chip = here // 2
        self.place = jnp.where(chip % 2 == 0, chip // 2, 7 - chip // 2) if self.chips == 8 else chip
        self.up = [
            (2 * order[p] + c, 2 * order[(p + 1) % self.chips] + c)
            for p in range(self.chips)
            for c in range(2)
        ]
        self.down = [(b, a) for a, b in self.up]
        self.cores = [(i, i ^ 1) for i in range(self.count)]
        self.far_up = self.chips // 2
        self.far_down = self.chips - 1 - self.far_up

    def chip(self, offset):
        place = (self.place + self.chips + offset) % self.chips
        if self.chips != 8:
            return place
        return jnp.where(place < 4, 2 * place, 15 - 2 * place)

    def start(self, blocks):
        pairs = blocks.reshape((self.chips, 2) + blocks.shape[1:])
        mine = lax.dynamic_index_in_dim(pairs, self.core, 1, keepdims=False)
        theirs = lax.dynamic_index_in_dim(pairs, 1 - self.core, 1, keepdims=False)
        received = lax.ppermute(theirs, "dp", self.cores)

        def part(offset):
            chip = self.chip(offset)
            return lax.dynamic_index_in_dim(mine, chip, 0, keepdims=False).astype(
                f32
            ) + lax.dynamic_index_in_dim(received, chip, 0, keepdims=False).astype(f32)

        return part, part(self.far_up).astype(bf16), part(-self.far_down).astype(bf16)

    def step(self, k, part, up, down):
        if k < self.far_up:
            up = lax.ppermute(up, "dp", self.up)
            if k < self.far_up - 1:
                up = (up.astype(f32) + part(self.far_up - 1 - k)).astype(bf16)
        if k < self.far_down:
            down = lax.ppermute(down, "dp", self.down)
            if k < self.far_down - 1:
                down = (down.astype(f32) + part(k + 1 - self.far_down)).astype(bf16)
        return up, down


def shift_tails(values, by, cross):
    count = lax.axis_size("dp")
    pairs = [
        (2 * i + s, 2 * (i + by) + (1 - s if cross else s))
        for i in range(count)
        for s in range(2)
        if 0 <= i + by < count
    ]
    return lax.ppermute(values, ("dp", "tensor"), pairs)


def first_half():
    return lax.broadcasted_iota(i32, (8, 128), 0) < 4


def flag(condition):
    return jnp.where(condition, f32(1.0), f32(0.0))


def keep_at(seg_ref, t, half):
    return jnp.where(
        half, flag(seg_ref[t + 1] == seg_ref[t]), flag(seg_ref[BL + t + 1] == seg_ref[BL + t])
    )


def chunked(seg_ref, begin, end, plain, kept, carried, back=False):
    size = 8
    count = (end - begin) // size

    def chunk(c, carried):
        first = begin + (count - 1 - c if back else c) * size
        same = jnp.logical_and(
            seg_ref[first] == seg_ref[first + size],
            seg_ref[BL + first] == seg_ref[BL + first + size],
        )

        def run(step):
            def go(carried):
                for k in range(size):
                    carried = step(first + (size - 1 - k if back else k), carried)
                return carried

            return go

        return lax.cond(same, run(plain), run(kept), carried)

    return lax.fori_loop(0, count, chunk, carried)


def scan_kernel(seg_ref, h_ref, rate_ref, c_ref, y_ref, s_ref, e_ref):
    half = first_half()
    decay = [jnp.exp(-rate_ref[n]) for n in range(STATE)]

    def plain(t, states):
        row = h_ref[t]
        return [states[n] * decay[n] + row for n in range(STATE)]

    def kept(t, states):
        keep = keep_at(seg_ref, t, half)
        row = h_ref[t]
        return [(states[n] * keep) * decay[n] + row for n in range(STATE)]

    def reading(step):
        def go(t, states):
            states = step(t, states)
            total = c_ref[0] * states[0]
            for n in range(1, STATE):
                total = total + c_ref[n] * states[n]
            y_ref[t - (BL - CTX)] = total
            return states

        return go

    states = [jnp.zeros((8, 128), f32)] * STATE
    states = chunked(seg_ref, 0, BL - CTX, plain, kept, states)
    states = chunked(seg_ref, BL - CTX, BL, reading(plain), reading(kept), states)
    joined = flag(seg_ref[2 * BL] == seg_ref[BL])
    for n in range(STATE):
        s_ref[n] = states[n]
        ends = states[n] + (joined * jnp.exp(-rate_ref[n] * BL)) * pltpu.roll(states[n], 4, 0)
        e_ref[n] = ends


def tail_kernel(
    seg_ref, use_ref, all_ref, s_ref, rate_ref, c_ref, y_ref, out_ref, start_ref, carry_ref
):
    half = first_half()
    before = seg_ref[0]
    joined = flag(seg_ref[BL] == before)
    decay = [jnp.exp(-rate_ref[n]) for n in range(STATE)]
    carry_ref[...] = jnp.zeros_like(carry_ref)

    def gather(j, _):
        @pl.when(use_ref[j] > 0)
        def _():
            for m in range(STATE // 2):
                pair = all_ref[j, 16 * m : 16 * m + 16, :].astype(f32)
                for k in range(2):
                    n = 2 * m + k
                    power = jnp.exp(-rate_ref[n] * (2 * BL))
                    carry_ref[n] = carry_ref[n] * power + pair[8 * k : 8 * k + 8]

        return 0

    lax.fori_loop(0, all_ref.shape[0], gather, 0)
    weighted = []
    for n in range(STATE):
        carried = pltpu.roll(carry_ref[n], 4, 0)
        mid = pltpu.roll(s_ref[n], 4, 0) + (joined * jnp.exp(-rate_ref[n] * BL)) * carry_ref[n]
        start = jnp.where(half, carried, mid)
        start_ref[n] = start
        weighted.append(c_ref[n] * start * jnp.exp(-rate_ref[n] * (BL - CTX + 1)))

    def step(t, parts):
        mask = jnp.where(
            half,
            flag(seg_ref[t + 1 + BL - CTX] == before),
            flag(seg_ref[BL + t + 1 + BL - CTX] == seg_ref[BL]),
        )
        total = parts[0]
        for n in range(1, STATE):
            total = total + parts[n]
        out_ref[t] = y_ref[t] + mask * total
        return [parts[n] * decay[n] for n in range(STATE)]

    lax.fori_loop(0, CTX, step, weighted, unroll=4)


def back_total_kernel(seg_ref, g_ref, rate_ref, c_ref, own_ref, out_ref):
    half = first_half()
    decay = [jnp.exp(-rate_ref[n]) for n in range(STATE)]

    def step(k, sums):
        t = CTX - 1 - k
        mask = jnp.where(
            half,
            flag(seg_ref[t + 1 + BL - CTX] == seg_ref[1]),
            flag(seg_ref[BL + t + 1 + BL - CTX] == seg_ref[BL]),
        )
        grad = mask * g_ref[t]
        return [decay[n] * (sums[n] + grad) for n in range(STATE)]

    sums = lax.fori_loop(0, CTX, step, [jnp.zeros((8, 128), f32)] * STATE, unroll=4)
    joined = flag(seg_ref[1] == seg_ref[BL])
    for n in range(STATE):
        total = sums[n] * c_ref[n] * jnp.exp(-rate_ref[n] * (BL - CTX))
        own_ref[n] = total
        out_ref[n] = total + (joined * jnp.exp(-rate_ref[n] * BL)) * pltpu.roll(total, 4, 0)


def sens_steps(seg_ref, h_ref, half, decay, count):
    def plain(t, both):
        row = h_ref[t]
        sens = [both[1][n] * decay[n] + both[0][n] for n in range(count)]
        states = [both[0][n] * decay[n] + row for n in range(count)]
        return [states, sens] + list(both[2:])

    def kept(t, both):
        keep = keep_at(seg_ref, t, half)
        row = h_ref[t]
        held = [v * keep for v in both[0]]
        sens = [(both[1][n] * keep) * decay[n] + held[n] for n in range(count)]
        states = [held[n] * decay[n] + row for n in range(count)]
        return [states, sens] + list(both[2:])

    return plain, kept


SENS_GROUP = 8


def sens_kernel(seg_ref, h_ref, start_ref, rate_ref, s_ref, z_ref):
    half = first_half()
    for first in range(0, STATE, SENS_GROUP):
        ids = range(first, first + SENS_GROUP)
        decay = [jnp.exp(-rate_ref[n]) for n in ids]
        plain, kept = sens_steps(seg_ref, h_ref, half, decay, SENS_GROUP)
        both = [[start_ref[n] for n in ids], [jnp.zeros((8, 128), f32)] * SENS_GROUP]
        both = chunked(seg_ref, 0, BL - CTX, plain, kept, both)
        for k, n in enumerate(ids):
            s_ref[n] = both[0][k]
            z_ref[n] = both[1][k]


def sens_tail_kernel(seg_ref, h_ref, g_ref, s_ref, z_ref, rate_ref, gc_ref, ga_ref, zend_ref):
    half = first_half()
    for first in range(0, STATE, SENS_GROUP):
        ids = range(first, first + SENS_GROUP)
        decay = [jnp.exp(-rate_ref[n]) for n in ids]

        def summing(step):
            def go(t, carried):
                states, sens, by_c, by_a = step(t, carried)
                grad = g_ref[t - (BL - CTX)]
                by_c = [by_c[n] + grad * states[n] for n in range(SENS_GROUP)]
                by_a = [by_a[n] + grad * sens[n] for n in range(SENS_GROUP)]
                return [states, sens, by_c, by_a]

            return go

        plain, kept = sens_steps(seg_ref, h_ref, half, decay, SENS_GROUP)
        zeros = [jnp.zeros((8, 128), f32)] * SENS_GROUP
        carried = [[s_ref[n] for n in ids], [z_ref[n] for n in ids], zeros, zeros]
        carried = chunked(seg_ref, BL - CTX, BL, summing(plain), summing(kept), carried)
        for k, n in enumerate(ids):
            zend_ref[n] = carried[1][k]
            gc_ref[n] = carried[2][k]
            ga_ref[n] = carried[3][k]


def back_scan_kernel(
    seg_ref,
    use_ref,
    all_ref,
    g_ref,
    own_ref,
    z_ref,
    ga_ref,
    rate_ref,
    c_ref,
    gh_ref,
    out_ref,
    later_ref,
):
    half = first_half()
    decay = [jnp.exp(-rate_ref[n]) for n in range(STATE)]
    joined = flag(seg_ref[2 * BL] == seg_ref[BL])
    later_ref[...] = jnp.zeros_like(later_ref)
    count = all_ref.shape[0]

    def gather(k, _):
        j = count - 1 - k

        @pl.when(use_ref[j] > 0)
        def _():
            for m in range(STATE // 2):
                pair = all_ref[j, 16 * m : 16 * m + 16, :].astype(f32)
                for k in range(2):
                    n = 2 * m + k
                    power = jnp.exp(-rate_ref[n] * (2 * BL))
                    later_ref[n] = later_ref[n] * power + pair[8 * k : 8 * k + 8]

        return 0

    lax.fori_loop(0, count, gather, 0)
    sums = []
    for n in range(STATE):
        first = (
            pltpu.roll(own_ref[n], 4, 0) + (joined * jnp.exp(-rate_ref[n] * BL)) * later_ref[n]
        )
        entering = jnp.where(half, first, pltpu.roll(later_ref[n], 4, 0))
        sums.append(entering)
        out_ref[n] = ga_ref[n] * c_ref[n] + entering * z_ref[n]

    def total_of(t, sums):
        total = sums[0]
        for n in range(1, STATE):
            total = total + sums[n]
        gh_ref[t] = total

    def plain(t, sums):
        total_of(t, sums)
        return [v * decay[n] for n, v in enumerate(sums)]

    def kept(t, sums):
        total_of(t, sums)
        keep = keep_at(seg_ref, t, half)
        return [(v * keep) * decay[n] for n, v in enumerate(sums)]

    def entered(step):
        def go(t, sums):
            grad = g_ref[t - (BL - CTX)]
            return step(t, [sums[n] + c_ref[n] * grad for n in range(STATE)])

        return go

    sums = chunked(seg_ref, BL - CTX, BL, entered(plain), entered(kept), sums, back=True)
    chunked(seg_ref, 0, BL - CTX, plain, kept, sums, back=True)


def to_lanes(values, blocks, steps):
    return (
        values.reshape(blocks, steps, 4, 128).transpose(1, 0, 2, 3).reshape(steps, blocks * 4, 128)
    )


def from_lanes(values, blocks, steps):
    return values.reshape(steps, blocks, 4, 128).transpose(1, 0, 2, 3).reshape(blocks, steps, 512)


def attend_kernel(
    host_ref,
    hid_ref,
    ctx_ref,
    wq_ref,
    wk_ref,
    wv_ref,
    segq_ref,
    segk_ref,
    q_ref,
    k_ref,
    v_ref,
    ck_ref,
    cv_ref,
    pc_ref,
    pb_ref,
    mix_ref,
):
    hid = hid_ref[...]
    ctx = ctx_ref[...]
    q_ref[...] = dot_nn(hid, wq_ref[0]).astype(bf16)
    k_ref[...] = dot_nn(hid, wk_ref[0]).astype(bf16)
    v_ref[...] = dot_nn(hid, wv_ref[0]).astype(bf16)
    ck_ref[...] = dot_nn(ctx, wk_ref[0]).astype(bf16)
    cv_ref[...] = dot_nn(ctx, wv_ref[0]).astype(bf16)
    ctx_ids = segk_ref[:, :CTX]
    for i in range(BL // QT):
        rows = slice(i * QT, (i + 1) * QT)
        reach = (i + 1) * QT
        ids = segq_ref[rows]
        ctx_ok = ctx_ids == ids
        place_q = lax.broadcasted_iota(i32, (QT, reach), 0) + i * QT
        place_k = lax.broadcasted_iota(i32, (QT, reach), 1)
        block_ok = jnp.logical_and(place_k <= place_q, segk_ref[:, CTX : CTX + reach] == ids)
        for head in range(TILE // HEAD_DIM):
            cols = slice(head * HEAD_DIM, (head + 1) * HEAD_DIM)
            query = q_ref[rows, cols]
            sc = dot_nt(query, ck_ref[:, cols]) * (score_scale * LOG2E)
            sb = dot_nt(query, k_ref[:reach, cols]) * (score_scale * LOG2E)
            sc = jnp.where(ctx_ok, sc, masked_score)
            sb = jnp.where(block_ok, sb, masked_score)
            top = jnp.maximum(
                jnp.max(sc, axis=1, keepdims=True), jnp.max(sb, axis=1, keepdims=True)
            )
            ec = jnp.exp2(sc - top)
            eb = jnp.exp2(sb - top)
            total = jnp.sum(ec, axis=1, keepdims=True) + jnp.sum(eb, axis=1, keepdims=True)
            inverse = 1.0 / total
            pc = (ec * inverse).astype(bf16)
            pb = (eb * inverse).astype(bf16)
            pc_ref[head, rows, :] = pc
            pb_ref[head, rows, :reach] = pb
            if reach < BL:
                pb_ref[head, rows, reach:] = jnp.zeros((QT, BL - reach), bf16)
            mixed = dot_nn(pc, cv_ref[:, cols]) + dot_nn(pb, v_ref[:reach, cols])
            mix_ref[rows, cols] = mixed.astype(bf16)


def attend_forward(hosts, block, hidden, context, attn_full, seg_col, seg_row, half_width):
    pairs = half_width // TILE

    def weight(position):
        return pl.BlockSpec((1, D, TILE), lambda p, s: (s[position], 0, p))

    def tile(rows):
        return pl.BlockSpec((rows, TILE), lambda p, s: (0, p))

    heads = half_width // HEAD_DIM
    per = TILE // HEAD_DIM
    return call(
        attend_kernel,
        (pairs,),
        [
            pl.BlockSpec((BL, D), lambda p, s: (block, 0)),
            pl.BlockSpec((CTX, D), lambda p, s: (block, 0)),
            weight(0),
            weight(1),
            weight(2),
            pl.BlockSpec((BL, 1), lambda p, s: (block, 0)),
            whole((1, CTX + BL)),
        ],
        [
            tile(BL),
            tile(BL),
            tile(BL),
            tile(CTX),
            tile(CTX),
            pl.BlockSpec((per, BL, CTX), lambda p, s: (p, 0, 0)),
            pl.BlockSpec((per, BL, BL), lambda p, s: (p, 0, 0)),
            tile(BL),
        ],
        [
            pltpu.HBM((BL, half_width), bf16),
            pltpu.HBM((BL, half_width), bf16),
            pltpu.HBM((BL, half_width), bf16),
            pltpu.HBM((CTX, half_width), bf16),
            pltpu.HBM((CTX, half_width), bf16),
            pltpu.HBM((heads, BL, CTX), bf16),
            pltpu.HBM((heads, BL, BL), bf16),
            sds((BL, half_width), bf16),
        ],
        prefetch=1,
        flops=8 * 10**9,
        nbytes=12 * 10**6,
    )(
        hosts,
        hbm(hidden),
        context,
        *hbm(attn_full, attn_full, attn_full),
        seg_col,
        seg_row,
    )


def attend_back_kernel(
    host_ref,
    own_ref,
    other_ref,
    cot_ref,
    mid_ref,
    gain_ref,
    tok_ref,
    first_gain_ref,
    wo_ref,
    wq_ref,
    wk_ref,
    wv_ref,
    q_ref,
    k_ref,
    v_ref,
    ck_ref,
    cv_ref,
    pc_ref,
    pb_ref,
    low_ref,
    gmid_ref,
    ggain_ref,
    dq_ref,
    dk_ref,
    dv_ref,
    dck_ref,
    dcv_ref,
    hown_ref,
    hsend_ref,
    cown_ref,
    csend_ref,
    sum_ref,
    dsc_ref,
    dsb_ref,
):
    step = pl.program_id(0)
    pairs = pl.num_programs(0) - 2

    @pl.when(step == 0)
    def _():
        grad = own_ref[...].astype(f32) + other_ref[...].astype(f32)
        middle = mid_ref[...]
        inverse = lax.rsqrt(jnp.mean(middle * middle, axis=1, keepdims=True) + epsilon_norm)
        scaled = middle * inverse
        ggain_ref[...] = jnp.sum(grad * scaled, axis=0, keepdims=True)
        weighted = grad * gain_ref[...]
        centre = jnp.mean(weighted * scaled, axis=1, keepdims=True)
        result = cot_ref[...].astype(f32) + inverse * (weighted - scaled * centre)
        gmid_ref[...] = result
        low_ref[...] = result.astype(bf16)

    @pl.when(step < pairs)
    def _():
        grad_mixed = dot_nn(low_ref[...], wo_ref[0]).astype(bf16)
        base = step * TILE
        for head in range(TILE // HEAD_DIM):
            cols = slice(head * HEAD_DIM, (head + 1) * HEAD_DIM)
            to = pl.ds(pl.multiple_of(base + head * HEAD_DIM, HEAD_DIM), HEAD_DIM)
            grad_head = grad_mixed[:, cols]
            for i in range(BL // QT):
                rows = slice(i * QT, (i + 1) * QT)
                reach = (i + 1) * QT
                grad_rows = grad_head[rows]
                gpc = dot_nt(grad_rows, cv_ref[:, cols])
                gpb = dot_nt(grad_rows, v_ref[:reach, cols])
                pc = pc_ref[head, rows, :].astype(f32)
                pb = pb_ref[head, rows, :reach].astype(f32)
                tc = pc * gpc
                tb = pb * gpb
                centre = jnp.sum(tc, axis=1, keepdims=True) + jnp.sum(tb, axis=1, keepdims=True)
                dsc_ref[head, rows, :] = (tc - pc * centre).astype(bf16)
                dsb_ref[head, rows, :reach] = (tb - pb * centre).astype(bf16)
                if reach < BL:
                    dsb_ref[head, rows, reach:] = jnp.zeros((QT, BL - reach), bf16)
            dsc = dsc_ref[head]
            dsb = dsb_ref[head]
            dq = (dot_nn(dsc, ck_ref[:, cols]) + dot_nn(dsb, k_ref[:, cols])) * score_scale
            dq_ref[:, to] = dq.astype(bf16)
            query = q_ref[:, cols]
            dk_ref[:, to] = (dot_tn(dsb, query) * score_scale).astype(bf16)
            dck_ref[:, to] = (dot_tn(dsc, query) * score_scale).astype(bf16)
            dv_ref[:, to] = dot_tn(pb_ref[head], grad_head).astype(bf16)
            dcv_ref[:, to] = dot_tn(pc_ref[head], grad_head).astype(bf16)

    def half():
        part = (
            dot_nt(dq_ref[...], wq_ref[0])
            + dot_nt(dk_ref[...], wk_ref[0])
            + dot_nt(dv_ref[...], wv_ref[0])
        )
        ctx_part = dot_nt(dck_ref[...], wk_ref[0]) + dot_nt(dcv_ref[...], wv_ref[0])
        row_sum = jnp.sum(
            part * (tok_ref[...].astype(f32) * first_gain_ref[...]), axis=1, keepdims=True
        )
        return part, ctx_part, row_sum

    @pl.when(step == pairs)
    def _():
        part, ctx_part, row_sum = half()
        hsend_ref[...] = part.astype(bf16)
        csend_ref[...] = ctx_part.astype(bf16)
        sum_ref[...] = row_sum

    @pl.when(step == pairs + 1)
    def _():
        part, ctx_part, row_sum = half()
        hown_ref[...] = part
        cown_ref[...] = ctx_part
        sum_ref[...] += row_sum


def attend_backward(
    hosts, block, own, other, cot_full, middle, gain, tok_full, first_gain, attn_full, kept, width
):
    pairs = width // TILE
    per = TILE // HEAD_DIM

    def pair(p):
        return jnp.minimum(p, pairs - 1)

    def side(p, s):
        return jnp.where(p <= pairs, 1 - s[8], s[8])

    def weight(position):
        return pl.BlockSpec((1, width, width), lambda p, s: (s[position], side(p, s), 0))

    def tile(rows):
        return pl.BlockSpec((rows, TILE), lambda p, s: (0, pair(p)))

    return call(
        attend_back_kernel,
        (pairs + 2,),
        [
            whole((BL, D)),
            whole((BL, D)),
            pl.BlockSpec((BL, D), lambda p, s: (block, 0)),
            whole((BL, D)),
            whole((1, D)),
            pl.BlockSpec((BL, width), lambda p, s: (block, side(p, s))),
            pl.BlockSpec((1, width), lambda p, s: (0, side(p, s))),
            pl.BlockSpec((1, D, TILE), lambda p, s: (s[3], 0, pair(p))),
            weight(0),
            weight(1),
            weight(2),
            tile(BL),
            tile(BL),
            tile(BL),
            tile(CTX),
            tile(CTX),
            pl.BlockSpec((per, BL, CTX), lambda p, s: (pair(p), 0, 0)),
            pl.BlockSpec((per, BL, BL), lambda p, s: (pair(p), 0, 0)),
        ],
        [
            whole((BL, D)),
            whole((BL, D)),
            whole((1, D)),
            whole((BL, width)),
            whole((BL, width)),
            whole((BL, width)),
            whole((CTX, width)),
            whole((CTX, width)),
            whole((BL, width)),
            whole((BL, width)),
            whole((CTX, width)),
            whole((CTX, width)),
            whole((BL, 1)),
        ],
        [
            pltpu.HBM((BL, D), bf16),
            pltpu.HBM((BL, D), f32),
            sds((1, D), f32),
            pltpu.HBM((BL, width), bf16),
            pltpu.HBM((BL, width), bf16),
            pltpu.HBM((BL, width), bf16),
            pltpu.HBM((CTX, width), bf16),
            pltpu.HBM((CTX, width), bf16),
            pltpu.HBM((BL, width), f32),
            sds((BL, width), bf16),
            sds((CTX, width), f32),
            sds((CTX, width), bf16),
            sds((BL, 1), f32),
        ],
        scratch=[pltpu.VMEM((per, BL, CTX), bf16), pltpu.VMEM((per, BL, BL), bf16)],
        prefetch=1,
        flops=12 * 10**9,
        nbytes=20 * 10**6,
    )(
        hosts,
        *hbm(own, other, cot_full, middle),
        gain,
        hbm(tok_full),
        first_gain,
        *hbm(attn_full, attn_full, attn_full, attn_full, *kept),
    )


def attn_grad_kernel(host_ref, *refs):
    (hid0, hid1, ctx0, ctx1, low0, low1), rest = refs[:6], refs[6:]
    (dq0, dk0, dv0, dck0, dcv0, mix0), rest = rest[:6], rest[6:]
    (dq1, dk1, dv1, dck1, dcv1, mix1), (out_ref,) = rest[:6], rest[6:]
    matrix = pl.program_id(0)

    @pl.when(matrix == 0)
    def _():
        out_ref[0] = (dot_tn(hid0[...], dq0[...]) + dot_tn(hid1[...], dq1[...])).astype(bf16)

    @pl.when(matrix == 1)
    def _():
        out_ref[0] = (
            dot_tn(hid0[...], dk0[...])
            + dot_tn(hid1[...], dk1[...])
            + dot_tn(ctx0[...], dck0[...])
            + dot_tn(ctx1[...], dck1[...])
        ).astype(bf16)

    @pl.when(matrix == 2)
    def _():
        out_ref[0] = (
            dot_tn(hid0[...], dv0[...])
            + dot_tn(hid1[...], dv1[...])
            + dot_tn(ctx0[...], dcv0[...])
            + dot_tn(ctx1[...], dcv1[...])
        ).astype(bf16)

    @pl.when(matrix == 3)
    def _():
        out_ref[0] = (dot_tn(low0[...], mix0[...]) + dot_tn(low1[...], mix1[...])).astype(bf16)


def attn_grads(hosts, hidden, context, lows, blocks, half_width):
    hid_specs = [
        pl.BlockSpec((BL, D), lambda m, s: (0, 0)),
        pl.BlockSpec((BL, D), lambda m, s: (1, 0)),
        pl.BlockSpec((CTX, D), lambda m, s: (0, 0)),
        pl.BlockSpec((CTX, D), lambda m, s: (1, 0)),
    ]
    block_specs = [
        whole((BL, half_width)),
        whole((BL, half_width)),
        whole((BL, half_width)),
        whole((CTX, half_width)),
        whole((CTX, half_width)),
        whole((BL, half_width)),
    ]
    return call(
        attn_grad_kernel,
        (4,),
        hid_specs + [whole((BL, D))] * 2 + block_specs * 2,
        [pl.BlockSpec((1, D, half_width), lambda m, s: (s[m], 0, 0))],
        [pltpu.HBM((OWNER_GROUPS, D, half_width), bf16)],
        prefetch=1,
        flops=46 * 10**8,
        nbytes=14 * 10**6,
    )(hosts, *hbm(hidden, hidden, context, context, *lows, *blocks[0], *blocks[1]))[0]


def mlp_kernel(
    host_ref,
    own_ref,
    other_ref,
    wo_ref,
    woo_ref,
    tok_ref,
    gain_ref,
    cot_ref,
    w1_ref,
    w2_ref,
    mid_ref,
    hid_ref,
    act_ref,
    pre_ref,
    low_ref,
    grad_ref,
):
    step = pl.program_id(0)

    @pl.when(step == 0)
    def _():
        middle = (
            tok_ref[...].astype(f32)
            + dot_nt(own_ref[...], wo_ref[0])
            + dot_nt(other_ref[...], woo_ref[...])
        )
        inverse = lax.rsqrt(jnp.mean(middle * middle, axis=1, keepdims=True) + epsilon_norm)
        mid_ref[...] = middle
        hid_ref[...] = (middle * inverse * gain_ref[...]).astype(bf16)
        grad_ref[...] = jnp.zeros_like(grad_ref)

    w1 = w1_ref[0]
    w2 = w2_ref[0]
    pre = dot_nn(hid_ref[...], w1)
    grad_act = dot_nn(cot_ref[...], w2)
    root = 0.7978845608028654
    square = pre * pre
    gate = 0.5 + 0.5 * jnp.tanh(pre * (root + (root * 0.044715) * square))
    act = pre * gate
    act_ref[...] = act.astype(bf16)
    slope = gate + act * (1.0 - gate) * (2.0 * root + (6.0 * root * 0.044715) * square)
    grad_pre = (slope * grad_act).astype(bf16)
    pre_ref[...] = grad_pre
    grad_ref[...] += dot_nt(grad_pre, w1)

    @pl.when(step == pl.num_programs(0) - 1)
    def _():
        low_ref[...] = grad_ref[...].astype(bf16)


def mlp_block(hosts, block, own, other, attn_full, wo_other, tok_full, gain, cot_full, mlp_full):
    half_width = own.shape[1]
    quarter = mlp_full.shape[2]
    hidden = 2 * quarter
    per = quarter // FT

    def weight(position):
        return pl.BlockSpec(
            (1, D, FT), lambda f, s: (s[4 + 2 * position + f // per], 0, lax.rem(f, per))
        )

    return call(
        mlp_kernel,
        (2 * per,),
        [
            whole((BL, half_width)),
            whole((BL, half_width)),
            pl.BlockSpec((1, D, half_width), lambda f, s: (s[3], 0, 0)),
            whole((D, half_width)),
            pl.BlockSpec((BL, D), lambda f, s: (block, 0)),
            whole((1, D)),
            pl.BlockSpec((BL, D), lambda f, s: (block, 0)),
            weight(0),
            weight(1),
        ],
        [
            whole((BL, D)),
            whole((BL, D)),
            pl.BlockSpec((BL, FT), lambda f, s: (0, f)),
            pl.BlockSpec((BL, FT), lambda f, s: (0, f)),
            whole((BL, D)),
        ],
        [
            pltpu.HBM((BL, D), f32),
            sds((BL, D), bf16),
            pltpu.HBM((BL, hidden), bf16),
            sds((BL, hidden), bf16),
            pltpu.HBM((BL, D), bf16),
        ],
        scratch=[pltpu.VMEM((BL, D), f32)],
        prefetch=1,
        flops=8 * 10**9,
        nbytes=24 * 10**6,
    )(
        hosts,
        own,
        other,
        hbm(attn_full),
        wo_other,
        tok_full,
        gain,
        cot_full,
        *hbm(mlp_full, mlp_full),
    )


def mlp_grad_kernel(host_ref, h0, h1, g0, g1, p0, p1, a0, a1, out_ref):
    matrix = pl.program_id(0)

    @pl.when(matrix == 0)
    def _():
        out_ref[0] = (dot_tn(h0[...], p0[...]) + dot_tn(h1[...], p1[...])).astype(bf16)

    @pl.when(matrix == 1)
    def _():
        out_ref[0] = (dot_tn(g0[...], a0[...]) + dot_tn(g1[...], a1[...])).astype(bf16)


def mlp_grads(hosts, hiddens, cot_full, pres, acts):
    hidden = acts[0].shape[1]
    quarter = hidden // 2
    per = quarter // FT
    last = 2 * per - 1
    used_first = pl.BlockSpec((BL, FT), lambda m, f, s: (0, jnp.where(m == 0, f, last)))
    used_second = pl.BlockSpec((BL, FT), lambda m, f, s: (0, jnp.where(m == 1, f, 0)))
    return call(
        mlp_grad_kernel,
        (2, 2 * per),
        [
            whole((BL, D)),
            whole((BL, D)),
            pl.BlockSpec((BL, D), lambda m, f, s: (0, 0)),
            pl.BlockSpec((BL, D), lambda m, f, s: (1, 0)),
            used_first,
            used_first,
            used_second,
            used_second,
        ],
        [
            pl.BlockSpec(
                (1, D, FT), lambda m, f, s: (s[4 + 2 * m + f // per], 0, lax.rem(f, per))
            )
        ],
        [pltpu.HBM((OWNER_GROUPS, D, quarter), bf16)],
        prefetch=1,
        flops=86 * 10**8,
        nbytes=20 * 10**6,
    )(
        hosts,
        hiddens[0],
        hiddens[1],
        cot_full,
        cot_full,
        *pres,
        *acts,
    )[0]


def mlp_out_kernel(host_ref, a0, a1, wa_ref, wb_ref, mid0, mid1, send_ref, own_ref):
    step = pl.program_id(0)
    quarter = wa_ref.shape[2]

    def rows(a_ref):
        return dot_nt(a_ref[:, :quarter], wa_ref[0]) + dot_nt(a_ref[:, quarter:], wb_ref[0])

    @pl.when(step == 0)
    def _():
        send_ref[:BL, :] = rows(a0).astype(bf16)
        send_ref[BL:, :] = rows(a1).astype(bf16)

    @pl.when(step == 1)
    def _():
        own_ref[:BL, :] = rows(a0) + mid0[...]
        own_ref[BL:, :] = rows(a1) + mid1[...]


def mlp_out(hosts, acts, mlp_full, middles, width):
    quarter = mlp_full.shape[2]

    def side(d, s):
        return jnp.where(d == 0, 1 - s[8], s[8])

    def weight(position):
        return pl.BlockSpec((1, width, quarter), lambda d, s: (s[position], side(d, s), 0))

    middle = pl.BlockSpec((BL, width), lambda d, s: (0, s[8]))
    return call(
        mlp_out_kernel,
        (2,),
        [whole((BL, 2 * quarter))] * 2 + [weight(6), weight(7), middle, middle],
        [whole((2 * BL, width))] * 2,
        [sds((2 * BL, width), bf16), pltpu.HBM((2 * BL, width), f32)],
        prefetch=1,
        flops=44 * 10**8,
        nbytes=12 * 10**6,
    )(hosts, *hbm(*acts, mlp_full, mlp_full, *middles))


def adam_step(gradient, moment_one, moment_two, weight, rate_table, decay_weight):
    step_count = f32(STEP)
    first_new = beta_first * moment_one + (1.0 - beta_first) * gradient
    second_new = beta_second * moment_two + (1.0 - beta_second) * gradient * gradient
    fixed_one = 1.0 - jnp.power(beta_first, step_count)
    fixed_two = 1.0 - jnp.power(beta_second, step_count)
    update = first_new / fixed_one / (jnp.sqrt(second_new / fixed_two) + epsilon_adam)
    return (first_new, second_new, weight - rate_table * (update + decay_weight * weight))


def body(
    tokens,
    cotangent,
    segments,
    owners,
    attn_master,
    attn_first,
    attn_second,
    mlp_master,
    mlp_first,
    mlp_second,
    ssm_params,
    ssm_first,
    ssm_second,
    norm_gains,
    gains_first,
    gains_second,
):
    rows = tokens.shape[1]
    width = tokens.shape[2]
    blocks = rows // BL
    dp_count = lax.axis_size("dp")
    dp_here = lax.axis_index("dp")
    side = lax.axis_index("tensor")
    group = dp_here // (dp_count // OWNER_GROUPS)
    quarter = mlp_master.shape[2] // 2

    def both_sides(own, other):
        return jnp.where(
            side == 0,
            jnp.concatenate([own, other], axis=-1),
            jnp.concatenate([other, own], axis=-1),
        )

    def side_of(values, which):
        return lax.dynamic_slice_in_dim(values, which * width, width, values.ndim - 1)

    smem = pl.BlockSpec(memory_space=pltpu.SMEM)
    vmem = pl.BlockSpec(memory_space=pltpu.VMEM)
    hosts, rates = pl.pallas_call(
        plan_kernel,
        in_specs=[smem, smem],
        out_specs=[smem, smem],
        out_shape=[sds((PLAN_SIZE,), i32), sds((4,), f32)],
    )(owners, jnp.stack([side, group]).astype(i32))
    attn_here = hosts[ATTN_HERE]
    mlp_here = hosts[MLP_HERE]
    near = hosts[NEAR] == 1
    ring = Ring()

    tok = tokens.reshape(rows, width)
    cot = cotangent.reshape(rows, width)
    tok_f = tok.astype(f32)
    square_here = jnp.sum(tok_f * tok_f, axis=1)
    square_other = swap_x(square_here)
    tok_other = swap_x(tok)
    gains_other = swap_x(norm_gains)
    inverse_one = lax.rsqrt((square_here + square_other) / D + epsilon_norm)
    scaled_own = tok_f * inverse_one[:, None]
    hidden_own = (scaled_own * norm_gains[0]).astype(bf16)
    gains_full = both_sides(norm_gains, gains_other)

    attn_low = attn_master.astype(bf16)
    mlp_low = mlp_master[0].astype(bf16)
    attn_moved = move(attn_low[1], hosts[WAY], ATTN_WAYS, False)
    attn_block = jnp.where(attn_here == 0, attn_moved, attn_low[0])
    attn_full = lax.all_gather(attn_block, "dp", axis=0, tiled=True)
    attn_full = attn_full.reshape(OWNER_GROUPS, D, width)
    mlp_moved = exchange_groups(gate(mlp_low[:, quarter:], square_other), near)

    seg = segments.reshape(rows)
    prior = lax.ppermute(seg[rows - CTX :] + 1, "dp", [(i, i + 1) for i in range(dp_count - 1)]) - 1
    seg_ext = jnp.concatenate([prior[CTX - 1 :], seg])
    seg_col = seg[:, None]

    param_lanes = ssm_params.transpose(0, 2, 1)
    decay_rate = jnp.exp(param_lanes[0]) * (BL ** (-0.5) / 32.0)
    drive_root = jnp.sqrt(-jnp.expm1(-2.0 * decay_rate))
    reading = param_lanes[2] * drive_root * param_lanes[1]

    def doubled(values):
        lanes = values.reshape(STATE, 4, 128)
        return jnp.concatenate([lanes] * blocks, axis=1)

    rate_lanes = doubled(decay_rate)
    reading_lanes = doubled(reading)
    state_shape = sds((STATE, 8, 128), f32)

    def plain(kernel, scalars, count, outs, cost, scratch=()):
        return pl.pallas_call(
            kernel,
            in_specs=[smem] * scalars + [vmem] * count,
            out_specs=[vmem] * len(outs),
            out_shape=outs,
            scratch_shapes=scratch,
            name=kernel.__name__,
            compiler_params=pltpu.CompilerParams(vmem_limit_bytes=16 * 1024 * 1024),
            cost_estimate=pl.CostEstimate(flops=cost // COST, bytes_accessed=10**6 // COST, transcendentals=0),
        )

    hidden_lanes = to_lanes(hidden_own.astype(f32), blocks, BL)
    tail_lanes = sds((CTX, 8, 128), f32)
    tail_part, state_ends, device_end = plain(
        scan_kernel, 1, 3, [tail_lanes, state_shape, state_shape], 4 * 10**9
    )(seg_ext, hidden_lanes, rate_lanes, reading_lanes)
    id_rows = jnp.where(
        (jnp.arange(16) == 0)[:, None], seg[rows - 1].astype(f32), seg[0].astype(f32)
    )
    message = jnp.concatenate(
        [device_end.reshape(STATE * 8, 128), jnp.broadcast_to(id_rows, (16, 128))], axis=0
    ).astype(bf16)
    hidden_full = join_sides(
        hosts,
        tok,
        tok_other,
        (inverse_one[:, None], norm_gains[0:1], gains_other[0:1]),
    )
    states_all = gather_round(message[None], 0)
    cot_other = swap_x(gate(cot, tok_other))
    for k in range(1, gather_rounds()):
        if k == gather_rounds() - 2:
            tok_other, states_all = together(tok_other, states_all)
        if k == gather_rounds() - 1:
            mlp_moved, states_all = together(mlp_moved, states_all)
        states_all = gather_round(states_all, k)
    states_all = gate(states_all, cot_other, hidden_full)
    mlp_block_low = jnp.where(mlp_here == 0, mlp_moved, mlp_low[:, :quarter])
    mlp_full = lax.all_gather(mlp_block_low, "dp", axis=0, tiled=True)
    mlp_full = mlp_full.reshape(OWNER_GROUPS, D, quarter)
    tok_full = join_sides(hosts, tok, tok_other)
    ids_all = states_all[:, STATE * 8 : STATE * 8 + 2, 0].astype(i32)
    places = jnp.arange(dp_count, dtype=i32)
    use_before = jnp.logical_and(places < dp_here, ids_all[:, 0] == seg_ext[0]).astype(i32)
    use_after = jnp.logical_and(places > dp_here, ids_all[:, 1] == seg[rows - 1]).astype(i32)
    tails, state_starts = plain(
        tail_kernel, 2, 5, [tail_lanes, state_shape], 10**9, [pltpu.VMEM((STATE, 8, 128), f32)]
    )(seg_ext, use_before, states_all, state_ends, rate_lanes, reading_lanes, tail_part)
    sens_states, sens_starts = plain(sens_kernel, 1, 3, [state_shape] * 2, 6 * 10**9)(
        seg_ext, hidden_lanes, state_starts, rate_lanes
    )
    tails = from_lanes(tails, blocks, CTX).astype(bf16)
    context_own = shift_tails(tails[blocks - 1], 1, False)
    context_other = shift_tails(tails[blocks - 1], 1, True)
    inner_own = tails[: blocks - 1]
    inner_other = swap_x(inner_own)
    context_full = jnp.concatenate(
        [
            both_sides(context_own, context_other)[None],
            both_sides(inner_own, inner_other),
        ],
        axis=0,
    ).reshape(-1, D)

    seg_rows = []
    for b in range(blocks):
        before = prior if b == 0 else seg[b * BL - CTX : b * BL]
        seg_rows.append(jnp.concatenate([before, seg[b * BL : (b + 1) * BL]])[None])
    kept = []
    mixed = []
    mixed_other = []
    for b in range(blocks):
        outs = attend_forward(
            hosts, b, hidden_full, context_full, attn_full, seg_col, seg_rows[b], width
        )
        kept.append(outs[:7])
        mixed.append(outs[7])
        mixed_other.append(swap_x(outs[7]))
    wo_own = lax.dynamic_index_in_dim(attn_full, hosts[3], 0, keepdims=False)
    wo_half = lax.dynamic_slice_in_dim(wo_own, ring.core * (D // 2), D // 2, 0)
    wo_half = gate(wo_half, inner_other)
    wo_first = swap_x(wo_half)
    wo_second = lax.ppermute(gate(wo_first, mixed[0]), "dp", ring.cores)
    joined = together(*mixed_other, sens_states, sens_starts)
    mixed_other, (sens_states, sens_starts) = list(joined[:blocks]), joined[blocks:]
    wo_other = jnp.where(
        ring.core == 0,
        jnp.concatenate([wo_first, wo_second], axis=0),
        jnp.concatenate([wo_second, wo_first], axis=0),
    )

    cot_full = join_sides(hosts, gate(cot, mixed[0]), cot_other)

    gain_two = gains_full[1:2]
    middles, hiddens, acts, pres, grads, grads_other = [], [], [], [], [], []
    for b in range(blocks):
        middle, hidden_two, act, grad_pre, grad_low = mlp_block(
            hosts,
            b,
            mixed[b],
            mixed_other[b],
            attn_full,
            wo_other,
            tok_full,
            gain_two,
            cot_full,
            mlp_full,
        )
        middles.append(middle)
        hiddens.append(hidden_two)
        acts.append(act)
        pres.append(grad_pre)
        grads.append(grad_low)
        grads_other.append(swap_x(grad_low))
    mlp_sum_in = mlp_grads(hosts, hiddens, cot_full, pres, acts)
    grads_other[0], mlp_sum_in = lax.optimization_barrier((grads_other[0], mlp_sum_in))
    mlp_sum = lax.psum_scatter(
        mlp_sum_in.reshape(OWNER_GROUPS * D, quarter), "dp", scatter_dimension=0, tiled=True
    )

    lows, grad_mids, gain_twos, grad_blocks = [], [], [], []
    parts, parts_sent, ctx_parts, ctx_sent, row_sums = [], [], [], [], []
    for b in range(blocks):
        if b == blocks - 1:
            acts[0] = gate(acts[0], *lows)
            out_send, out_own = mlp_out(hosts, acts, mlp_full, middles, width)
            out_received = swap_x(out_send)
            grads[b] = gate(grads[b], out_own)
        outs = attend_backward(
            hosts,
            b,
            gate(grads[b], *lows),
            grads_other[b],
            cot_full,
            middles[b],
            gain_two,
            tok_full,
            gains_full[0:1],
            attn_full,
            kept[b],
            width,
        )
        lows.append(outs[0])
        grad_mids.append(side_of(outs[1], side))
        gain_twos.append(side_of(outs[2], side))
        grad_blocks.append(list(outs[3:8]) + [mixed[b]])
        parts.append(outs[8])
        parts_sent.append(outs[9])
        ctx_parts.append(outs[10])
        ctx_sent.append(outs[11])
        row_sums.append(outs[12][:, 0])
    grad_tails = jnp.stack(
        [ctx_parts[b] + swap_x(ctx_sent[b]).astype(f32) for b in range(1, blocks)]
        + [
            shift_tails(ctx_parts[0].astype(bf16), -1, False).astype(f32)
            + shift_tails(ctx_sent[0], -1, True).astype(f32)
        ]
    )
    tail_grad_lanes = to_lanes(grad_tails.reshape(blocks * CTX, width), blocks, CTX)
    own_back, device_back = plain(back_total_kernel, 1, 3, [state_shape, state_shape], 10**9)(
        seg_ext, tail_grad_lanes, rate_lanes, reading_lanes
    )
    back_all = gather_round(device_back.reshape(STATE * 8, 128).astype(bf16)[None], 0)
    lows[0] = gate(lows[0], back_all)
    attn_sum_in = attn_grads(hosts, hidden_full, context_full, lows, grad_blocks, width)
    received = [swap_x(v) for v in parts_sent]
    for k in range(1, gather_rounds()):
        if k == 2:
            back_all, attn_sum_in = together(back_all, attn_sum_in)
        back_all = gather_round(back_all, k)
    part, up, down = ring.start(attn_sum_in.reshape(dp_count, -1, width))
    up, down, back_all = together(up, down, back_all)
    grad_c_lanes, grad_a_lanes, sens_end = plain(
        sens_tail_kernel, 1, 5, [state_shape] * 3, 2 * 10**9
    )(seg_ext, hidden_lanes, tail_grad_lanes, sens_states, sens_starts, rate_lanes)
    grad_lanes, grad_a_lanes = plain(
        back_scan_kernel,
        2,
        7,
        [sds((BL, 8, 128), f32), state_shape],
        4 * 10**9,
        [pltpu.VMEM((STATE, 8, 128), f32)],
    )(
        seg_ext,
        use_after,
        back_all,
        tail_grad_lanes,
        own_back,
        sens_end,
        grad_a_lanes,
        rate_lanes,
        reading_lanes,
    )
    for k in range(ring.far_up):
        if k == 1:
            up, down = together(up, down, grad_lanes)[:2]
        up, down = ring.step(k, part, up, down)
    attn_sum = (part(0) + up.astype(f32) + down.astype(f32)).astype(bf16)
    grad_channels = lax.optimization_barrier(
        from_lanes(grad_lanes, blocks, BL).reshape(rows, width)
    )

    part_own = jnp.concatenate(parts, axis=0)
    received = jnp.concatenate(received, axis=0)
    row_here = inverse_one * jnp.concatenate(row_sums) + jnp.sum(
        grad_channels * (scaled_own * norm_gains[0]), axis=1
    )
    row_other = swap_x(row_here)
    row_total = row_here + row_other
    block_out = (out_own + out_received.astype(f32)).astype(bf16)
    grad_hidden = part_own + received.astype(f32) + grad_channels
    grad_tokens = jnp.concatenate(grad_mids, axis=0) + inverse_one[:, None] * (
        grad_hidden * norm_gains[0] - scaled_own * (row_total / D)[:, None]
    )
    gain_one = jnp.sum(grad_hidden * scaled_own, axis=0)
    gain_two_sum = sum(gain_twos)[0]

    def merged(values):
        return sum(values[:, 4 * b : 4 * b + 4] for b in range(blocks)).reshape(STATE, width)

    small = jnp.concatenate(
        [merged(grad_c_lanes), merged(grad_a_lanes), gain_one[None], gain_two_sum[None]], axis=0
    )
    small, mlp_sum = together(small, mlp_sum)
    mlp_back = exchange_groups(mlp_sum, near)
    small, mlp_back = total_dp(small, mlp_back)
    grad_c, grad_a = small[:STATE], small[STATE : 2 * STATE]
    gains_grad = small[2 * STATE :]
    decay_step = jnp.exp(-decay_rate)
    grad_read = grad_c * drive_root * param_lanes[1]
    grad_drive = grad_c * drive_root * param_lanes[2]
    grad_a = grad_a - grad_c * param_lanes[1] * param_lanes[2] * decay_step / drive_root
    grad_log = -decay_rate * decay_step * grad_a
    ssm_grad = jnp.stack([grad_log, grad_drive, grad_read]).transpose(0, 2, 1)

    attn_back = move(gate(attn_sum, small), hosts[WAY], ATTN_WAYS, True)
    attn_grad = jnp.stack(
        [
            jnp.where(attn_here >= 1, attn_sum.astype(f32), 0.0),
            jnp.where(attn_here == 2, attn_back.astype(f32), 0.0),
        ]
    )
    mlp_grad = jnp.where(
        mlp_here == 1, jnp.concatenate([mlp_sum, mlp_back], axis=1).astype(f32), 0.0
    )[None]

    attn_rates = rates[:2, None, None]
    mlp_rates = rates[2]
    ssm_rates = jnp.asarray([1.0, 0.8, 0.25], f32)[:, None, None]
    gain_rates = jnp.asarray([0.6, 0.6], f32)[:, None]
    attn_one, attn_two, attn_new = adam_step(
        attn_grad, attn_first, attn_second, attn_master, attn_rates, matrix_decay
    )
    mlp_one, mlp_two, mlp_new = adam_step(
        mlp_grad, mlp_first, mlp_second, mlp_master, mlp_rates, matrix_decay
    )
    ssm_one, ssm_two, ssm_new = adam_step(
        ssm_grad, ssm_first, ssm_second, ssm_params, ssm_rates, 0.0
    )
    gain_first_new, gain_second_new, gains_new = adam_step(
        gains_grad, gains_first, gains_second, norm_gains, gain_rates, 0.0
    )
    return (
        block_out.reshape(tokens.shape),
        grad_tokens.reshape(tokens.shape),
        attn_grad,
        attn_one,
        attn_two,
        attn_new,
        attn_new.astype(bf16),
        mlp_grad,
        mlp_one,
        mlp_two,
        mlp_new,
        mlp_new.astype(bf16),
        ssm_grad,
        ssm_one,
        ssm_two,
        ssm_new,
        gains_grad,
        gain_first_new,
        gain_second_new,
        gains_new,
    )


def solution(mesh):
    in_specs = (
        P(None, "dp", "tensor"),
        P(None, "dp", "tensor"),
        P(None, "dp"),
        P(),
        P(None, "dp", "tensor"),
        P(None, "dp", "tensor"),
        P(None, "dp", "tensor"),
        P(None, "dp", "tensor"),
        P(None, "dp", "tensor"),
        P(None, "dp", "tensor"),
        P(None, "tensor", None),
        P(None, "tensor", None),
        P(None, "tensor", None),
        P(None, "tensor"),
        P(None, "tensor"),
        P(None, "tensor"),
    )
    out_specs = (
        P(None, "dp", "tensor"),
        P(None, "dp", "tensor"),
        P(None, "dp", "tensor"),
        P(None, "dp", "tensor"),
        P(None, "dp", "tensor"),
        P(None, "dp", "tensor"),
        P(None, "dp", "tensor"),
        P(None, "dp", "tensor"),
        P(None, "dp", "tensor"),
        P(None, "dp", "tensor"),
        P(None, "dp", "tensor"),
        P(None, "dp", "tensor"),
        P(None, "tensor", None),
        P(None, "tensor", None),
        P(None, "tensor", None),
        P(None, "tensor", None),
        P(None, "tensor"),
        P(None, "tensor"),
        P(None, "tensor"),
        P(None, "tensor"),
    )
    return jax.shard_map(body, mesh=mesh, in_specs=in_specs, out_specs=out_specs, check_vma=False)
```

```python
import functools
import itertools

import jax
import jax.numpy as jnp
from jax import lax
from jax.experimental import pallas as pl
from jax.experimental.pallas import tpu as pltpu
from jax.sharding import PartitionSpec as P

D = 1024
HEAD_DIM = 128
FF = 4096
STATE = 16
CTX = 128
BL = 512
OWNER_GROUPS = 4
STEP = 5

epsilon_norm = 1e-05
beta_first = 0.9
beta_second = 0.95
epsilon_adam = 1e-08
matrix_decay = 0.1
masked_score = -1e30
score_scale = HEAD_DIM ** (-0.5)
f32 = jnp.float32
bf16 = jnp.bfloat16
i32 = jnp.int32
SWAP = [(0, 1), (1, 0)]
COST = 1000
TILE = 256
QT = 256
FT = 512
LOG2E = 1.4426950408889634


def dot_nn(left, right):
    return lax.dot_general(left, right, (((1,), (0,)), ((), ())), preferred_element_type=f32)


def dot_nt(left, right):
    return lax.dot_general(left, right, (((1,), (1,)), ((), ())), preferred_element_type=f32)


def dot_tn(left, right):
    return lax.dot_general(left, right, (((0,), (0,)), ((), ())), preferred_element_type=f32)


def call(
    kernel, grid, in_specs, out_specs, out_shape, scratch=(), prefetch=0, flops=0, nbytes=0, room=36
):
    return pl.pallas_call(
        kernel,
        grid_spec=pltpu.PrefetchScalarGridSpec(
            num_scalar_prefetch=prefetch,
            grid=grid,
            in_specs=in_specs,
            out_specs=out_specs,
            scratch_shapes=scratch,
        ),
        out_shape=out_shape,
        name=kernel.__name__,
        compiler_params=pltpu.CompilerParams(vmem_limit_bytes=room * 1024 * 1024),
        cost_estimate=pl.CostEstimate(flops=flops // COST, bytes_accessed=nbytes // COST, transcendentals=0),
    )


def whole(shape):
    return pl.BlockSpec(shape, lambda *_: (0,) * len(shape), pipeline_mode=pl.Buffered(1))


def sds(shape, dtype):
    return jax.ShapeDtypeStruct(shape, dtype)


def hbm(*values):
    held = tuple(pltpu.with_memory_space_constraint(v, pltpu.HBM) for v in values)
    return held[0] if len(held) == 1 else held


def swap_x(values):
    return lax.ppermute(values, "tensor", SWAP)


def gate(value, *others):
    if not others:
        return value
    return lax.optimization_barrier((value,) + others)[0]


def together(*values):
    return lax.optimization_barrier(values)


def gather_rounds():
    return max(lax.axis_size("dp") - 1, 0).bit_length()


def gather_round(held, k):
    step = 1 << k
    count = lax.axis_size("dp")
    other = lax.ppermute(held, "dp", [(i, i ^ step) for i in range(count)])
    later = (lax.axis_index("dp") // step) % 2 == 1
    return jnp.where(
        later,
        jnp.concatenate([other, held], axis=0),
        jnp.concatenate([held, other], axis=0),
    )


def total_dp(values, beside):
    count = lax.axis_size("dp")
    for k in range(gather_rounds()):
        if k == 1:
            values, beside = together(values, beside)
        values = values + lax.ppermute(values, "dp", [(i, i ^ (1 << k)) for i in range(count)])
    return values, beside


def routes(full_count, empty_count):
    groups = range(OWNER_GROUPS)
    ways = []
    for full in itertools.combinations(groups, full_count):
        rest = [g for g in groups if g not in full]
        for empty in itertools.combinations(rest, empty_count):
            ways.append((full, empty))
    return ways


ATTN_WAYS = routes(1, 1) + routes(2, 2)


def way_code(full, empty):
    code = 0
    for g in range(OWNER_GROUPS):
        digit = 2 if g in full else (0 if g in empty else 1)
        code += digit * 3**g
    return code


def one_if(condition):
    return jnp.where(condition, jnp.int32(1), jnp.int32(0))


HOST_MLP, SIDE, WAY, NEAR, ATTN_HERE, MLP_HERE, PLAN_SIZE = 4, 8, 9, 10, 11, 12, 16
ATTN_RATES = [0.5 * D ** (-0.5)] * 3 + [0.5 * (D // 16) ** (-0.5)]
MLP_RATES = [0.5 * D ** (-0.5), 0.5 * FF ** (-0.5)]
IDLE_RATE = 0.5 * D ** (-0.5)


def plan_kernel(owner_ref, here_ref, out_ref, rate_ref):
    groups = range(OWNER_GROUPS)
    side, group = here_ref[0], here_ref[1]
    owner = [owner_ref[m] for m in range(6)]
    slot = [
        sum([one_if(owner[k] == owner[m]) for k in range(m)], jnp.int32(0)) for m in range(4)
    ]
    count = [sum([one_if(owner[m] == g) for m in range(4)], jnp.int32(0)) for g in groups]
    full_rank = [sum([one_if(count[h] == 2) for h in range(g)], jnp.int32(0)) for g in groups]
    empty_rank = [sum([one_if(count[h] == 0) for h in range(g)], jnp.int32(0)) for g in groups]
    taker = [
        sum(
            [
                jnp.where(
                    jnp.logical_and(count[h] == 0, empty_rank[h] == full_rank[g]), jnp.int32(h), 0
                )
                for h in groups
            ],
            jnp.int32(0),
        )
        for g in groups
    ]
    for m in range(4):
        second = sum([jnp.where(owner[m] == g, taker[g], 0) for g in groups], jnp.int32(0))
        out_ref[m] = jnp.where(slot[m] == 0, owner[m], second)
    code = sum([count[g] * 3**g for g in groups], jnp.int32(0))
    out_ref[WAY] = sum(
        [
            jnp.where(code == way_code(*way), jnp.int32(k), 0)
            for k, way in enumerate(ATTN_WAYS)
        ],
        jnp.int32(0),
    )
    low = sum([one_if(owner[m] < 2) for m in (4, 5)], jnp.int32(0))
    near = low == 1
    for k, m in enumerate((4, 5)):
        out_ref[HOST_MLP + 2 * k] = owner[m]
        bit = jnp.where(near, jnp.int32(1), jnp.int32(2))
        out_ref[HOST_MLP + 2 * k + 1] = jnp.bitwise_xor(owner[m], bit)
    out_ref[SIDE] = side
    out_ref[NEAR] = one_if(near)
    out_ref[ATTN_HERE] = sum([one_if(owner[m] == group) for m in range(4)], jnp.int32(0))
    out_ref[MLP_HERE] = sum([one_if(owner[m] == group) for m in (4, 5)], jnp.int32(0))
    for k in range(MLP_HERE + 1, PLAN_SIZE):
        out_ref[k] = jnp.int32(0)
    for place in range(2):
        rate = f32(IDLE_RATE)
        for m in range(4):
            hit = jnp.logical_and(owner[m] == group, slot[m] == place)
            rate = jnp.where(hit, f32(ATTN_RATES[m]), rate)
        rate_ref[place] = rate
    rate = f32(IDLE_RATE)
    for k, m in enumerate((4, 5)):
        rate = jnp.where(owner[m] == group, f32(MLP_RATES[k]), rate)
    rate_ref[2] = rate
    rate_ref[3] = f32(0.0)


def move(values, index, ways, back):
    size = lax.axis_size("dp") // OWNER_GROUPS

    def branch(way):
        pairs = []
        for a, b in zip(*way):
            if back:
                a, b = b, a
            pairs += [(a * size + j, b * size + j) for j in range(size)]
        return lambda v: lax.ppermute(v, "dp", pairs)

    return lax.switch(index, [branch(way) for way in ways], values)


def exchange_groups(values, near):
    size = lax.axis_size("dp") // OWNER_GROUPS

    def across(bit):
        return lax.ppermute(
            values,
            "dp",
            [(g * size + j, (g ^ bit) * size + j) for g in range(OWNER_GROUPS) for j in range(size)],
        )

    return jnp.where(near, across(1), across(2))


def ring_order(count):
    chips = count // 2
    if chips == 8:
        return [0, 2, 4, 6, 7, 5, 3, 1]
    return list(range(chips))


def join_kernel(host_ref, own_ref, other_ref, out_ref):
    @pl.when(pl.program_id(0) == 0)
    def _():
        out_ref[...] = own_ref[...]

    @pl.when(pl.program_id(0) == 1)
    def _():
        out_ref[...] = other_ref[...]


def join_scaled_kernel(
    host_ref, own_ref, other_ref, inverse_ref, gain_ref, gain_other_ref, out_ref
):
    @pl.when(pl.program_id(0) == 0)
    def _():
        out_ref[...] = (own_ref[...].astype(f32) * inverse_ref[...] * gain_ref[...]).astype(bf16)

    @pl.when(pl.program_id(0) == 1)
    def _():
        out_ref[...] = (
            other_ref[...].astype(f32) * inverse_ref[...] * gain_other_ref[...]
        ).astype(bf16)


def join_sides(hosts, own, other, scales=()):
    rows, width = own.shape
    return call(
        join_scaled_kernel if scales else join_kernel,
        (2,),
        [whole(v.shape) for v in (own, other) + tuple(scales)],
        [
            pl.BlockSpec(
                (rows, width), lambda d, s: (0, jnp.where(d == 0, s[SIDE], 1 - s[SIDE]))
            )
        ],
        [pltpu.HBM((rows, 2 * width), bf16)],
        prefetch=1,
        nbytes=8 * rows * width,
        room=12,
    )(hosts, own, other, *scales)[0]


class Ring:
    def __init__(self):
        self.count = lax.axis_size("dp")
        self.chips = self.count // 2
        order = ring_order(self.count)
        here = lax.axis_index("dp")
        self.core = here % 2
        chip = here // 2
        self.place = jnp.where(chip % 2 == 0, chip // 2, 7 - chip // 2) if self.chips == 8 else chip
        self.up = [
            (2 * order[p] + c, 2 * order[(p + 1) % self.chips] + c)
            for p in range(self.chips)
            for c in range(2)
        ]
        self.down = [(b, a) for a, b in self.up]
        self.cores = [(i, i ^ 1) for i in range(self.count)]
        self.far_up = self.chips // 2
        self.far_down = self.chips - 1 - self.far_up

    def chip(self, offset):
        place = (self.place + self.chips + offset) % self.chips
        if self.chips != 8:
            return place
        return jnp.where(place < 4, 2 * place, 15 - 2 * place)

    def start(self, blocks):
        pairs = blocks.reshape((self.chips, 2) + blocks.shape[1:])
        mine = lax.dynamic_index_in_dim(pairs, self.core, 1, keepdims=False)
        theirs = lax.dynamic_index_in_dim(pairs, 1 - self.core, 1, keepdims=False)
        received = lax.ppermute(theirs, "dp", self.cores)

        def part(offset):
            chip = self.chip(offset)
            return lax.dynamic_index_in_dim(mine, chip, 0, keepdims=False).astype(
                f32
            ) + lax.dynamic_index_in_dim(received, chip, 0, keepdims=False).astype(f32)

        return part, part(self.far_up).astype(bf16), part(-self.far_down).astype(bf16)

    def step(self, k, part, up, down):
        if k < self.far_up:
            up = lax.ppermute(up, "dp", self.up)
            if k < self.far_up - 1:
                up = (up.astype(f32) + part(self.far_up - 1 - k)).astype(bf16)
        if k < self.far_down:
            down = lax.ppermute(down, "dp", self.down)
            if k < self.far_down - 1:
                down = (down.astype(f32) + part(k + 1 - self.far_down)).astype(bf16)
        return up, down


def shift_tails(values, by, cross):
    count = lax.axis_size("dp")
    pairs = [
        (2 * i + s, 2 * (i + by) + (1 - s if cross else s))
        for i in range(count)
        for s in range(2)
        if 0 <= i + by < count
    ]
    return lax.ppermute(values, ("dp", "tensor"), pairs)


def first_half():
    return lax.broadcasted_iota(i32, (8, 128), 0) < 4


def flag(condition):
    return jnp.where(condition, f32(1.0), f32(0.0))


def keep_at(seg_ref, t, half):
    return jnp.where(
        half, flag(seg_ref[t + 1] == seg_ref[t]), flag(seg_ref[BL + t + 1] == seg_ref[BL + t])
    )


def chunked(seg_ref, begin, end, plain, kept, carried, back=False):
    size = 8
    count = (end - begin) // size

    def chunk(c, carried):
        first = begin + (count - 1 - c if back else c) * size
        same = jnp.logical_and(
            seg_ref[first] == seg_ref[first + size],
            seg_ref[BL + first] == seg_ref[BL + first + size],
        )

        def run(step):
            def go(carried):
                for k in range(size):
                    carried = step(first + (size - 1 - k if back else k), carried)
                return carried

            return go

        return lax.cond(same, run(plain), run(kept), carried)

    return lax.fori_loop(0, count, chunk, carried)


def scan_kernel(seg_ref, h_ref, rate_ref, c_ref, y_ref, s_ref, e_ref):
    half = first_half()
    decay = [jnp.exp(-rate_ref[n]) for n in range(STATE)]

    def plain(t, states):
        row = h_ref[t]
        return [states[n] * decay[n] + row for n in range(STATE)]

    def kept(t, states):
        keep = keep_at(seg_ref, t, half)
        row = h_ref[t]
        return [(states[n] * keep) * decay[n] + row for n in range(STATE)]

    def reading(step):
        def go(t, states):
            states = step(t, states)
            total = c_ref[0] * states[0]
            for n in range(1, STATE):
                total = total + c_ref[n] * states[n]
            y_ref[t - (BL - CTX)] = total
            return states

        return go

    states = [jnp.zeros((8, 128), f32)] * STATE
    states = chunked(seg_ref, 0, BL - CTX, plain, kept, states)
    states = chunked(seg_ref, BL - CTX, BL, reading(plain), reading(kept), states)
    joined = flag(seg_ref[2 * BL] == seg_ref[BL])
    for n in range(STATE):
        s_ref[n] = states[n]
        ends = states[n] + (joined * jnp.exp(-rate_ref[n] * BL)) * pltpu.roll(states[n], 4, 0)
        e_ref[n] = ends


def tail_kernel(
    seg_ref, use_ref, all_ref, s_ref, rate_ref, c_ref, y_ref, out_ref, start_ref, carry_ref
):
    half = first_half()
    before = seg_ref[0]
    joined = flag(seg_ref[BL] == before)
    decay = [jnp.exp(-rate_ref[n]) for n in range(STATE)]
    carry_ref[...] = jnp.zeros_like(carry_ref)

    def gather(j, _):
        @pl.when(use_ref[j] > 0)
        def _():
            for m in range(STATE // 2):
                pair = all_ref[j, 16 * m : 16 * m + 16, :].astype(f32)
                for k in range(2):
                    n = 2 * m + k
                    power = jnp.exp(-rate_ref[n] * (2 * BL))
                    carry_ref[n] = carry_ref[n] * power + pair[8 * k : 8 * k + 8]

        return 0

    lax.fori_loop(0, all_ref.shape[0], gather, 0)
    weighted = []
    for n in range(STATE):
        carried = pltpu.roll(carry_ref[n], 4, 0)
        mid = pltpu.roll(s_ref[n], 4, 0) + (joined * jnp.exp(-rate_ref[n] * BL)) * carry_ref[n]
        start = jnp.where(half, carried, mid)
        start_ref[n] = start
        weighted.append(c_ref[n] * start * jnp.exp(-rate_ref[n] * (BL - CTX + 1)))

    def step(t, parts):
        mask = jnp.where(
            half,
            flag(seg_ref[t + 1 + BL - CTX] == before),
            flag(seg_ref[BL + t + 1 + BL - CTX] == seg_ref[BL]),
        )
        total = parts[0]
        for n in range(1, STATE):
            total = total + parts[n]
        out_ref[t] = y_ref[t] + mask * total
        return [parts[n] * decay[n] for n in range(STATE)]

    lax.fori_loop(0, CTX, step, weighted, unroll=4)


def back_total_kernel(seg_ref, g_ref, rate_ref, c_ref, own_ref, out_ref):
    half = first_half()
    decay = [jnp.exp(-rate_ref[n]) for n in range(STATE)]

    def step(k, sums):
        t = CTX - 1 - k
        mask = jnp.where(
            half,
            flag(seg_ref[t + 1 + BL - CTX] == seg_ref[1]),
            flag(seg_ref[BL + t + 1 + BL - CTX] == seg_ref[BL]),
        )
        grad = mask * g_ref[t]
        return [decay[n] * (sums[n] + grad) for n in range(STATE)]

    sums = lax.fori_loop(0, CTX, step, [jnp.zeros((8, 128), f32)] * STATE, unroll=4)
    joined = flag(seg_ref[1] == seg_ref[BL])
    for n in range(STATE):
        total = sums[n] * c_ref[n] * jnp.exp(-rate_ref[n] * (BL - CTX))
        own_ref[n] = total
        out_ref[n] = total + (joined * jnp.exp(-rate_ref[n] * BL)) * pltpu.roll(total, 4, 0)


def sens_steps(seg_ref, h_ref, half, decay, count):
    def plain(t, both):
        row = h_ref[t]
        sens = [both[1][n] * decay[n] + both[0][n] for n in range(count)]
        states = [both[0][n] * decay[n] + row for n in range(count)]
        return [states, sens] + list(both[2:])

    def kept(t, both):
        keep = keep_at(seg_ref, t, half)
        row = h_ref[t]
        held = [v * keep for v in both[0]]
        sens = [(both[1][n] * keep) * decay[n] + held[n] for n in range(count)]
        states = [held[n] * decay[n] + row for n in range(count)]
        return [states, sens] + list(both[2:])

    return plain, kept


SENS_GROUP = 8


def sens_kernel(seg_ref, h_ref, start_ref, rate_ref, s_ref, z_ref):
    half = first_half()
    for first in range(0, STATE, SENS_GROUP):
        ids = range(first, first + SENS_GROUP)
        decay = [jnp.exp(-rate_ref[n]) for n in ids]
        plain, kept = sens_steps(seg_ref, h_ref, half, decay, SENS_GROUP)
        both = [[start_ref[n] for n in ids], [jnp.zeros((8, 128), f32)] * SENS_GROUP]
        both = chunked(seg_ref, 0, BL - CTX, plain, kept, both)
        for k, n in enumerate(ids):
            s_ref[n] = both[0][k]
            z_ref[n] = both[1][k]


def sens_tail_kernel(seg_ref, h_ref, g_ref, s_ref, z_ref, rate_ref, gc_ref, ga_ref, zend_ref):
    half = first_half()
    for first in range(0, STATE, SENS_GROUP):
        ids = range(first, first + SENS_GROUP)
        decay = [jnp.exp(-rate_ref[n]) for n in ids]

        def summing(step):
            def go(t, carried):
                states, sens, by_c, by_a = step(t, carried)
                grad = g_ref[t - (BL - CTX)]
                by_c = [by_c[n] + grad * states[n] for n in range(SENS_GROUP)]
                by_a = [by_a[n] + grad * sens[n] for n in range(SENS_GROUP)]
                return [states, sens, by_c, by_a]

            return go

        plain, kept = sens_steps(seg_ref, h_ref, half, decay, SENS_GROUP)
        zeros = [jnp.zeros((8, 128), f32)] * SENS_GROUP
        carried = [[s_ref[n] for n in ids], [z_ref[n] for n in ids], zeros, zeros]
        carried = chunked(seg_ref, BL - CTX, BL, summing(plain), summing(kept), carried)
        for k, n in enumerate(ids):
            zend_ref[n] = carried[1][k]
            gc_ref[n] = carried[2][k]
            ga_ref[n] = carried[3][k]


def back_scan_kernel(
    seg_ref,
    use_ref,
    all_ref,
    g_ref,
    own_ref,
    z_ref,
    ga_ref,
    rate_ref,
    c_ref,
    gh_ref,
    out_ref,
    later_ref,
):
    half = first_half()
    decay = [jnp.exp(-rate_ref[n]) for n in range(STATE)]
    joined = flag(seg_ref[2 * BL] == seg_ref[BL])
    later_ref[...] = jnp.zeros_like(later_ref)
    count = all_ref.shape[0]

    def gather(k, _):
        j = count - 1 - k

        @pl.when(use_ref[j] > 0)
        def _():
            for m in range(STATE // 2):
                pair = all_ref[j, 16 * m : 16 * m + 16, :].astype(f32)
                for k in range(2):
                    n = 2 * m + k
                    power = jnp.exp(-rate_ref[n] * (2 * BL))
                    later_ref[n] = later_ref[n] * power + pair[8 * k : 8 * k + 8]

        return 0

    lax.fori_loop(0, count, gather, 0)
    sums = []
    for n in range(STATE):
        first = (
            pltpu.roll(own_ref[n], 4, 0) + (joined * jnp.exp(-rate_ref[n] * BL)) * later_ref[n]
        )
        entering = jnp.where(half, first, pltpu.roll(later_ref[n], 4, 0))
        sums.append(entering)
        out_ref[n] = ga_ref[n] * c_ref[n] + entering * z_ref[n]

    def total_of(t, sums):
        total = sums[0]
        for n in range(1, STATE):
            total = total + sums[n]
        gh_ref[t] = total

    def plain(t, sums):
        total_of(t, sums)
        return [v * decay[n] for n, v in enumerate(sums)]

    def kept(t, sums):
        total_of(t, sums)
        keep = keep_at(seg_ref, t, half)
        return [(v * keep) * decay[n] for n, v in enumerate(sums)]

    def entered(step):
        def go(t, sums):
            grad = g_ref[t - (BL - CTX)]
            return step(t, [sums[n] + c_ref[n] * grad for n in range(STATE)])

        return go

    sums = chunked(seg_ref, BL - CTX, BL, entered(plain), entered(kept), sums, back=True)
    chunked(seg_ref, 0, BL - CTX, plain, kept, sums, back=True)


def to_lanes(values, blocks, steps):
    return (
        values.reshape(blocks, steps, 4, 128).transpose(1, 0, 2, 3).reshape(steps, blocks * 4, 128)
    )


def from_lanes(values, blocks, steps):
    return values.reshape(steps, blocks, 4, 128).transpose(1, 0, 2, 3).reshape(blocks, steps, 512)


def attend_kernel(
    host_ref,
    hid_ref,
    ctx_ref,
    wq_ref,
    wk_ref,
    wv_ref,
    segq_ref,
    segk_ref,
    q_ref,
    k_ref,
    v_ref,
    ck_ref,
    cv_ref,
    pc_ref,
    pb_ref,
    mix_ref,
):
    hid = hid_ref[...]
    ctx = ctx_ref[...]
    q_ref[...] = dot_nn(hid, wq_ref[0]).astype(bf16)
    k_ref[...] = dot_nn(hid, wk_ref[0]).astype(bf16)
    v_ref[...] = dot_nn(hid, wv_ref[0]).astype(bf16)
    ck_ref[...] = dot_nn(ctx, wk_ref[0]).astype(bf16)
    cv_ref[...] = dot_nn(ctx, wv_ref[0]).astype(bf16)
    ctx_ids = segk_ref[:, :CTX]
    for i in range(BL // QT):
        rows = slice(i * QT, (i + 1) * QT)
        reach = (i + 1) * QT
        ids = segq_ref[rows]
        ctx_ok = ctx_ids == ids
        place_q = lax.broadcasted_iota(i32, (QT, reach), 0) + i * QT
        place_k = lax.broadcasted_iota(i32, (QT, reach), 1)
        block_ok = jnp.logical_and(place_k <= place_q, segk_ref[:, CTX : CTX + reach] == ids)
        for head in range(TILE // HEAD_DIM):
            cols = slice(head * HEAD_DIM, (head + 1) * HEAD_DIM)
            query = q_ref[rows, cols]
            sc = dot_nt(query, ck_ref[:, cols]) * (score_scale * LOG2E)
            sb = dot_nt(query, k_ref[:reach, cols]) * (score_scale * LOG2E)
            sc = jnp.where(ctx_ok, sc, masked_score)
            sb = jnp.where(block_ok, sb, masked_score)
            top = jnp.maximum(
                jnp.max(sc, axis=1, keepdims=True), jnp.max(sb, axis=1, keepdims=True)
            )
            ec = jnp.exp2(sc - top)
            eb = jnp.exp2(sb - top)
            total = jnp.sum(ec, axis=1, keepdims=True) + jnp.sum(eb, axis=1, keepdims=True)
            inverse = 1.0 / total
            pc = (ec * inverse).astype(bf16)
            pb = (eb * inverse).astype(bf16)
            pc_ref[head, rows, :] = pc
            pb_ref[head, rows, :reach] = pb
            if reach < BL:
                pb_ref[head, rows, reach:] = jnp.zeros((QT, BL - reach), bf16)
            mixed = dot_nn(pc, cv_ref[:, cols]) + dot_nn(pb, v_ref[:reach, cols])
            mix_ref[rows, cols] = mixed.astype(bf16)


def attend_forward(hosts, block, hidden, context, attn_full, seg_col, seg_row, half_width):
    pairs = half_width // TILE

    def weight(position):
        return pl.BlockSpec((1, D, TILE), lambda p, s: (s[position], 0, p))

    def tile(rows):
        return pl.BlockSpec((rows, TILE), lambda p, s: (0, p))

    heads = half_width // HEAD_DIM
    per = TILE // HEAD_DIM
    return call(
        attend_kernel,
        (pairs,),
        [
            pl.BlockSpec((BL, D), lambda p, s: (block, 0)),
            pl.BlockSpec((CTX, D), lambda p, s: (block, 0)),
            weight(0),
            weight(1),
            weight(2),
            pl.BlockSpec((BL, 1), lambda p, s: (block, 0)),
            whole((1, CTX + BL)),
        ],
        [
            tile(BL),
            tile(BL),
            tile(BL),
            tile(CTX),
            tile(CTX),
            pl.BlockSpec((per, BL, CTX), lambda p, s: (p, 0, 0)),
            pl.BlockSpec((per, BL, BL), lambda p, s: (p, 0, 0)),
            tile(BL),
        ],
        [
            pltpu.HBM((BL, half_width), bf16),
            pltpu.HBM((BL, half_width), bf16),
            pltpu.HBM((BL, half_width), bf16),
            pltpu.HBM((CTX, half_width), bf16),
            pltpu.HBM((CTX, half_width), bf16),
            pltpu.HBM((heads, BL, CTX), bf16),
            pltpu.HBM((heads, BL, BL), bf16),
            sds((BL, half_width), bf16),
        ],
        prefetch=1,
        flops=8 * 10**9,
        nbytes=12 * 10**6,
    )(
        hosts,
        hbm(hidden),
        context,
        *hbm(attn_full, attn_full, attn_full),
        seg_col,
        seg_row,
    )


def attend_back_kernel(
    host_ref,
    own_ref,
    other_ref,
    cot_ref,
    mid_ref,
    gain_ref,
    tok_ref,
    first_gain_ref,
    wo_ref,
    wq_ref,
    wk_ref,
    wv_ref,
    q_ref,
    k_ref,
    v_ref,
    ck_ref,
    cv_ref,
    pc_ref,
    pb_ref,
    low_ref,
    gmid_ref,
    ggain_ref,
    dq_ref,
    dk_ref,
    dv_ref,
    dck_ref,
    dcv_ref,
    hown_ref,
    hsend_ref,
    cown_ref,
    csend_ref,
    sum_ref,
    dsc_ref,
    dsb_ref,
):
    step = pl.program_id(0)
    pairs = pl.num_programs(0) - 2

    @pl.when(step == 0)
    def _():
        grad = own_ref[...].astype(f32) + other_ref[...].astype(f32)
        middle = mid_ref[...]
        inverse = lax.rsqrt(jnp.mean(middle * middle, axis=1, keepdims=True) + epsilon_norm)
        scaled = middle * inverse
        ggain_ref[...] = jnp.sum(grad * scaled, axis=0, keepdims=True)
        weighted = grad * gain_ref[...]
        centre = jnp.mean(weighted * scaled, axis=1, keepdims=True)
        result = cot_ref[...].astype(f32) + inverse * (weighted - scaled * centre)
        gmid_ref[...] = result
        low_ref[...] = result.astype(bf16)

    @pl.when(step < pairs)
    def _():
        grad_mixed = dot_nn(low_ref[...], wo_ref[0]).astype(bf16)
        base = step * TILE
        for head in range(TILE // HEAD_DIM):
            cols = slice(head * HEAD_DIM, (head + 1) * HEAD_DIM)
            to = pl.ds(pl.multiple_of(base + head * HEAD_DIM, HEAD_DIM), HEAD_DIM)
            grad_head = grad_mixed[:, cols]
            for i in range(BL // QT):
                rows = slice(i * QT, (i + 1) * QT)
                reach = (i + 1) * QT
                grad_rows = grad_head[rows]
                gpc = dot_nt(grad_rows, cv_ref[:, cols])
                gpb = dot_nt(grad_rows, v_ref[:reach, cols])
                pc = pc_ref[head, rows, :].astype(f32)
                pb = pb_ref[head, rows, :reach].astype(f32)
                tc = pc * gpc
                tb = pb * gpb
                centre = jnp.sum(tc, axis=1, keepdims=True) + jnp.sum(tb, axis=1, keepdims=True)
                dsc_ref[head, rows, :] = (tc - pc * centre).astype(bf16)
                dsb_ref[head, rows, :reach] = (tb - pb * centre).astype(bf16)
                if reach < BL:
                    dsb_ref[head, rows, reach:] = jnp.zeros((QT, BL - reach), bf16)
            dsc = dsc_ref[head]
            dsb = dsb_ref[head]
            dq = (dot_nn(dsc, ck_ref[:, cols]) + dot_nn(dsb, k_ref[:, cols])) * score_scale
            dq_ref[:, to] = dq.astype(bf16)
            query = q_ref[:, cols]
            dk_ref[:, to] = (dot_tn(dsb, query) * score_scale).astype(bf16)
            dck_ref[:, to] = (dot_tn(dsc, query) * score_scale).astype(bf16)
            dv_ref[:, to] = dot_tn(pb_ref[head], grad_head).astype(bf16)
            dcv_ref[:, to] = dot_tn(pc_ref[head], grad_head).astype(bf16)

    def half():
        part = (
            dot_nt(dq_ref[...], wq_ref[0])
            + dot_nt(dk_ref[...], wk_ref[0])
            + dot_nt(dv_ref[...], wv_ref[0])
        )
        ctx_part = dot_nt(dck_ref[...], wk_ref[0]) + dot_nt(dcv_ref[...], wv_ref[0])
        row_sum = jnp.sum(
            part * (tok_ref[...].astype(f32) * first_gain_ref[...]), axis=1, keepdims=True
        )
        return part, ctx_part, row_sum

    @pl.when(step == pairs)
    def _():
        part, ctx_part, row_sum = half()
        hsend_ref[...] = part.astype(bf16)
        csend_ref[...] = ctx_part.astype(bf16)
        sum_ref[...] = row_sum

    @pl.when(step == pairs + 1)
    def _():
        part, ctx_part, row_sum = half()
        hown_ref[...] = part
        cown_ref[...] = ctx_part
        sum_ref[...] += row_sum


def attend_backward(
    hosts, block, own, other, cot_full, middle, gain, tok_full, first_gain, attn_full, kept, width
):
    pairs = width // TILE
    per = TILE // HEAD_DIM

    def pair(p):
        return jnp.minimum(p, pairs - 1)

    def side(p, s):
        return jnp.where(p <= pairs, 1 - s[8], s[8])

    def weight(position):
        return pl.BlockSpec((1, width, width), lambda p, s: (s[position], side(p, s), 0))

    def tile(rows):
        return pl.BlockSpec((rows, TILE), lambda p, s: (0, pair(p)))

    return call(
        attend_back_kernel,
        (pairs + 2,),
        [
            whole((BL, D)),
            whole((BL, D)),
            pl.BlockSpec((BL, D), lambda p, s: (block, 0)),
            whole((BL, D)),
            whole((1, D)),
            pl.BlockSpec((BL, width), lambda p, s: (block, side(p, s))),
            pl.BlockSpec((1, width), lambda p, s: (0, side(p, s))),
            pl.BlockSpec((1, D, TILE), lambda p, s: (s[3], 0, pair(p))),
            weight(0),
            weight(1),
            weight(2),
            tile(BL),
            tile(BL),
            tile(BL),
            tile(CTX),
            tile(CTX),
            pl.BlockSpec((per, BL, CTX), lambda p, s: (pair(p), 0, 0)),
            pl.BlockSpec((per, BL, BL), lambda p, s: (pair(p), 0, 0)),
        ],
        [
            whole((BL, D)),
            whole((BL, D)),
            whole((1, D)),
            whole((BL, width)),
            whole((BL, width)),
            whole((BL, width)),
            whole((CTX, width)),
            whole((CTX, width)),
            whole((BL, width)),
            whole((BL, width)),
            whole((CTX, width)),
            whole((CTX, width)),
            whole((BL, 1)),
        ],
        [
            pltpu.HBM((BL, D), bf16),
            pltpu.HBM((BL, D), f32),
            sds((1, D), f32),
            pltpu.HBM((BL, width), bf16),
            pltpu.HBM((BL, width), bf16),
            pltpu.HBM((BL, width), bf16),
            pltpu.HBM((CTX, width), bf16),
            pltpu.HBM((CTX, width), bf16),
            pltpu.HBM((BL, width), f32),
            sds((BL, width), bf16),
            sds((CTX, width), f32),
            sds((CTX, width), bf16),
            sds((BL, 1), f32),
        ],
        scratch=[pltpu.VMEM((per, BL, CTX), bf16), pltpu.VMEM((per, BL, BL), bf16)],
        prefetch=1,
        flops=12 * 10**9,
        nbytes=20 * 10**6,
    )(
        hosts,
        *hbm(own, other, cot_full, middle),
        gain,
        hbm(tok_full),
        first_gain,
        *hbm(attn_full, attn_full, attn_full, attn_full, *kept),
    )


def attn_grad_kernel(host_ref, *refs):
    (hid0, hid1, ctx0, ctx1, low0, low1), rest = refs[:6], refs[6:]
    (dq0, dk0, dv0, dck0, dcv0, mix0), rest = rest[:6], rest[6:]
    (dq1, dk1, dv1, dck1, dcv1, mix1), (out_ref,) = rest[:6], rest[6:]
    matrix = pl.program_id(0)

    @pl.when(matrix == 0)
    def _():
        out_ref[0] = (dot_tn(hid0[...], dq0[...]) + dot_tn(hid1[...], dq1[...])).astype(bf16)

    @pl.when(matrix == 1)
    def _():
        out_ref[0] = (
            dot_tn(hid0[...], dk0[...])
            + dot_tn(hid1[...], dk1[...])
            + dot_tn(ctx0[...], dck0[...])
            + dot_tn(ctx1[...], dck1[...])
        ).astype(bf16)

    @pl.when(matrix == 2)
    def _():
        out_ref[0] = (
            dot_tn(hid0[...], dv0[...])
            + dot_tn(hid1[...], dv1[...])
            + dot_tn(ctx0[...], dcv0[...])
            + dot_tn(ctx1[...], dcv1[...])
        ).astype(bf16)

    @pl.when(matrix == 3)
    def _():
        out_ref[0] = (dot_tn(low0[...], mix0[...]) + dot_tn(low1[...], mix1[...])).astype(bf16)


def attn_grads(hosts, hidden, context, lows, blocks, half_width):
    hid_specs = [
        pl.BlockSpec((BL, D), lambda m, s: (0, 0)),
        pl.BlockSpec((BL, D), lambda m, s: (1, 0)),
        pl.BlockSpec((CTX, D), lambda m, s: (0, 0)),
        pl.BlockSpec((CTX, D), lambda m, s: (1, 0)),
    ]
    block_specs = [
        whole((BL, half_width)),
        whole((BL, half_width)),
        whole((BL, half_width)),
        whole((CTX, half_width)),
        whole((CTX, half_width)),
        whole((BL, half_width)),
    ]
    return call(
        attn_grad_kernel,
        (4,),
        hid_specs + [whole((BL, D))] * 2 + block_specs * 2,
        [pl.BlockSpec((1, D, half_width), lambda m, s: (s[m], 0, 0))],
        [pltpu.HBM((OWNER_GROUPS, D, half_width), bf16)],
        prefetch=1,
        flops=46 * 10**8,
        nbytes=14 * 10**6,
    )(hosts, *hbm(hidden, hidden, context, context, *lows, *blocks[0], *blocks[1]))[0]


def mlp_kernel(
    host_ref,
    own_ref,
    other_ref,
    wo_ref,
    woo_ref,
    tok_ref,
    gain_ref,
    cot_ref,
    w1_ref,
    w2_ref,
    mid_ref,
    hid_ref,
    act_ref,
    pre_ref,
    low_ref,
    grad_ref,
):
    step = pl.program_id(0)

    @pl.when(step == 0)
    def _():
        middle = (
            tok_ref[...].astype(f32)
            + dot_nt(own_ref[...], wo_ref[0])
            + dot_nt(other_ref[...], woo_ref[...])
        )
        inverse = lax.rsqrt(jnp.mean(middle * middle, axis=1, keepdims=True) + epsilon_norm)
        mid_ref[...] = middle
        hid_ref[...] = (middle * inverse * gain_ref[...]).astype(bf16)
        grad_ref[...] = jnp.zeros_like(grad_ref)

    w1 = w1_ref[0]
    w2 = w2_ref[0]
    pre = dot_nn(hid_ref[...], w1)
    grad_act = dot_nn(cot_ref[...], w2)
    root = 0.7978845608028654
    square = pre * pre
    gate = 0.5 + 0.5 * jnp.tanh(pre * (root + (root * 0.044715) * square))
    act = pre * gate
    act_ref[...] = act.astype(bf16)
    slope = gate + act * (1.0 - gate) * (2.0 * root + (6.0 * root * 0.044715) * square)
    grad_pre = (slope * grad_act).astype(bf16)
    pre_ref[...] = grad_pre
    grad_ref[...] += dot_nt(grad_pre, w1)

    @pl.when(step == pl.num_programs(0) - 1)
    def _():
        low_ref[...] = grad_ref[...].astype(bf16)


def mlp_block(hosts, block, own, other, attn_full, wo_other, tok_full, gain, cot_full, mlp_full):
    half_width = own.shape[1]
    quarter = mlp_full.shape[2]
    hidden = 2 * quarter
    per = quarter // FT

    def weight(position):
        return pl.BlockSpec(
            (1, D, FT), lambda f, s: (s[4 + 2 * position + f // per], 0, lax.rem(f, per))
        )

    return call(
        mlp_kernel,
        (2 * per,),
        [
            whole((BL, half_width)),
            whole((BL, half_width)),
            pl.BlockSpec((1, D, half_width), lambda f, s: (s[3], 0, 0)),
            whole((D, half_width)),
            pl.BlockSpec((BL, D), lambda f, s: (block, 0)),
            whole((1, D)),
            pl.BlockSpec((BL, D), lambda f, s: (block, 0)),
            weight(0),
            weight(1),
        ],
        [
            whole((BL, D)),
            whole((BL, D)),
            pl.BlockSpec((BL, FT), lambda f, s: (0, f)),
            pl.BlockSpec((BL, FT), lambda f, s: (0, f)),
            whole((BL, D)),
        ],
        [
            pltpu.HBM((BL, D), f32),
            sds((BL, D), bf16),
            pltpu.HBM((BL, hidden), bf16),
            sds((BL, hidden), bf16),
            pltpu.HBM((BL, D), bf16),
        ],
        scratch=[pltpu.VMEM((BL, D), f32)],
        prefetch=1,
        flops=8 * 10**9,
        nbytes=24 * 10**6,
    )(
        hosts,
        own,
        other,
        hbm(attn_full),
        wo_other,
        tok_full,
        gain,
        cot_full,
        *hbm(mlp_full, mlp_full),
    )


def mlp_grad_kernel(host_ref, h0, h1, g0, g1, p0, p1, a0, a1, out_ref):
    matrix = pl.program_id(0)

    @pl.when(matrix == 0)
    def _():
        out_ref[0] = (dot_tn(h0[...], p0[...]) + dot_tn(h1[...], p1[...])).astype(bf16)

    @pl.when(matrix == 1)
    def _():
        out_ref[0] = (dot_tn(g0[...], a0[...]) + dot_tn(g1[...], a1[...])).astype(bf16)


def mlp_grads(hosts, hiddens, cot_full, pres, acts):
    hidden = acts[0].shape[1]
    quarter = hidden // 2
    per = quarter // FT
    last = 2 * per - 1
    used_first = pl.BlockSpec((BL, FT), lambda m, f, s: (0, jnp.where(m == 0, f, last)))
    used_second = pl.BlockSpec((BL, FT), lambda m, f, s: (0, jnp.where(m == 1, f, 0)))
    return call(
        mlp_grad_kernel,
        (2, 2 * per),
        [
            whole((BL, D)),
            whole((BL, D)),
            pl.BlockSpec((BL, D), lambda m, f, s: (0, 0)),
            pl.BlockSpec((BL, D), lambda m, f, s: (1, 0)),
            used_first,
            used_first,
            used_second,
            used_second,
        ],
        [
            pl.BlockSpec(
                (1, D, FT), lambda m, f, s: (s[4 + 2 * m + f // per], 0, lax.rem(f, per))
            )
        ],
        [pltpu.HBM((OWNER_GROUPS, D, quarter), bf16)],
        prefetch=1,
        flops=86 * 10**8,
        nbytes=20 * 10**6,
    )(
        hosts,
        hiddens[0],
        hiddens[1],
        cot_full,
        cot_full,
        *pres,
        *acts,
    )[0]


def mlp_out_kernel(host_ref, a0, a1, wa_ref, wb_ref, mid0, mid1, send_ref, own_ref):
    step = pl.program_id(0)
    quarter = wa_ref.shape[2]

    def rows(a_ref):
        return dot_nt(a_ref[:, :quarter], wa_ref[0]) + dot_nt(a_ref[:, quarter:], wb_ref[0])

    @pl.when(step == 0)
    def _():
        send_ref[:BL, :] = rows(a0).astype(bf16)
        send_ref[BL:, :] = rows(a1).astype(bf16)

    @pl.when(step == 1)
    def _():
        own_ref[:BL, :] = rows(a0) + mid0[...]
        own_ref[BL:, :] = rows(a1) + mid1[...]


def mlp_out(hosts, acts, mlp_full, middles, width):
    quarter = mlp_full.shape[2]

    def side(d, s):
        return jnp.where(d == 0, 1 - s[8], s[8])

    def weight(position):
        return pl.BlockSpec((1, width, quarter), lambda d, s: (s[position], side(d, s), 0))

    middle = pl.BlockSpec((BL, width), lambda d, s: (0, s[8]))
    return call(
        mlp_out_kernel,
        (2,),
        [whole((BL, 2 * quarter))] * 2 + [weight(6), weight(7), middle, middle],
        [whole((2 * BL, width))] * 2,
        [sds((2 * BL, width), bf16), pltpu.HBM((2 * BL, width), f32)],
        prefetch=1,
        flops=44 * 10**8,
        nbytes=12 * 10**6,
    )(hosts, *hbm(*acts, mlp_full, mlp_full, *middles))


def adam_step(gradient, moment_one, moment_two, weight, rate_table, decay_weight):
    step_count = f32(STEP)
    first_new = beta_first * moment_one + (1.0 - beta_first) * gradient
    second_new = beta_second * moment_two + (1.0 - beta_second) * gradient * gradient
    fixed_one = 1.0 - jnp.power(beta_first, step_count)
    fixed_two = 1.0 - jnp.power(beta_second, step_count)
    update = first_new / fixed_one / (jnp.sqrt(second_new / fixed_two) + epsilon_adam)
    return (first_new, second_new, weight - rate_table * (update + decay_weight * weight))


def body(
    tokens,
    cotangent,
    segments,
    owners,
    attn_master,
    attn_first,
    attn_second,
    mlp_master,
    mlp_first,
    mlp_second,
    ssm_params,
    ssm_first,
    ssm_second,
    norm_gains,
    gains_first,
    gains_second,
):
    rows = tokens.shape[1]
    width = tokens.shape[2]
    blocks = rows // BL
    dp_count = lax.axis_size("dp")
    dp_here = lax.axis_index("dp")
    side = lax.axis_index("tensor")
    group = dp_here // (dp_count // OWNER_GROUPS)
    quarter = mlp_master.shape[2] // 2

    def both_sides(own, other):
        return jnp.where(
            side == 0,
            jnp.concatenate([own, other], axis=-1),
            jnp.concatenate([other, own], axis=-1),
        )

    def side_of(values, which):
        return lax.dynamic_slice_in_dim(values, which * width, width, values.ndim - 1)

    smem = pl.BlockSpec(memory_space=pltpu.SMEM)
    vmem = pl.BlockSpec(memory_space=pltpu.VMEM)
    hosts, rates = pl.pallas_call(
        plan_kernel,
        in_specs=[smem, smem],
        out_specs=[smem, smem],
        out_shape=[sds((PLAN_SIZE,), i32), sds((4,), f32)],
    )(owners, jnp.stack([side, group]).astype(i32))
    attn_here = hosts[ATTN_HERE]
    mlp_here = hosts[MLP_HERE]
    near = hosts[NEAR] == 1
    ring = Ring()

    tok = tokens.reshape(rows, width)
    cot = cotangent.reshape(rows, width)
    tok_f = tok.astype(f32)
    square_here = jnp.sum(tok_f * tok_f, axis=1)
    square_other = swap_x(square_here)
    tok_other = swap_x(tok)
    gains_other = swap_x(norm_gains)
    inverse_one = lax.rsqrt((square_here + square_other) / D + epsilon_norm)
    scaled_own = tok_f * inverse_one[:, None]
    hidden_own = (scaled_own * norm_gains[0]).astype(bf16)
    gains_full = both_sides(norm_gains, gains_other)

    attn_low = attn_master.astype(bf16)
    mlp_low = mlp_master[0].astype(bf16)
    attn_moved = move(attn_low[1], hosts[WAY], ATTN_WAYS, False)
    attn_block = jnp.where(attn_here == 0, attn_moved, attn_low[0])
    attn_full = lax.all_gather(attn_block, "dp", axis=0, tiled=True)
    attn_full = attn_full.reshape(OWNER_GROUPS, D, width)
    mlp_moved = exchange_groups(gate(mlp_low[:, quarter:], square_other), near)

    seg = segments.reshape(rows)
    prior = lax.ppermute(seg[rows - CTX :] + 1, "dp", [(i, i + 1) for i in range(dp_count - 1)]) - 1
    seg_ext = jnp.concatenate([prior[CTX - 1 :], seg])
    seg_col = seg[:, None]

    param_lanes = ssm_params.transpose(0, 2, 1)
    decay_rate = jnp.exp(param_lanes[0]) * (BL ** (-0.5) / 32.0)
    drive_root = jnp.sqrt(-jnp.expm1(-2.0 * decay_rate))
    reading = param_lanes[2] * drive_root * param_lanes[1]

    def doubled(values):
        lanes = values.reshape(STATE, 4, 128)
        return jnp.concatenate([lanes] * blocks, axis=1)

    rate_lanes = doubled(decay_rate)
    reading_lanes = doubled(reading)
    state_shape = sds((STATE, 8, 128), f32)

    def plain(kernel, scalars, count, outs, cost, scratch=()):
        return pl.pallas_call(
            kernel,
            in_specs=[smem] * scalars + [vmem] * count,
            out_specs=[vmem] * len(outs),
            out_shape=outs,
            scratch_shapes=scratch,
            name=kernel.__name__,
            compiler_params=pltpu.CompilerParams(vmem_limit_bytes=16 * 1024 * 1024),
            cost_estimate=pl.CostEstimate(flops=cost // COST, bytes_accessed=10**6 // COST, transcendentals=0),
        )

    hidden_lanes = to_lanes(hidden_own.astype(f32), blocks, BL)
    tail_lanes = sds((CTX, 8, 128), f32)
    tail_part, state_ends, device_end = plain(
        scan_kernel, 1, 3, [tail_lanes, state_shape, state_shape], 4 * 10**9
    )(seg_ext, hidden_lanes, rate_lanes, reading_lanes)
    id_rows = jnp.where(
        (jnp.arange(16) == 0)[:, None], seg[rows - 1].astype(f32), seg[0].astype(f32)
    )
    message = jnp.concatenate(
        [device_end.reshape(STATE * 8, 128), jnp.broadcast_to(id_rows, (16, 128))], axis=0
    ).astype(bf16)
    hidden_full = join_sides(
        hosts,
        tok,
        tok_other,
        (inverse_one[:, None], norm_gains[0:1], gains_other[0:1]),
    )
    states_all = gather_round(message[None], 0)
    cot_other = swap_x(gate(cot, tok_other))
    for k in range(1, gather_rounds()):
        if k == gather_rounds() - 2:
            tok_other, states_all = together(tok_other, states_all)
        if k == gather_rounds() - 1:
            mlp_moved, states_all = together(mlp_moved, states_all)
        states_all = gather_round(states_all, k)
    states_all = gate(states_all, cot_other, hidden_full)
    mlp_block_low = jnp.where(mlp_here == 0, mlp_moved, mlp_low[:, :quarter])
    mlp_full = lax.all_gather(mlp_block_low, "dp", axis=0, tiled=True)
    mlp_full = mlp_full.reshape(OWNER_GROUPS, D, quarter)
    tok_full = join_sides(hosts, tok, tok_other)
    ids_all = states_all[:, STATE * 8 : STATE * 8 + 2, 0].astype(i32)
    places = jnp.arange(dp_count, dtype=i32)
    use_before = jnp.logical_and(places < dp_here, ids_all[:, 0] == seg_ext[0]).astype(i32)
    use_after = jnp.logical_and(places > dp_here, ids_all[:, 1] == seg[rows - 1]).astype(i32)
    tails, state_starts = plain(
        tail_kernel, 2, 5, [tail_lanes, state_shape], 10**9, [pltpu.VMEM((STATE, 8, 128), f32)]
    )(seg_ext, use_before, states_all, state_ends, rate_lanes, reading_lanes, tail_part)
    sens_states, sens_starts = plain(sens_kernel, 1, 3, [state_shape] * 2, 6 * 10**9)(
        seg_ext, hidden_lanes, state_starts, rate_lanes
    )
    tails = from_lanes(tails, blocks, CTX).astype(bf16)
    context_own = shift_tails(tails[blocks - 1], 1, False)
    context_other = shift_tails(tails[blocks - 1], 1, True)
    inner_own = tails[: blocks - 1]
    inner_other = swap_x(inner_own)
    context_full = jnp.concatenate(
        [
            both_sides(context_own, context_other)[None],
            both_sides(inner_own, inner_other),
        ],
        axis=0,
    ).reshape(-1, D)

    seg_rows = []
    for b in range(blocks):
        before = prior if b == 0 else seg[b * BL - CTX : b * BL]
        seg_rows.append(jnp.concatenate([before, seg[b * BL : (b + 1) * BL]])[None])
    kept = []
    mixed = []
    mixed_other = []
    for b in range(blocks):
        outs = attend_forward(
            hosts, b, hidden_full, context_full, attn_full, seg_col, seg_rows[b], width
        )
        kept.append(outs[:7])
        mixed.append(outs[7])
        mixed_other.append(swap_x(outs[7]))
    wo_own = lax.dynamic_index_in_dim(attn_full, hosts[3], 0, keepdims=False)
    wo_half = lax.dynamic_slice_in_dim(wo_own, ring.core * (D // 2), D // 2, 0)
    wo_half = gate(wo_half, inner_other)
    wo_first = swap_x(wo_half)
    wo_second = lax.ppermute(gate(wo_first, mixed[0]), "dp", ring.cores)
    joined = together(*mixed_other, sens_states, sens_starts)
    mixed_other, (sens_states, sens_starts) = list(joined[:blocks]), joined[blocks:]
    wo_other = jnp.where(
        ring.core == 0,
        jnp.concatenate([wo_first, wo_second], axis=0),
        jnp.concatenate([wo_second, wo_first], axis=0),
    )

    cot_full = join_sides(hosts, gate(cot, mixed[0]), cot_other)

    gain_two = gains_full[1:2]
    middles, hiddens, acts, pres, grads, grads_other = [], [], [], [], [], []
    for b in range(blocks):
        middle, hidden_two, act, grad_pre, grad_low = mlp_block(
            hosts,
            b,
            mixed[b],
            mixed_other[b],
            attn_full,
            wo_other,
            tok_full,
            gain_two,
            cot_full,
            mlp_full,
        )
        middles.append(middle)
        hiddens.append(hidden_two)
        acts.append(act)
        pres.append(grad_pre)
        grads.append(grad_low)
        grads_other.append(swap_x(grad_low))
    mlp_sum_in = mlp_grads(hosts, hiddens, cot_full, pres, acts)
    grads_other[0], mlp_sum_in = lax.optimization_barrier((grads_other[0], mlp_sum_in))
    mlp_sum = lax.psum_scatter(
        mlp_sum_in.reshape(OWNER_GROUPS * D, quarter), "dp", scatter_dimension=0, tiled=True
    )

    lows, grad_mids, gain_twos, grad_blocks = [], [], [], []
    parts, parts_sent, ctx_parts, ctx_sent, row_sums = [], [], [], [], []
    for b in range(blocks):
        if b == blocks - 1:
            acts[0] = gate(acts[0], *lows)
            out_send, out_own = mlp_out(hosts, acts, mlp_full, middles, width)
            out_received = swap_x(out_send)
            grads[b] = gate(grads[b], out_own)
        outs = attend_backward(
            hosts,
            b,
            gate(grads[b], *lows),
            grads_other[b],
            cot_full,
            middles[b],
            gain_two,
            tok_full,
            gains_full[0:1],
            attn_full,
            kept[b],
            width,
        )
        lows.append(outs[0])
        grad_mids.append(side_of(outs[1], side))
        gain_twos.append(side_of(outs[2], side))
        grad_blocks.append(list(outs[3:8]) + [mixed[b]])
        parts.append(outs[8])
        parts_sent.append(outs[9])
        ctx_parts.append(outs[10])
        ctx_sent.append(outs[11])
        row_sums.append(outs[12][:, 0])
    grad_tails = jnp.stack(
        [ctx_parts[b] + swap_x(ctx_sent[b]).astype(f32) for b in range(1, blocks)]
        + [
            shift_tails(ctx_parts[0].astype(bf16), -1, False).astype(f32)
            + shift_tails(ctx_sent[0], -1, True).astype(f32)
        ]
    )
    tail_grad_lanes = gate(
        to_lanes(grad_tails.reshape(blocks * CTX, width), blocks, CTX), out_received
    )
    own_back, device_back = plain(back_total_kernel, 1, 3, [state_shape, state_shape], 10**9)(
        seg_ext, tail_grad_lanes, rate_lanes, reading_lanes
    )
    back_all = gather_round(device_back.reshape(STATE * 8, 128).astype(bf16)[None], 0)
    lows[0] = gate(lows[0], back_all)
    attn_sum_in = attn_grads(hosts, hidden_full, context_full, lows, grad_blocks, width)
    received = [swap_x(v) for v in parts_sent]
    for k in range(1, gather_rounds() - 1):
        if k == 2:
            back_all, attn_sum_in = together(back_all, attn_sum_in)
        back_all = gather_round(back_all, k)
    part, up, down = ring.start(attn_sum_in.reshape(dp_count, -1, width))
    up, down, back_all = together(up, down, back_all)
    back_all = gather_round(back_all, gather_rounds() - 1)
    up, down = ring.step(0, part, up, down)
    up, down, back_all, mlp_sum = together(up, down, back_all, mlp_sum)
    mlp_back = exchange_groups(mlp_sum, near)
    grad_c_lanes, grad_a_lanes, sens_end = plain(
        sens_tail_kernel, 1, 5, [state_shape] * 3, 2 * 10**9
    )(seg_ext, hidden_lanes, tail_grad_lanes, sens_states, sens_starts, rate_lanes)
    grad_lanes, grad_a_lanes = plain(
        back_scan_kernel,
        2,
        7,
        [sds((BL, 8, 128), f32), state_shape],
        4 * 10**9,
        [pltpu.VMEM((STATE, 8, 128), f32)],
    )(
        seg_ext,
        use_after,
        back_all,
        tail_grad_lanes,
        own_back,
        sens_end,
        grad_a_lanes,
        rate_lanes,
        reading_lanes,
    )
    for k in range(1, ring.far_up):
        up, down = ring.step(k, part, up, down)
    attn_sum = (part(0) + up.astype(f32) + down.astype(f32)).astype(bf16)
    grad_channels = lax.optimization_barrier(
        from_lanes(grad_lanes, blocks, BL).reshape(rows, width)
    )

    part_own = jnp.concatenate(parts, axis=0)
    received = jnp.concatenate(received, axis=0)
    row_here = inverse_one * jnp.concatenate(row_sums) + jnp.sum(
        grad_channels * (scaled_own * norm_gains[0]), axis=1
    )
    row_other = swap_x(row_here)
    row_total = row_here + row_other
    block_out = (out_own + gate(out_received, row_other).astype(f32)).astype(bf16)
    grad_hidden = part_own + received.astype(f32) + grad_channels
    grad_tokens = jnp.concatenate(grad_mids, axis=0) + inverse_one[:, None] * (
        grad_hidden * norm_gains[0] - scaled_own * (row_total / D)[:, None]
    )
    gain_one = jnp.sum(grad_hidden * scaled_own, axis=0)
    gain_two_sum = sum(gain_twos)[0]

    def merged(values):
        return sum(values[:, 4 * b : 4 * b + 4] for b in range(blocks)).reshape(STATE, width)

    small = jnp.concatenate(
        [merged(grad_c_lanes), merged(grad_a_lanes), gain_one[None], gain_two_sum[None]], axis=0
    )
    small, mlp_back = total_dp(small, mlp_back)
    grad_c, grad_a = small[:STATE], small[STATE : 2 * STATE]
    gains_grad = small[2 * STATE :]
    decay_step = jnp.exp(-decay_rate)
    grad_read = grad_c * drive_root * param_lanes[1]
    grad_drive = grad_c * drive_root * param_lanes[2]
    grad_a = grad_a - grad_c * param_lanes[1] * param_lanes[2] * decay_step / drive_root
    grad_log = -decay_rate * decay_step * grad_a
    ssm_grad = jnp.stack([grad_log, grad_drive, grad_read]).transpose(0, 2, 1)

    attn_back = move(gate(attn_sum, small), hosts[WAY], ATTN_WAYS, True)
    attn_grad = jnp.stack(
        [
            jnp.where(attn_here >= 1, attn_sum.astype(f32), 0.0),
            jnp.where(attn_here == 2, attn_back.astype(f32), 0.0),
        ]
    )
    mlp_grad = jnp.where(
        mlp_here == 1, jnp.concatenate([mlp_sum, mlp_back], axis=1).astype(f32), 0.0
    )[None]

    attn_rates = rates[:2, None, None]
    mlp_rates = rates[2]
    ssm_rates = jnp.asarray([1.0, 0.8, 0.25], f32)[:, None, None]
    gain_rates = jnp.asarray([0.6, 0.6], f32)[:, None]
    attn_one, attn_two, attn_new = adam_step(
        attn_grad, attn_first, attn_second, attn_master, attn_rates, matrix_decay
    )
    mlp_one, mlp_two, mlp_new = adam_step(
        mlp_grad, mlp_first, mlp_second, mlp_master, mlp_rates, matrix_decay
    )
    ssm_one, ssm_two, ssm_new = adam_step(
        ssm_grad, ssm_first, ssm_second, ssm_params, ssm_rates, 0.0
    )
    gain_first_new, gain_second_new, gains_new = adam_step(
        gains_grad, gains_first, gains_second, norm_gains, gain_rates, 0.0
    )
    return (
        block_out.reshape(tokens.shape),
        grad_tokens.reshape(tokens.shape),
        attn_grad,
        attn_one,
        attn_two,
        attn_new,
        attn_new.astype(bf16),
        mlp_grad,
        mlp_one,
        mlp_two,
        mlp_new,
        mlp_new.astype(bf16),
        ssm_grad,
        ssm_one,
        ssm_two,
        ssm_new,
        gains_grad,
        gain_first_new,
        gain_second_new,
        gains_new,
    )


def solution(mesh):
    in_specs = (
        P(None, "dp", "tensor"),
        P(None, "dp", "tensor"),
        P(None, "dp"),
        P(),
        P(None, "dp", "tensor"),
        P(None, "dp", "tensor"),
        P(None, "dp", "tensor"),
        P(None, "dp", "tensor"),
        P(None, "dp", "tensor"),
        P(None, "dp", "tensor"),
        P(None, "tensor", None),
        P(None, "tensor", None),
        P(None, "tensor", None),
        P(None, "tensor"),
        P(None, "tensor"),
        P(None, "tensor"),
    )
    out_specs = (
        P(None, "dp", "tensor"),
        P(None, "dp", "tensor"),
        P(None, "dp", "tensor"),
        P(None, "dp", "tensor"),
        P(None, "dp", "tensor"),
        P(None, "dp", "tensor"),
        P(None, "dp", "tensor"),
        P(None, "dp", "tensor"),
        P(None, "dp", "tensor"),
        P(None, "dp", "tensor"),
        P(None, "dp", "tensor"),
        P(None, "dp", "tensor"),
        P(None, "tensor", None),
        P(None, "tensor", None),
        P(None, "tensor", None),
        P(None, "tensor", None),
        P(None, "tensor"),
        P(None, "tensor"),
        P(None, "tensor"),
        P(None, "tensor"),
    )
    return jax.shard_map(body, mesh=mesh, in_specs=in_specs, out_specs=out_specs, check_vma=False)
```

```python
import functools
import itertools

import jax
import jax.numpy as jnp
from jax import lax
from jax.experimental import pallas as pl
from jax.experimental.pallas import tpu as pltpu
from jax.sharding import PartitionSpec as P

D = 1024
HEAD_DIM = 128
FF = 4096
STATE = 16
CTX = 128
BL = 512
OWNER_GROUPS = 4
STEP = 5

epsilon_norm = 1e-05
beta_first = 0.9
beta_second = 0.95
epsilon_adam = 1e-08
matrix_decay = 0.1
masked_score = -1e30
score_scale = HEAD_DIM ** (-0.5)
f32 = jnp.float32
bf16 = jnp.bfloat16
i32 = jnp.int32
SWAP = [(0, 1), (1, 0)]
COST = 1000
TILE = 256
QT = 256
FT = 512
LOG2E = 1.4426950408889634


def dot_nn(left, right):
    return lax.dot_general(left, right, (((1,), (0,)), ((), ())), preferred_element_type=f32)


def dot_nt(left, right):
    return lax.dot_general(left, right, (((1,), (1,)), ((), ())), preferred_element_type=f32)


def dot_tn(left, right):
    return lax.dot_general(left, right, (((0,), (0,)), ((), ())), preferred_element_type=f32)


def call(
    kernel, grid, in_specs, out_specs, out_shape, scratch=(), prefetch=0, flops=0, nbytes=0, room=36
):
    return pl.pallas_call(
        kernel,
        grid_spec=pltpu.PrefetchScalarGridSpec(
            num_scalar_prefetch=prefetch,
            grid=grid,
            in_specs=in_specs,
            out_specs=out_specs,
            scratch_shapes=scratch,
        ),
        out_shape=out_shape,
        name=kernel.__name__,
        compiler_params=pltpu.CompilerParams(vmem_limit_bytes=room * 1024 * 1024),
        cost_estimate=pl.CostEstimate(flops=flops // COST, bytes_accessed=nbytes // COST, transcendentals=0),
    )


def whole(shape):
    return pl.BlockSpec(shape, lambda *_: (0,) * len(shape), pipeline_mode=pl.Buffered(1))


def sds(shape, dtype):
    return jax.ShapeDtypeStruct(shape, dtype)


def hbm(*values):
    held = tuple(pltpu.with_memory_space_constraint(v, pltpu.HBM) for v in values)
    return held[0] if len(held) == 1 else held


def swap_x(values):
    return lax.ppermute(values, "tensor", SWAP)


def gate(value, *others):
    if not others:
        return value
    return lax.optimization_barrier((value,) + others)[0]


def together(*values):
    return lax.optimization_barrier(values)


def gather_rounds():
    return max(lax.axis_size("dp") - 1, 0).bit_length()


def gather_round(held, k):
    step = 1 << k
    count = lax.axis_size("dp")
    other = lax.ppermute(held, "dp", [(i, i ^ step) for i in range(count)])
    later = (lax.axis_index("dp") // step) % 2 == 1
    return jnp.where(
        later,
        jnp.concatenate([other, held], axis=0),
        jnp.concatenate([held, other], axis=0),
    )


def total_dp(values, beside):
    count = lax.axis_size("dp")
    for k in range(gather_rounds()):
        if k == gather_rounds() - 1:
            values, beside = together(values, beside)
        values = values + lax.ppermute(values, "dp", [(i, i ^ (1 << k)) for i in range(count)])
    return values, beside


def routes(full_count, empty_count):
    groups = range(OWNER_GROUPS)
    ways = []
    for full in itertools.combinations(groups, full_count):
        rest = [g for g in groups if g not in full]
        for empty in itertools.combinations(rest, empty_count):
            ways.append((full, empty))
    return ways


ATTN_WAYS = routes(1, 1) + routes(2, 2)


def way_code(full, empty):
    code = 0
    for g in range(OWNER_GROUPS):
        digit = 2 if g in full else (0 if g in empty else 1)
        code += digit * 3**g
    return code


def one_if(condition):
    return jnp.where(condition, jnp.int32(1), jnp.int32(0))


HOST_MLP, SIDE, WAY, NEAR, ATTN_HERE, MLP_HERE, PLAN_SIZE = 4, 8, 9, 10, 11, 12, 16
ATTN_RATES = [0.5 * D ** (-0.5)] * 3 + [0.5 * (D // 16) ** (-0.5)]
MLP_RATES = [0.5 * D ** (-0.5), 0.5 * FF ** (-0.5)]
IDLE_RATE = 0.5 * D ** (-0.5)


def plan_kernel(owner_ref, here_ref, out_ref, rate_ref):
    groups = range(OWNER_GROUPS)
    side, group = here_ref[0], here_ref[1]
    owner = [owner_ref[m] for m in range(6)]
    slot = [
        sum([one_if(owner[k] == owner[m]) for k in range(m)], jnp.int32(0)) for m in range(4)
    ]
    count = [sum([one_if(owner[m] == g) for m in range(4)], jnp.int32(0)) for g in groups]
    full_rank = [sum([one_if(count[h] == 2) for h in range(g)], jnp.int32(0)) for g in groups]
    empty_rank = [sum([one_if(count[h] == 0) for h in range(g)], jnp.int32(0)) for g in groups]
    taker = [
        sum(
            [
                jnp.where(
                    jnp.logical_and(count[h] == 0, empty_rank[h] == full_rank[g]), jnp.int32(h), 0
                )
                for h in groups
            ],
            jnp.int32(0),
        )
        for g in groups
    ]
    for m in range(4):
        second = sum([jnp.where(owner[m] == g, taker[g], 0) for g in groups], jnp.int32(0))
        out_ref[m] = jnp.where(slot[m] == 0, owner[m], second)
    code = sum([count[g] * 3**g for g in groups], jnp.int32(0))
    out_ref[WAY] = sum(
        [
            jnp.where(code == way_code(*way), jnp.int32(k), 0)
            for k, way in enumerate(ATTN_WAYS)
        ],
        jnp.int32(0),
    )
    low = sum([one_if(owner[m] < 2) for m in (4, 5)], jnp.int32(0))
    near = low == 1
    for k, m in enumerate((4, 5)):
        out_ref[HOST_MLP + 2 * k] = owner[m]
        bit = jnp.where(near, jnp.int32(1), jnp.int32(2))
        out_ref[HOST_MLP + 2 * k + 1] = jnp.bitwise_xor(owner[m], bit)
    out_ref[SIDE] = side
    out_ref[NEAR] = one_if(near)
    out_ref[ATTN_HERE] = sum([one_if(owner[m] == group) for m in range(4)], jnp.int32(0))
    out_ref[MLP_HERE] = sum([one_if(owner[m] == group) for m in (4, 5)], jnp.int32(0))
    for k in range(MLP_HERE + 1, PLAN_SIZE):
        out_ref[k] = jnp.int32(0)
    for place in range(2):
        rate = f32(IDLE_RATE)
        for m in range(4):
            hit = jnp.logical_and(owner[m] == group, slot[m] == place)
            rate = jnp.where(hit, f32(ATTN_RATES[m]), rate)
        rate_ref[place] = rate
    rate = f32(IDLE_RATE)
    for k, m in enumerate((4, 5)):
        rate = jnp.where(owner[m] == group, f32(MLP_RATES[k]), rate)
    rate_ref[2] = rate
    rate_ref[3] = f32(0.0)


def move(values, index, ways, back):
    size = lax.axis_size("dp") // OWNER_GROUPS

    def branch(way):
        pairs = []
        for a, b in zip(*way):
            if back:
                a, b = b, a
            pairs += [(a * size + j, b * size + j) for j in range(size)]
        return lambda v: lax.ppermute(v, "dp", pairs)

    return lax.switch(index, [branch(way) for way in ways], values)


def exchange_groups(values, near):
    size = lax.axis_size("dp") // OWNER_GROUPS

    def across(bit):
        return lax.ppermute(
            values,
            "dp",
            [(g * size + j, (g ^ bit) * size + j) for g in range(OWNER_GROUPS) for j in range(size)],
        )

    return jnp.where(near, across(1), across(2))


def ring_order(count):
    chips = count // 2
    if chips == 8:
        return [0, 2, 4, 6, 7, 5, 3, 1]
    return list(range(chips))


def join_kernel(host_ref, own_ref, other_ref, out_ref):
    @pl.when(pl.program_id(0) == 0)
    def _():
        out_ref[...] = own_ref[...]

    @pl.when(pl.program_id(0) == 1)
    def _():
        out_ref[...] = other_ref[...]


def join_scaled_kernel(
    host_ref, own_ref, other_ref, inverse_ref, gain_ref, gain_other_ref, out_ref
):
    @pl.when(pl.program_id(0) == 0)
    def _():
        out_ref[...] = (own_ref[...].astype(f32) * inverse_ref[...] * gain_ref[...]).astype(bf16)

    @pl.when(pl.program_id(0) == 1)
    def _():
        out_ref[...] = (
            other_ref[...].astype(f32) * inverse_ref[...] * gain_other_ref[...]
        ).astype(bf16)


def join_sides(hosts, own, other, scales=()):
    rows, width = own.shape
    return call(
        join_scaled_kernel if scales else join_kernel,
        (2,),
        [whole(v.shape) for v in (own, other) + tuple(scales)],
        [
            pl.BlockSpec(
                (rows, width), lambda d, s: (0, jnp.where(d == 0, s[SIDE], 1 - s[SIDE]))
            )
        ],
        [pltpu.HBM((rows, 2 * width), bf16)],
        prefetch=1,
        nbytes=8 * rows * width,
        room=12,
    )(hosts, own, other, *scales)[0]


class Ring:
    def __init__(self):
        self.count = lax.axis_size("dp")
        self.chips = self.count // 2
        order = ring_order(self.count)
        here = lax.axis_index("dp")
        self.core = here % 2
        chip = here // 2
        self.place = jnp.where(chip % 2 == 0, chip // 2, 7 - chip // 2) if self.chips == 8 else chip
        self.up = [
            (2 * order[p] + c, 2 * order[(p + 1) % self.chips] + c)
            for p in range(self.chips)
            for c in range(2)
        ]
        self.down = [(b, a) for a, b in self.up]
        self.cores = [(i, i ^ 1) for i in range(self.count)]
        self.far_up = self.chips // 2
        self.far_down = self.chips - 1 - self.far_up

    def chip(self, offset):
        place = (self.place + self.chips + offset) % self.chips
        if self.chips != 8:
            return place
        return jnp.where(place < 4, 2 * place, 15 - 2 * place)

    def start(self, blocks):
        pairs = blocks.reshape((self.chips, 2) + blocks.shape[1:])
        mine = lax.dynamic_index_in_dim(pairs, self.core, 1, keepdims=False)
        theirs = lax.dynamic_index_in_dim(pairs, 1 - self.core, 1, keepdims=False)
        received = lax.ppermute(theirs, "dp", self.cores)

        def part(offset):
            chip = self.chip(offset)
            return lax.dynamic_index_in_dim(mine, chip, 0, keepdims=False).astype(
                f32
            ) + lax.dynamic_index_in_dim(received, chip, 0, keepdims=False).astype(f32)

        return part, part(self.far_up).astype(bf16), part(-self.far_down).astype(bf16)

    def step(self, k, part, up, down):
        if k < self.far_up:
            up = lax.ppermute(up, "dp", self.up)
            if k < self.far_up - 1:
                up = (up.astype(f32) + part(self.far_up - 1 - k)).astype(bf16)
        if k < self.far_down:
            down = lax.ppermute(down, "dp", self.down)
            if k < self.far_down - 1:
                down = (down.astype(f32) + part(k + 1 - self.far_down)).astype(bf16)
        return up, down


def shift_tails(values, by, cross):
    count = lax.axis_size("dp")
    pairs = [
        (2 * i + s, 2 * (i + by) + (1 - s if cross else s))
        for i in range(count)
        for s in range(2)
        if 0 <= i + by < count
    ]
    return lax.ppermute(values, ("dp", "tensor"), pairs)


def first_half():
    return lax.broadcasted_iota(i32, (8, 128), 0) < 4


def flag(condition):
    return jnp.where(condition, f32(1.0), f32(0.0))


def keep_at(seg_ref, t, half):
    return jnp.where(
        half, flag(seg_ref[t + 1] == seg_ref[t]), flag(seg_ref[BL + t + 1] == seg_ref[BL + t])
    )


def chunked(seg_ref, begin, end, plain, kept, carried, back=False):
    size = 8
    count = (end - begin) // size

    def chunk(c, carried):
        first = begin + (count - 1 - c if back else c) * size
        same = jnp.logical_and(
            seg_ref[first] == seg_ref[first + size],
            seg_ref[BL + first] == seg_ref[BL + first + size],
        )

        def run(step):
            def go(carried):
                for k in range(size):
                    carried = step(first + (size - 1 - k if back else k), carried)
                return carried

            return go

        return lax.cond(same, run(plain), run(kept), carried)

    return lax.fori_loop(0, count, chunk, carried)


def scan_kernel(seg_ref, h_ref, rate_ref, c_ref, y_ref, s_ref, e_ref):
    half = first_half()
    decay = [jnp.exp(-rate_ref[n]) for n in range(STATE)]

    def plain(t, states):
        row = h_ref[t]
        return [states[n] * decay[n] + row for n in range(STATE)]

    def kept(t, states):
        keep = keep_at(seg_ref, t, half)
        row = h_ref[t]
        return [(states[n] * keep) * decay[n] + row for n in range(STATE)]

    def reading(step):
        def go(t, states):
            states = step(t, states)
            total = c_ref[0] * states[0]
            for n in range(1, STATE):
                total = total + c_ref[n] * states[n]
            y_ref[t - (BL - CTX)] = total
            return states

        return go

    states = [jnp.zeros((8, 128), f32)] * STATE
    states = chunked(seg_ref, 0, BL - CTX, plain, kept, states)
    states = chunked(seg_ref, BL - CTX, BL, reading(plain), reading(kept), states)
    joined = flag(seg_ref[2 * BL] == seg_ref[BL])
    for n in range(STATE):
        s_ref[n] = states[n]
        ends = states[n] + (joined * jnp.exp(-rate_ref[n] * BL)) * pltpu.roll(states[n], 4, 0)
        e_ref[n] = ends


def tail_kernel(
    seg_ref, use_ref, all_ref, s_ref, rate_ref, c_ref, y_ref, out_ref, start_ref, carry_ref
):
    half = first_half()
    before = seg_ref[0]
    joined = flag(seg_ref[BL] == before)
    decay = [jnp.exp(-rate_ref[n]) for n in range(STATE)]
    carry_ref[...] = jnp.zeros_like(carry_ref)

    def gather(j, _):
        @pl.when(use_ref[j] > 0)
        def _():
            for m in range(STATE // 2):
                pair = all_ref[j, 16 * m : 16 * m + 16, :].astype(f32)
                for k in range(2):
                    n = 2 * m + k
                    power = jnp.exp(-rate_ref[n] * (2 * BL))
                    carry_ref[n] = carry_ref[n] * power + pair[8 * k : 8 * k + 8]

        return 0

    lax.fori_loop(0, all_ref.shape[0], gather, 0)
    weighted = []
    for n in range(STATE):
        carried = pltpu.roll(carry_ref[n], 4, 0)
        mid = pltpu.roll(s_ref[n], 4, 0) + (joined * jnp.exp(-rate_ref[n] * BL)) * carry_ref[n]
        start = jnp.where(half, carried, mid)
        start_ref[n] = start
        weighted.append(c_ref[n] * start * jnp.exp(-rate_ref[n] * (BL - CTX + 1)))

    def step(t, parts):
        mask = jnp.where(
            half,
            flag(seg_ref[t + 1 + BL - CTX] == before),
            flag(seg_ref[BL + t + 1 + BL - CTX] == seg_ref[BL]),
        )
        total = parts[0]
        for n in range(1, STATE):
            total = total + parts[n]
        out_ref[t] = y_ref[t] + mask * total
        return [parts[n] * decay[n] for n in range(STATE)]

    lax.fori_loop(0, CTX, step, weighted, unroll=4)


def back_total_kernel(seg_ref, g_ref, rate_ref, c_ref, own_ref, out_ref):
    half = first_half()
    decay = [jnp.exp(-rate_ref[n]) for n in range(STATE)]

    def step(k, sums):
        t = CTX - 1 - k
        mask = jnp.where(
            half,
            flag(seg_ref[t + 1 + BL - CTX] == seg_ref[1]),
            flag(seg_ref[BL + t + 1 + BL - CTX] == seg_ref[BL]),
        )
        grad = mask * g_ref[t]
        return [decay[n] * (sums[n] + grad) for n in range(STATE)]

    sums = lax.fori_loop(0, CTX, step, [jnp.zeros((8, 128), f32)] * STATE, unroll=4)
    joined = flag(seg_ref[1] == seg_ref[BL])
    for n in range(STATE):
        total = sums[n] * c_ref[n] * jnp.exp(-rate_ref[n] * (BL - CTX))
        own_ref[n] = total
        out_ref[n] = total + (joined * jnp.exp(-rate_ref[n] * BL)) * pltpu.roll(total, 4, 0)


def sens_steps(seg_ref, h_ref, half, decay, count):
    def plain(t, both):
        row = h_ref[t]
        sens = [both[1][n] * decay[n] + both[0][n] for n in range(count)]
        states = [both[0][n] * decay[n] + row for n in range(count)]
        return [states, sens] + list(both[2:])

    def kept(t, both):
        keep = keep_at(seg_ref, t, half)
        row = h_ref[t]
        held = [v * keep for v in both[0]]
        sens = [(both[1][n] * keep) * decay[n] + held[n] for n in range(count)]
        states = [held[n] * decay[n] + row for n in range(count)]
        return [states, sens] + list(both[2:])

    return plain, kept


SENS_GROUP = 8


def sens_kernel(seg_ref, h_ref, start_ref, rate_ref, s_ref, z_ref):
    half = first_half()
    for first in range(0, STATE, SENS_GROUP):
        ids = range(first, first + SENS_GROUP)
        decay = [jnp.exp(-rate_ref[n]) for n in ids]
        plain, kept = sens_steps(seg_ref, h_ref, half, decay, SENS_GROUP)
        both = [[start_ref[n] for n in ids], [jnp.zeros((8, 128), f32)] * SENS_GROUP]
        both = chunked(seg_ref, 0, BL - CTX, plain, kept, both)
        for k, n in enumerate(ids):
            s_ref[n] = both[0][k]
            z_ref[n] = both[1][k]


def sens_tail_kernel(seg_ref, h_ref, g_ref, s_ref, z_ref, rate_ref, gc_ref, ga_ref, zend_ref):
    half = first_half()
    for first in range(0, STATE, SENS_GROUP):
        ids = range(first, first + SENS_GROUP)
        decay = [jnp.exp(-rate_ref[n]) for n in ids]

        def summing(step):
            def go(t, carried):
                states, sens, by_c, by_a = step(t, carried)
                grad = g_ref[t - (BL - CTX)]
                by_c = [by_c[n] + grad * states[n] for n in range(SENS_GROUP)]
                by_a = [by_a[n] + grad * sens[n] for n in range(SENS_GROUP)]
                return [states, sens, by_c, by_a]

            return go

        plain, kept = sens_steps(seg_ref, h_ref, half, decay, SENS_GROUP)
        zeros = [jnp.zeros((8, 128), f32)] * SENS_GROUP
        carried = [[s_ref[n] for n in ids], [z_ref[n] for n in ids], zeros, zeros]
        carried = chunked(seg_ref, BL - CTX, BL, summing(plain), summing(kept), carried)
        for k, n in enumerate(ids):
            zend_ref[n] = carried[1][k]
            gc_ref[n] = carried[2][k]
            ga_ref[n] = carried[3][k]


def back_scan_kernel(
    seg_ref,
    use_ref,
    all_ref,
    g_ref,
    own_ref,
    z_ref,
    ga_ref,
    rate_ref,
    c_ref,
    gh_ref,
    out_ref,
    later_ref,
):
    half = first_half()
    decay = [jnp.exp(-rate_ref[n]) for n in range(STATE)]
    joined = flag(seg_ref[2 * BL] == seg_ref[BL])
    later_ref[...] = jnp.zeros_like(later_ref)
    count = all_ref.shape[0]

    def gather(k, _):
        j = count - 1 - k

        @pl.when(use_ref[j] > 0)
        def _():
            for m in range(STATE // 2):
                pair = all_ref[j, 16 * m : 16 * m + 16, :].astype(f32)
                for k in range(2):
                    n = 2 * m + k
                    power = jnp.exp(-rate_ref[n] * (2 * BL))
                    later_ref[n] = later_ref[n] * power + pair[8 * k : 8 * k + 8]

        return 0

    lax.fori_loop(0, count, gather, 0)
    sums = []
    for n in range(STATE):
        first = (
            pltpu.roll(own_ref[n], 4, 0) + (joined * jnp.exp(-rate_ref[n] * BL)) * later_ref[n]
        )
        entering = jnp.where(half, first, pltpu.roll(later_ref[n], 4, 0))
        sums.append(entering)
        out_ref[n] = ga_ref[n] * c_ref[n] + entering * z_ref[n]

    def total_of(t, sums):
        total = sums[0]
        for n in range(1, STATE):
            total = total + sums[n]
        gh_ref[t] = total

    def plain(t, sums):
        total_of(t, sums)
        return [v * decay[n] for n, v in enumerate(sums)]

    def kept(t, sums):
        total_of(t, sums)
        keep = keep_at(seg_ref, t, half)
        return [(v * keep) * decay[n] for n, v in enumerate(sums)]

    def entered(step):
        def go(t, sums):
            grad = g_ref[t - (BL - CTX)]
            return step(t, [sums[n] + c_ref[n] * grad for n in range(STATE)])

        return go

    sums = chunked(seg_ref, BL - CTX, BL, entered(plain), entered(kept), sums, back=True)
    chunked(seg_ref, 0, BL - CTX, plain, kept, sums, back=True)


def to_lanes(values, blocks, steps):
    return (
        values.reshape(blocks, steps, 4, 128).transpose(1, 0, 2, 3).reshape(steps, blocks * 4, 128)
    )


def from_lanes(values, blocks, steps):
    return values.reshape(steps, blocks, 4, 128).transpose(1, 0, 2, 3).reshape(blocks, steps, 512)


def attend_kernel(
    host_ref,
    hid_ref,
    ctx_ref,
    wq_ref,
    wk_ref,
    wv_ref,
    segq_ref,
    segk_ref,
    q_ref,
    k_ref,
    v_ref,
    ck_ref,
    cv_ref,
    pc_ref,
    pb_ref,
    mix_ref,
):
    hid = hid_ref[...]
    ctx = ctx_ref[...]
    q_ref[...] = dot_nn(hid, wq_ref[0]).astype(bf16)
    k_ref[...] = dot_nn(hid, wk_ref[0]).astype(bf16)
    v_ref[...] = dot_nn(hid, wv_ref[0]).astype(bf16)
    ck_ref[...] = dot_nn(ctx, wk_ref[0]).astype(bf16)
    cv_ref[...] = dot_nn(ctx, wv_ref[0]).astype(bf16)
    ctx_ids = segk_ref[:, :CTX]
    for i in range(BL // QT):
        rows = slice(i * QT, (i + 1) * QT)
        reach = (i + 1) * QT
        ids = segq_ref[rows]
        ctx_ok = ctx_ids == ids
        place_q = lax.broadcasted_iota(i32, (QT, reach), 0) + i * QT
        place_k = lax.broadcasted_iota(i32, (QT, reach), 1)
        block_ok = jnp.logical_and(place_k <= place_q, segk_ref[:, CTX : CTX + reach] == ids)
        for head in range(TILE // HEAD_DIM):
            cols = slice(head * HEAD_DIM, (head + 1) * HEAD_DIM)
            query = q_ref[rows, cols]
            sc = dot_nt(query, ck_ref[:, cols]) * (score_scale * LOG2E)
            sb = dot_nt(query, k_ref[:reach, cols]) * (score_scale * LOG2E)
            sc = jnp.where(ctx_ok, sc, masked_score)
            sb = jnp.where(block_ok, sb, masked_score)
            top = jnp.maximum(
                jnp.max(sc, axis=1, keepdims=True), jnp.max(sb, axis=1, keepdims=True)
            )
            ec = jnp.exp2(sc - top)
            eb = jnp.exp2(sb - top)
            total = jnp.sum(ec, axis=1, keepdims=True) + jnp.sum(eb, axis=1, keepdims=True)
            inverse = 1.0 / total
            pc = (ec * inverse).astype(bf16)
            pb = (eb * inverse).astype(bf16)
            pc_ref[head, rows, :] = pc
            pb_ref[head, rows, :reach] = pb
            if reach < BL:
                pb_ref[head, rows, reach:] = jnp.zeros((QT, BL - reach), bf16)
            mixed = dot_nn(pc, cv_ref[:, cols]) + dot_nn(pb, v_ref[:reach, cols])
            mix_ref[rows, cols] = mixed.astype(bf16)


def attend_forward(hosts, block, hidden, context, attn_full, seg_col, seg_row, half_width):
    pairs = half_width // TILE

    def weight(position):
        return pl.BlockSpec((1, D, TILE), lambda p, s: (s[position], 0, p))

    def tile(rows):
        return pl.BlockSpec((rows, TILE), lambda p, s: (0, p))

    heads = half_width // HEAD_DIM
    per = TILE // HEAD_DIM
    return call(
        attend_kernel,
        (pairs,),
        [
            pl.BlockSpec((BL, D), lambda p, s: (block, 0)),
            pl.BlockSpec((CTX, D), lambda p, s: (block, 0)),
            weight(0),
            weight(1),
            weight(2),
            pl.BlockSpec((BL, 1), lambda p, s: (block, 0)),
            whole((1, CTX + BL)),
        ],
        [
            tile(BL),
            tile(BL),
            tile(BL),
            tile(CTX),
            tile(CTX),
            pl.BlockSpec((per, BL, CTX), lambda p, s: (p, 0, 0)),
            pl.BlockSpec((per, BL, BL), lambda p, s: (p, 0, 0)),
            tile(BL),
        ],
        [
            pltpu.HBM((BL, half_width), bf16),
            pltpu.HBM((BL, half_width), bf16),
            pltpu.HBM((BL, half_width), bf16),
            pltpu.HBM((CTX, half_width), bf16),
            pltpu.HBM((CTX, half_width), bf16),
            pltpu.HBM((heads, BL, CTX), bf16),
            pltpu.HBM((heads, BL, BL), bf16),
            sds((BL, half_width), bf16),
        ],
        prefetch=1,
        flops=8 * 10**9,
        nbytes=12 * 10**6,
    )(
        hosts,
        hbm(hidden),
        context,
        *hbm(attn_full, attn_full, attn_full),
        seg_col,
        seg_row,
    )


def attend_back_kernel(
    host_ref,
    own_ref,
    other_ref,
    cot_ref,
    mid_ref,
    gain_ref,
    tok_ref,
    first_gain_ref,
    wo_ref,
    wq_ref,
    wk_ref,
    wv_ref,
    q_ref,
    k_ref,
    v_ref,
    ck_ref,
    cv_ref,
    pc_ref,
    pb_ref,
    low_ref,
    gmid_ref,
    ggain_ref,
    dq_ref,
    dk_ref,
    dv_ref,
    dck_ref,
    dcv_ref,
    hown_ref,
    hsend_ref,
    cown_ref,
    csend_ref,
    sum_ref,
    dsc_ref,
    dsb_ref,
):
    step = pl.program_id(0)
    pairs = pl.num_programs(0) - 2

    @pl.when(step == 0)
    def _():
        grad = own_ref[...].astype(f32) + other_ref[...].astype(f32)
        middle = mid_ref[...]
        inverse = lax.rsqrt(jnp.mean(middle * middle, axis=1, keepdims=True) + epsilon_norm)
        scaled = middle * inverse
        ggain_ref[...] = jnp.sum(grad * scaled, axis=0, keepdims=True)
        weighted = grad * gain_ref[...]
        centre = jnp.mean(weighted * scaled, axis=1, keepdims=True)
        result = cot_ref[...].astype(f32) + inverse * (weighted - scaled * centre)
        gmid_ref[...] = result
        low_ref[...] = result.astype(bf16)

    @pl.when(step < pairs)
    def _():
        grad_mixed = dot_nn(low_ref[...], wo_ref[0]).astype(bf16)
        base = step * TILE
        for head in range(TILE // HEAD_DIM):
            cols = slice(head * HEAD_DIM, (head + 1) * HEAD_DIM)
            to = pl.ds(pl.multiple_of(base + head * HEAD_DIM, HEAD_DIM), HEAD_DIM)
            grad_head = grad_mixed[:, cols]
            for i in range(BL // QT):
                rows = slice(i * QT, (i + 1) * QT)
                reach = (i + 1) * QT
                grad_rows = grad_head[rows]
                gpc = dot_nt(grad_rows, cv_ref[:, cols])
                gpb = dot_nt(grad_rows, v_ref[:reach, cols])
                pc = pc_ref[head, rows, :].astype(f32)
                pb = pb_ref[head, rows, :reach].astype(f32)
                tc = pc * gpc
                tb = pb * gpb
                centre = jnp.sum(tc, axis=1, keepdims=True) + jnp.sum(tb, axis=1, keepdims=True)
                dsc_ref[head, rows, :] = (tc - pc * centre).astype(bf16)
                dsb_ref[head, rows, :reach] = (tb - pb * centre).astype(bf16)
                if reach < BL:
                    dsb_ref[head, rows, reach:] = jnp.zeros((QT, BL - reach), bf16)
            dsc = dsc_ref[head]
            dsb = dsb_ref[head]
            dq = (dot_nn(dsc, ck_ref[:, cols]) + dot_nn(dsb, k_ref[:, cols])) * score_scale
            dq_ref[:, to] = dq.astype(bf16)
            query = q_ref[:, cols]
            dk_ref[:, to] = (dot_tn(dsb, query) * score_scale).astype(bf16)
            dck_ref[:, to] = (dot_tn(dsc, query) * score_scale).astype(bf16)
            dv_ref[:, to] = dot_tn(pb_ref[head], grad_head).astype(bf16)
            dcv_ref[:, to] = dot_tn(pc_ref[head], grad_head).astype(bf16)

    def half():
        part = (
            dot_nt(dq_ref[...], wq_ref[0])
            + dot_nt(dk_ref[...], wk_ref[0])
            + dot_nt(dv_ref[...], wv_ref[0])
        )
        ctx_part = dot_nt(dck_ref[...], wk_ref[0]) + dot_nt(dcv_ref[...], wv_ref[0])
        row_sum = jnp.sum(
            part * (tok_ref[...].astype(f32) * first_gain_ref[...]), axis=1, keepdims=True
        )
        return part, ctx_part, row_sum

    @pl.when(step == pairs)
    def _():
        part, ctx_part, row_sum = half()
        hsend_ref[...] = part.astype(bf16)
        csend_ref[...] = ctx_part.astype(bf16)
        sum_ref[...] = row_sum

    @pl.when(step == pairs + 1)
    def _():
        part, ctx_part, row_sum = half()
        hown_ref[...] = part
        cown_ref[...] = ctx_part
        sum_ref[...] += row_sum


def attend_backward(
    hosts, block, own, other, cot_full, middle, gain, tok_full, first_gain, attn_full, kept, width
):
    pairs = width // TILE
    per = TILE // HEAD_DIM

    def pair(p):
        return jnp.minimum(p, pairs - 1)

    def side(p, s):
        return jnp.where(p <= pairs, 1 - s[8], s[8])

    def weight(position):
        return pl.BlockSpec((1, width, width), lambda p, s: (s[position], side(p, s), 0))

    def tile(rows):
        return pl.BlockSpec((rows, TILE), lambda p, s: (0, pair(p)))

    return call(
        attend_back_kernel,
        (pairs + 2,),
        [
            whole((BL, D)),
            whole((BL, D)),
            pl.BlockSpec((BL, D), lambda p, s: (block, 0)),
            whole((BL, D)),
            whole((1, D)),
            pl.BlockSpec((BL, width), lambda p, s: (block, side(p, s))),
            pl.BlockSpec((1, width), lambda p, s: (0, side(p, s))),
            pl.BlockSpec((1, D, TILE), lambda p, s: (s[3], 0, pair(p))),
            weight(0),
            weight(1),
            weight(2),
            tile(BL),
            tile(BL),
            tile(BL),
            tile(CTX),
            tile(CTX),
            pl.BlockSpec((per, BL, CTX), lambda p, s: (pair(p), 0, 0)),
            pl.BlockSpec((per, BL, BL), lambda p, s: (pair(p), 0, 0)),
        ],
        [
            whole((BL, D)),
            whole((BL, D)),
            whole((1, D)),
            whole((BL, width)),
            whole((BL, width)),
            whole((BL, width)),
            whole((CTX, width)),
            whole((CTX, width)),
            whole((BL, width)),
            whole((BL, width)),
            whole((CTX, width)),
            whole((CTX, width)),
            whole((BL, 1)),
        ],
        [
            pltpu.HBM((BL, D), bf16),
            pltpu.HBM((BL, D), f32),
            sds((1, D), f32),
            pltpu.HBM((BL, width), bf16),
            pltpu.HBM((BL, width), bf16),
            pltpu.HBM((BL, width), bf16),
            pltpu.HBM((CTX, width), bf16),
            pltpu.HBM((CTX, width), bf16),
            pltpu.HBM((BL, width), f32),
            sds((BL, width), bf16),
            sds((CTX, width), f32),
            sds((CTX, width), bf16),
            sds((BL, 1), f32),
        ],
        scratch=[pltpu.VMEM((per, BL, CTX), bf16), pltpu.VMEM((per, BL, BL), bf16)],
        prefetch=1,
        flops=12 * 10**9,
        nbytes=20 * 10**6,
    )(
        hosts,
        *hbm(own, other, cot_full, middle),
        gain,
        hbm(tok_full),
        first_gain,
        *hbm(attn_full, attn_full, attn_full, attn_full, *kept),
    )


def attn_grad_kernel(host_ref, *refs):
    (hid0, hid1, ctx0, ctx1, low0, low1), rest = refs[:6], refs[6:]
    (dq0, dk0, dv0, dck0, dcv0, mix0), rest = rest[:6], rest[6:]
    (dq1, dk1, dv1, dck1, dcv1, mix1), (out_ref,) = rest[:6], rest[6:]
    matrix = pl.program_id(0)

    @pl.when(matrix == 0)
    def _():
        out_ref[0] = (dot_tn(hid0[...], dq0[...]) + dot_tn(hid1[...], dq1[...])).astype(bf16)

    @pl.when(matrix == 1)
    def _():
        out_ref[0] = (
            dot_tn(hid0[...], dk0[...])
            + dot_tn(hid1[...], dk1[...])
            + dot_tn(ctx0[...], dck0[...])
            + dot_tn(ctx1[...], dck1[...])
        ).astype(bf16)

    @pl.when(matrix == 2)
    def _():
        out_ref[0] = (
            dot_tn(hid0[...], dv0[...])
            + dot_tn(hid1[...], dv1[...])
            + dot_tn(ctx0[...], dcv0[...])
            + dot_tn(ctx1[...], dcv1[...])
        ).astype(bf16)

    @pl.when(matrix == 3)
    def _():
        out_ref[0] = (dot_tn(low0[...], mix0[...]) + dot_tn(low1[...], mix1[...])).astype(bf16)


def attn_grads(hosts, hidden, context, lows, blocks, half_width):
    hid_specs = [
        pl.BlockSpec((BL, D), lambda m, s: (0, 0)),
        pl.BlockSpec((BL, D), lambda m, s: (1, 0)),
        pl.BlockSpec((CTX, D), lambda m, s: (0, 0)),
        pl.BlockSpec((CTX, D), lambda m, s: (1, 0)),
    ]
    block_specs = [
        whole((BL, half_width)),
        whole((BL, half_width)),
        whole((BL, half_width)),
        whole((CTX, half_width)),
        whole((CTX, half_width)),
        whole((BL, half_width)),
    ]
    return call(
        attn_grad_kernel,
        (4,),
        hid_specs + [whole((BL, D))] * 2 + block_specs * 2,
        [pl.BlockSpec((1, D, half_width), lambda m, s: (s[m], 0, 0))],
        [pltpu.HBM((OWNER_GROUPS, D, half_width), bf16)],
        prefetch=1,
        flops=46 * 10**8,
        nbytes=14 * 10**6,
    )(hosts, *hbm(hidden, hidden, context, context, *lows, *blocks[0], *blocks[1]))[0]


def mlp_kernel(
    host_ref,
    own_ref,
    other_ref,
    wo_ref,
    woo_ref,
    tok_ref,
    gain_ref,
    cot_ref,
    w1_ref,
    w2_ref,
    mid_ref,
    hid_ref,
    act_ref,
    pre_ref,
    low_ref,
    grad_ref,
):
    step = pl.program_id(0)

    @pl.when(step == 0)
    def _():
        middle = (
            tok_ref[...].astype(f32)
            + dot_nt(own_ref[...], wo_ref[0])
            + dot_nt(other_ref[...], woo_ref[...])
        )
        inverse = lax.rsqrt(jnp.mean(middle * middle, axis=1, keepdims=True) + epsilon_norm)
        mid_ref[...] = middle
        hid_ref[...] = (middle * inverse * gain_ref[...]).astype(bf16)
        grad_ref[...] = jnp.zeros_like(grad_ref)

    w1 = w1_ref[0]
    w2 = w2_ref[0]
    pre = dot_nn(hid_ref[...], w1)
    grad_act = dot_nn(cot_ref[...], w2)
    root = 0.7978845608028654
    square = pre * pre
    gate = 0.5 + 0.5 * jnp.tanh(pre * (root + (root * 0.044715) * square))
    act = pre * gate
    act_ref[...] = act.astype(bf16)
    slope = gate + act * (1.0 - gate) * (2.0 * root + (6.0 * root * 0.044715) * square)
    grad_pre = (slope * grad_act).astype(bf16)
    pre_ref[...] = grad_pre
    grad_ref[...] += dot_nt(grad_pre, w1)

    @pl.when(step == pl.num_programs(0) - 1)
    def _():
        low_ref[...] = grad_ref[...].astype(bf16)


def mlp_block(hosts, block, own, other, attn_full, wo_other, tok_full, gain, cot_full, mlp_full):
    half_width = own.shape[1]
    quarter = mlp_full.shape[2]
    hidden = 2 * quarter
    per = quarter // FT

    def weight(position):
        return pl.BlockSpec(
            (1, D, FT), lambda f, s: (s[4 + 2 * position + f // per], 0, lax.rem(f, per))
        )

    return call(
        mlp_kernel,
        (2 * per,),
        [
            whole((BL, half_width)),
            whole((BL, half_width)),
            pl.BlockSpec((1, D, half_width), lambda f, s: (s[3], 0, 0)),
            whole((D, half_width)),
            pl.BlockSpec((BL, D), lambda f, s: (block, 0)),
            whole((1, D)),
            pl.BlockSpec((BL, D), lambda f, s: (block, 0)),
            weight(0),
            weight(1),
        ],
        [
            whole((BL, D)),
            whole((BL, D)),
            pl.BlockSpec((BL, FT), lambda f, s: (0, f)),
            pl.BlockSpec((BL, FT), lambda f, s: (0, f)),
            whole((BL, D)),
        ],
        [
            pltpu.HBM((BL, D), f32),
            sds((BL, D), bf16),
            sds((BL, hidden), bf16),
            sds((BL, hidden), bf16),
            pltpu.HBM((BL, D), bf16),
        ],
        scratch=[pltpu.VMEM((BL, D), f32)],
        prefetch=1,
        flops=8 * 10**9,
        nbytes=24 * 10**6,
    )(
        hosts,
        own,
        other,
        hbm(attn_full),
        wo_other,
        tok_full,
        gain,
        cot_full,
        *hbm(mlp_full, mlp_full),
    )


def mlp_grad_kernel(host_ref, h0, h1, g0, g1, p0, p1, a0, a1, out_ref):
    matrix = pl.program_id(0)

    @pl.when(matrix == 0)
    def _():
        out_ref[0] = (dot_tn(h0[...], p0[...]) + dot_tn(h1[...], p1[...])).astype(bf16)

    @pl.when(matrix == 1)
    def _():
        out_ref[0] = (dot_tn(g0[...], a0[...]) + dot_tn(g1[...], a1[...])).astype(bf16)


def mlp_grads(hosts, hiddens, cot_full, pres, acts):
    hidden = acts[0].shape[1]
    quarter = hidden // 2
    per = quarter // FT
    last = 2 * per - 1
    used_first = pl.BlockSpec((BL, FT), lambda m, f, s: (0, jnp.where(m == 0, f, last)))
    used_second = pl.BlockSpec((BL, FT), lambda m, f, s: (0, jnp.where(m == 1, f, 0)))
    return call(
        mlp_grad_kernel,
        (2, 2 * per),
        [
            whole((BL, D)),
            whole((BL, D)),
            pl.BlockSpec((BL, D), lambda m, f, s: (0, 0)),
            pl.BlockSpec((BL, D), lambda m, f, s: (1, 0)),
            used_first,
            used_first,
            used_second,
            used_second,
        ],
        [
            pl.BlockSpec(
                (1, D, FT), lambda m, f, s: (s[4 + 2 * m + f // per], 0, lax.rem(f, per))
            )
        ],
        [pltpu.HBM((OWNER_GROUPS, D, quarter), bf16)],
        prefetch=1,
        flops=86 * 10**8,
        nbytes=20 * 10**6,
    )(
        hosts,
        hiddens[0],
        hiddens[1],
        cot_full,
        cot_full,
        *pres,
        *acts,
    )[0]


def mlp_out_kernel(host_ref, a0, a1, wa_ref, wb_ref, mid0, mid1, send_ref, own_ref):
    step = pl.program_id(0)
    quarter = wa_ref.shape[2]

    def rows(a_ref):
        return dot_nt(a_ref[:, :quarter], wa_ref[0]) + dot_nt(a_ref[:, quarter:], wb_ref[0])

    @pl.when(step == 0)
    def _():
        send_ref[:BL, :] = rows(a0).astype(bf16)
        send_ref[BL:, :] = rows(a1).astype(bf16)

    @pl.when(step == 1)
    def _():
        own_ref[:BL, :] = rows(a0) + mid0[...]
        own_ref[BL:, :] = rows(a1) + mid1[...]


def mlp_out(hosts, acts, mlp_full, middles, width):
    quarter = mlp_full.shape[2]

    def side(d, s):
        return jnp.where(d == 0, 1 - s[8], s[8])

    def weight(position):
        return pl.BlockSpec((1, width, quarter), lambda d, s: (s[position], side(d, s), 0))

    middle = pl.BlockSpec((BL, width), lambda d, s: (0, s[8]))
    return call(
        mlp_out_kernel,
        (2,),
        [whole((BL, 2 * quarter))] * 2 + [weight(6), weight(7), middle, middle],
        [whole((2 * BL, width))] * 2,
        [sds((2 * BL, width), bf16), pltpu.HBM((2 * BL, width), f32)],
        prefetch=1,
        flops=44 * 10**8,
        nbytes=12 * 10**6,
    )(hosts, *hbm(*acts, mlp_full, mlp_full, *middles))


def adam_step(gradient, moment_one, moment_two, weight, rate_table, decay_weight):
    step_count = f32(STEP)
    first_new = beta_first * moment_one + (1.0 - beta_first) * gradient
    second_new = beta_second * moment_two + (1.0 - beta_second) * gradient * gradient
    fixed_one = 1.0 - jnp.power(beta_first, step_count)
    fixed_two = 1.0 - jnp.power(beta_second, step_count)
    update = first_new / fixed_one / (jnp.sqrt(second_new / fixed_two) + epsilon_adam)
    return (first_new, second_new, weight - rate_table * (update + decay_weight * weight))


def body(
    tokens,
    cotangent,
    segments,
    owners,
    attn_master,
    attn_first,
    attn_second,
    mlp_master,
    mlp_first,
    mlp_second,
    ssm_params,
    ssm_first,
    ssm_second,
    norm_gains,
    gains_first,
    gains_second,
):
    rows = tokens.shape[1]
    width = tokens.shape[2]
    blocks = rows // BL
    dp_count = lax.axis_size("dp")
    dp_here = lax.axis_index("dp")
    side = lax.axis_index("tensor")
    group = dp_here // (dp_count // OWNER_GROUPS)
    quarter = mlp_master.shape[2] // 2

    def both_sides(own, other):
        return jnp.where(
            side == 0,
            jnp.concatenate([own, other], axis=-1),
            jnp.concatenate([other, own], axis=-1),
        )

    def side_of(values, which):
        return lax.dynamic_slice_in_dim(values, which * width, width, values.ndim - 1)

    smem = pl.BlockSpec(memory_space=pltpu.SMEM)
    vmem = pl.BlockSpec(memory_space=pltpu.VMEM)
    hosts, rates = pl.pallas_call(
        plan_kernel,
        in_specs=[smem, smem],
        out_specs=[smem, smem],
        out_shape=[sds((PLAN_SIZE,), i32), sds((4,), f32)],
    )(owners, jnp.stack([side, group]).astype(i32))
    attn_here = hosts[ATTN_HERE]
    mlp_here = hosts[MLP_HERE]
    near = hosts[NEAR] == 1
    ring = Ring()

    tok = tokens.reshape(rows, width)
    cot = cotangent.reshape(rows, width)
    tok_f = tok.astype(f32)
    square_here = jnp.sum(tok_f * tok_f, axis=1)
    square_other = swap_x(square_here)
    tok_other = swap_x(tok)
    gains_other = swap_x(norm_gains)
    inverse_one = lax.rsqrt((square_here + square_other) / D + epsilon_norm)
    scaled_own = tok_f * inverse_one[:, None]
    hidden_own = (scaled_own * norm_gains[0]).astype(bf16)
    gains_full = both_sides(norm_gains, gains_other)

    attn_low = attn_master.astype(bf16)
    mlp_low = mlp_master[0].astype(bf16)
    attn_moved = move(attn_low[1], hosts[WAY], ATTN_WAYS, False)
    attn_block = jnp.where(attn_here == 0, attn_moved, attn_low[0])
    attn_full = lax.all_gather(attn_block, "dp", axis=0, tiled=True)
    attn_full = attn_full.reshape(OWNER_GROUPS, D, width)
    mlp_moved = exchange_groups(gate(mlp_low[:, quarter:], square_other), near)

    seg = segments.reshape(rows)
    prior = lax.ppermute(seg[rows - CTX :] + 1, "dp", [(i, i + 1) for i in range(dp_count - 1)]) - 1
    seg_ext = jnp.concatenate([prior[CTX - 1 :], seg])
    seg_col = seg[:, None]

    param_lanes = ssm_params.transpose(0, 2, 1)
    decay_rate = jnp.exp(param_lanes[0]) * (BL ** (-0.5) / 32.0)
    drive_root = jnp.sqrt(-jnp.expm1(-2.0 * decay_rate))
    reading = param_lanes[2] * drive_root * param_lanes[1]

    def doubled(values):
        lanes = values.reshape(STATE, 4, 128)
        return jnp.concatenate([lanes] * blocks, axis=1)

    rate_lanes = doubled(decay_rate)
    reading_lanes = doubled(reading)
    state_shape = sds((STATE, 8, 128), f32)

    def plain(kernel, scalars, count, outs, cost, scratch=()):
        return pl.pallas_call(
            kernel,
            in_specs=[smem] * scalars + [vmem] * count,
            out_specs=[vmem] * len(outs),
            out_shape=outs,
            scratch_shapes=scratch,
            name=kernel.__name__,
            compiler_params=pltpu.CompilerParams(vmem_limit_bytes=16 * 1024 * 1024),
            cost_estimate=pl.CostEstimate(flops=cost // COST, bytes_accessed=10**6 // COST, transcendentals=0),
        )

    hidden_lanes = to_lanes(hidden_own.astype(f32), blocks, BL)
    tail_lanes = sds((CTX, 8, 128), f32)
    tail_part, state_ends, device_end = plain(
        scan_kernel, 1, 3, [tail_lanes, state_shape, state_shape], 4 * 10**9
    )(seg_ext, hidden_lanes, rate_lanes, reading_lanes)
    id_rows = jnp.where(
        (jnp.arange(16) == 0)[:, None], seg[rows - 1].astype(f32), seg[0].astype(f32)
    )
    message = jnp.concatenate(
        [device_end.reshape(STATE * 8, 128), jnp.broadcast_to(id_rows, (16, 128))], axis=0
    ).astype(bf16)
    hidden_full = join_sides(
        hosts,
        tok,
        tok_other,
        (inverse_one[:, None], norm_gains[0:1], gains_other[0:1]),
    )
    states_all = gather_round(message[None], 0)
    cot_other = swap_x(gate(cot, tok_other))
    for k in range(1, gather_rounds()):
        if k == gather_rounds() - 2:
            tok_other, states_all = together(tok_other, states_all)
        if k == gather_rounds() - 1:
            mlp_moved, states_all = together(mlp_moved, states_all)
        states_all = gather_round(states_all, k)
    states_all = gate(states_all, cot_other, hidden_full)
    mlp_block_low = jnp.where(mlp_here == 0, mlp_moved, mlp_low[:, :quarter])
    mlp_full = lax.all_gather(mlp_block_low, "dp", axis=0, tiled=True)
    mlp_full = mlp_full.reshape(OWNER_GROUPS, D, quarter)
    tok_full = join_sides(hosts, tok, tok_other)
    ids_all = states_all[:, STATE * 8 : STATE * 8 + 2, 0].astype(i32)
    places = jnp.arange(dp_count, dtype=i32)
    use_before = jnp.logical_and(places < dp_here, ids_all[:, 0] == seg_ext[0]).astype(i32)
    use_after = jnp.logical_and(places > dp_here, ids_all[:, 1] == seg[rows - 1]).astype(i32)
    tails, state_starts = plain(
        tail_kernel, 2, 5, [tail_lanes, state_shape], 10**9, [pltpu.VMEM((STATE, 8, 128), f32)]
    )(seg_ext, use_before, states_all, state_ends, rate_lanes, reading_lanes, tail_part)
    sens_states, sens_starts = plain(sens_kernel, 1, 3, [state_shape] * 2, 6 * 10**9)(
        seg_ext, hidden_lanes, state_starts, rate_lanes
    )
    tails = from_lanes(tails, blocks, CTX).astype(bf16)
    context_own = shift_tails(tails[blocks - 1], 1, False)
    context_other = shift_tails(tails[blocks - 1], 1, True)
    inner_own = tails[: blocks - 1]
    inner_other = swap_x(inner_own)
    context_full = jnp.concatenate(
        [
            both_sides(context_own, context_other)[None],
            both_sides(inner_own, inner_other),
        ],
        axis=0,
    ).reshape(-1, D)

    seg_rows = []
    for b in range(blocks):
        before = prior if b == 0 else seg[b * BL - CTX : b * BL]
        seg_rows.append(jnp.concatenate([before, seg[b * BL : (b + 1) * BL]])[None])
    kept = []
    mixed = []
    mixed_other = []
    for b in range(blocks):
        outs = attend_forward(
            hosts, b, hidden_full, context_full, attn_full, seg_col, seg_rows[b], width
        )
        kept.append(outs[:7])
        mixed.append(outs[7])
        mixed_other.append(swap_x(outs[7]))
    wo_own = lax.dynamic_index_in_dim(attn_full, hosts[3], 0, keepdims=False)
    wo_half = lax.dynamic_slice_in_dim(wo_own, ring.core * (D // 2), D // 2, 0)
    wo_half = gate(wo_half, inner_other)
    wo_first = swap_x(wo_half)
    wo_second = lax.ppermute(gate(wo_first, mixed[0]), "dp", ring.cores)
    joined = together(*mixed_other, sens_states, sens_starts)
    mixed_other, (sens_states, sens_starts) = list(joined[:blocks]), joined[blocks:]
    wo_other = jnp.where(
        ring.core == 0,
        jnp.concatenate([wo_first, wo_second], axis=0),
        jnp.concatenate([wo_second, wo_first], axis=0),
    )

    cot_full = join_sides(hosts, gate(cot, mixed[0]), cot_other)

    gain_two = gains_full[1:2]
    middles, hiddens, acts, pres, grads, grads_other = [], [], [], [], [], []
    for b in range(blocks):
        middle, hidden_two, act, grad_pre, grad_low = mlp_block(
            hosts,
            b,
            mixed[b],
            mixed_other[b],
            attn_full,
            wo_other,
            tok_full,
            gain_two,
            cot_full,
            mlp_full,
        )
        middles.append(middle)
        hiddens.append(hidden_two)
        acts.append(act)
        pres.append(grad_pre)
        grads.append(grad_low)
        grads_other.append(swap_x(grad_low))
    mlp_sum_in = mlp_grads(hosts, hiddens, cot_full, pres, acts)
    grads_other[0], mlp_sum_in = lax.optimization_barrier((grads_other[0], mlp_sum_in))
    mlp_sum = lax.psum_scatter(
        mlp_sum_in.reshape(OWNER_GROUPS * D, quarter), "dp", scatter_dimension=0, tiled=True
    )

    lows, grad_mids, gain_twos, grad_blocks = [], [], [], []
    parts, parts_sent, ctx_parts, ctx_sent, row_sums = [], [], [], [], []
    for b in range(blocks):
        if b == blocks - 1:
            acts[0] = gate(acts[0], *lows)
            out_send, out_own = mlp_out(hosts, acts, mlp_full, middles, width)
            out_received = swap_x(out_send)
            grads[b] = gate(grads[b], out_own)
        outs = attend_backward(
            hosts,
            b,
            gate(grads[b], *lows),
            grads_other[b],
            cot_full,
            middles[b],
            gain_two,
            tok_full,
            gains_full[0:1],
            attn_full,
            kept[b],
            width,
        )
        lows.append(outs[0])
        grad_mids.append(side_of(outs[1], side))
        gain_twos.append(side_of(outs[2], side))
        grad_blocks.append(list(outs[3:8]) + [mixed[b]])
        parts.append(outs[8])
        parts_sent.append(outs[9])
        ctx_parts.append(outs[10])
        ctx_sent.append(outs[11])
        row_sums.append(outs[12][:, 0])
    grad_tails = jnp.stack(
        [ctx_parts[b] + swap_x(ctx_sent[b]).astype(f32) for b in range(1, blocks)]
        + [
            shift_tails(ctx_parts[0].astype(bf16), -1, False).astype(f32)
            + shift_tails(ctx_sent[0], -1, True).astype(f32)
        ]
    )
    tail_grad_lanes = to_lanes(grad_tails.reshape(blocks * CTX, width), blocks, CTX)
    own_back, device_back = plain(back_total_kernel, 1, 3, [state_shape, state_shape], 10**9)(
        seg_ext, tail_grad_lanes, rate_lanes, reading_lanes
    )
    attn_sum_in = attn_grads(hosts, hidden_full, context_full, lows, grad_blocks, width)
    received = [swap_x(v) for v in parts_sent]

    back_all = gather_round(device_back.reshape(STATE * 8, 128).astype(bf16)[None], 0)
    part, up, down = ring.start(attn_sum_in.reshape(dp_count, -1, width))
    steps = 0
    for k in range(1, gather_rounds()):
        up, down, back_all = together(up, down, back_all)
        back_all = gather_round(back_all, k)
        if steps < ring.far_up - 2:
            up, down = ring.step(steps, part, up, down)
            steps += 1
    mlp_sum, back_all, up, down = together(mlp_sum, back_all, up, down)
    mlp_back = exchange_groups(mlp_sum, near)
    grad_c_lanes, grad_a_lanes, sens_end = plain(
        sens_tail_kernel, 1, 5, [state_shape] * 3, 2 * 10**9
    )(seg_ext, hidden_lanes, tail_grad_lanes, sens_states, sens_starts, rate_lanes)
    grad_lanes, grad_a_lanes = plain(
        back_scan_kernel,
        2,
        7,
        [sds((BL, 8, 128), f32), state_shape],
        4 * 10**9,
        [pltpu.VMEM((STATE, 8, 128), f32)],
    )(
        seg_ext,
        use_after,
        back_all,
        tail_grad_lanes,
        own_back,
        sens_end,
        grad_a_lanes,
        rate_lanes,
        reading_lanes,
    )
    for k in range(steps, ring.far_up):
        up, down = ring.step(k, part, up, down)
    attn_sum = (part(0) + up.astype(f32) + down.astype(f32)).astype(bf16)
    grad_channels = lax.optimization_barrier(
        from_lanes(grad_lanes, blocks, BL).reshape(rows, width)
    )

    part_own = jnp.concatenate(parts, axis=0)
    received = jnp.concatenate(received, axis=0)
    row_here = inverse_one * jnp.concatenate(row_sums) + jnp.sum(
        grad_channels * (scaled_own * norm_gains[0]), axis=1
    )
    row_other = swap_x(row_here)
    row_total = row_here + row_other
    block_out = (out_own + out_received.astype(f32)).astype(bf16)
    grad_hidden = part_own + received.astype(f32) + grad_channels
    grad_tokens = jnp.concatenate(grad_mids, axis=0) + inverse_one[:, None] * (
        grad_hidden * norm_gains[0] - scaled_own * (row_total / D)[:, None]
    )
    gain_one = jnp.sum(grad_hidden * scaled_own, axis=0)
    gain_two_sum = sum(gain_twos)[0]

    def merged(values):
        return sum(values[:, 4 * b : 4 * b + 4] for b in range(blocks)).reshape(STATE, width)

    small = jnp.concatenate(
        [merged(grad_c_lanes), merged(grad_a_lanes), gain_one[None], gain_two_sum[None]], axis=0
    )
    small, mlp_back = total_dp(small, mlp_back)
    grad_c, grad_a = small[:STATE], small[STATE : 2 * STATE]
    gains_grad = small[2 * STATE :]
    decay_step = jnp.exp(-decay_rate)
    grad_read = grad_c * drive_root * param_lanes[1]
    grad_drive = grad_c * drive_root * param_lanes[2]
    grad_a = grad_a - grad_c * param_lanes[1] * param_lanes[2] * decay_step / drive_root
    grad_log = -decay_rate * decay_step * grad_a
    ssm_grad = jnp.stack([grad_log, grad_drive, grad_read]).transpose(0, 2, 1)

    attn_back = move(gate(attn_sum, small), hosts[WAY], ATTN_WAYS, True)
    attn_grad = jnp.stack(
        [
            jnp.where(attn_here >= 1, attn_sum.astype(f32), 0.0),
            jnp.where(attn_here == 2, attn_back.astype(f32), 0.0),
        ]
    )
    mlp_grad = jnp.where(
        mlp_here == 1, jnp.concatenate([mlp_sum, mlp_back], axis=1).astype(f32), 0.0
    )[None]

    attn_rates = rates[:2, None, None]
    mlp_rates = rates[2]
    ssm_rates = jnp.asarray([1.0, 0.8, 0.25], f32)[:, None, None]
    gain_rates = jnp.asarray([0.6, 0.6], f32)[:, None]
    attn_one, attn_two, attn_new = adam_step(
        attn_grad, attn_first, attn_second, attn_master, attn_rates, matrix_decay
    )
    mlp_one, mlp_two, mlp_new = adam_step(
        mlp_grad, mlp_first, mlp_second, mlp_master, mlp_rates, matrix_decay
    )
    ssm_one, ssm_two, ssm_new = adam_step(
        ssm_grad, ssm_first, ssm_second, ssm_params, ssm_rates, 0.0
    )
    gain_first_new, gain_second_new, gains_new = adam_step(
        gains_grad, gains_first, gains_second, norm_gains, gain_rates, 0.0
    )
    return (
        block_out.reshape(tokens.shape),
        grad_tokens.reshape(tokens.shape),
        attn_grad,
        attn_one,
        attn_two,
        attn_new,
        attn_new.astype(bf16),
        mlp_grad,
        mlp_one,
        mlp_two,
        mlp_new,
        mlp_new.astype(bf16),
        ssm_grad,
        ssm_one,
        ssm_two,
        ssm_new,
        gains_grad,
        gain_first_new,
        gain_second_new,
        gains_new,
    )


def solution(mesh):
    in_specs = (
        P(None, "dp", "tensor"),
        P(None, "dp", "tensor"),
        P(None, "dp"),
        P(),
        P(None, "dp", "tensor"),
        P(None, "dp", "tensor"),
        P(None, "dp", "tensor"),
        P(None, "dp", "tensor"),
        P(None, "dp", "tensor"),
        P(None, "dp", "tensor"),
        P(None, "tensor", None),
        P(None, "tensor", None),
        P(None, "tensor", None),
        P(None, "tensor"),
        P(None, "tensor"),
        P(None, "tensor"),
    )
    out_specs = (
        P(None, "dp", "tensor"),
        P(None, "dp", "tensor"),
        P(None, "dp", "tensor"),
        P(None, "dp", "tensor"),
        P(None, "dp", "tensor"),
        P(None, "dp", "tensor"),
        P(None, "dp", "tensor"),
        P(None, "dp", "tensor"),
        P(None, "dp", "tensor"),
        P(None, "dp", "tensor"),
        P(None, "dp", "tensor"),
        P(None, "dp", "tensor"),
        P(None, "tensor", None),
        P(None, "tensor", None),
        P(None, "tensor", None),
        P(None, "tensor", None),
        P(None, "tensor"),
        P(None, "tensor"),
        P(None, "tensor"),
        P(None, "tensor"),
    )
    return jax.shard_map(body, mesh=mesh, in_specs=in_specs, out_specs=out_specs, check_vma=False)
```
